32 devices in a mesh: gx: 16 (over z, x, core), gy: 2 (over y).
Axes of the slice: x: 2, y: 2, z: 4, core: 2. Of those that a mesh axis runs over, the one named last changes fastest.
Arguments:
- flow_field: bfloat16 [64, 32, 64, 128], P('gx', 'gy'), may hold values from -6 to 6
- spectral_weight: bfloat16 [512, 64, 2, 64, 128], P(('gy', 'gx')), may hold values from -1 to 1
- conv_weight: bfloat16 [3, 3, 3, 128, 128], replicated, may hold values from -0.109375 to 0.109375
- channel_bias: float32 [128], replicated, may hold values from -3 to 3
Outputs:
- activated: bfloat16 [64, 32, 64, 128], P('gx', 'gy')
The draws below stay inside these ranges and needn't reach their ends.
All inputs are finite; a program needn't handle non-finite values.
Results may differ from the reference program's by a relative error of at most 0.018.
Values may be sent and summed in bfloat16 or wider, within the bound.
No kernel may reach another device: no remote copies, remote signals or barrier semaphores. Data moves between devices by JAX's collectives and lax.ppermute only.
A program may use at most 128 MiB of HBM per device.

```python
import math
import jax
import jax.numpy as jnp
from jax import lax

C = 128
MX = 64
MY = 16
MZ = 16
CZ = 64
NX = 64
NY = 32


def shard_levels(own_key, extent, shards, low, high):
    def one(dim, shards_of):
        steps = jax.random.uniform(jax.random.fold_in(jax.random.fold_in(own_key, 6), dim), (shards_of,), jnp.float32, low / len(shards), high / len(shards))
        return jnp.repeat(jnp.exp(steps), extent[dim] // shards_of).reshape((-1,) + (1,) * (len(extent) - dim - 1))

    factor_of = one(*shards[0])
    for cut in shards[1:]:
        factor_of = factor_of * one(*cut)
    return factor_of


def noise(stream_key, extent, spread, bound, split=(), kind=jnp.bfloat16):
    drawn = spread * jax.random.normal(stream_key, extent, jnp.float32)
    if split:
        drawn = drawn * shard_levels(stream_key, extent, split, -0.22, 0.18)
    return jnp.clip(drawn, -bound, bound).astype(kind)


def setup_inputs(seed: int = 0) -> dict:
    arg_keys = jax.random.split(jax.random.key(seed), 5)
    flow_field = noise(arg_keys[0], (NX, NY, CZ, C), 1.0, 6.0, ((0, 16), (1, 2)))
    spectral_weight = noise(arg_keys[1], (2 * MY * MZ, MX, 2, C // 2, C), (C // 4) ** -0.5, 1.0, ((0, 32),))
    conv_weight = noise(arg_keys[2], (3, 3, 3, C, C), (27 * C) ** -0.5, 0.109375)
    channel_bias = noise(arg_keys[3], (C,), 0.5, 3.0, (), jnp.float32)
    return {"flow_field": flow_field, "spectral_weight": spectral_weight, "conv_weight": conv_weight, "channel_bias": channel_bias}


def signed_modes(mode_count):
    position = jnp.arange(mode_count, dtype=jnp.int32)
    return jnp.where(position < mode_count // 2, position, position - mode_count)


def angle_grid(first, second, length):
    phase_turns = (first[:, None] * second[None, :]) % length
    return phase_turns.astype(jnp.float32) * (2.0 * math.pi / length)


def real_table(first, second, length, factor):
    angles = angle_grid(first, second, length)
    return jnp.stack([jnp.cos(angles) * factor, -jnp.sin(angles) * factor])


def complex_table(first, second, length, factor, direction):
    angles = angle_grid(first, second, length)
    cosine = jnp.cos(angles) * factor
    sine_part = jnp.sin(angles) * factor
    return jnp.stack([jnp.stack([cosine, direction * sine_part]), jnp.stack([-direction * sine_part, cosine])])


def reference(flow_field, spectral_weight, conv_weight, channel_bias):
    size_x, size_y, size_z, channels = flow_field.shape
    highest = lax.Precision.HIGHEST
    grid_x = jnp.arange(size_x, dtype=jnp.int32)
    grid_y = jnp.arange(size_y, dtype=jnp.int32)
    grid_z = jnp.arange(size_z, dtype=jnp.int32)
    modes_z = jnp.arange(MZ, dtype=jnp.int32)
    forward_z = real_table(grid_z, modes_z, size_z, size_z ** -0.5).astype(jnp.bfloat16).astype(jnp.float32)
    forward_y = complex_table(grid_y, signed_modes(MY), size_y, size_y ** -0.5, -1.0)
    forward_x = complex_table(grid_x, signed_modes(MX), size_x, size_x ** -0.5, -1.0)
    backward_x = complex_table(signed_modes(MX), grid_x, size_x, MX ** -0.5, 1.0)
    backward_y = complex_table(signed_modes(MY), grid_y, size_y, MY ** -0.5, 1.0)
    backward_z = real_table(modes_z, grid_z, size_z, MZ ** -0.5).astype(jnp.bfloat16).astype(jnp.float32)

    def plane_modes(plane):
        z_spectrum = jnp.einsum('yzc,pzk->pykc', plane.astype(jnp.float32), forward_z, precision=highest)
        return jnp.einsum('pykc,pqyj->qjkc', z_spectrum, forward_y, precision=highest)

    y_spectrum = lax.map(plane_modes, flow_field)
    x_spectrum = jnp.einsum('xpjkc,pqxm->qmjkc', y_spectrum, forward_x, precision=highest)
    x_input = x_spectrum.astype(jnp.bfloat16).astype(jnp.float32).reshape(2, MX, 2 * MY * MZ, channels // 2)
    products = jnp.einsum('pmjc,jmqco->pqmjo', x_input, spectral_weight.astype(jnp.float32), precision=highest)
    mixed_modes = jnp.stack([products[0, 0] - products[1, 1], products[0, 1] + products[1, 0]])
    mixed_modes = mixed_modes.reshape(2, MX, MY * MZ, 2, channels).sum(axis=3).reshape(2, MX, MY, MZ, channels)
    x_inverse = jnp.einsum('pmjkc,pqmx->xqjkc', mixed_modes, backward_x, precision=highest)
    padded = jnp.pad(flow_field, ((1, 1), (1, 1), (1, 1), (0, 0)))
    kernel = conv_weight.astype(jnp.float32).reshape(3, 3, 3 * channels, channels)

    def plane_out(pieces):
        coefficients, start = pieces
        y_inverse = jnp.einsum('pjkc,pqjy->qykc', coefficients, backward_y, precision=highest)
        y_inverse = y_inverse.astype(jnp.bfloat16).astype(jnp.float32)
        spectral = jnp.einsum('pykc,pkz->yzc', y_inverse, backward_z, precision=highest)
        slab = lax.dynamic_slice_in_dim(padded, start, 3, 0).astype(jnp.float32)
        stacked = jnp.concatenate([slab[:, :, 0:size_z], slab[:, :, 1:size_z + 1], slab[:, :, 2:size_z + 2]], axis=3)
        accumulated = jnp.zeros((size_y, size_z, channels), jnp.float32)
        for shift_x in range(3):
            for shift_y in range(3):
                accumulated = accumulated + jnp.dot(stacked[shift_x, shift_y:shift_y + size_y], kernel[shift_x, shift_y], precision=highest, preferred_element_type=jnp.float32)
        return jax.nn.gelu(spectral + accumulated + channel_bias, approximate=True).astype(jnp.bfloat16)

    return lax.map(plane_out, (x_inverse, jnp.arange(size_x, dtype=jnp.int32)))
```

```python
import functools
import math

import jax
import jax.numpy as jnp
import numpy as np
from jax import lax
from jax.experimental import pallas as pl
from jax.experimental.pallas import tpu as pltpu
from jax.sharding import PartitionSpec as P

MX = 64
MY = 16
MZ = 16


def frequencies(mode_count):
    position = np.arange(mode_count)
    return np.where(position < mode_count // 2, position, position - mode_count)


def wave(first, second, length, factor):
    turns = (np.asarray(first)[:, None] * np.asarray(second)[None, :]) % length
    angles = turns * (2.0 * math.pi / length)
    return (np.cos(angles) + 1j * np.sin(angles)) * factor


def rounded(values):
    return values.astype(np.float32).astype(jnp.bfloat16).astype(np.float64)


def item_modes(shards_x, shards_y, pairs):
    index = np.arange(shards_y * shards_x * pairs).reshape(shards_y, shards_x, pairs)
    return index // MZ, index % MZ


def forward_yz_table(shards_x, shards_y, pairs, cells_y, cells_z):
    full_y = shards_y * cells_y
    turn_z = wave(np.arange(MZ), np.arange(cells_z), cells_z, cells_z**-0.5)
    turn_z = rounded(turn_z.real) - 1j * rounded(turn_z.imag)
    turn_y = np.conj(wave(frequencies(MY), np.arange(full_y), full_y, full_y**-0.5))
    mode_y, mode_z = item_modes(shards_x, shards_y, pairs)
    table = np.empty(
        (shards_y, shards_y, shards_x, pairs, 2, cells_y, cells_z), np.float32
    )
    for own in range(shards_y):
        rows = turn_y[:, own * cells_y : (own + 1) * cells_y]
        for step in range(shards_y):
            owner = (own + step) % shards_y
            product = rows[mode_y[owner]][..., :, None] * turn_z[mode_z[owner]][..., None, :]
            table[own, step, :, :, 0] = product.real
            table[own, step, :, :, 1] = product.imag
    return table.reshape(
        shards_y, shards_y, shards_x * pairs * 2, cells_y * cells_z
    ).astype(jnp.bfloat16)


def backward_yz_table(shards_x, shards_y, pairs, cells_y, cells_z):
    full_y = shards_y * cells_y
    turn_z = wave(np.arange(MZ), np.arange(cells_z), cells_z, MZ**-0.5)
    turn_z = rounded(turn_z.real) + 1j * rounded(turn_z.imag)
    turn_y = wave(frequencies(MY), np.arange(full_y), full_y, MY**-0.5)
    mode_y, mode_z = item_modes(shards_x, shards_y, pairs)
    table = np.empty(
        (shards_y, shards_y, cells_y, cells_z, shards_x, pairs, 2), np.float32
    )
    for own in range(shards_y):
        rows = turn_y[:, own * cells_y : (own + 1) * cells_y]
        for step in range(shards_y):
            owner = (own - step) % shards_y
            product = rows[mode_y[owner]][..., :, None] * turn_z[mode_z[owner]][..., None, :]
            product = np.moveaxis(product, (2, 3), (0, 1))
            table[own, step, ..., 0] = product.real
            table[own, step, ..., 1] = -product.imag
    return table.reshape(
        shards_y, shards_y, cells_y * cells_z, shards_x * pairs * 2
    ).astype(jnp.bfloat16)


def forward_x_table(full_x, pairs):
    turn = np.conj(wave(frequencies(MX), np.arange(full_x), full_x, full_x**-0.5))
    parts = np.empty((2, MX, 2, full_x, pairs, 2), np.float32)
    cosine, sine = turn.real[:, :, None], turn.imag[:, :, None]
    parts[0, :, 0, :, :, 0], parts[0, :, 0, :, :, 1] = cosine, -sine
    parts[0, :, 1, :, :, 0], parts[0, :, 1, :, :, 1] = sine, cosine
    parts[1, :, 0] = -parts[0, :, 1]
    parts[1, :, 1] = parts[0, :, 0]
    return parts.reshape(2 * MX * 2, full_x * pairs * 2).astype(jnp.bfloat16)


def backward_x_table(full_x, pairs):
    turn = wave(frequencies(MX), np.arange(full_x), full_x, MX**-0.5).T
    parts = np.empty((full_x, pairs, 2, MX, 2), np.float32)
    cosine, sine = turn.real[:, None, :], turn.imag[:, None, :]
    parts[:, :, 0, :, 0], parts[:, :, 0, :, 1] = cosine, -sine
    parts[:, :, 1, :, 0], parts[:, :, 1, :, 1] = sine, cosine
    return parts.reshape(full_x * pairs * 2, MX * 2).astype(jnp.bfloat16)


def dot(left, right):
    return jnp.dot(left, right, preferred_element_type=jnp.float32)


def forward_kernel(own_ref, table_ref, flow_ref, out_ref):
    cells_x = flow_ref.shape[0]
    shards_x, _, rows, channels = out_ref.shape
    width = 2 if cells_x % 2 == 0 else 1
    for x in range(0, cells_x, width):
        columns = [flow_ref[x + i] for i in range(width)]
        result = dot(table_ref[0, 0], jnp.concatenate(columns, axis=1))
        for i in range(width):
            part = result[:, i * channels : (i + 1) * channels]
            out_ref[:, x + i] = part.astype(out_ref.dtype).reshape(shards_x, rows, channels)


def forward_yz(own_y, table, flow, step, shards_x):
    cells_x, positions, channels = flow.shape
    rows = table.shape[2]
    return pl.pallas_call(
        forward_kernel,
        grid_spec=pltpu.PrefetchScalarGridSpec(
            num_scalar_prefetch=1,
            grid=(1,),
            in_specs=[
                pl.BlockSpec((1, 1, rows, positions), lambda i, own: (own[0], step, 0, 0)),
                pl.BlockSpec((cells_x, positions, channels), lambda i, own: (0, 0, 0)),
            ],
            out_specs=pl.BlockSpec(
                (shards_x, cells_x, rows // shards_x, channels), lambda i, own: (0, 0, 0, 0)
            ),
        ),
        out_shape=jax.ShapeDtypeStruct(
            (shards_x, cells_x, rows // shards_x, channels), jnp.bfloat16
        ),
        compiler_params=pltpu.CompilerParams(vmem_limit_bytes=24 << 20),
        cost_estimate=pl.CostEstimate(
            flops=4 * rows * positions * cells_x * channels,
            bytes_accessed=2 * positions * (rows + cells_x * channels),
            transcendentals=0,
        ),
    )(own_y, table, flow)


def mixing_kernel(rows_ref, forward_ref, backward_ref, weight_ref, out_ref, left, mixed, total):
    pair = pl.program_id(0)
    pairs = pl.num_programs(0)
    spectrum_rows = mixed.shape[0]
    channels = rows_ref.shape[1]
    half = channels // 2

    def owned(shape, axis):
        index = lax.broadcasted_iota(jnp.int32, shape, axis)
        return lax.rem(lax.div(index, 2), out_ref.shape[1] // 2) == pair

    table = forward_ref[...]
    table = jnp.where(owned(table.shape, 1), table, jnp.zeros_like(table))
    both = dot(table, rows_ref[...])
    value, turned = both[:spectrum_rows], both[spectrum_rows:]
    low = lax.broadcasted_iota(jnp.int32, value.shape, 1) < half
    first = jnp.where(low, value, pltpu.roll(turned, half, axis=1))
    second = jnp.where(low, pltpu.roll(value, half, axis=1), turned)
    left[:, :channels] = first.astype(left.dtype)
    left[:, channels:] = second.astype(left.dtype)

    group = 16
    row = lax.broadcasted_iota(jnp.int32, (group, channels), 0) // 2

    def mix(step, carry):
        start = pl.multiple_of(step * group, group)
        lhs = left[pl.ds(start, group), :]
        gathered = jnp.zeros((group, channels), jnp.float32)
        for i in range(0, group // 2, 2):
            mode = step * (group // 2) + i
            tiles = [
                jnp.concatenate([weight_ref[0, mode + k], weight_ref[1, mode + k]], axis=0)
                for k in range(2)
            ]
            product = dot(lhs, jnp.concatenate(tiles, axis=1))
            for k in range(2):
                gathered = jnp.where(
                    row == i + k, product[:, k * channels : (k + 1) * channels], gathered
                )
        mixed[pl.ds(start, group), :] = gathered.astype(mixed.dtype)
        return carry

    lax.fori_loop(0, spectrum_rows // group, mix, 0)

    table = backward_ref[...]
    table = jnp.where(owned(table.shape, 0), table, jnp.zeros_like(table))
    added = dot(table, mixed[...])

    @pl.when(pair == 0)
    def _():
        total[...] = added

    @pl.when(pair > 0)
    def _():
        total[...] += added

    @pl.when(pair == pairs - 1)
    def _():
        out_ref[...] = total[...].reshape(out_ref.shape).astype(out_ref.dtype)


def mixing(rows, forward_x, backward_x, weight, pairs):
    row_count, channels = rows.shape
    full_x = row_count // (2 * pairs)
    depth = weight.shape[2]
    whole = lambda i: (0, 0)
    return pl.pallas_call(
        mixing_kernel,
        grid=(pairs,),
        in_specs=[
            pl.BlockSpec(rows.shape, whole),
            pl.BlockSpec(forward_x.shape, whole),
            pl.BlockSpec(backward_x.shape, whole),
            pl.BlockSpec((2, MX, depth, channels), lambda i: (i, 0, 0, 0)),
        ],
        out_specs=pl.BlockSpec((full_x, 2 * pairs, channels), lambda i: (0, 0, 0)),
        out_shape=jax.ShapeDtypeStruct((full_x, 2 * pairs, channels), jnp.bfloat16),
        scratch_shapes=[
            pltpu.VMEM((2 * MX, 2 * channels), jnp.bfloat16),
            pltpu.VMEM((2 * MX, channels), jnp.bfloat16),
            pltpu.VMEM((row_count, channels), jnp.float32),
        ],
        compiler_params=pltpu.CompilerParams(vmem_limit_bytes=40 << 20),
        cost_estimate=pl.CostEstimate(
            flops=8 * weight.size, bytes_accessed=2 * weight.size, transcendentals=0
        ),
    )(rows, forward_x, backward_x, weight)


def final_kernel(own_ref, table_ref, *refs):
    *coefficient_refs, convolved_ref, bias_ref, out_ref = refs
    cells_x, cells_y, cells_z, channels = out_ref.shape
    width = 2 if cells_x % 2 == 0 else 1
    bias = bias_ref[...]
    for x in range(0, cells_x, width):
        total = None
        for step, ref in enumerate(coefficient_refs):
            depth = ref.shape[0] * ref.shape[2]
            columns = [ref[:, x + i].reshape(depth, channels) for i in range(width)]
            product = dot(table_ref[0, step], jnp.concatenate(columns, axis=1))
            total = product if total is None else total + product
        for i in range(width):
            spectral = total[:, i * channels : (i + 1) * channels]
            spectral = spectral.reshape(cells_y, cells_z, channels)
            value = spectral + convolved_ref[x + i].astype(jnp.float32) + bias
            out_ref[x + i] = jax.nn.gelu(value, approximate=True).astype(out_ref.dtype)


def final(own_y, table, coefficients, convolved, bias):
    cells_x, cells_y, cells_z, channels = convolved.shape
    parts = 4 if cells_y % 4 == 0 else 1
    rows = cells_y // parts * cells_z
    block = (cells_x, cells_y // parts, cells_z, channels)
    depth = table.shape[3]
    return pl.pallas_call(
        final_kernel,
        grid_spec=pltpu.PrefetchScalarGridSpec(
            num_scalar_prefetch=1,
            grid=(parts,),
            in_specs=[
                pl.BlockSpec((1, table.shape[1], rows, depth), lambda i, own: (own[0], 0, i, 0)),
                *(pl.BlockSpec(c.shape, lambda i, own: (0, 0, 0, 0)) for c in coefficients),
                pl.BlockSpec(block, lambda i, own: (0, i, 0, 0)),
                pl.BlockSpec((1, channels), lambda i, own: (0, 0)),
            ],
            out_specs=pl.BlockSpec(block, lambda i, own: (0, i, 0, 0)),
        ),
        out_shape=jax.ShapeDtypeStruct(convolved.shape, jnp.bfloat16),
        compiler_params=pltpu.CompilerParams(vmem_limit_bytes=24 << 20),
        cost_estimate=pl.CostEstimate(
            flops=2 * table.shape[1] * table.shape[2] * depth * cells_x * channels,
            bytes_accessed=6 * convolved.size,
            transcendentals=convolved.size,
        ),
    )(own_y, table, *coefficients, convolved, bias)


def convolution_kernel(
    own_ref, flow_ref, left_ref, right_ref, front_ref, back_ref, weight_ref, out_ref, stacked
):
    cells_x, cells_y, cells_z, channels = flow_ref.shape
    shards_y = own_ref[1]
    own_y = own_ref[0]
    z = lax.broadcasted_iota(jnp.int32, (cells_z, channels), 0)

    def place(x, y, cells):
        wide = cells.astype(jnp.float32)
        before = jnp.where(z == 0, 0.0, pltpu.roll(wide, 1, axis=0))
        after = jnp.where(z == cells_z - 1, 0.0, pltpu.roll(wide, cells_z - 1, axis=0))
        stacked[x, y, :, :channels] = before.astype(stacked.dtype)
        stacked[x, y, :, channels : 2 * channels] = cells
        stacked[x, y, :, 2 * channels :] = after.astype(stacked.dtype)

    def inner(x, read):
        def one(y, carry):
            place(x, y + 1, read(y))
            return carry

        lax.fori_loop(0, cells_y, one, 0, unroll=2)

    inner(0, lambda y: left_ref[0, y])
    inner(cells_x + 1, lambda y: right_ref[0, y])
    for x in range(cells_x):
        inner(x + 1, lambda y, x=x: flow_ref[x, y])

    blank = jnp.zeros((cells_x + 2, cells_z, 3 * channels), stacked.dtype)

    @pl.when(own_y > 0)
    def _():
        for x in range(cells_x + 2):
            place(x, 0, front_ref[x, 0])

    @pl.when(own_y == 0)
    def _():
        stacked[:, 0] = blank

    @pl.when(own_y < shards_y - 1)
    def _():
        for x in range(cells_x + 2):
            place(x, cells_y + 1, back_ref[x, 0])

    @pl.when(own_y == shards_y - 1)
    def _():
        stacked[:, cells_y + 1] = blank

    rows = 4 if cells_y % 4 == 0 else 1

    def chunk(index, carry):
        x = index // (cells_y // rows)
        y = index % (cells_y // rows) * rows
        total = jnp.zeros((rows * cells_z, channels), jnp.float32)
        for a in range(3):
            for b in range(3):
                block = stacked[x + a, pl.ds(y + b, rows)]
                total = total + dot(block.reshape(rows * cells_z, 3 * channels), weight_ref[a, b])
        out_ref[x, pl.ds(y, rows)] = total.reshape(rows, cells_z, channels).astype(out_ref.dtype)
        return carry

    lax.fori_loop(0, cells_x * (cells_y // rows), chunk, 0)


def convolution(own_y, shards_y, flow, left, right, front, back, weight):
    cells_x, cells_y, cells_z, channels = flow.shape
    scalars = jnp.concatenate([own_y, jnp.full((1,), shards_y, jnp.int32)])
    vmem = pl.BlockSpec(memory_space=pltpu.VMEM)
    return pl.pallas_call(
        convolution_kernel,
        in_specs=[pl.BlockSpec(memory_space=pltpu.SMEM)] + [vmem] * 6,
        out_specs=vmem,
        out_shape=jax.ShapeDtypeStruct(flow.shape, jnp.bfloat16),
        scratch_shapes=[
            pltpu.VMEM((cells_x + 2, cells_y + 2, cells_z, 3 * channels), jnp.bfloat16)
        ],
        compiler_params=pltpu.CompilerParams(vmem_limit_bytes=24 << 20),
        cost_estimate=pl.CostEstimate(
            flops=2 * 2 * flow.size * 27 * channels,
            bytes_accessed=6 * flow.size,
            transcendentals=0,
        ),
    )(scalars, flow, left, right, front, back, weight)


def signed_modes(mode_count):
    position = jnp.arange(mode_count, dtype=jnp.int32)
    return jnp.where(position < mode_count // 2, position, position - mode_count)


def angle_grid(first, second, length):
    phase_turns = first[:, None] * second[None, :] % length
    return phase_turns.astype(jnp.float32) * (2.0 * math.pi / length)


def real_table(first, second, length, factor):
    angles = angle_grid(first, second, length)
    return jnp.stack([jnp.cos(angles) * factor, -jnp.sin(angles) * factor])


def complex_table(first, second, length, factor, direction):
    angles = angle_grid(first, second, length)
    cosine = jnp.cos(angles) * factor
    sine_part = jnp.sin(angles) * factor
    return jnp.stack(
        [jnp.stack([cosine, direction * sine_part]), jnp.stack([-direction * sine_part, cosine])]
    )


def split_pair_spectral(flow_field, spectral_weight):
    highest = lax.Precision.HIGHEST
    cells_x, cells_y, cells_z, channels = flow_field.shape
    count_x = lax.axis_size("gx")
    count_y = lax.axis_size("gy")
    full_x = cells_x * count_x
    full_y = cells_y * count_y
    item_count = spectral_weight.shape[0]
    local_y = lax.axis_index("gy") * cells_y + jnp.arange(cells_y, dtype=jnp.int32)
    grid_x = jnp.arange(full_x, dtype=jnp.int32)
    grid_z = jnp.arange(cells_z, dtype=jnp.int32)
    modes_z = jnp.arange(MZ, dtype=jnp.int32)
    forward_z = real_table(grid_z, modes_z, cells_z, cells_z ** (-0.5)).astype(jnp.bfloat16)
    z_spectrum = jnp.einsum(
        "xyzc,pzk->pxykc", flow_field, forward_z, preferred_element_type=jnp.float32
    )
    columns = lax.all_to_all(
        z_spectrum.astype(jnp.bfloat16), "gy", split_axis=4, concat_axis=2, tiled=True
    ).astype(z_spectrum.dtype)
    whole_y = jnp.arange(full_y, dtype=jnp.int32)
    forward_full = complex_table(whole_y, signed_modes(MY), full_y, full_y ** (-0.5), -1.0)
    y_spectrum = jnp.einsum("pxykc,pqyj->qxjkc", columns, forward_full, precision=highest)
    owned = lax.all_to_all(
        y_spectrum.astype(jnp.bfloat16), "gy", split_axis=2, concat_axis=4, tiled=True
    ).astype(y_spectrum.dtype)
    owned_modes = owned.reshape(2, cells_x, count_x, item_count, channels // 2)
    gathered_rows = lax.all_to_all(
        owned_modes.astype(jnp.bfloat16), "gx", split_axis=2, concat_axis=1, tiled=True
    ).astype(owned_modes.dtype)
    gathered_rows = gathered_rows.reshape(2, full_x, item_count, channels // 2)
    forward_x = complex_table(grid_x, signed_modes(MX), full_x, full_x ** (-0.5), -1.0)
    x_spectrum = jnp.einsum("pxjc,pqxm->qmjc", gathered_rows, forward_x, precision=highest).astype(
        jnp.bfloat16
    )
    products = jnp.einsum(
        "pmjc,jmqco->pqmjo", x_spectrum, spectral_weight, preferred_element_type=jnp.float32
    )
    mixed_modes = jnp.stack([products[0, 0] - products[1, 1], products[0, 1] + products[1, 0]])
    backward_x = complex_table(signed_modes(MX), grid_x, full_x, MX ** (-0.5), 1.0)
    inverse_x = jnp.einsum("pmjc,pqmx->qxjc", mixed_modes, backward_x, precision=highest)
    inverse_x = inverse_x.reshape(2, full_x, 1, item_count, channels)
    returned = lax.all_to_all(
        inverse_x.astype(jnp.bfloat16), "gx", split_axis=1, concat_axis=2, tiled=True
    ).astype(inverse_x.dtype)
    band_rows = MY // count_y
    summed = returned.reshape(2, cells_x, band_rows * MZ, 2, channels).sum(axis=3)
    summed = summed.reshape(2, cells_x, band_rows, MZ, channels)
    coefficients = lax.all_gather(summed.astype(jnp.bfloat16), "gy", axis=2, tiled=True).astype(
        summed.dtype
    )
    backward_y = complex_table(signed_modes(MY), local_y, full_y, MY ** (-0.5), 1.0)
    y_inverse = jnp.einsum("pxjkc,pqjy->qxykc", coefficients, backward_y, precision=highest).astype(
        jnp.bfloat16
    )
    backward_z = real_table(modes_z, grid_z, cells_z, MZ ** (-0.5)).astype(jnp.bfloat16)
    return jnp.einsum("pxykc,pkz->xyzc", y_inverse, backward_z, preferred_element_type=jnp.float32)


def edges(first, last, axis):
    size = lax.axis_size(axis)
    if size == 2:
        facing = jnp.where(lax.axis_index(axis) == 0, last, first)
        arrived = lax.ppermute(facing, axis, [(0, 1), (1, 0)])
        return arrived, arrived
    up = [(i, i + 1) for i in range(size - 1)]
    down = [(i + 1, i) for i in range(size - 1)]
    return lax.ppermute(last, axis, up), lax.ppermute(first, axis, down)


def convolve(own_y, flow, weight):
    shards_y = lax.axis_size("gy")
    channels = flow.shape[3]
    left, right = edges(flow[:1], flow[-1:], "gx")
    rows = [jnp.concatenate([left[:, i], flow[:, i], right[:, i]])[:, None] for i in (0, -1)]
    front, back = edges(rows[0], rows[1], "gy")
    kernel = weight.reshape(3, 3, 3 * channels, channels)
    return convolution(own_y, shards_y, flow, left, right, front, back, kernel)


def shifted(size, step):
    return [(i, (i + step) % size) for i in range(size)]


def body(flow, spectral_weight, conv_weight, bias):
    cells_x, cells_y, cells_z, channels = flow.shape
    shards_x, shards_y = lax.axis_size("gx"), lax.axis_size("gy")
    items = spectral_weight.shape[0]
    pairs = items // 2
    own_y = lax.axis_index("gy").astype(jnp.int32).reshape(1)
    if items % 2:
        spectral = split_pair_spectral(flow, spectral_weight)
        convolved = convolve(own_y, flow, conv_weight).astype(jnp.float32)
        return jax.nn.gelu(spectral + convolved + bias, approximate=True).astype(jnp.bfloat16)
    sizes = (shards_x, shards_y, pairs, cells_y, cells_z)
    full_x = cells_x * shards_x

    table = jnp.asarray(forward_yz_table(*sizes))
    columns = flow.reshape(cells_x, cells_y * cells_z, channels)
    sent = [
        lax.ppermute(
            forward_yz(own_y, table, columns, step, shards_x), "gy", shifted(shards_y, step)
        )
        for step in range(1, shards_y)
    ]
    total = forward_yz(own_y, table, columns, 0, shards_x).astype(jnp.float32)
    for part in sent:
        total = total + part.astype(jnp.float32)
    rows = lax.all_to_all(total.astype(jnp.bfloat16), "gx", 0, 0, tiled=True)

    convolved = convolve(own_y, flow, conv_weight)

    weight = spectral_weight.reshape(items, MX, channels, channels)
    returned = mixing(
        rows.reshape(full_x * 2 * pairs, channels),
        jnp.asarray(forward_x_table(full_x, pairs)),
        jnp.asarray(backward_x_table(full_x, pairs)),
        weight,
        pairs,
    )
    returned = returned.reshape(shards_x, cells_x, 2 * pairs, channels)
    returned = lax.all_to_all(returned, "gx", 0, 0, tiled=True)
    coefficients = [returned] + [
        lax.ppermute(returned, "gy", shifted(shards_y, step)) for step in range(1, shards_y)
    ]
    return final(
        own_y,
        jnp.asarray(backward_yz_table(*sizes)),
        coefficients,
        convolved,
        bias.reshape(1, channels),
    )


def solution(mesh):
    placed = (P("gx", "gy", None, None), P(("gy", "gx"), None, None, None, None), P(), P())
    return jax.shard_map(
        body, mesh=mesh, in_specs=placed, out_specs=P("gx", "gy", None, None), check_vma=False
    )
```

```python
import functools
import math

import jax
import jax.numpy as jnp
import numpy as np
from jax import lax
from jax.experimental import pallas as pl
from jax.experimental.pallas import tpu as pltpu
from jax.sharding import PartitionSpec as P

MX = 64
MY = 16
MZ = 16


def frequencies(mode_count):
    position = np.arange(mode_count)
    return np.where(position < mode_count // 2, position, position - mode_count)


def wave(first, second, length, factor):
    turns = (np.asarray(first)[:, None] * np.asarray(second)[None, :]) % length
    angles = turns * (2.0 * math.pi / length)
    return (np.cos(angles) + 1j * np.sin(angles)) * factor


def rounded(values):
    return values.astype(np.float32).astype(jnp.bfloat16).astype(np.float64)


def item_modes(shards_x, shards_y, pairs):
    index = np.arange(shards_y * shards_x * pairs).reshape(shards_y, shards_x, pairs)
    return index // MZ, index % MZ


def forward_yz_table(shards_x, shards_y, pairs, cells_y, cells_z):
    full_y = shards_y * cells_y
    turn_z = wave(np.arange(MZ), np.arange(cells_z), cells_z, cells_z**-0.5)
    turn_z = rounded(turn_z.real) - 1j * rounded(turn_z.imag)
    turn_y = np.conj(wave(frequencies(MY), np.arange(full_y), full_y, full_y**-0.5))
    mode_y, mode_z = item_modes(shards_x, shards_y, pairs)
    table = np.empty(
        (shards_y, shards_y, shards_x, pairs, 2, cells_y, cells_z), np.float32
    )
    for own in range(shards_y):
        rows = turn_y[:, own * cells_y : (own + 1) * cells_y]
        for step in range(shards_y):
            owner = (own + step) % shards_y
            product = rows[mode_y[owner]][..., :, None] * turn_z[mode_z[owner]][..., None, :]
            table[own, step, :, :, 0] = product.real
            table[own, step, :, :, 1] = product.imag
    return table.reshape(
        shards_y, shards_y, shards_x * pairs * 2, cells_y * cells_z
    ).astype(jnp.bfloat16)


def backward_yz_table(shards_x, shards_y, pairs, cells_y, cells_z):
    full_y = shards_y * cells_y
    turn_z = wave(np.arange(MZ), np.arange(cells_z), cells_z, MZ**-0.5)
    turn_z = rounded(turn_z.real) + 1j * rounded(turn_z.imag)
    turn_y = wave(frequencies(MY), np.arange(full_y), full_y, MY**-0.5)
    mode_y, mode_z = item_modes(shards_x, shards_y, pairs)
    table = np.empty(
        (shards_y, shards_y, cells_y, cells_z, shards_x, pairs, 2), np.float32
    )
    for own in range(shards_y):
        rows = turn_y[:, own * cells_y : (own + 1) * cells_y]
        for step in range(shards_y):
            owner = (own - step) % shards_y
            product = rows[mode_y[owner]][..., :, None] * turn_z[mode_z[owner]][..., None, :]
            product = np.moveaxis(product, (2, 3), (0, 1))
            table[own, step, ..., 0] = product.real
            table[own, step, ..., 1] = -product.imag
    return table.reshape(
        shards_y, shards_y, cells_y * cells_z, shards_x * pairs * 2
    ).astype(jnp.bfloat16)


def forward_x_table(full_x):
    turn = np.conj(wave(frequencies(MX), np.arange(full_x), full_x, full_x**-0.5))
    parts = np.empty((2, MX, 2, 2, full_x), np.float32)
    parts[0, :, 0, 0], parts[0, :, 0, 1] = turn.real, -turn.imag
    parts[0, :, 1, 0], parts[0, :, 1, 1] = turn.imag, turn.real
    parts[1, :, 0] = -parts[0, :, 1]
    parts[1, :, 1] = parts[0, :, 0]
    return parts.reshape(2 * MX * 2, 2 * full_x).astype(jnp.bfloat16)


def backward_x_table(full_x):
    turn = wave(frequencies(MX), np.arange(full_x), full_x, MX**-0.5).T
    parts = np.empty((2, full_x, MX, 2), np.float32)
    parts[0, :, :, 0], parts[0, :, :, 1] = turn.real, -turn.imag
    parts[1, :, :, 0], parts[1, :, :, 1] = turn.imag, turn.real
    return parts.reshape(2 * full_x, MX * 2).astype(jnp.bfloat16)


def dot(left, right):
    return jnp.dot(left, right, preferred_element_type=jnp.float32)


def forward_parts(table_ref, flow_ref, shape):
    cells_x = flow_ref.shape[0]
    shards_x, _, rows, channels = shape
    width = 2 if cells_x % 2 == 0 else 1
    for x in range(0, cells_x, width):
        columns = [flow_ref[x + i] for i in range(width)]
        result = dot(table_ref[0, 0], jnp.concatenate(columns, axis=1))
        for i in range(width):
            part = result[:, i * channels : (i + 1) * channels]
            yield x + i, part.reshape(shards_x, rows, channels)


def send_kernel(own_ref, table_ref, flow_ref, out_ref, *edge_refs):
    for x, part in forward_parts(table_ref, flow_ref, out_ref.shape):
        out_ref[:, x] = part.astype(out_ref.dtype)
    for ref, x in zip(edge_refs, (0, flow_ref.shape[0] - 1)):
        ref[...] = flow_ref[x]


def keep_kernel(own_ref, table_ref, flow_ref, *refs):
    *arrived_refs, out_ref = refs
    for x, part in forward_parts(table_ref, flow_ref, out_ref.shape):
        for ref in arrived_refs:
            part = part + ref[:, x].astype(jnp.float32)
        out_ref[:, x] = part.astype(out_ref.dtype)


def forward_yz(own_y, table, flow, step, shards_x, arrived=(), edges=False):
    cells_x, positions, channels = flow.shape
    rows = table.shape[2]
    shape = (shards_x, cells_x, rows // shards_x, channels)
    shapes = [jax.ShapeDtypeStruct(shape, jnp.bfloat16)]
    if edges:
        shapes += [jax.ShapeDtypeStruct((positions, channels), flow.dtype)] * 2
    whole = lambda dims: pl.BlockSpec(dims, lambda i, own: (0,) * len(dims))
    limit = {} if edges else {"vmem_limit_bytes": 24 << 20}
    return pl.pallas_call(
        keep_kernel if arrived else send_kernel,
        grid_spec=pltpu.PrefetchScalarGridSpec(
            num_scalar_prefetch=1,
            grid=(1,),
            in_specs=[
                pl.BlockSpec((1, 1, rows, positions), lambda i, own: (own[0], step, 0, 0)),
                whole(flow.shape),
                *(whole(part.shape) for part in arrived),
            ],
            out_specs=[whole(one.shape) for one in shapes],
        ),
        out_shape=shapes,
        compiler_params=pltpu.CompilerParams(**limit),
        cost_estimate=pl.CostEstimate(
            flops=4 * rows * positions * cells_x * channels,
            bytes_accessed=2 * positions * (rows + cells_x * channels),
            transcendentals=0,
        ),
    )(own_y, table, flow, *arrived)


def mixing_kernel(
    rows_ref, forward_ref, backward_ref, weight_ref, out_ref, held, sems, wide, left, mixed
):
    slots, _, modes, _, channels = held.shape
    pairs = weight_ref.shape[0] // 2
    full_x = rows_ref.shape[0] // (2 * pairs)
    half = channels // 2
    parts = MX // modes
    chunks = pairs * parts
    span = 2 * MX

    def copy(chunk):
        slot = lax.rem(chunk, slots)
        pair, part = lax.div(chunk, parts), lax.rem(chunk, parts)
        return pltpu.make_async_copy(
            weight_ref.at[pl.ds(2 * pair, 2), pl.ds(part * modes, modes)],
            held.at[slot],
            sems.at[slot],
        )

    for chunk in range(min(slots, chunks)):
        copy(chunk).start()

    wide[...] = rows_ref[...].astype(jnp.float32)
    low = lax.broadcasted_iota(jnp.int32, (span, channels), 1) < half
    for pair in range(pairs):
        columns = [wide[pl.ds(2 * pair + p, full_x, stride=2 * pairs), :] for p in range(2)]
        columns = jnp.concatenate(columns, axis=0).astype(jnp.bfloat16)
        both = dot(forward_ref[...], columns)
        value, turned = both[:span], both[span:]
        first = jnp.where(low, value, pltpu.roll(turned, half, axis=1))
        second = jnp.where(low, pltpu.roll(value, half, axis=1), turned)
        left[pl.ds(pair * span, span), :channels] = first.astype(left.dtype)
        left[pl.ds(pair * span, span), channels:] = second.astype(left.dtype)

    group = 16
    row = lax.broadcasted_iota(jnp.int32, (group, channels), 0) // 2

    def mix(chunk, carry):
        slot = lax.rem(chunk, slots)
        copy(chunk).wait()
        for step in range(2 * modes // group):
            start = pl.multiple_of(chunk * 2 * modes + step * group, group)
            lhs = left[pl.ds(start, group), :]
            gathered = jnp.zeros((group, channels), jnp.float32)
            for i in range(0, group // 2, 2):
                mode = step * (group // 2) + i
                tiles = [
                    jnp.concatenate([held[slot, 0, mode + k], held[slot, 1, mode + k]], axis=0)
                    for k in range(2)
                ]
                product = dot(lhs, jnp.concatenate(tiles, axis=1))
                for k in range(2):
                    gathered = jnp.where(
                        row == i + k, product[:, k * channels : (k + 1) * channels], gathered
                    )
            mixed[pl.ds(start, group), :] = gathered.astype(mixed.dtype)

        @pl.when(chunk + slots < chunks)
        def _():
            copy(chunk + slots).start()

        return carry

    lax.fori_loop(0, chunks, mix, 0)

    for pair in range(pairs):
        result = dot(backward_ref[...], mixed[pl.ds(pair * span, span), :])
        for p in range(2):
            wide[pl.ds(2 * pair + p, full_x, stride=2 * pairs), :] = result[
                p * full_x : (p + 1) * full_x
            ]
    out_ref[...] = wide[...].astype(out_ref.dtype)


def mixing(rows, forward_x, backward_x, weight):
    row_count, channels = rows.shape
    depth = weight.shape[2]
    pairs = weight.shape[0] // 2
    slots, modes = 4, MX // 2
    vmem = pl.BlockSpec(memory_space=pltpu.VMEM)
    return pl.pallas_call(
        mixing_kernel,
        in_specs=[vmem, vmem, vmem, pl.BlockSpec(memory_space=pl.ANY)],
        out_specs=vmem,
        out_shape=jax.ShapeDtypeStruct(rows.shape, jnp.bfloat16),
        scratch_shapes=[
            pltpu.VMEM((slots, 2, modes, depth, channels), jnp.bfloat16),
            pltpu.SemaphoreType.DMA((slots,)),
            pltpu.VMEM((row_count, channels), jnp.float32),
            pltpu.VMEM((pairs * 2 * MX, 2 * channels), jnp.bfloat16),
            pltpu.VMEM((pairs * 2 * MX, channels), jnp.bfloat16),
        ],
        compiler_params=pltpu.CompilerParams(vmem_limit_bytes=40 << 20),
        cost_estimate=pl.CostEstimate(
            flops=8 * weight.size, bytes_accessed=2 * weight.size, transcendentals=0
        ),
    )(rows, forward_x, backward_x, weight)


def final_kernel(own_ref, table_ref, *refs):
    *coefficient_refs, convolved_ref, bias_ref, out_ref = refs
    cells_x, cells_y, cells_z, channels = out_ref.shape
    width = 2 if cells_x % 2 == 0 else 1
    bias = bias_ref[...]
    for x in range(0, cells_x, width):
        total = None
        for step, ref in enumerate(coefficient_refs):
            depth = ref.shape[0] * ref.shape[2]
            columns = [ref[:, x + i].reshape(depth, channels) for i in range(width)]
            product = dot(table_ref[0, step], jnp.concatenate(columns, axis=1))
            total = product if total is None else total + product
        for i in range(width):
            spectral = total[:, i * channels : (i + 1) * channels]
            spectral = spectral.reshape(cells_y, cells_z, channels)
            value = spectral + convolved_ref[x + i].astype(jnp.float32) + bias
            out_ref[x + i] = jax.nn.gelu(value, approximate=True).astype(out_ref.dtype)


def final(own_y, table, coefficients, convolved, bias):
    cells_x, cells_y, cells_z, channels = convolved.shape
    parts = 4 if cells_y % 4 == 0 else 1
    rows = cells_y // parts * cells_z
    block = (cells_x, cells_y // parts, cells_z, channels)
    depth = table.shape[3]
    return pl.pallas_call(
        final_kernel,
        grid_spec=pltpu.PrefetchScalarGridSpec(
            num_scalar_prefetch=1,
            grid=(parts,),
            in_specs=[
                pl.BlockSpec((1, table.shape[1], rows, depth), lambda i, own: (own[0], 0, i, 0)),
                *(pl.BlockSpec(c.shape, lambda i, own: (0, 0, 0, 0)) for c in coefficients),
                pl.BlockSpec(block, lambda i, own: (0, i, 0, 0)),
                pl.BlockSpec((1, channels), lambda i, own: (0, 0)),
            ],
            out_specs=pl.BlockSpec(block, lambda i, own: (0, i, 0, 0)),
        ),
        out_shape=jax.ShapeDtypeStruct(convolved.shape, jnp.bfloat16),
        compiler_params=pltpu.CompilerParams(vmem_limit_bytes=24 << 20),
        cost_estimate=pl.CostEstimate(
            flops=2 * table.shape[1] * table.shape[2] * depth * cells_x * channels,
            bytes_accessed=6 * convolved.size,
            transcendentals=convolved.size,
        ),
    )(own_y, table, *coefficients, convolved, bias)


def convolution_kernel(
    own_ref, flow_ref, left_ref, right_ref, front_ref, back_ref, weight_ref, out_ref, stacked
):
    cells_x, cells_y, cells_z, channels = flow_ref.shape
    shards_y = own_ref[1]
    own_y = own_ref[0]

    def place(x, y, cells):
        wide = cells.astype(jnp.float32)
        count = cells.shape[0]
        z = lax.broadcasted_iota(jnp.int32, wide.shape, 1)
        before = jnp.where(z == 0, 0.0, pltpu.roll(wide, 1, axis=1))
        after = jnp.where(z == cells_z - 1, 0.0, pltpu.roll(wide, cells_z - 1, axis=1))
        stacked[x, pl.ds(y, count), :, :channels] = before.astype(stacked.dtype)
        stacked[x, pl.ds(y, count), :, channels : 2 * channels] = cells
        stacked[x, pl.ds(y, count), :, 2 * channels :] = after.astype(stacked.dtype)

    rows = 4 if cells_y % 4 == 0 else 1

    def inner(x, read):
        def one(step, carry):
            place(x, step * rows + 1, read(pl.ds(step * rows, rows)))
            return carry

        lax.fori_loop(0, cells_y // rows, one, 0)

    inner(0, lambda y: left_ref[0, y])
    inner(cells_x + 1, lambda y: right_ref[0, y])
    for x in range(cells_x):
        inner(x + 1, lambda y, x=x: flow_ref[x, y])

    blank = jnp.zeros((cells_x + 2, cells_z, 3 * channels), stacked.dtype)

    @pl.when(own_y > 0)
    def _():
        for x in range(cells_x + 2):
            place(x, 0, front_ref[x])

    @pl.when(own_y == 0)
    def _():
        stacked[:, 0] = blank

    @pl.when(own_y < shards_y - 1)
    def _():
        for x in range(cells_x + 2):
            place(x, cells_y + 1, back_ref[x])

    @pl.when(own_y == shards_y - 1)
    def _():
        stacked[:, cells_y + 1] = blank

    width = 2 if cells_x % 2 == 0 else 1
    taps = [(a, b) for a in range(width + 2) for b in range(3)]
    none = jnp.zeros(weight_ref.shape[2:], weight_ref.dtype)

    def kernel_of(a, b):
        return jnp.concatenate(
            [weight_ref[a - i, b] if 0 <= a - i < 3 else none for i in range(width)], axis=1
        )

    def chunk(index, carry):
        x = lax.div(index, cells_y // rows) * width
        y = lax.rem(index, cells_y // rows) * rows
        total = jnp.zeros((rows * cells_z, width * channels), jnp.float32)
        for i in range(0, len(taps), width):
            group = taps[i : i + width]
            blocks = [
                stacked[x + a, pl.ds(y + b, rows)].reshape(rows * cells_z, 3 * channels)
                for a, b in group
            ]
            weights = [kernel_of(a, b) for a, b in group]
            total = total + dot(
                jnp.concatenate(blocks, axis=1), jnp.concatenate(weights, axis=0)
            )
        for i in range(width):
            part = total[:, i * channels : (i + 1) * channels].reshape(rows, cells_z, channels)
            out_ref[x + i, pl.ds(y, rows)] = part.astype(out_ref.dtype)
        return carry

    lax.fori_loop(0, cells_x // width * (cells_y // rows), chunk, 0)


def convolution(own_y, shards_y, flow, left, right, front, back, weight):
    cells_x, cells_y, cells_z, channels = flow.shape
    scalars = jnp.concatenate([own_y, jnp.full((1,), shards_y, jnp.int32)])
    vmem = pl.BlockSpec(memory_space=pltpu.VMEM)
    return pl.pallas_call(
        convolution_kernel,
        in_specs=[pl.BlockSpec(memory_space=pltpu.SMEM)] + [vmem] * 6,
        out_specs=vmem,
        out_shape=jax.ShapeDtypeStruct(flow.shape, jnp.bfloat16),
        scratch_shapes=[
            pltpu.VMEM((cells_x + 2, cells_y + 2, cells_z, 3 * channels), jnp.bfloat16)
        ],
        compiler_params=pltpu.CompilerParams(vmem_limit_bytes=24 << 20),
        cost_estimate=pl.CostEstimate(
            flops=2 * 2 * flow.size * 27 * channels,
            bytes_accessed=6 * flow.size,
            transcendentals=0,
        ),
    )(scalars, flow, left, right, front, back, weight)


def signed_modes(mode_count):
    position = jnp.arange(mode_count, dtype=jnp.int32)
    return jnp.where(position < mode_count // 2, position, position - mode_count)


def angle_grid(first, second, length):
    phase_turns = first[:, None] * second[None, :] % length
    return phase_turns.astype(jnp.float32) * (2.0 * math.pi / length)


def real_table(first, second, length, factor):
    angles = angle_grid(first, second, length)
    return jnp.stack([jnp.cos(angles) * factor, -jnp.sin(angles) * factor])


def complex_table(first, second, length, factor, direction):
    angles = angle_grid(first, second, length)
    cosine = jnp.cos(angles) * factor
    sine_part = jnp.sin(angles) * factor
    return jnp.stack(
        [jnp.stack([cosine, direction * sine_part]), jnp.stack([-direction * sine_part, cosine])]
    )


def split_pair_spectral(flow_field, spectral_weight):
    highest = lax.Precision.HIGHEST
    cells_x, cells_y, cells_z, channels = flow_field.shape
    count_x = lax.axis_size("gx")
    count_y = lax.axis_size("gy")
    full_x = cells_x * count_x
    full_y = cells_y * count_y
    item_count = spectral_weight.shape[0]
    local_y = lax.axis_index("gy") * cells_y + jnp.arange(cells_y, dtype=jnp.int32)
    grid_x = jnp.arange(full_x, dtype=jnp.int32)
    grid_z = jnp.arange(cells_z, dtype=jnp.int32)
    modes_z = jnp.arange(MZ, dtype=jnp.int32)
    forward_z = real_table(grid_z, modes_z, cells_z, cells_z ** (-0.5)).astype(jnp.bfloat16)
    z_spectrum = jnp.einsum(
        "xyzc,pzk->pxykc", flow_field, forward_z, preferred_element_type=jnp.float32
    )
    columns = lax.all_to_all(
        z_spectrum.astype(jnp.bfloat16), "gy", split_axis=4, concat_axis=2, tiled=True
    ).astype(z_spectrum.dtype)
    whole_y = jnp.arange(full_y, dtype=jnp.int32)
    forward_full = complex_table(whole_y, signed_modes(MY), full_y, full_y ** (-0.5), -1.0)
    y_spectrum = jnp.einsum("pxykc,pqyj->qxjkc", columns, forward_full, precision=highest)
    owned = lax.all_to_all(
        y_spectrum.astype(jnp.bfloat16), "gy", split_axis=2, concat_axis=4, tiled=True
    ).astype(y_spectrum.dtype)
    owned_modes = owned.reshape(2, cells_x, count_x, item_count, channels // 2)
    gathered_rows = lax.all_to_all(
        owned_modes.astype(jnp.bfloat16), "gx", split_axis=2, concat_axis=1, tiled=True
    ).astype(owned_modes.dtype)
    gathered_rows = gathered_rows.reshape(2, full_x, item_count, channels // 2)
    forward_x = complex_table(grid_x, signed_modes(MX), full_x, full_x ** (-0.5), -1.0)
    x_spectrum = jnp.einsum("pxjc,pqxm->qmjc", gathered_rows, forward_x, precision=highest).astype(
        jnp.bfloat16
    )
    products = jnp.einsum(
        "pmjc,jmqco->pqmjo", x_spectrum, spectral_weight, preferred_element_type=jnp.float32
    )
    mixed_modes = jnp.stack([products[0, 0] - products[1, 1], products[0, 1] + products[1, 0]])
    backward_x = complex_table(signed_modes(MX), grid_x, full_x, MX ** (-0.5), 1.0)
    inverse_x = jnp.einsum("pmjc,pqmx->qxjc", mixed_modes, backward_x, precision=highest)
    inverse_x = inverse_x.reshape(2, full_x, 1, item_count, channels)
    returned = lax.all_to_all(
        inverse_x.astype(jnp.bfloat16), "gx", split_axis=1, concat_axis=2, tiled=True
    ).astype(inverse_x.dtype)
    band_rows = MY // count_y
    summed = returned.reshape(2, cells_x, band_rows * MZ, 2, channels).sum(axis=3)
    summed = summed.reshape(2, cells_x, band_rows, MZ, channels)
    coefficients = lax.all_gather(summed.astype(jnp.bfloat16), "gy", axis=2, tiled=True).astype(
        summed.dtype
    )
    backward_y = complex_table(signed_modes(MY), local_y, full_y, MY ** (-0.5), 1.0)
    y_inverse = jnp.einsum("pxjkc,pqjy->qxykc", coefficients, backward_y, precision=highest).astype(
        jnp.bfloat16
    )
    backward_z = real_table(modes_z, grid_z, cells_z, MZ ** (-0.5)).astype(jnp.bfloat16)
    return jnp.einsum("pxykc,pkz->xyzc", y_inverse, backward_z, preferred_element_type=jnp.float32)


def edges(first, last, axis):
    size = lax.axis_size(axis)
    if size == 2:
        facing = jnp.where(lax.axis_index(axis) == 0, last, first)
        arrived = lax.ppermute(facing, axis, [(0, 1), (1, 0)])
        return arrived, arrived
    up = [(i, i + 1) for i in range(size - 1)]
    down = [(i + 1, i) for i in range(size - 1)]
    return lax.ppermute(last, axis, up), lax.ppermute(first, axis, down)


def convolve(own_y, flow, left, right, weight):
    shards_y = lax.axis_size("gy")
    channels = flow.shape[3]
    rows = [jnp.concatenate([left[:, i], flow[:, i], right[:, i]])[:, None] for i in (0, -1)]
    front, back = edges(rows[0], rows[1], "gy")
    kernel = weight.reshape(3, 3, 3 * channels, channels)
    return convolution(own_y, shards_y, flow, left, right, front, back, kernel)


def shifted(size, step):
    return [(i, (i + step) % size) for i in range(size)]


def body(flow, spectral_weight, conv_weight, bias):
    cells_x, cells_y, cells_z, channels = flow.shape
    shards_x, shards_y = lax.axis_size("gx"), lax.axis_size("gy")
    items = spectral_weight.shape[0]
    pairs = items // 2
    own_y = lax.axis_index("gy").astype(jnp.int32).reshape(1)
    if items % 2:
        spectral = split_pair_spectral(flow, spectral_weight)
        left, right = edges(flow[:1], flow[-1:], "gx")
        convolved = convolve(own_y, flow, left, right, conv_weight).astype(jnp.float32)
        return jax.nn.gelu(spectral + convolved + bias, approximate=True).astype(jnp.bfloat16)
    sizes = (shards_x, shards_y, pairs, cells_y, cells_z)
    full_x = cells_x * shards_x

    table = jnp.asarray(forward_yz_table(*sizes))
    columns = flow.reshape(cells_x, cells_y * cells_z, channels)
    arrived = []
    first = last = None
    for step in range(1, shards_y):
        sent, *layers = forward_yz(own_y, table, columns, step, shards_x, edges=step == 1)
        arrived.append(lax.ppermute(sent, "gy", shifted(shards_y, step)))
        if layers:
            first, last = (layer.reshape(1, cells_y, cells_z, channels) for layer in layers)
    left, right = edges(first, last, "gx")
    arrived, left, right = lax.optimization_barrier((arrived, left, right))
    (total,) = forward_yz(own_y, table, columns, 0, shards_x, arrived)
    rows = lax.all_to_all(total, "gx", 0, 0, tiled=True)

    convolved = convolve(own_y, flow, left, right, conv_weight)
    rows, convolved = lax.optimization_barrier((rows, convolved))

    returned = mixing(
        rows.reshape(full_x * 2 * pairs, channels),
        jnp.asarray(forward_x_table(full_x)),
        jnp.asarray(backward_x_table(full_x)),
        spectral_weight.reshape(items, MX, channels, channels),
    )
    returned = returned.reshape(shards_x, cells_x, 2 * pairs, channels)
    returned = lax.all_to_all(returned, "gx", 0, 0, tiled=True)
    coefficients = [returned] + [
        lax.ppermute(returned, "gy", shifted(shards_y, step)) for step in range(1, shards_y)
    ]
    return final(
        own_y,
        jnp.asarray(backward_yz_table(*sizes)),
        coefficients,
        convolved,
        bias.reshape(1, channels),
    )


def solution(mesh):
    placed = (P("gx", "gy", None, None), P(("gy", "gx"), None, None, None, None), P(), P())
    return jax.shard_map(
        body, mesh=mesh, in_specs=placed, out_specs=P("gx", "gy", None, None), check_vma=False
    )
```

```python
import functools
import math

import jax
import jax.numpy as jnp
import numpy as np
from jax import lax
from jax.experimental import pallas as pl
from jax.experimental.pallas import tpu as pltpu
from jax.sharding import PartitionSpec as P

MX = 64
MY = 16
MZ = 16


def frequencies(mode_count):
    position = np.arange(mode_count)
    return np.where(position < mode_count // 2, position, position - mode_count)


def wave(first, second, length, factor):
    turns = (np.asarray(first)[:, None] * np.asarray(second)[None, :]) % length
    angles = turns * (2.0 * math.pi / length)
    return (np.cos(angles) + 1j * np.sin(angles)) * factor


def rounded(values):
    return values.astype(np.float32).astype(jnp.bfloat16).astype(np.float64)


def item_modes(shards_x, shards_y, pairs):
    index = np.arange(shards_y * shards_x * pairs).reshape(shards_y, shards_x, pairs)
    return index // MZ, index % MZ


def forward_yz_table(shards_x, shards_y, pairs, cells_y, cells_z):
    full_y = shards_y * cells_y
    turn_z = wave(np.arange(MZ), np.arange(cells_z), cells_z, cells_z**-0.5)
    turn_z = rounded(turn_z.real) - 1j * rounded(turn_z.imag)
    turn_y = np.conj(wave(frequencies(MY), np.arange(full_y), full_y, full_y**-0.5))
    mode_y, mode_z = item_modes(shards_x, shards_y, pairs)
    table = np.empty((shards_y, shards_y, shards_x, pairs, 2, cells_y, cells_z), np.float32)
    for own in range(shards_y):
        rows = turn_y[:, own * cells_y : (own + 1) * cells_y]
        product = rows[mode_y][..., :, None] * turn_z[mode_z][..., None, :]
        table[own, :, :, :, 0] = product.real
        table[own, :, :, :, 1] = product.imag
    return table.reshape(shards_y, -1, cells_y * cells_z).astype(jnp.bfloat16)


def backward_yz_table(shards_x, shards_y, pairs, cells_y, cells_z):
    full_y = shards_y * cells_y
    turn_z = wave(np.arange(MZ), np.arange(cells_z), cells_z, MZ**-0.5)
    turn_z = rounded(turn_z.real) + 1j * rounded(turn_z.imag)
    turn_y = wave(frequencies(MY), np.arange(full_y), full_y, MY**-0.5)
    mode_y, mode_z = item_modes(shards_x, shards_y, pairs)
    table = np.empty((shards_y, cells_y, cells_z, shards_y, shards_x, pairs, 2), np.float32)
    for own in range(shards_y):
        rows = turn_y[:, own * cells_y : (own + 1) * cells_y]
        product = rows[mode_y][..., :, None] * turn_z[mode_z][..., None, :]
        product = np.moveaxis(product, (3, 4), (0, 1))
        table[own, ..., 0] = product.real
        table[own, ..., 1] = -product.imag
    return table.reshape(shards_y, cells_y * cells_z, -1).astype(jnp.bfloat16)


def forward_x_table(full_x):
    turn = np.conj(wave(frequencies(MX), np.arange(full_x), full_x, full_x**-0.5))
    parts = np.empty((2, MX, 2, 2, full_x), np.float32)
    parts[0, :, 0, 0], parts[0, :, 0, 1] = turn.real, -turn.imag
    parts[0, :, 1, 0], parts[0, :, 1, 1] = turn.imag, turn.real
    parts[1, :, 0] = -parts[0, :, 1]
    parts[1, :, 1] = parts[0, :, 0]
    return parts.reshape(2 * MX * 2, 2 * full_x).astype(jnp.bfloat16)


def backward_x_table(full_x):
    turn = wave(frequencies(MX), np.arange(full_x), full_x, MX**-0.5).T
    parts = np.empty((2, full_x, MX, 2), np.float32)
    parts[0, :, :, 0], parts[0, :, :, 1] = turn.real, -turn.imag
    parts[1, :, :, 0], parts[1, :, :, 1] = turn.imag, turn.real
    return parts.reshape(2 * full_x, MX * 2).astype(jnp.bfloat16)


def dot(left, right):
    return jnp.dot(left, right, preferred_element_type=jnp.float32)


def forward_kernel(own_ref, table_ref, flow_ref, out_ref):
    cells_x = flow_ref.shape[0]
    _, shards_x, _, rows, channels = out_ref.shape
    width = 2 if cells_x % 2 == 0 else 1
    for x in range(0, cells_x, width):
        columns = [flow_ref[x + i] for i in range(width)]
        result = dot(table_ref[0], jnp.concatenate(columns, axis=1))
        for i in range(width):
            part = result[:, i * channels : (i + 1) * channels].astype(out_ref.dtype)
            out_ref[0, :, x + i] = part.reshape(shards_x, rows, channels)


def forward_yz(own_y, table, flow, shards_x):
    cells_x, positions, channels = flow.shape
    shards_y, rows, _ = table.shape
    rows = rows // shards_y
    shape = (shards_y, shards_x, cells_x, rows // shards_x, channels)
    return pl.pallas_call(
        forward_kernel,
        grid_spec=pltpu.PrefetchScalarGridSpec(
            num_scalar_prefetch=1,
            grid=(shards_y,),
            in_specs=[
                pl.BlockSpec((1, rows, positions), lambda i, own: (own[0], i, 0)),
                pl.BlockSpec(flow.shape, lambda i, own: (0, 0, 0)),
            ],
            out_specs=pl.BlockSpec((1, *shape[1:]), lambda i, own: (i, 0, 0, 0, 0)),
        ),
        out_shape=jax.ShapeDtypeStruct(shape, jnp.bfloat16),
        cost_estimate=pl.CostEstimate(
            flops=2 * shards_y * rows * positions * cells_x * channels,
            bytes_accessed=2 * positions * (shards_y * rows + cells_x * channels),
            transcendentals=0,
        ),
    )(own_y, table, flow)


def mixing_kernel(
    rows_ref, forward_ref, backward_ref, weight_ref, out_ref, held, sems, wide, left, mixed
):
    slots, _, modes, _, channels = held.shape
    pairs = weight_ref.shape[0] // 2
    full_x = rows_ref.shape[1] // (2 * pairs)
    half = channels // 2
    parts = MX // modes
    chunks = pairs * parts
    span = 2 * MX

    def copy(chunk):
        slot = lax.rem(chunk, slots)
        pair, part = lax.div(chunk, parts), lax.rem(chunk, parts)
        return pltpu.make_async_copy(
            weight_ref.at[pl.ds(2 * pair, 2), pl.ds(part * modes, modes)],
            held.at[slot],
            sems.at[slot],
        )

    for chunk in range(min(slots, chunks)):
        copy(chunk).start()

    wide[...] = sum(rows_ref[i].astype(jnp.float32) for i in range(rows_ref.shape[0]))
    low = lax.broadcasted_iota(jnp.int32, (span, channels), 1) < half
    for pair in range(pairs):
        columns = [wide[pl.ds(2 * pair + p, full_x, stride=2 * pairs), :] for p in range(2)]
        columns = jnp.concatenate(columns, axis=0).astype(jnp.bfloat16)
        both = dot(forward_ref[...], columns)
        value, turned = both[:span], both[span:]
        first = jnp.where(low, value, pltpu.roll(turned, half, axis=1))
        second = jnp.where(low, pltpu.roll(value, half, axis=1), turned)
        left[pl.ds(pair * span, span), :channels] = first.astype(left.dtype)
        left[pl.ds(pair * span, span), channels:] = second.astype(left.dtype)

    group = 16
    row = lax.broadcasted_iota(jnp.int32, (group, channels), 0) // 2

    def mix(chunk, carry):
        slot = lax.rem(chunk, slots)
        copy(chunk).wait()
        for step in range(2 * modes // group):
            start = pl.multiple_of(chunk * 2 * modes + step * group, group)
            lhs = left[pl.ds(start, group), :]
            gathered = jnp.zeros((group, channels), jnp.float32)
            for i in range(0, group // 2, 2):
                mode = step * (group // 2) + i
                tiles = [
                    jnp.concatenate([held[slot, 0, mode + k], held[slot, 1, mode + k]], axis=0)
                    for k in range(2)
                ]
                product = dot(lhs, jnp.concatenate(tiles, axis=1))
                for k in range(2):
                    gathered = jnp.where(
                        row == i + k, product[:, k * channels : (k + 1) * channels], gathered
                    )
            mixed[pl.ds(start, group), :] = gathered.astype(mixed.dtype)

        @pl.when(chunk + slots < chunks)
        def _():
            copy(chunk + slots).start()

        return carry

    lax.fori_loop(0, chunks, mix, 0)

    for pair in range(pairs):
        result = dot(backward_ref[...], mixed[pl.ds(pair * span, span), :])
        for p in range(2):
            wide[pl.ds(2 * pair + p, full_x, stride=2 * pairs), :] = result[
                p * full_x : (p + 1) * full_x
            ]
    for i in range(out_ref.shape[0]):
        out_ref[i] = wide[...].astype(out_ref.dtype)


def mixing(rows, forward_x, backward_x, weight):
    _, row_count, channels = rows.shape
    depth = weight.shape[2]
    pairs = weight.shape[0] // 2
    slots, modes = 4, MX // 2
    vmem = pl.BlockSpec(memory_space=pltpu.VMEM)
    return pl.pallas_call(
        mixing_kernel,
        in_specs=[vmem, vmem, vmem, pl.BlockSpec(memory_space=pl.ANY)],
        out_specs=vmem,
        out_shape=jax.ShapeDtypeStruct(rows.shape, jnp.bfloat16),
        scratch_shapes=[
            pltpu.VMEM((slots, 2, modes, depth, channels), jnp.bfloat16),
            pltpu.SemaphoreType.DMA((slots,)),
            pltpu.VMEM((row_count, channels), jnp.float32),
            pltpu.VMEM((pairs * 2 * MX, 2 * channels), jnp.bfloat16),
            pltpu.VMEM((pairs * 2 * MX, channels), jnp.bfloat16),
        ],
        compiler_params=pltpu.CompilerParams(vmem_limit_bytes=40 << 20),
        cost_estimate=pl.CostEstimate(
            flops=8 * weight.size, bytes_accessed=2 * weight.size, transcendentals=0
        ),
    )(rows, forward_x, backward_x, weight)


def final_kernel(own_ref, table_ref, coefficient_ref, convolved_ref, bias_ref, out_ref):
    cells_x, cells_y, cells_z, channels = out_ref.shape
    depth = table_ref.shape[2]
    width = 2 if cells_x % 2 == 0 else 1
    bias = bias_ref[...]
    for x in range(0, cells_x, width):
        columns = [coefficient_ref[:, x + i].reshape(depth, channels) for i in range(width)]
        total = dot(table_ref[0], jnp.concatenate(columns, axis=1))
        for i in range(width):
            spectral = total[:, i * channels : (i + 1) * channels]
            spectral = spectral.reshape(cells_y, cells_z, channels)
            value = spectral + convolved_ref[x + i].astype(jnp.float32) + bias
            out_ref[x + i] = jax.nn.gelu(value, approximate=True).astype(out_ref.dtype)


def final(own_y, table, coefficients, convolved, bias):
    cells_x, cells_y, cells_z, channels = convolved.shape
    parts = 4 if cells_y % 4 == 0 else 1
    rows = cells_y // parts * cells_z
    block = (cells_x, cells_y // parts, cells_z, channels)
    depth = table.shape[2]
    return pl.pallas_call(
        final_kernel,
        grid_spec=pltpu.PrefetchScalarGridSpec(
            num_scalar_prefetch=1,
            grid=(parts,),
            in_specs=[
                pl.BlockSpec((1, rows, depth), lambda i, own: (own[0], i, 0)),
                pl.BlockSpec(coefficients.shape, lambda i, own: (0, 0, 0, 0)),
                pl.BlockSpec(block, lambda i, own: (0, i, 0, 0)),
                pl.BlockSpec((1, channels), lambda i, own: (0, 0)),
            ],
            out_specs=pl.BlockSpec(block, lambda i, own: (0, i, 0, 0)),
        ),
        out_shape=jax.ShapeDtypeStruct(convolved.shape, jnp.bfloat16),
        compiler_params=pltpu.CompilerParams(vmem_limit_bytes=24 << 20),
        cost_estimate=pl.CostEstimate(
            flops=2 * table.shape[1] * depth * cells_x * channels,
            bytes_accessed=6 * convolved.size,
            transcendentals=convolved.size,
        ),
    )(own_y, table, coefficients, convolved, bias)


def stack(stacked, at, cells):
    count, cells_z, channels = cells.shape
    wide = cells.astype(jnp.float32)
    z = lax.broadcasted_iota(jnp.int32, wide.shape, 1)
    before = jnp.where(z == 0, 0.0, pltpu.roll(wide, 1, axis=1))
    after = jnp.where(z == cells_z - 1, 0.0, pltpu.roll(wide, cells_z - 1, axis=1))
    x, y = at
    stacked[x, pl.ds(y, count), :, :channels] = before.astype(stacked.dtype)
    stacked[x, pl.ds(y, count), :, channels : 2 * channels] = cells
    stacked[x, pl.ds(y, count), :, 2 * channels :] = after.astype(stacked.dtype)


def stack_planes(stacked, count, cells_y, read):
    rows = 4 if cells_y % 4 == 0 else 1
    for x in range(count):

        def one(step, carry, x=x):
            stack(stacked, (x, step * rows + 1), read(x, pl.ds(step * rows, rows)))
            return carry

        lax.fori_loop(0, cells_y // rows, one, 0)


def own_planes_kernel(
    flags_ref, flow_ref, front_ref, back_ref, weight_ref, out_ref, stacked
):
    cells_x, cells_y, cells_z, channels = flow_ref.shape
    stack_planes(stacked, cells_x, cells_y, lambda x, y: flow_ref[x, y])
    blank = jnp.zeros((cells_x, cells_z, 3 * channels), stacked.dtype)
    for flag, ref, y in ((0, front_ref, 0), (1, back_ref, cells_y + 1)):

        @pl.when(flags_ref[flag] > 0)
        def _(ref=ref, y=y):
            for x in range(cells_x):
                stack(stacked, (x, y), ref[x])

        @pl.when(flags_ref[flag] == 0)
        def _(y=y):
            stacked[:, y] = blank

    rows = 4 if cells_y % 4 == 0 else 1
    width = 2 if cells_x % 2 == 0 else 1
    none = jnp.zeros(weight_ref.shape[2:], weight_ref.dtype)

    for x in range(0, cells_x, width):
        planes = [p for p in range(x - 1, x + width + 1) if 0 <= p < cells_x]
        taps = [(p, b) for p in planes for b in range(3)]

        def chunk(index, carry, x=x, taps=taps):
            y = index * rows
            total = jnp.zeros((rows * cells_z, width * channels), jnp.float32)
            for i in range(0, len(taps), 3):
                blocks, kernels = [], []
                for p, b in taps[i : i + 3]:
                    block = stacked[p, pl.ds(y + b, rows)]
                    blocks.append(block.reshape(rows * cells_z, 3 * channels))
                    offsets = [p - (x + k) + 1 for k in range(width)]
                    kernels.append(
                        jnp.concatenate(
                            [weight_ref[a, b] if 0 <= a < 3 else none for a in offsets], axis=1
                        )
                    )
                total = total + dot(
                    jnp.concatenate(blocks, axis=1), jnp.concatenate(kernels, axis=0)
                )
            for k in range(width):
                part = total[:, k * channels : (k + 1) * channels]
                out_ref[x + k, pl.ds(y, rows)] = part.reshape(rows, cells_z, channels)
            return carry

        lax.fori_loop(0, cells_y // rows, chunk, 0)


def beside_planes_kernel(left_ref, right_ref, weight_ref, partial_ref, out_ref, stacked):
    cells_x, cells_y, cells_z, channels = out_ref.shape
    refs = (left_ref, right_ref)
    for x in range(2):
        stack(stacked, (x, 0), refs[x][pl.ds(0, 1)])
        stack(stacked, (x, cells_y + 1), refs[x][pl.ds(cells_y + 1, 1)])

    rows = 4 if cells_y % 4 == 0 else 1
    for x in range(2):

        def one(step, carry, x=x):
            stack(stacked, (x, step * rows + 1), refs[x][pl.ds(step * rows + 1, rows)])
            return carry

        lax.fori_loop(0, cells_y // rows, one, 0)

    added = {0: [(0, 0)]}
    added.setdefault(cells_x - 1, []).append((1, 2))
    for x in range(cells_x):

        def chunk(index, carry, x=x):
            y = index * rows
            total = partial_ref[x, pl.ds(y, rows)].reshape(rows * cells_z, channels)
            for plane, a in added.get(x, ()):
                blocks = [
                    stacked[plane, pl.ds(y + b, rows)].reshape(rows * cells_z, 3 * channels)
                    for b in range(3)
                ]
                kernels = [weight_ref[a, b] for b in range(3)]
                total = total + dot(
                    jnp.concatenate(blocks, axis=1), jnp.concatenate(kernels, axis=0)
                )
            part = total.reshape(rows, cells_z, channels)
            out_ref[x, pl.ds(y, rows)] = part.astype(out_ref.dtype)
            return carry

        lax.fori_loop(0, cells_y // rows, chunk, 0)


def own_planes(flags, flow, front, back, weight):
    cells_x, cells_y, cells_z, channels = flow.shape
    vmem = pl.BlockSpec(memory_space=pltpu.VMEM)
    return pl.pallas_call(
        own_planes_kernel,
        in_specs=[pl.BlockSpec(memory_space=pltpu.SMEM)] + [vmem] * 4,
        out_specs=vmem,
        out_shape=jax.ShapeDtypeStruct(flow.shape, jnp.float32),
        scratch_shapes=[pltpu.VMEM((cells_x, cells_y + 2, cells_z, 3 * channels), flow.dtype)],
        compiler_params=pltpu.CompilerParams(vmem_limit_bytes=24 << 20),
        cost_estimate=pl.CostEstimate(
            flops=2 * 2 * flow.size * 27 * channels,
            bytes_accessed=6 * flow.size,
            transcendentals=0,
        ),
    )(flags, flow, front, back, weight)


def beside_planes(left, right, weight, partial):
    cells_x, cells_y, cells_z, channels = partial.shape
    vmem = pl.BlockSpec(memory_space=pltpu.VMEM)
    return pl.pallas_call(
        beside_planes_kernel,
        in_specs=[vmem] * 4,
        out_specs=vmem,
        out_shape=jax.ShapeDtypeStruct(partial.shape, jnp.bfloat16),
        scratch_shapes=[pltpu.VMEM((2, cells_y + 2, cells_z, 3 * channels), jnp.bfloat16)],
        compiler_params=pltpu.CompilerParams(vmem_limit_bytes=24 << 20),
        cost_estimate=pl.CostEstimate(
            flops=2 * partial.size * 27 * channels,
            bytes_accessed=6 * partial.size,
            transcendentals=0,
        ),
    )(left, right, weight, partial)


def signed_modes(mode_count):
    position = jnp.arange(mode_count, dtype=jnp.int32)
    return jnp.where(position < mode_count // 2, position, position - mode_count)


def angle_grid(first, second, length):
    phase_turns = first[:, None] * second[None, :] % length
    return phase_turns.astype(jnp.float32) * (2.0 * math.pi / length)


def real_table(first, second, length, factor):
    angles = angle_grid(first, second, length)
    return jnp.stack([jnp.cos(angles) * factor, -jnp.sin(angles) * factor])


def complex_table(first, second, length, factor, direction):
    angles = angle_grid(first, second, length)
    cosine = jnp.cos(angles) * factor
    sine_part = jnp.sin(angles) * factor
    return jnp.stack(
        [jnp.stack([cosine, direction * sine_part]), jnp.stack([-direction * sine_part, cosine])]
    )


def split_pair_spectral(flow_field, spectral_weight):
    highest = lax.Precision.HIGHEST
    cells_x, cells_y, cells_z, channels = flow_field.shape
    count_x = lax.axis_size("gx")
    count_y = lax.axis_size("gy")
    full_x = cells_x * count_x
    full_y = cells_y * count_y
    item_count = spectral_weight.shape[0]
    local_y = lax.axis_index("gy") * cells_y + jnp.arange(cells_y, dtype=jnp.int32)
    grid_x = jnp.arange(full_x, dtype=jnp.int32)
    grid_z = jnp.arange(cells_z, dtype=jnp.int32)
    modes_z = jnp.arange(MZ, dtype=jnp.int32)
    forward_z = real_table(grid_z, modes_z, cells_z, cells_z ** (-0.5)).astype(jnp.bfloat16)
    z_spectrum = jnp.einsum(
        "xyzc,pzk->pxykc", flow_field, forward_z, preferred_element_type=jnp.float32
    )
    columns = lax.all_to_all(
        z_spectrum.astype(jnp.bfloat16), "gy", split_axis=4, concat_axis=2, tiled=True
    ).astype(z_spectrum.dtype)
    whole_y = jnp.arange(full_y, dtype=jnp.int32)
    forward_full = complex_table(whole_y, signed_modes(MY), full_y, full_y ** (-0.5), -1.0)
    y_spectrum = jnp.einsum("pxykc,pqyj->qxjkc", columns, forward_full, precision=highest)
    owned = lax.all_to_all(
        y_spectrum.astype(jnp.bfloat16), "gy", split_axis=2, concat_axis=4, tiled=True
    ).astype(y_spectrum.dtype)
    owned_modes = owned.reshape(2, cells_x, count_x, item_count, channels // 2)
    gathered_rows = lax.all_to_all(
        owned_modes.astype(jnp.bfloat16), "gx", split_axis=2, concat_axis=1, tiled=True
    ).astype(owned_modes.dtype)
    gathered_rows = gathered_rows.reshape(2, full_x, item_count, channels // 2)
    forward_x = complex_table(grid_x, signed_modes(MX), full_x, full_x ** (-0.5), -1.0)
    x_spectrum = jnp.einsum("pxjc,pqxm->qmjc", gathered_rows, forward_x, precision=highest).astype(
        jnp.bfloat16
    )
    products = jnp.einsum(
        "pmjc,jmqco->pqmjo", x_spectrum, spectral_weight, preferred_element_type=jnp.float32
    )
    mixed_modes = jnp.stack([products[0, 0] - products[1, 1], products[0, 1] + products[1, 0]])
    backward_x = complex_table(signed_modes(MX), grid_x, full_x, MX ** (-0.5), 1.0)
    inverse_x = jnp.einsum("pmjc,pqmx->qxjc", mixed_modes, backward_x, precision=highest)
    inverse_x = inverse_x.reshape(2, full_x, 1, item_count, channels)
    returned = lax.all_to_all(
        inverse_x.astype(jnp.bfloat16), "gx", split_axis=1, concat_axis=2, tiled=True
    ).astype(inverse_x.dtype)
    band_rows = MY // count_y
    summed = returned.reshape(2, cells_x, band_rows * MZ, 2, channels).sum(axis=3)
    summed = summed.reshape(2, cells_x, band_rows, MZ, channels)
    coefficients = lax.all_gather(summed.astype(jnp.bfloat16), "gy", axis=2, tiled=True).astype(
        summed.dtype
    )
    backward_y = complex_table(signed_modes(MY), local_y, full_y, MY ** (-0.5), 1.0)
    y_inverse = jnp.einsum("pxjkc,pqjy->qxykc", coefficients, backward_y, precision=highest).astype(
        jnp.bfloat16
    )
    backward_z = real_table(modes_z, grid_z, cells_z, MZ ** (-0.5)).astype(jnp.bfloat16)
    return jnp.einsum("pxykc,pkz->xyzc", y_inverse, backward_z, preferred_element_type=jnp.float32)


def edges(first, last, axis):
    size = lax.axis_size(axis)
    if size == 2:
        facing = jnp.where(lax.axis_index(axis) == 0, last, first)
        arrived = lax.ppermute(facing, axis, [(0, 1), (1, 0)])
        return arrived, arrived
    up = [(i, i + 1) for i in range(size - 1)]
    down = [(i + 1, i) for i in range(size - 1)]
    return lax.ppermute(last, axis, up), lax.ppermute(first, axis, down)


def with_rows(flags, front, plane, back):
    front = jnp.where(flags[0] > 0, front, jnp.zeros_like(front))
    back = jnp.where(flags[1] > 0, back, jnp.zeros_like(back))
    return jnp.concatenate([front, plane, back], axis=1)


def body(flow, spectral_weight, conv_weight, bias):
    cells_x, cells_y, cells_z, channels = flow.shape
    shards_x, shards_y = lax.axis_size("gx"), lax.axis_size("gy")
    items = spectral_weight.shape[0]
    pairs = items // 2
    own_y = lax.axis_index("gy").astype(jnp.int32).reshape(1)
    flags = jnp.concatenate([own_y > 0, own_y < shards_y - 1]).astype(jnp.int32)
    kernel = conv_weight.reshape(3, 3, 3 * channels, channels)
    fits = items % 2 == 0
    axes = ("gy", "gx")
    if fits:
        sizes = (shards_x, shards_y, pairs, cells_y, cells_z)
        columns = flow.reshape(cells_x, cells_y * cells_z, channels)
        sent = forward_yz(own_y, jnp.asarray(forward_yz_table(*sizes)), columns, shards_x)
        sent = sent.reshape(-1, *sent.shape[2:])

    ends = (flow[:, :1], flow[:, -1:])
    if fits:
        sent, ends = lax.optimization_barrier((sent, ends))
        rows = lax.all_to_all(sent, axes, 0, 0, tiled=True)
    front, back = edges(*ends, "gy")
    partial = own_planes(flags, flow, front, back, kernel)
    first, last = (
        with_rows(flags, front[x], flow[x], back[x]) for x in (slice(0, 1), slice(-1, None))
    )
    partial, first, last = lax.optimization_barrier((partial, first, last))
    left, right = edges(first, last, "gx")

    if not fits:
        spectral = split_pair_spectral(flow, spectral_weight)
        convolved = beside_planes(left[0], right[0], kernel, partial).astype(jnp.float32)
        return jax.nn.gelu(spectral + convolved + bias, approximate=True).astype(jnp.bfloat16)

    rows, partial = lax.optimization_barrier((rows, partial))
    full_x = cells_x * shards_x
    returned = mixing(
        rows.reshape(shards_y, full_x * 2 * pairs, channels),
        jnp.asarray(forward_x_table(full_x)),
        jnp.asarray(backward_x_table(full_x)),
        spectral_weight.reshape(items, MX, channels, channels),
    )
    returned, left, right = lax.optimization_barrier((returned, left, right))
    convolved = beside_planes(left[0], right[0], kernel, partial)
    returned = returned.reshape(shards_y * shards_x, cells_x, 2 * pairs, channels)
    returned = lax.all_to_all(returned, axes, 0, 0, tiled=True)
    return final(
        own_y,
        jnp.asarray(backward_yz_table(*sizes)),
        returned,
        convolved,
        bias.reshape(1, channels),
    )


def solution(mesh):
    placed = (P("gx", "gy", None, None), P(("gy", "gx"), None, None, None, None), P(), P())
    return jax.shard_map(
        body, mesh=mesh, in_specs=placed, out_specs=P("gx", "gy", None, None), check_vma=False
    )
```

```python
import functools
import math

import jax
import jax.numpy as jnp
import numpy as np
from jax import lax
from jax.experimental import pallas as pl
from jax.experimental.pallas import tpu as pltpu
from jax.sharding import PartitionSpec as P

MX = 64
MY = 16
MZ = 16


def frequencies(mode_count):
    position = np.arange(mode_count)
    return np.where(position < mode_count // 2, position, position - mode_count)


def wave(first, second, length, factor):
    turns = (np.asarray(first)[:, None] * np.asarray(second)[None, :]) % length
    angles = turns * (2.0 * math.pi / length)
    return (np.cos(angles) + 1j * np.sin(angles)) * factor


def rounded(values):
    return values.astype(np.float32).astype(jnp.bfloat16).astype(np.float64)


def item_modes(shards_x, shards_y, pairs):
    index = np.arange(shards_y * shards_x * pairs).reshape(shards_y, shards_x, pairs)
    return index // MZ, index % MZ


def forward_yz_table(shards_x, shards_y, pairs, cells_y, cells_z):
    full_y = shards_y * cells_y
    turn_z = wave(np.arange(MZ), np.arange(cells_z), cells_z, cells_z**-0.5)
    turn_z = rounded(turn_z.real) - 1j * rounded(turn_z.imag)
    turn_y = np.conj(wave(frequencies(MY), np.arange(full_y), full_y, full_y**-0.5))
    mode_y, mode_z = item_modes(shards_x, shards_y, pairs)
    table = np.empty((shards_y, shards_y, shards_x, pairs, 2, cells_y, cells_z), np.float32)
    for own in range(shards_y):
        rows = turn_y[:, own * cells_y : (own + 1) * cells_y]
        product = rows[mode_y][..., :, None] * turn_z[mode_z][..., None, :]
        table[own, :, :, :, 0] = product.real
        table[own, :, :, :, 1] = product.imag
    return table.reshape(shards_y, -1, cells_y * cells_z).astype(jnp.bfloat16)


def backward_yz_table(shards_x, shards_y, pairs, cells_y, cells_z):
    full_y = shards_y * cells_y
    turn_z = wave(np.arange(MZ), np.arange(cells_z), cells_z, MZ**-0.5)
    turn_z = rounded(turn_z.real) + 1j * rounded(turn_z.imag)
    turn_y = wave(frequencies(MY), np.arange(full_y), full_y, MY**-0.5)
    mode_y, mode_z = item_modes(shards_x, shards_y, pairs)
    table = np.empty((shards_y, cells_y, cells_z, shards_y, shards_x, pairs, 2), np.float32)
    for own in range(shards_y):
        rows = turn_y[:, own * cells_y : (own + 1) * cells_y]
        product = rows[mode_y][..., :, None] * turn_z[mode_z][..., None, :]
        product = np.moveaxis(product, (3, 4), (0, 1))
        table[own, ..., 0] = product.real
        table[own, ..., 1] = -product.imag
    return table.reshape(shards_y, cells_y * cells_z, -1).astype(jnp.bfloat16)


def forward_x_table(full_x):
    turn = np.conj(wave(frequencies(MX), np.arange(full_x), full_x, full_x**-0.5))
    parts = np.empty((2, MX, 2, 2, full_x), np.float32)
    parts[0, :, 0, 0], parts[0, :, 0, 1] = turn.real, -turn.imag
    parts[0, :, 1, 0], parts[0, :, 1, 1] = turn.imag, turn.real
    parts[1, :, 0] = -parts[0, :, 1]
    parts[1, :, 1] = parts[0, :, 0]
    return parts.reshape(2 * MX * 2, 2 * full_x).astype(jnp.bfloat16)


def backward_x_table(full_x):
    turn = wave(frequencies(MX), np.arange(full_x), full_x, MX**-0.5).T
    parts = np.empty((2, full_x, MX, 2), np.float32)
    parts[0, :, :, 0], parts[0, :, :, 1] = turn.real, -turn.imag
    parts[1, :, :, 0], parts[1, :, :, 1] = turn.imag, turn.real
    return parts.reshape(2 * full_x, MX * 2).astype(jnp.bfloat16)


def dot(left, right):
    return jnp.dot(left, right, preferred_element_type=jnp.float32)


def peer(index, step, count):
    if count & (count - 1) == 0:
        return index ^ step
    return lax.rem(index + step, count)


def origin(index, step, count):
    if count & (count - 1) == 0:
        return index ^ step
    return lax.rem(index + (count - step), count)


def place(me, shards):
    outer, inner = shards
    across = lax.rem(me, outer * inner)
    return lax.div(me, outer * inner), lax.div(across, inner), lax.rem(across, inner)


def in_vmem(count):
    return [pl.BlockSpec(memory_space=pltpu.VMEM)] * count


IN_SMEM = pl.BlockSpec(memory_space=pltpu.SMEM)


def forward_kernel(shards, pieces, edges, me_ref, table_ref, flow_ref, *refs):
    cells_x = flow_ref.shape[0]
    outer, inner = shards
    rows, channels = refs[0].shape[-2:]
    _, own, _ = place(me_ref[0], shards)
    steps = [step for piece in pieces for step in piece]
    block = inner * rows
    table = [
        table_ref[0, pl.ds(pl.multiple_of(peer(own, step, outer) * block, block), block), :]
        for step in steps
    ]
    table = jnp.concatenate(table, axis=0)
    width = 2 if cells_x % 2 == 0 else 1
    for x in range(0, cells_x, width):
        columns = [flow_ref[x + i] for i in range(width)]
        result = dot(table, jnp.concatenate(columns, axis=1))
        for i in range(width):
            part = result[:, i * channels : (i + 1) * channels]
            at = 0
            for ref, piece in zip(refs, pieces):
                for slot in range(len(piece)):
                    value = part[at : at + block].reshape(inner, rows, channels)
                    ref[slot, :, x + i] = value.astype(ref.dtype)
                    at += block
    if edges:
        refs[-2][...] = flow_ref[0]
        refs[-1][...] = flow_ref[cells_x - 1]


def forward_yz(me, table, flow, step, shards, shards_y, pieces, dtype, edges=False):
    cells_x, positions, channels = flow.shape
    outer, inner = shards
    rows = table.shape[1] // shards_y
    unit = (inner, cells_x, rows // (outer * inner), channels)
    shapes = [jax.ShapeDtypeStruct((len(piece), *unit), dtype) for piece in pieces]
    if edges:
        shapes += [jax.ShapeDtypeStruct((positions, channels), flow.dtype)] * 2
    whole = lambda dims: pl.BlockSpec(dims, lambda i, me: (0,) * len(dims))

    def owner(i, me):
        own = lax.div(me[0], outer * inner)
        return own, lax.rem(own + step, shards_y), 0

    limit = {"vmem_limit_bytes": 24 << 20} if step == 0 else {}
    return pl.pallas_call(
        functools.partial(forward_kernel, shards, pieces, edges),
        grid_spec=pltpu.PrefetchScalarGridSpec(
            num_scalar_prefetch=1,
            grid=(1,),
            in_specs=[pl.BlockSpec((1, rows, positions), owner), whole(flow.shape)],
            out_specs=[whole(one.shape) for one in shapes],
        ),
        out_shape=shapes,
        compiler_params=pltpu.CompilerParams(**limit),
        cost_estimate=pl.CostEstimate(
            flops=2 * rows * positions * cells_x * channels,
            bytes_accessed=2 * positions * (rows + cells_x * channels),
            transcendentals=0,
        ),
    )(me, table, flow)


def add_kernel(count, *refs):
    out_refs = refs[count:]
    for slot, out_ref in enumerate(out_refs):
        total = refs[0][slot]
        for ref in refs[1:count]:
            total = total + ref[slot].astype(jnp.float32)
        out_ref[...] = total.astype(out_ref.dtype)


def add_pieces(own, arrived):
    slots, *unit = own.shape
    return pl.pallas_call(
        functools.partial(add_kernel, 1 + len(arrived)),
        in_specs=in_vmem(1 + len(arrived)),
        out_specs=in_vmem(slots),
        out_shape=[jax.ShapeDtypeStruct(unit, jnp.bfloat16)] * slots,
        cost_estimate=pl.CostEstimate(flops=own.size, bytes_accessed=0, transcendentals=0),
        compiler_params=pltpu.CompilerParams(vmem_limit_bytes=16 << 20),
    )(own, *arrived)


def regroup_kernel(shards, chosen, me_ref, *refs):
    _, _, own = place(me_ref[0], shards)
    count = refs[0].shape[0]
    in_refs, out_refs = refs[:-count], refs[-count:]
    for step, out_ref in enumerate(out_refs):
        at = peer(own, step, count) if chosen else step
        for slot, in_ref in enumerate(in_refs):
            out_ref[slot] = in_ref[at]


def regroup(me, arrays, shards, chosen):
    count, *unit = arrays[0].shape
    return pl.pallas_call(
        functools.partial(regroup_kernel, shards, chosen),
        in_specs=[IN_SMEM] + in_vmem(len(arrays)),
        out_specs=in_vmem(count),
        out_shape=[jax.ShapeDtypeStruct((len(arrays), *unit), arrays[0].dtype)] * count,
        cost_estimate=pl.CostEstimate(
            flops=arrays[0].size, bytes_accessed=0, transcendentals=0
        ),
        compiler_params=pltpu.CompilerParams(vmem_limit_bytes=16 << 20),
    )(me, *arrays)


def edge_kernel(me_ref, left_ref, flow_ref, right_ref, out_ref):
    out_ref[0] = left_ref[0]
    out_ref[1 : 1 + flow_ref.shape[0]] = flow_ref[...]
    out_ref[1 + flow_ref.shape[0]] = right_ref[0]


def y_edge(me, left, flow, right, per_y, row):
    cells_x, cells_y, cells_z, channels = flow.shape
    at = lambda i, me: (0, row(lax.div(me[0], per_y)), 0, 0)
    shape = (cells_x + 2, 1, cells_z, channels)
    return pl.pallas_call(
        edge_kernel,
        grid_spec=pltpu.PrefetchScalarGridSpec(
            num_scalar_prefetch=1,
            grid=(1,),
            in_specs=[
                pl.BlockSpec((1, 1, cells_z, channels), at),
                pl.BlockSpec((cells_x, 1, cells_z, channels), at),
                pl.BlockSpec((1, 1, cells_z, channels), at),
            ],
            out_specs=pl.BlockSpec(shape, lambda i, me: (0, 0, 0, 0)),
        ),
        out_shape=jax.ShapeDtypeStruct(shape, flow.dtype),
    )(me, left, flow, right)


def mixing_kernel(shards, shards_y, me_ref, *refs):
    outer, inner = shards
    row_refs, refs = refs[:inner], refs[inner:]
    forward_ref, backward_ref, weight_ref, flow_ref, left_ref, right_ref, *refs = refs
    front_ref, back_ref, kernel_ref, *refs = refs
    out_refs, refs = refs[:inner], refs[inner:]
    convolved_ref, held, sems, wide, left, mixed, stacked = refs

    slots, _, modes, _, channels = held.shape
    _, cells_x, item_rows, _ = row_refs[0].shape
    cells_y, cells_z = flow_ref.shape[1:3]
    pairs = item_rows // 2
    full_x = outer * inner * cells_x
    half = channels // 2
    span = 2 * MX
    block = cells_x * item_rows
    own_y, own_outer, own_inner = place(me_ref[0], shards)

    def copy(pair):
        slot = lax.rem(pair, slots)
        return pltpu.make_async_copy(
            weight_ref.at[pl.ds(2 * pair, 2)], held.at[slot], sems.at[slot]
        )

    for pair in range(min(slots - 1, pairs)):
        copy(pair).start()

    def rows_of(outer_index, inner_index):
        start = pl.multiple_of((outer_index * inner + inner_index) * block, block)
        return pl.ds(start, block)

    for step in range(inner):
        source = origin(own_inner, step, inner)
        for slot in range(outer):
            value = row_refs[step][slot].reshape(block, channels)
            at = rows_of(origin(own_outer, slot, outer), source)
            wide[at, :] = value.astype(jnp.float32)
    low = lax.broadcasted_iota(jnp.int32, (span, channels), 1) < half
    for pair in range(pairs):
        columns = [wide[pl.ds(2 * pair + p, full_x, stride=item_rows), :] for p in range(2)]
        columns = jnp.concatenate(columns, axis=0).astype(jnp.bfloat16)
        both = dot(forward_ref[...], columns)
        value, turned = both[:span], both[span:]
        first = jnp.where(low, value, pltpu.roll(turned, half, axis=1))
        second = jnp.where(low, pltpu.roll(value, half, axis=1), turned)
        left[pl.ds(pair * span, span), :channels] = first.astype(left.dtype)
        left[pl.ds(pair * span, span), channels:] = second.astype(left.dtype)

    group = 16
    row = lax.broadcasted_iota(jnp.int32, (group, channels), 0) // 2

    def mix(pair, slot):
        for step in range(span // group):
            start = pl.multiple_of(pair * span + step * group, group)
            lhs = left[pl.ds(start, group), :]
            gathered = jnp.zeros((group, channels), jnp.float32)
            for i in range(0, group // 2, 2):
                mode = step * (group // 2) + i
                tiles = [
                    jnp.concatenate([held[slot, 0, mode + k], held[slot, 1, mode + k]], axis=0)
                    for k in range(2)
                ]
                product = dot(lhs, jnp.concatenate(tiles, axis=1))
                for k in range(2):
                    gathered = jnp.where(
                        row == i + k, product[:, k * channels : (k + 1) * channels], gathered
                    )
            mixed[pl.ds(start, group), :] = gathered.astype(mixed.dtype)

    width = 2 if cells_x % 2 == 0 else 1
    rows = stacked.shape[1] - 2
    y_units = cells_y // rows
    units = cells_x // width * y_units

    def stack(plane, at, cells):
        deep = cells.astype(jnp.float32)
        z = lax.broadcasted_iota(jnp.int32, deep.shape, 1)
        before = jnp.where(z == 0, 0.0, pltpu.roll(deep, 1, axis=1))
        after = jnp.where(z == cells_z - 1, 0.0, pltpu.roll(deep, cells_z - 1, axis=1))
        at = pl.ds(at, cells.shape[0])
        stacked[plane, at, :, :channels] = before.astype(stacked.dtype)
        stacked[plane, at, :, channels : 2 * channels] = cells
        stacked[plane, at, :, 2 * channels :] = after.astype(stacked.dtype)

    def stack_unit(unit):
        x, y = lax.div(unit, y_units) * width, lax.rem(unit, y_units) * rows
        for plane in range(width + 2):
            source = x + plane - 1

            def fill(inside, low_edge, high_edge, plane=plane):
                stack(plane, 1, inside(pl.ds(y, rows)))

                @pl.when(y > 0)
                def _():
                    stack(plane, 0, inside(pl.ds(y - 1, 1)))

                @pl.when(y == 0)
                def _():
                    edge = low_edge()
                    stack(plane, 0, jnp.where(own_y > 0, edge, jnp.zeros_like(edge)))

                @pl.when(y + rows < cells_y)
                def _():
                    stack(plane, rows + 1, inside(pl.ds(y + rows, 1)))

                @pl.when(y + rows == cells_y)
                def _():
                    edge = high_edge()
                    last = own_y == shards_y - 1
                    stack(plane, rows + 1, jnp.where(last, jnp.zeros_like(edge), edge))

            edges = (lambda: front_ref[source + 1], lambda: back_ref[source + 1])
            if plane == 0:

                @pl.when(source < 0)
                def _():
                    fill(lambda at: left_ref[0, at], *edges)

            if plane == width + 1:

                @pl.when(source == cells_x)
                def _():
                    fill(lambda at: right_ref[0, at], *edges)

            @pl.when(jnp.logical_and(source >= 0, source < cells_x))
            def _():
                inside = jnp.clip(source, 0, cells_x - 1)
                fill(lambda at: flow_ref[inside, at], *edges)

    none = jnp.zeros(kernel_ref.shape[2:], kernel_ref.dtype)
    taps = [(a, b) for a in range(width + 2) for b in range(3)]

    def convolve_unit(unit):
        x, y = lax.div(unit, y_units) * width, lax.rem(unit, y_units) * rows
        total = jnp.zeros((rows * cells_z, width * channels), jnp.float32)
        for i in range(0, len(taps), 2):
            blocks, kernels = [], []
            for a, b in taps[i : i + 2]:
                part = stacked[a, pl.ds(b, rows)]
                blocks.append(part.reshape(rows * cells_z, 3 * channels))
                parts = [kernel_ref[a - k, b] if 0 <= a - k < 3 else none for k in range(width)]
                kernels.append(jnp.concatenate(parts, axis=1))
            total = total + dot(jnp.concatenate(blocks, axis=1), jnp.concatenate(kernels, axis=0))
        for k in range(width):
            part = total[:, k * channels : (k + 1) * channels].reshape(rows, cells_z, channels)
            convolved_ref[x + k, pl.ds(y, rows)] = part.astype(convolved_ref.dtype)

    def both(pair, carry):
        stack_unit(pair)

        @pl.when(pair + slots - 1 < pairs)
        def _():
            copy(pair + slots - 1).start()

        copy(pair).wait()
        convolve_unit(pair)
        mix(pair, lax.rem(pair, slots))
        return carry

    shared = min(units, pairs)
    lax.fori_loop(0, shared, both, 0)

    def only_mix(pair, carry):
        @pl.when(pair + slots - 1 < pairs)
        def _():
            copy(pair + slots - 1).start()

        copy(pair).wait()
        mix(pair, lax.rem(pair, slots))
        return carry

    def only_convolve(unit, carry):
        stack_unit(unit)
        convolve_unit(unit)
        return carry

    if shared < pairs:
        lax.fori_loop(shared, pairs, only_mix, 0)
    if shared < units:
        lax.fori_loop(shared, units, only_convolve, 0)

    for pair in range(pairs):
        result = dot(backward_ref[...], mixed[pl.ds(pair * span, span), :])
        for p in range(2):
            wide[pl.ds(2 * pair + p, full_x, stride=item_rows), :] = result[
                p * full_x : (p + 1) * full_x
            ]
    for step in range(inner):
        target = peer(own_inner, step, inner)
        for slot in range(outer):
            value = wide[rows_of(peer(own_outer, slot, outer), target), :]
            value = value.reshape(cells_x, item_rows, channels)
            out_refs[step][slot] = value.astype(out_refs[step].dtype)


def mixing(me, rows, forward_x, backward_x, weight, halos, kernel, shards, shards_y):
    outer, inner = shards
    _, cells_x, item_rows, channels = rows[0].shape
    depth = weight.shape[2]
    flow = halos[0]
    _, cells_y, cells_z, _ = flow.shape
    pairs = item_rows // 2
    row_count = outer * inner * cells_x * item_rows
    slots = 3
    y_rows = 4 if cells_y % 4 == 0 else 1
    width = 2 if cells_x % 2 == 0 else 1
    return pl.pallas_call(
        functools.partial(mixing_kernel, shards, shards_y),
        in_specs=[IN_SMEM]
        + in_vmem(inner + 2)
        + [pl.BlockSpec(memory_space=pl.ANY)]
        + in_vmem(len(halos) + 1),
        out_specs=in_vmem(inner + 1),
        out_shape=[jax.ShapeDtypeStruct(rows[0].shape, jnp.bfloat16)] * inner
        + [jax.ShapeDtypeStruct(flow.shape, jnp.bfloat16)],
        scratch_shapes=[
            pltpu.VMEM((slots, 2, MX, depth, channels), jnp.bfloat16),
            pltpu.SemaphoreType.DMA((slots,)),
            pltpu.VMEM((row_count, channels), jnp.float32),
            pltpu.VMEM((pairs * 2 * MX, 2 * channels), jnp.bfloat16),
            pltpu.VMEM((pairs * 2 * MX, channels), jnp.bfloat16),
            pltpu.VMEM((width + 2, y_rows + 2, cells_z, 3 * channels), jnp.bfloat16),
        ],
        compiler_params=pltpu.CompilerParams(vmem_limit_bytes=44 << 20),
        cost_estimate=pl.CostEstimate(
            flops=8 * weight.size, bytes_accessed=2 * weight.size, transcendentals=0
        ),
    )(me, *rows, forward_x, backward_x, weight, *halos, kernel)


def final_kernel(shards, shards_y, me_ref, table_ref, *refs):
    outer, inner = shards
    *piece_refs, convolved_ref, bias_ref, out_ref, held = refs
    cells_x, cells_y, cells_z, channels = out_ref.shape
    own_y, own_outer, own_inner = place(me_ref[0], shards)
    rows = piece_refs[0].shape[2]

    @pl.when(pl.program_id(0) == 0)
    def _():
        for number, ref in enumerate(piece_refs):
            step, slot = divmod(number, outer)
            source_y = lax.rem(own_y + (shards_y - step), shards_y)
            source = source_y * outer + origin(own_outer, slot, outer)
            for part in range(inner):
                at = (source * inner + origin(own_inner, part, inner)) * rows
                for x in range(cells_x):
                    held[x, pl.ds(pl.multiple_of(at, rows), rows), :] = ref[part, x]

    width = 2 if cells_x % 2 == 0 else 1
    bias = bias_ref[...]
    for x in range(0, cells_x, width):
        columns = [held[x + i] for i in range(width)]
        total = dot(table_ref[0], jnp.concatenate(columns, axis=1))
        for i in range(width):
            spectral = total[:, i * channels : (i + 1) * channels]
            spectral = spectral.reshape(cells_y, cells_z, channels)
            value = spectral + convolved_ref[x + i].astype(jnp.float32) + bias
            out_ref[x + i] = jax.nn.gelu(value, approximate=True).astype(out_ref.dtype)


def final(me, table, pieces, convolved, bias, shards, shards_y):
    cells_x, cells_y, cells_z, channels = convolved.shape
    parts = 4 if cells_y % 4 == 0 else 1
    rows = cells_y // parts * cells_z
    block = (cells_x, cells_y // parts, cells_z, channels)
    depth = table.shape[2]
    outer, inner = shards
    return pl.pallas_call(
        functools.partial(final_kernel, shards, shards_y),
        grid_spec=pltpu.PrefetchScalarGridSpec(
            num_scalar_prefetch=1,
            grid=(parts,),
            in_specs=[
                pl.BlockSpec(
                    (1, rows, depth), lambda i, me: (lax.div(me[0], outer * inner), i, 0)
                ),
                *in_vmem(len(pieces)),
                pl.BlockSpec(block, lambda i, me: (0, i, 0, 0)),
                pl.BlockSpec((1, channels), lambda i, me: (0, 0)),
            ],
            out_specs=pl.BlockSpec(block, lambda i, me: (0, i, 0, 0)),
            scratch_shapes=[pltpu.VMEM((cells_x, depth, channels), jnp.bfloat16)],
        ),
        out_shape=jax.ShapeDtypeStruct(convolved.shape, jnp.bfloat16),
        compiler_params=pltpu.CompilerParams(vmem_limit_bytes=24 << 20),
        cost_estimate=pl.CostEstimate(
            flops=2 * table.shape[1] * depth * cells_x * channels,
            bytes_accessed=6 * convolved.size,
            transcendentals=convolved.size,
        ),
    )(me, table, *pieces, convolved, bias)


def with_halo(array, sides, width):
    for axis, dim in sides:
        size, length = (lax.axis_size(axis), array.shape[dim])
        up = [(i, (i + 1) % size) for i in range(size - 1)]
        down = [(j, i) for i, j in up]
        last = lax.slice_in_dim(array, length - width, length, axis=dim)
        initial = lax.slice_in_dim(array, 0, width, axis=dim)
        before = lax.ppermute(last, axis, up)
        after = lax.ppermute(initial, axis, down)
        array = jnp.concatenate([before, array, after], axis=dim)
    return array


def signed_modes(mode_count):
    position = jnp.arange(mode_count, dtype=jnp.int32)
    return jnp.where(position < mode_count // 2, position, position - mode_count)


def angle_grid(first, second, length):
    phase_turns = first[:, None] * second[None, :] % length
    return phase_turns.astype(jnp.float32) * (2.0 * math.pi / length)


def real_table(first, second, length, factor):
    angles = angle_grid(first, second, length)
    return jnp.stack([jnp.cos(angles) * factor, -jnp.sin(angles) * factor])


def complex_table(first, second, length, factor, direction):
    angles = angle_grid(first, second, length)
    cosine = jnp.cos(angles) * factor
    sine_part = jnp.sin(angles) * factor
    return jnp.stack(
        [jnp.stack([cosine, direction * sine_part]), jnp.stack([-direction * sine_part, cosine])]
    )


def split_pair_spectral(flow_field, spectral_weight):
    highest = lax.Precision.HIGHEST
    cells_x, cells_y, cells_z, channels = flow_field.shape
    count_x = lax.axis_size("gx")
    count_y = lax.axis_size("gy")
    full_x = cells_x * count_x
    full_y = cells_y * count_y
    item_count = spectral_weight.shape[0]
    local_y = lax.axis_index("gy") * cells_y + jnp.arange(cells_y, dtype=jnp.int32)
    grid_x = jnp.arange(full_x, dtype=jnp.int32)
    grid_z = jnp.arange(cells_z, dtype=jnp.int32)
    modes_z = jnp.arange(MZ, dtype=jnp.int32)
    forward_z = real_table(grid_z, modes_z, cells_z, cells_z ** (-0.5)).astype(jnp.bfloat16)
    z_spectrum = jnp.einsum(
        "xyzc,pzk->pxykc", flow_field, forward_z, preferred_element_type=jnp.float32
    )
    columns = lax.all_to_all(
        z_spectrum.astype(jnp.bfloat16), "gy", split_axis=4, concat_axis=2, tiled=True
    ).astype(z_spectrum.dtype)
    whole_y = jnp.arange(full_y, dtype=jnp.int32)
    forward_full = complex_table(whole_y, signed_modes(MY), full_y, full_y ** (-0.5), -1.0)
    y_spectrum = jnp.einsum("pxykc,pqyj->qxjkc", columns, forward_full, precision=highest)
    owned = lax.all_to_all(
        y_spectrum.astype(jnp.bfloat16), "gy", split_axis=2, concat_axis=4, tiled=True
    ).astype(y_spectrum.dtype)
    owned_modes = owned.reshape(2, cells_x, count_x, item_count, channels // 2)
    gathered_rows = lax.all_to_all(
        owned_modes.astype(jnp.bfloat16), "gx", split_axis=2, concat_axis=1, tiled=True
    ).astype(owned_modes.dtype)
    gathered_rows = gathered_rows.reshape(2, full_x, item_count, channels // 2)
    forward_x = complex_table(grid_x, signed_modes(MX), full_x, full_x ** (-0.5), -1.0)
    x_spectrum = jnp.einsum("pxjc,pqxm->qmjc", gathered_rows, forward_x, precision=highest).astype(
        jnp.bfloat16
    )
    products = jnp.einsum(
        "pmjc,jmqco->pqmjo", x_spectrum, spectral_weight, preferred_element_type=jnp.float32
    )
    mixed_modes = jnp.stack([products[0, 0] - products[1, 1], products[0, 1] + products[1, 0]])
    backward_x = complex_table(signed_modes(MX), grid_x, full_x, MX ** (-0.5), 1.0)
    inverse_x = jnp.einsum("pmjc,pqmx->qxjc", mixed_modes, backward_x, precision=highest)
    inverse_x = inverse_x.reshape(2, full_x, 1, item_count, channels)
    returned = lax.all_to_all(
        inverse_x.astype(jnp.bfloat16), "gx", split_axis=1, concat_axis=2, tiled=True
    ).astype(inverse_x.dtype)
    band_rows = MY // count_y
    summed = returned.reshape(2, cells_x, band_rows * MZ, 2, channels).sum(axis=3)
    summed = summed.reshape(2, cells_x, band_rows, MZ, channels)
    coefficients = lax.all_gather(summed.astype(jnp.bfloat16), "gy", axis=2, tiled=True).astype(
        summed.dtype
    )
    backward_y = complex_table(signed_modes(MY), local_y, full_y, MY ** (-0.5), 1.0)
    y_inverse = jnp.einsum("pxjkc,pqjy->qxykc", coefficients, backward_y, precision=highest).astype(
        jnp.bfloat16
    )
    backward_z = real_table(modes_z, grid_z, cells_z, MZ ** (-0.5)).astype(jnp.bfloat16)
    return jnp.einsum("pxykc,pkz->xyzc", y_inverse, backward_z, preferred_element_type=jnp.float32)


def split_pair_convolve(flow_field, conv_weight):
    cells_x, cells_y, cells_z, channels = flow_field.shape
    padded = with_halo(flow_field, (("gx", 0), ("gy", 1)), 1)
    padded = jnp.pad(padded, ((0, 0), (0, 0), (1, 1), (0, 0)))
    stacked = jnp.concatenate(
        [padded[:, :, 0:cells_z], padded[:, :, 1 : cells_z + 1], padded[:, :, 2 : cells_z + 2]],
        axis=3,
    )
    kernel = conv_weight.reshape(3, 3, 3 * channels, channels)
    accumulated = jnp.zeros((cells_x, cells_y, cells_z, channels), jnp.float32)
    for shift_x in range(3):
        for shift_y in range(3):
            accumulated = accumulated + jnp.dot(
                stacked[shift_x : shift_x + cells_x, shift_y : shift_y + cells_y],
                kernel[shift_x, shift_y],
                preferred_element_type=jnp.float32,
            )
    return accumulated


def neighbours(first, last, axis):
    size = lax.axis_size(axis)
    up = [(i, i + 1) for i in range(size - 1)]
    down = [(i + 1, i) for i in range(size - 1)]
    return lax.ppermute(last, axis, up), lax.ppermute(first, axis, down)


def exchange(array, step, shards, along_outer):
    outer, inner = shards
    pairs = []
    for i in range(outer * inner):
        a, b = divmod(i, inner)
        count, own = (outer, a) if along_outer else (inner, b)
        to = own ^ step if count & (count - 1) == 0 else (own + step) % count
        pairs.append((i, to * inner + b if along_outer else a * inner + to))
    return lax.ppermute(array, "gx", pairs)


def over_y(array, step, shards_y):
    return lax.ppermute(array, "gy", [(i, (i + step) % shards_y) for i in range(shards_y)])


def body(flow, spectral_weight, conv_weight, bias):
    cells_x, cells_y, cells_z, channels = flow.shape
    shards_x, shards_y = lax.axis_size("gx"), lax.axis_size("gy")
    items = spectral_weight.shape[0]
    pairs = items // 2
    if items % 2 or shards_y < 2:
        spectral = split_pair_spectral(flow, spectral_weight)
        convolved = split_pair_convolve(flow, conv_weight)
        return jax.nn.gelu(spectral + convolved + bias, approximate=True).astype(jnp.bfloat16)

    inner = max(d for d in range(1, shards_x + 1) if shards_x % d == 0 and d * d <= shards_x)
    shards = (shards_x // inner, inner)
    outer = shards[0]
    me = lax.axis_index(("gy", "gx")).astype(jnp.int32).reshape(1)
    sizes = (shards_x, shards_y, pairs, cells_y, cells_z)
    full_x = cells_x * shards_x
    kernel = conv_weight.reshape(3, 3, 3 * channels, channels)

    table = jnp.asarray(forward_yz_table(*sizes))
    columns = flow.reshape(cells_x, cells_y * cells_z, channels)
    order = list(range(outer - 1, -1, -1))
    cut = (outer + 1) // 2
    pieces = [piece for piece in (order[:cut], order[cut:]) if piece]
    arrived = [[] for _ in pieces]
    for step in range(1, shards_y):
        sent = forward_yz(me, table, columns, step, shards, shards_y, pieces, jnp.bfloat16)
        for into, piece in zip(arrived, sent):
            into.append(over_y(piece, step, shards_y))
    *kept, first, last = forward_yz(
        me, table, columns, 0, shards, shards_y, pieces, jnp.float32, edges=True
    )
    first, last = (x.reshape(1, cells_y, cells_z, channels) for x in (first, last))

    left, right = neighbours(first, last, "gx")
    if shards_y == 2:
        facing = lambda own: jnp.where(own == 0, cells_y - 1, 0)
        edge = y_edge(me, left, flow, right, shards_x, facing)
        front = back = over_y(edge, 1, shards_y)
    else:
        low = y_edge(me, left, flow, right, shards_x, lambda own: 0)
        high = y_edge(me, left, flow, right, shards_x, lambda own: cells_y - 1)
        front, back = neighbours(low, high, "gy")

    by_outer = [None] * outer
    for piece, own, parts in zip(pieces, kept, arrived):
        for step, total in zip(piece, add_pieces(own, parts)):
            by_outer[step] = exchange(total, step, shards, True) if step else total
    by_inner = regroup(me, by_outer, shards, True)
    rows = [by_inner[0]] + [exchange(by_inner[s], s, shards, False) for s in range(1, inner)]

    *returned, convolved = mixing(
        me,
        rows,
        jnp.asarray(forward_x_table(full_x)),
        jnp.asarray(backward_x_table(full_x)),
        spectral_weight.reshape(items, MX, channels, channels),
        (flow, left, right, front, back),
        kernel,
        shards,
        shards_y,
    )

    returned = [returned[0]] + [
        exchange(returned[s], s, shards, False) for s in range(1, inner)
    ]
    returned = regroup(me, returned, shards, False)
    returned = [returned[0]] + [exchange(returned[s], s, shards, True) for s in range(1, outer)]
    coefficients = list(returned)
    for step in range(1, shards_y):
        coefficients += [over_y(part, step, shards_y) for part in returned]
    return final(
        me,
        jnp.asarray(backward_yz_table(*sizes)),
        coefficients,
        convolved,
        bias.reshape(1, channels),
        shards,
        shards_y,
    )


def solution(mesh):
    placed = (P("gx", "gy", None, None), P(("gy", "gx"), None, None, None, None), P(), P())
    return jax.shard_map(
        body, mesh=mesh, in_specs=placed, out_specs=P("gx", "gy", None, None), check_vma=False
    )
```

```python
import functools
import math

import jax
import jax.numpy as jnp
import numpy as np
from jax import lax
from jax.experimental import pallas as pl
from jax.experimental.pallas import tpu as pltpu
from jax.sharding import PartitionSpec as P

MX = 64
MY = 16
MZ = 16


def frequencies(mode_count):
    position = np.arange(mode_count)
    return np.where(position < mode_count // 2, position, position - mode_count)


def wave(first, second, length, factor):
    turns = (np.asarray(first)[:, None] * np.asarray(second)[None, :]) % length
    angles = turns * (2.0 * math.pi / length)
    return (np.cos(angles) + 1j * np.sin(angles)) * factor


def rounded(values):
    return values.astype(np.float32).astype(jnp.bfloat16).astype(np.float64)


def item_modes(shards_x, shards_y, pairs):
    index = np.arange(shards_y * shards_x * pairs).reshape(shards_y, shards_x, pairs)
    return index // MZ, index % MZ


def forward_yz_table(shards_x, shards_y, pairs, cells_y, cells_z):
    full_y = shards_y * cells_y
    turn_z = wave(np.arange(MZ), np.arange(cells_z), cells_z, cells_z**-0.5)
    turn_z = rounded(turn_z.real) - 1j * rounded(turn_z.imag)
    turn_y = np.conj(wave(frequencies(MY), np.arange(full_y), full_y, full_y**-0.5))
    mode_y, mode_z = item_modes(shards_x, shards_y, pairs)
    table = np.empty((shards_y, shards_y, shards_x, pairs, 2, cells_y, cells_z), np.float32)
    for own in range(shards_y):
        rows = turn_y[:, own * cells_y : (own + 1) * cells_y]
        product = rows[mode_y][..., :, None] * turn_z[mode_z][..., None, :]
        table[own, :, :, :, 0] = product.real
        table[own, :, :, :, 1] = product.imag
    return table.reshape(shards_y, -1, cells_y * cells_z).astype(jnp.bfloat16)


def backward_yz_table(shards_x, shards_y, pairs, cells_y, cells_z):
    full_y = shards_y * cells_y
    turn_z = wave(np.arange(MZ), np.arange(cells_z), cells_z, MZ**-0.5)
    turn_z = rounded(turn_z.real) + 1j * rounded(turn_z.imag)
    turn_y = wave(frequencies(MY), np.arange(full_y), full_y, MY**-0.5)
    mode_y, mode_z = item_modes(shards_x, shards_y, pairs)
    table = np.empty((shards_y, cells_y, cells_z, shards_y, shards_x, pairs, 2), np.float32)
    for own in range(shards_y):
        rows = turn_y[:, own * cells_y : (own + 1) * cells_y]
        product = rows[mode_y][..., :, None] * turn_z[mode_z][..., None, :]
        product = np.moveaxis(product, (3, 4), (0, 1))
        table[own, ..., 0] = product.real
        table[own, ..., 1] = -product.imag
    return table.reshape(shards_y, cells_y * cells_z, -1).astype(jnp.bfloat16)


def forward_x_table(full_x):
    turn = np.conj(wave(frequencies(MX), np.arange(full_x), full_x, full_x**-0.5))
    parts = np.empty((2, MX, 2, 2, full_x), np.float32)
    parts[0, :, 0, 0], parts[0, :, 0, 1] = turn.real, -turn.imag
    parts[0, :, 1, 0], parts[0, :, 1, 1] = turn.imag, turn.real
    parts[1, :, 0] = -parts[0, :, 1]
    parts[1, :, 1] = parts[0, :, 0]
    return parts.reshape(2 * MX * 2, 2 * full_x).astype(jnp.bfloat16)


def backward_x_table(full_x):
    turn = wave(frequencies(MX), np.arange(full_x), full_x, MX**-0.5).T
    parts = np.empty((2, full_x, MX, 2), np.float32)
    parts[0, :, :, 0], parts[0, :, :, 1] = turn.real, -turn.imag
    parts[1, :, :, 0], parts[1, :, :, 1] = turn.imag, turn.real
    return parts.reshape(2 * full_x, MX * 2).astype(jnp.bfloat16)


def dot(left, right):
    return jnp.dot(left, right, preferred_element_type=jnp.float32)


def peer(index, step, count):
    if count & (count - 1) == 0:
        return index ^ step
    return lax.rem(index + step, count)


def origin(index, step, count):
    if count & (count - 1) == 0:
        return index ^ step
    return lax.rem(index + (count - step), count)


def place(me, shards):
    outer, inner = shards
    across = lax.rem(me, outer * inner)
    return lax.div(me, outer * inner), lax.div(across, inner), lax.rem(across, inner)


def in_vmem(count):
    return [pl.BlockSpec(memory_space=pltpu.VMEM)] * count


IN_SMEM = pl.BlockSpec(memory_space=pltpu.SMEM)


def forward_kernel(shards, pieces, edges, me_ref, table_ref, flow_ref, *refs):
    cells_x = flow_ref.shape[0]
    outer, inner = shards
    rows, channels = refs[0].shape[-2:]
    _, own, _ = place(me_ref[0], shards)
    steps = [step for piece in pieces for step in piece]
    block = inner * rows
    table = [
        table_ref[0, pl.ds(pl.multiple_of(peer(own, step, outer) * block, block), block), :]
        for step in steps
    ]
    table = jnp.concatenate(table, axis=0)
    width = 2 if cells_x % 2 == 0 else 1
    for x in range(0, cells_x, width):
        columns = [flow_ref[x + i] for i in range(width)]
        result = dot(table, jnp.concatenate(columns, axis=1))
        for i in range(width):
            part = result[:, i * channels : (i + 1) * channels]
            at = 0
            for ref, piece in zip(refs, pieces):
                for slot in range(len(piece)):
                    value = part[at : at + block].reshape(inner, rows, channels)
                    ref[slot, :, x + i] = value.astype(ref.dtype)
                    at += block
    if edges:
        first, last, low, high = refs[-4:]
        first[...] = flow_ref[0]
        last[...] = flow_ref[cells_x - 1]
        cells_z = low.shape[1]
        low[...] = flow_ref[:, :cells_z]
        high[...] = flow_ref[:, flow_ref.shape[1] - cells_z :]


def forward_yz(me, table, flow, step, shards, shards_y, pieces, dtype, edges=0):
    cells_x, positions, channels = flow.shape
    outer, inner = shards
    rows = table.shape[1] // shards_y
    unit = (inner, cells_x, rows // (outer * inner), channels)
    shapes = [jax.ShapeDtypeStruct((len(piece), *unit), dtype) for piece in pieces]
    if edges:
        shapes += [jax.ShapeDtypeStruct((positions, channels), flow.dtype)] * 2
        shapes += [jax.ShapeDtypeStruct((cells_x, edges, channels), flow.dtype)] * 2
    whole = lambda dims: pl.BlockSpec(dims, lambda i, me: (0,) * len(dims))

    def owner(i, me):
        own = lax.div(me[0], outer * inner)
        return own, lax.rem(own + step, shards_y), 0

    limit = {} if step else {"vmem_limit_bytes": 10 << 20}
    return pl.pallas_call(
        functools.partial(forward_kernel, shards, pieces, edges),
        grid_spec=pltpu.PrefetchScalarGridSpec(
            num_scalar_prefetch=1,
            grid=(1,),
            in_specs=[pl.BlockSpec((1, rows, positions), owner), whole(flow.shape)],
            out_specs=[whole(one.shape) for one in shapes],
        ),
        out_shape=shapes,
        compiler_params=pltpu.CompilerParams(**limit),
        cost_estimate=pl.CostEstimate(
            flops=2 * rows * positions * cells_x * channels,
            bytes_accessed=2 * positions * (rows + cells_x * channels),
            transcendentals=0,
        ),
    )(me, table, flow)


def add_kernel(count, *refs):
    out_refs = refs[count:]
    for slot, out_ref in enumerate(out_refs):
        total = refs[0][slot]
        for ref in refs[1:count]:
            total = total + ref[slot].astype(jnp.float32)
        out_ref[...] = total.astype(out_ref.dtype)


def add_pieces(own, arrived):
    slots, *unit = own.shape
    return pl.pallas_call(
        functools.partial(add_kernel, 1 + len(arrived)),
        in_specs=in_vmem(1 + len(arrived)),
        out_specs=in_vmem(slots),
        out_shape=[jax.ShapeDtypeStruct(unit, jnp.bfloat16)] * slots,
        cost_estimate=pl.CostEstimate(flops=own.size, bytes_accessed=0, transcendentals=0),
        compiler_params=pltpu.CompilerParams(vmem_limit_bytes=10 << 20),
    )(own, *arrived)


def regroup_kernel(shards, chosen, me_ref, *refs):
    _, _, own = place(me_ref[0], shards)
    count = refs[0].shape[0]
    in_refs, out_refs = refs[:-count], refs[-count:]
    for step, out_ref in enumerate(out_refs):
        at = peer(own, step, count) if chosen else step
        for slot, in_ref in enumerate(in_refs):
            out_ref[slot] = in_ref[at]


def regroup(me, arrays, shards, chosen):
    count, *unit = arrays[0].shape
    return pl.pallas_call(
        functools.partial(regroup_kernel, shards, chosen),
        in_specs=[IN_SMEM] + in_vmem(len(arrays)),
        out_specs=in_vmem(count),
        out_shape=[jax.ShapeDtypeStruct((len(arrays), *unit), arrays[0].dtype)] * count,
        cost_estimate=pl.CostEstimate(
            flops=arrays[0].size, bytes_accessed=0, transcendentals=0
        ),
        compiler_params=pltpu.CompilerParams(vmem_limit_bytes=10 << 20),
    )(me, *arrays)


def edge_kernel(choose, per_y, me_ref, left_ref, low_ref, high_ref, right_ref, out_ref):
    cells_x, cells_y = low_ref.shape[0], left_ref.shape[1]

    def fill(row, rows_ref):
        out_ref[0, 0] = left_ref[0, row]
        out_ref[1 : 1 + cells_x, 0] = rows_ref[...]
        out_ref[1 + cells_x, 0] = right_ref[0, row]

    is_low = choose(lax.div(me_ref[0], per_y))

    @pl.when(is_low)
    def _():
        fill(0, low_ref)

    @pl.when(jnp.logical_not(is_low))
    def _():
        fill(cells_y - 1, high_ref)


def y_edge(me, left, low, high, right, per_y, choose):
    cells_x, cells_z, channels = low.shape
    return pl.pallas_call(
        functools.partial(edge_kernel, choose, per_y),
        in_specs=[IN_SMEM] + in_vmem(4),
        out_specs=in_vmem(1)[0],
        out_shape=jax.ShapeDtypeStruct((cells_x + 2, 1, cells_z, channels), low.dtype),
        compiler_params=pltpu.CompilerParams(vmem_limit_bytes=4 << 20),
    )(me, left, low, high, right)


def preload_kernel(pair, weight_ref, out_ref, sem):
    copy = pltpu.make_async_copy(weight_ref.at[pl.ds(2 * pair, 2)], out_ref, sem)
    copy.start()
    copy.wait()


def preload(weight, pair):
    shape = (2, *weight.shape[1:])
    return pl.pallas_call(
        functools.partial(preload_kernel, pair),
        in_specs=[pl.BlockSpec(memory_space=pltpu.HBM)],
        out_specs=in_vmem(1)[0],
        out_shape=jax.ShapeDtypeStruct(shape, weight.dtype),
        scratch_shapes=[pltpu.SemaphoreType.DMA],
        compiler_params=pltpu.CompilerParams(vmem_limit_bytes=36 << 20),
        cost_estimate=pl.CostEstimate(
            flops=0, bytes_accessed=2 * math.prod(shape), transcendentals=0
        ),
    )(weight)


def mixing_kernel(shards, loaded, me_ref, *refs):
    outer, inner = shards
    row_refs, refs = refs[:inner], refs[inner:]
    forward_ref, backward_ref, weight_ref, *refs = refs
    loaded_refs, refs = refs[:loaded], refs[loaded:]
    out_refs, (held, sems, wide, left, mixed) = refs[:inner], refs[inner:]

    channels = wide.shape[1]
    _, cells_x, item_rows, _ = row_refs[0].shape
    pairs = item_rows // 2
    full_x = outer * inner * cells_x
    half = channels // 2
    span = 2 * MX
    block = cells_x * item_rows
    _, own_outer, own_inner = place(me_ref[0], shards)

    def copy(pair):
        slot = pair - loaded
        return pltpu.make_async_copy(
            weight_ref.at[pl.ds(2 * pair, 2)], held.at[slot], sems.at[slot]
        )

    for pair in range(loaded, pairs):
        copy(pair).start()

    def rows_of(outer_index, inner_index):
        start = pl.multiple_of((outer_index * inner + inner_index) * block, block)
        return pl.ds(start, block)

    for step in range(inner):
        source = origin(own_inner, step, inner)
        for slot in range(outer):
            value = row_refs[step][slot].reshape(block, channels)
            at = rows_of(origin(own_outer, slot, outer), source)
            wide[at, :] = value.astype(jnp.float32)
    low = lax.broadcasted_iota(jnp.int32, (span, channels), 1) < half
    for pair in range(pairs):
        columns = [wide[pl.ds(2 * pair + p, full_x, stride=item_rows), :] for p in range(2)]
        columns = jnp.concatenate(columns, axis=0).astype(jnp.bfloat16)
        both = dot(forward_ref[...], columns)
        value, turned = both[:span], both[span:]
        first = jnp.where(low, value, pltpu.roll(turned, half, axis=1))
        second = jnp.where(low, pltpu.roll(value, half, axis=1), turned)
        left[pl.ds(pair * span, span), :channels] = first.astype(left.dtype)
        left[pl.ds(pair * span, span), channels:] = second.astype(left.dtype)

    group = 16
    row = lax.broadcasted_iota(jnp.int32, (group, channels), 0) // 2

    def mix(pair, tile_of):
        for step in range(span // group):
            start = pl.multiple_of(pair * span + step * group, group)
            lhs = left[pl.ds(start, group), :]
            gathered = jnp.zeros((group, channels), jnp.float32)
            for i in range(0, group // 2, 2):
                mode = step * (group // 2) + i
                tiles = [
                    jnp.concatenate([tile_of(h, mode + k) for h in range(2)], axis=0)
                    for k in range(2)
                ]
                product = dot(lhs, jnp.concatenate(tiles, axis=1))
                for k in range(2):
                    gathered = jnp.where(
                        row == i + k, product[:, k * channels : (k + 1) * channels], gathered
                    )
            mixed[pl.ds(start, group), :] = gathered.astype(mixed.dtype)

    for pair, ref in enumerate(loaded_refs):
        mix(pair, lambda h, mode, ref=ref: ref[h, mode])

    def streamed(pair, carry):
        copy(pair).wait()
        mix(pair, lambda h, mode: held[pair - loaded, h, mode])
        return carry

    lax.fori_loop(loaded, pairs, streamed, 0)

    for pair in range(pairs):
        result = dot(backward_ref[...], mixed[pl.ds(pair * span, span), :])
        for p in range(2):
            wide[pl.ds(2 * pair + p, full_x, stride=item_rows), :] = result[
                p * full_x : (p + 1) * full_x
            ]
    for step in range(inner):
        target = peer(own_inner, step, inner)
        for slot in range(outer):
            value = wide[rows_of(peer(own_outer, slot, outer), target), :]
            value = value.reshape(cells_x, item_rows, channels)
            out_refs[step][slot] = value.astype(out_refs[step].dtype)


def mixing(me, rows, forward_x, backward_x, weight, loaded, shards):
    outer, inner = shards
    _, cells_x, item_rows, channels = rows[0].shape
    pairs = item_rows // 2
    row_count = outer * inner * cells_x * item_rows
    return pl.pallas_call(
        functools.partial(mixing_kernel, shards, len(loaded)),
        in_specs=[IN_SMEM]
        + in_vmem(inner + 2)
        + [pl.BlockSpec(memory_space=pltpu.HBM)]
        + in_vmem(len(loaded)),
        out_specs=in_vmem(inner),
        out_shape=[jax.ShapeDtypeStruct(rows[0].shape, jnp.bfloat16)] * inner,
        scratch_shapes=[
            pltpu.VMEM((pairs - len(loaded), 2, *weight.shape[1:]), weight.dtype),
            pltpu.SemaphoreType.DMA((pairs - len(loaded),)),
            pltpu.VMEM((row_count, channels), jnp.float32),
            pltpu.VMEM((pairs * 2 * MX, 2 * channels), jnp.bfloat16),
            pltpu.VMEM((pairs * 2 * MX, channels), jnp.bfloat16),
        ],
        compiler_params=pltpu.CompilerParams(vmem_limit_bytes=36 << 20),
        cost_estimate=pl.CostEstimate(
            flops=8 * weight.size, bytes_accessed=2 * weight.size, transcendentals=0
        ),
    )(me, *rows, forward_x, backward_x, weight, *loaded)


def convolution_kernel(x, shards_y, per_y, me_ref, *refs):
    *plane_refs, front_ref, back_ref, kernel_ref, out_ref, stacked = refs
    cells_y, cells_z, channels = out_ref.shape
    own_y = lax.div(me_ref[0], per_y)

    def stack(plane, at, cells):
        deep = cells.astype(jnp.float32)
        z = lax.broadcasted_iota(jnp.int32, deep.shape, 1)
        before = jnp.where(z == 0, 0.0, pltpu.roll(deep, 1, axis=1))
        after = jnp.where(z == cells_z - 1, 0.0, pltpu.roll(deep, cells_z - 1, axis=1))
        at = pl.ds(at, cells.shape[0])
        stacked[plane, at, :, :channels] = before.astype(stacked.dtype)
        stacked[plane, at, :, channels : 2 * channels] = cells
        stacked[plane, at, :, 2 * channels :] = after.astype(stacked.dtype)

    rows = 4 if cells_y % 4 == 0 else 1
    for plane, ref in enumerate(plane_refs):

        def one(step, carry, plane=plane, ref=ref):
            stack(plane, step * rows + 1, ref[0, pl.ds(step * rows, rows)])
            return carry

        lax.fori_loop(0, cells_y // rows, one, 0)
        edge = front_ref[x + plane]
        stack(plane, 0, jnp.where(own_y > 0, edge, jnp.zeros_like(edge)))
        edge = back_ref[x + plane]
        stack(plane, cells_y + 1, jnp.where(own_y < shards_y - 1, edge, jnp.zeros_like(edge)))

    taps = [(a, b) for a in range(3) for b in range(3)]

    def chunk(index, carry):
        y = index * rows
        total = jnp.zeros((rows * cells_z, channels), jnp.float32)
        for a in range(3):
            blocks, kernels = [], []
            for b in range(3):
                part = stacked[a, pl.ds(y + b, rows)]
                blocks.append(part.reshape(rows * cells_z, 3 * channels))
                kernels.append(kernel_ref[a, b])
            total = total + dot(jnp.concatenate(blocks, axis=1), jnp.concatenate(kernels, axis=0))
        out_ref[pl.ds(y, rows)] = total.reshape(rows, cells_z, channels).astype(out_ref.dtype)
        return carry

    lax.fori_loop(0, cells_y // rows, chunk, 0)


def convolution(me, x, flow, left, right, front, back, kernel, shards_y, per_y):
    cells_x, cells_y, cells_z, channels = flow.shape
    specs, planes = [], []
    for p in (x - 1, x, x + 1):
        inside = 0 <= p < cells_x
        planes.append(flow if inside else (left if p < 0 else right))
        at = p if inside else 0
        specs.append(
            pl.BlockSpec((1, cells_y, cells_z, channels), lambda i, at=at: (at, 0, 0, 0))
        )
    whole = lambda array: pl.BlockSpec(array.shape, lambda i: (0,) * array.ndim)
    return pl.pallas_call(
        functools.partial(convolution_kernel, x, shards_y, per_y),
        grid=(1,),
        in_specs=[IN_SMEM] + specs + [whole(front), whole(back), whole(kernel)],
        out_specs=pl.BlockSpec((cells_y, cells_z, channels), lambda i: (0, 0, 0)),
        out_shape=jax.ShapeDtypeStruct((cells_y, cells_z, channels), jnp.bfloat16),
        scratch_shapes=[pltpu.VMEM((3, cells_y + 2, cells_z, 3 * channels), flow.dtype)],
        compiler_params=pltpu.CompilerParams(vmem_limit_bytes=10 << 20),
        cost_estimate=pl.CostEstimate(
            flops=2 * 27 * cells_y * cells_z * channels * channels,
            bytes_accessed=10 * cells_y * cells_z * channels,
            transcendentals=0,
        ),
    )(me, *planes, front, back, kernel)


def final_kernel(shards, shards_y, me_ref, table_ref, *refs):
    outer, inner = shards
    *piece_refs, bias_ref, out_ref, held = refs
    cells_x, cells_y, cells_z, channels = out_ref.shape
    piece_refs, convolved_refs = piece_refs[:-cells_x], piece_refs[-cells_x:]
    own_y, own_outer, own_inner = place(me_ref[0], shards)
    rows = piece_refs[0].shape[2]

    @pl.when(pl.program_id(0) == 0)
    def _():
        for number, ref in enumerate(piece_refs):
            step, slot = divmod(number, outer)
            source_y = lax.rem(own_y + (shards_y - step), shards_y)
            source = source_y * outer + origin(own_outer, slot, outer)
            for part in range(inner):
                at = (source * inner + origin(own_inner, part, inner)) * rows
                for x in range(cells_x):
                    held[x, pl.ds(pl.multiple_of(at, rows), rows), :] = ref[part, x]

    width = 2 if cells_x % 2 == 0 else 1
    bias = bias_ref[...]
    part = pl.program_id(0)
    count = cells_y * cells_z
    table = table_ref[own_y, pl.ds(pl.multiple_of(part * count, count), count), :]
    for x in range(0, cells_x, width):
        columns = [held[x + i] for i in range(width)]
        total = dot(table, jnp.concatenate(columns, axis=1))
        for i in range(width):
            spectral = total[:, i * channels : (i + 1) * channels]
            spectral = spectral.reshape(cells_y, cells_z, channels)
            convolved = convolved_refs[x + i][pl.ds(part * cells_y, cells_y)]
            value = spectral + convolved.astype(jnp.float32) + bias
            out_ref[x + i] = jax.nn.gelu(value, approximate=True).astype(out_ref.dtype)


def final(me, table, pieces, convolved, bias, shards, shards_y):
    cells_x = len(convolved)
    cells_y, cells_z, channels = convolved[0].shape
    parts = 4 if cells_y % 4 == 0 else 1
    block = (cells_x, cells_y // parts, cells_z, channels)
    depth = table.shape[2]
    return pl.pallas_call(
        functools.partial(final_kernel, shards, shards_y),
        grid_spec=pltpu.PrefetchScalarGridSpec(
            num_scalar_prefetch=1,
            grid=(parts,),
            in_specs=[
                *in_vmem(2 + len(pieces) + cells_x),
            ],
            out_specs=pl.BlockSpec(block, lambda i, me: (0, i, 0, 0)),
            scratch_shapes=[pltpu.VMEM((cells_x, depth, channels), jnp.bfloat16)],
        ),
        out_shape=jax.ShapeDtypeStruct((cells_x, *convolved[0].shape), jnp.bfloat16),
        compiler_params=pltpu.CompilerParams(vmem_limit_bytes=10 << 20),
        cost_estimate=pl.CostEstimate(
            flops=2 * table.shape[1] * depth * cells_x * channels,
            bytes_accessed=6 * cells_x * convolved[0].size,
            transcendentals=cells_x * convolved[0].size,
        ),
    )(me, table, *pieces, *convolved, bias)


def with_halo(array, sides, width):
    for axis, dim in sides:
        size, length = (lax.axis_size(axis), array.shape[dim])
        up = [(i, (i + 1) % size) for i in range(size - 1)]
        down = [(j, i) for i, j in up]
        last = lax.slice_in_dim(array, length - width, length, axis=dim)
        initial = lax.slice_in_dim(array, 0, width, axis=dim)
        before = lax.ppermute(last, axis, up)
        after = lax.ppermute(initial, axis, down)
        array = jnp.concatenate([before, array, after], axis=dim)
    return array


def signed_modes(mode_count):
    position = jnp.arange(mode_count, dtype=jnp.int32)
    return jnp.where(position < mode_count // 2, position, position - mode_count)


def angle_grid(first, second, length):
    phase_turns = first[:, None] * second[None, :] % length
    return phase_turns.astype(jnp.float32) * (2.0 * math.pi / length)


def real_table(first, second, length, factor):
    angles = angle_grid(first, second, length)
    return jnp.stack([jnp.cos(angles) * factor, -jnp.sin(angles) * factor])


def complex_table(first, second, length, factor, direction):
    angles = angle_grid(first, second, length)
    cosine = jnp.cos(angles) * factor
    sine_part = jnp.sin(angles) * factor
    return jnp.stack(
        [jnp.stack([cosine, direction * sine_part]), jnp.stack([-direction * sine_part, cosine])]
    )


def split_pair_spectral(flow_field, spectral_weight):
    highest = lax.Precision.HIGHEST
    cells_x, cells_y, cells_z, channels = flow_field.shape
    count_x = lax.axis_size("gx")
    count_y = lax.axis_size("gy")
    full_x = cells_x * count_x
    full_y = cells_y * count_y
    item_count = spectral_weight.shape[0]
    local_y = lax.axis_index("gy") * cells_y + jnp.arange(cells_y, dtype=jnp.int32)
    grid_x = jnp.arange(full_x, dtype=jnp.int32)
    grid_z = jnp.arange(cells_z, dtype=jnp.int32)
    modes_z = jnp.arange(MZ, dtype=jnp.int32)
    forward_z = real_table(grid_z, modes_z, cells_z, cells_z ** (-0.5)).astype(jnp.bfloat16)
    z_spectrum = jnp.einsum(
        "xyzc,pzk->pxykc", flow_field, forward_z, preferred_element_type=jnp.float32
    )
    columns = lax.all_to_all(
        z_spectrum.astype(jnp.bfloat16), "gy", split_axis=4, concat_axis=2, tiled=True
    ).astype(z_spectrum.dtype)
    whole_y = jnp.arange(full_y, dtype=jnp.int32)
    forward_full = complex_table(whole_y, signed_modes(MY), full_y, full_y ** (-0.5), -1.0)
    y_spectrum = jnp.einsum("pxykc,pqyj->qxjkc", columns, forward_full, precision=highest)
    owned = lax.all_to_all(
        y_spectrum.astype(jnp.bfloat16), "gy", split_axis=2, concat_axis=4, tiled=True
    ).astype(y_spectrum.dtype)
    owned_modes = owned.reshape(2, cells_x, count_x, item_count, channels // 2)
    gathered_rows = lax.all_to_all(
        owned_modes.astype(jnp.bfloat16), "gx", split_axis=2, concat_axis=1, tiled=True
    ).astype(owned_modes.dtype)
    gathered_rows = gathered_rows.reshape(2, full_x, item_count, channels // 2)
    forward_x = complex_table(grid_x, signed_modes(MX), full_x, full_x ** (-0.5), -1.0)
    x_spectrum = jnp.einsum("pxjc,pqxm->qmjc", gathered_rows, forward_x, precision=highest).astype(
        jnp.bfloat16
    )
    products = jnp.einsum(
        "pmjc,jmqco->pqmjo", x_spectrum, spectral_weight, preferred_element_type=jnp.float32
    )
    mixed_modes = jnp.stack([products[0, 0] - products[1, 1], products[0, 1] + products[1, 0]])
    backward_x = complex_table(signed_modes(MX), grid_x, full_x, MX ** (-0.5), 1.0)
    inverse_x = jnp.einsum("pmjc,pqmx->qxjc", mixed_modes, backward_x, precision=highest)
    inverse_x = inverse_x.reshape(2, full_x, 1, item_count, channels)
    returned = lax.all_to_all(
        inverse_x.astype(jnp.bfloat16), "gx", split_axis=1, concat_axis=2, tiled=True
    ).astype(inverse_x.dtype)
    band_rows = MY // count_y
    summed = returned.reshape(2, cells_x, band_rows * MZ, 2, channels).sum(axis=3)
    summed = summed.reshape(2, cells_x, band_rows, MZ, channels)
    coefficients = lax.all_gather(summed.astype(jnp.bfloat16), "gy", axis=2, tiled=True).astype(
        summed.dtype
    )
    backward_y = complex_table(signed_modes(MY), local_y, full_y, MY ** (-0.5), 1.0)
    y_inverse = jnp.einsum("pxjkc,pqjy->qxykc", coefficients, backward_y, precision=highest).astype(
        jnp.bfloat16
    )
    backward_z = real_table(modes_z, grid_z, cells_z, MZ ** (-0.5)).astype(jnp.bfloat16)
    return jnp.einsum("pxykc,pkz->xyzc", y_inverse, backward_z, preferred_element_type=jnp.float32)


def split_pair_convolve(flow_field, conv_weight):
    cells_x, cells_y, cells_z, channels = flow_field.shape
    padded = with_halo(flow_field, (("gx", 0), ("gy", 1)), 1)
    padded = jnp.pad(padded, ((0, 0), (0, 0), (1, 1), (0, 0)))
    stacked = jnp.concatenate(
        [padded[:, :, 0:cells_z], padded[:, :, 1 : cells_z + 1], padded[:, :, 2 : cells_z + 2]],
        axis=3,
    )
    kernel = conv_weight.reshape(3, 3, 3 * channels, channels)
    accumulated = jnp.zeros((cells_x, cells_y, cells_z, channels), jnp.float32)
    for shift_x in range(3):
        for shift_y in range(3):
            accumulated = accumulated + jnp.dot(
                stacked[shift_x : shift_x + cells_x, shift_y : shift_y + cells_y],
                kernel[shift_x, shift_y],
                preferred_element_type=jnp.float32,
            )
    return accumulated


def neighbours(first, last, axis):
    size = lax.axis_size(axis)
    up = [(i, i + 1) for i in range(size - 1)]
    down = [(i + 1, i) for i in range(size - 1)]
    return lax.ppermute(last, axis, up), lax.ppermute(first, axis, down)


def exchange(array, step, shards, along_outer):
    outer, inner = shards
    pairs = []
    for i in range(outer * inner):
        a, b = divmod(i, inner)
        count, own = (outer, a) if along_outer else (inner, b)
        to = own ^ step if count & (count - 1) == 0 else (own + step) % count
        pairs.append((i, to * inner + b if along_outer else a * inner + to))
    return lax.ppermute(array, "gx", pairs)


def over_y(array, step, shards_y):
    return lax.ppermute(array, "gy", [(i, (i + step) % shards_y) for i in range(shards_y)])


def body(flow, spectral_weight, conv_weight, bias):
    cells_x, cells_y, cells_z, channels = flow.shape
    shards_x, shards_y = lax.axis_size("gx"), lax.axis_size("gy")
    items = spectral_weight.shape[0]
    pairs = items // 2
    if items % 2 or shards_y < 2:
        spectral = split_pair_spectral(flow, spectral_weight)
        convolved = split_pair_convolve(flow, conv_weight)
        return jax.nn.gelu(spectral + convolved + bias, approximate=True).astype(jnp.bfloat16)

    inner = max(d for d in range(1, shards_x + 1) if shards_x % d == 0 and d * d <= shards_x)
    shards = (shards_x // inner, inner)
    outer = shards[0]
    me = lax.axis_index(("gy", "gx")).astype(jnp.int32).reshape(1)
    sizes = (shards_x, shards_y, pairs, cells_y, cells_z)
    full_x = cells_x * shards_x
    kernel = conv_weight.reshape(3, 3, 3 * channels, channels)

    weight = spectral_weight.reshape(items, MX, channels, channels)

    table = jnp.asarray(forward_yz_table(*sizes))
    columns = flow.reshape(cells_x, cells_y * cells_z, channels)
    order = list(range(outer - 1, -1, -1))
    cut = (outer + 1) // 2
    pieces = [piece for piece in (order[:cut], order[cut:]) if piece]
    arrived = [[] for _ in pieces]
    for step in range(1, shards_y):
        sent = forward_yz(me, table, columns, step, shards, shards_y, pieces, jnp.bfloat16)
        sent, columns, weight = lax.optimization_barrier((sent, columns, weight))
        for into, piece in zip(arrived, sent):
            into.append(over_y(piece, step, shards_y))
    *kept, first, last, low, high = forward_yz(
        me, table, columns, 0, shards, shards_y, pieces, jnp.float32, edges=cells_z
    )
    first, last = (x.reshape(1, cells_y, cells_z, channels) for x in (first, last))

    left, right = neighbours(first, last, "gx")

    by_outer = [None] * outer
    for piece, own, parts in zip(pieces, kept, arrived):
        for step, total in zip(piece, add_pieces(own, parts)):
            by_outer[step] = exchange(total, step, shards, True) if step else total
    by_inner = regroup(me, by_outer, shards, True)
    early = 1 if pairs > 2 else 0
    loaded = [preload(weight, pair) for pair in range(early)]
    by_inner, weight = lax.optimization_barrier((by_inner, weight))
    rows = [by_inner[0]] + [exchange(by_inner[s], s, shards, False) for s in range(1, inner)]
    loaded += [preload(weight, pair) for pair in range(early, min(early + 2, pairs - 1))]


    returned = mixing(
        me,
        rows,
        jnp.asarray(forward_x_table(full_x)),
        jnp.asarray(backward_x_table(full_x)),
        weight,
        loaded,
        shards,
    )
    returned, left, right = lax.optimization_barrier((returned, left, right))
    if shards_y == 2:
        edge = y_edge(me, left, low, high, right, shards_x, lambda own: own > 0)
        front = back = over_y(edge, 1, shards_y)
    else:
        ends = [
            y_edge(me, left, low, high, right, shards_x, lambda own, use=use: own >= use)
            for use in (0, shards_y)
        ]
        front, back = neighbours(*ends, "gy")
    planes = (flow, left, right, front, back, kernel)
    convolved = [
        convolution(me, x, *planes, shards_y, shards_x) for x in range(cells_x)
    ]

    returned = [returned[0]] + [
        exchange(returned[s], s, shards, False) for s in range(1, inner)
    ]
    returned = regroup(me, returned, shards, False)
    returned = [returned[0]] + [exchange(returned[s], s, shards, True) for s in range(1, outer)]
    coefficients = list(returned)
    for step in range(1, shards_y):
        coefficients += [over_y(part, step, shards_y) for part in returned]
    return final(
        me,
        jnp.asarray(backward_yz_table(*sizes)),
        coefficients,
        convolved,
        bias.reshape(1, channels),
        shards,
        shards_y,
    )


def solution(mesh):
    placed = (P("gx", "gy", None, None), P(("gy", "gx"), None, None, None, None), P(), P())
    return jax.shard_map(
        body, mesh=mesh, in_specs=placed, out_specs=P("gx", "gy", None, None), check_vma=False
    )
```

```python
import functools
import math

import jax
import jax.numpy as jnp
import numpy as np
from jax import lax
from jax.experimental import pallas as pl
from jax.experimental.pallas import tpu as pltpu
from jax.sharding import PartitionSpec as P

MX = 64
MY = 16
MZ = 16


def frequencies(mode_count):
    position = np.arange(mode_count)
    return np.where(position < mode_count // 2, position, position - mode_count)


def wave(first, second, length, factor):
    turns = (np.asarray(first)[:, None] * np.asarray(second)[None, :]) % length
    angles = turns * (2.0 * math.pi / length)
    return (np.cos(angles) + 1j * np.sin(angles)) * factor


def rounded(values):
    return values.astype(np.float32).astype(jnp.bfloat16).astype(np.float64)


def item_modes(shards_x, shards_y, pairs):
    index = np.arange(shards_y * shards_x * pairs).reshape(shards_y, shards_x, pairs)
    return index // MZ, index % MZ


def forward_yz_table(shards_x, shards_y, pairs, cells_y, cells_z):
    full_y = shards_y * cells_y
    turn_z = wave(np.arange(MZ), np.arange(cells_z), cells_z, cells_z**-0.5)
    turn_z = rounded(turn_z.real) - 1j * rounded(turn_z.imag)
    turn_y = np.conj(wave(frequencies(MY), np.arange(full_y), full_y, full_y**-0.5))
    mode_y, mode_z = item_modes(shards_x, shards_y, pairs)
    table = np.empty((shards_y, shards_y, shards_x, pairs, 2, cells_y, cells_z), np.float32)
    for own in range(shards_y):
        rows = turn_y[:, own * cells_y : (own + 1) * cells_y]
        product = rows[mode_y][..., :, None] * turn_z[mode_z][..., None, :]
        table[own, :, :, :, 0] = product.real
        table[own, :, :, :, 1] = product.imag
    return table.reshape(shards_y, -1, cells_y * cells_z).astype(jnp.bfloat16)


def backward_yz_table(shards_x, shards_y, pairs, cells_y, cells_z):
    full_y = shards_y * cells_y
    turn_z = wave(np.arange(MZ), np.arange(cells_z), cells_z, MZ**-0.5)
    turn_z = rounded(turn_z.real) + 1j * rounded(turn_z.imag)
    turn_y = wave(frequencies(MY), np.arange(full_y), full_y, MY**-0.5)
    mode_y, mode_z = item_modes(shards_x, shards_y, pairs)
    table = np.empty((shards_y, cells_y, cells_z, shards_y, shards_x, pairs, 2), np.float32)
    for own in range(shards_y):
        rows = turn_y[:, own * cells_y : (own + 1) * cells_y]
        product = rows[mode_y][..., :, None] * turn_z[mode_z][..., None, :]
        product = np.moveaxis(product, (3, 4), (0, 1))
        table[own, ..., 0] = product.real
        table[own, ..., 1] = -product.imag
    return table.reshape(shards_y, cells_y * cells_z, -1).astype(jnp.bfloat16)


def forward_x_table(full_x):
    turn = np.conj(wave(frequencies(MX), np.arange(full_x), full_x, full_x**-0.5))
    parts = np.empty((2, MX, 2, 2, full_x), np.float32)
    parts[0, :, 0, 0], parts[0, :, 0, 1] = turn.real, -turn.imag
    parts[0, :, 1, 0], parts[0, :, 1, 1] = turn.imag, turn.real
    parts[1, :, 0] = -parts[0, :, 1]
    parts[1, :, 1] = parts[0, :, 0]
    return parts.reshape(2 * MX * 2, 2 * full_x).astype(jnp.bfloat16)


def backward_x_table(full_x):
    turn = wave(frequencies(MX), np.arange(full_x), full_x, MX**-0.5).T
    parts = np.empty((2, full_x, MX, 2), np.float32)
    parts[0, :, :, 0], parts[0, :, :, 1] = turn.real, -turn.imag
    parts[1, :, :, 0], parts[1, :, :, 1] = turn.imag, turn.real
    return parts.reshape(2 * full_x, MX * 2).astype(jnp.bfloat16)


def dot(left, right):
    return jnp.dot(left, right, preferred_element_type=jnp.float32)


def peer(index, step, count):
    if count & (count - 1) == 0:
        return index ^ step
    return lax.rem(index + step, count)


def origin(index, step, count):
    if count & (count - 1) == 0:
        return index ^ step
    return lax.rem(index + (count - step), count)


def place(me, shards):
    outer, inner = shards
    across = lax.rem(me, outer * inner)
    return lax.div(me, outer * inner), lax.div(across, inner), lax.rem(across, inner)


def in_vmem(count):
    return [pl.BlockSpec(memory_space=pltpu.VMEM)] * count


IN_SMEM = pl.BlockSpec(memory_space=pltpu.SMEM)


def forward_kernel(shards, shards_y, pieces, step, me_ref, table_ref, flow_ref, *refs):
    *refs, table, flow, table_sems, flow_sems = refs
    cells_x = flow.shape[0]
    outer, inner = shards
    rows, channels = refs[0].shape[-2:]
    own_y, own, _ = place(me_ref[0], shards)
    owner = lax.rem(own_y + step, shards_y)
    steps = [step for piece in pieces for step in piece]
    block = inner * rows
    copies = []
    for i, other in enumerate(steps):
        start = (owner * outer + peer(own, other, outer)) * block
        source = table_ref.at[own_y, pl.ds(pl.multiple_of(start, block), block)]
        copies.append(
            pltpu.make_async_copy(source, table.at[pl.ds(i * block, block)], table_sems.at[i])
        )
    loads = [
        pltpu.make_async_copy(flow_ref.at[x], flow.at[x], flow_sems.at[x])
        for x in range(cells_x)
    ]
    for copy in copies + loads:
        copy.start()
    for copy in copies:
        copy.wait()
    width = 2 if cells_x % 2 == 0 else 1
    for x in range(0, cells_x, width):
        for i in range(width):
            loads[x + i].wait()
        columns = [flow[x + i] for i in range(width)]
        result = dot(table[...], jnp.concatenate(columns, axis=1))
        for i in range(width):
            part = result[:, i * channels : (i + 1) * channels]
            at = 0
            for ref, piece in zip(refs, pieces):
                for slot in range(len(piece)):
                    value = part[at : at + block].reshape(inner, rows, channels)
                    ref[slot, :, x + i] = value.astype(ref.dtype)
                    at += block
    if len(refs) > len(pieces):
        first, last, low, high = refs[-4:]
        first[...] = flow[0]
        last[...] = flow[cells_x - 1]
        cells_z = low.shape[1]
        low[...] = flow[:, :cells_z]
        high[...] = flow[:, flow.shape[1] - cells_z :]


def forward_yz(me, table, flow, step, shards, shards_y, pieces, dtype, edges=0):
    cells_x, positions, channels = flow.shape
    outer, inner = shards
    rows = table.shape[1] // shards_y
    unit = (inner, cells_x, rows // (outer * inner), channels)
    shapes = [jax.ShapeDtypeStruct((len(piece), *unit), dtype) for piece in pieces]
    if edges:
        shapes += [jax.ShapeDtypeStruct((positions, channels), flow.dtype)] * 2
        shapes += [jax.ShapeDtypeStruct((cells_x, edges, channels), flow.dtype)] * 2
    return pl.pallas_call(
        functools.partial(forward_kernel, shards, shards_y, pieces, step),
        in_specs=[IN_SMEM] + [pl.BlockSpec(memory_space=pltpu.HBM)] * 2,
        out_specs=in_vmem(len(shapes)),
        out_shape=shapes,
        scratch_shapes=[
            pltpu.VMEM((rows, positions), table.dtype),
            pltpu.VMEM(flow.shape, flow.dtype),
            pltpu.SemaphoreType.DMA((outer,)),
            pltpu.SemaphoreType.DMA((cells_x,)),
        ],
        compiler_params=pltpu.CompilerParams(vmem_limit_bytes=(60 if step else 10) << 20),
        cost_estimate=pl.CostEstimate(
            flops=2 * rows * positions * cells_x * channels,
            bytes_accessed=2 * positions * (rows + cells_x * channels),
            transcendentals=0,
        ),
    )(me, table, flow)


def add_kernel(count, *refs):
    out_refs = refs[count:]
    for slot, out_ref in enumerate(out_refs):
        total = refs[0][slot]
        for ref in refs[1:count]:
            total = total + ref[slot].astype(jnp.float32)
        out_ref[...] = total.astype(out_ref.dtype)


def add_pieces(own, arrived):
    slots, *unit = own.shape
    return pl.pallas_call(
        functools.partial(add_kernel, 1 + len(arrived)),
        in_specs=in_vmem(1 + len(arrived)),
        out_specs=in_vmem(slots),
        out_shape=[jax.ShapeDtypeStruct(unit, jnp.bfloat16)] * slots,
        cost_estimate=pl.CostEstimate(flops=own.size, bytes_accessed=0, transcendentals=0),
        compiler_params=pltpu.CompilerParams(vmem_limit_bytes=10 << 20),
    )(own, *arrived)


def regroup_kernel(shards, chosen, me_ref, *refs):
    _, _, own = place(me_ref[0], shards)
    count = refs[0].shape[0]
    in_refs, out_refs = refs[:-count], refs[-count:]
    for step, out_ref in enumerate(out_refs):
        at = peer(own, step, count) if chosen else step
        for slot, in_ref in enumerate(in_refs):
            out_ref[slot] = in_ref[at]


def regroup(me, arrays, shards, chosen):
    count, *unit = arrays[0].shape
    return pl.pallas_call(
        functools.partial(regroup_kernel, shards, chosen),
        in_specs=[IN_SMEM] + in_vmem(len(arrays)),
        out_specs=in_vmem(count),
        out_shape=[jax.ShapeDtypeStruct((len(arrays), *unit), arrays[0].dtype)] * count,
        cost_estimate=pl.CostEstimate(
            flops=arrays[0].size, bytes_accessed=0, transcendentals=0
        ),
        compiler_params=pltpu.CompilerParams(vmem_limit_bytes=10 << 20),
    )(me, *arrays)


def edge_kernel(choose, per_y, me_ref, left_ref, low_ref, high_ref, right_ref, out_ref):
    cells_x, cells_y = low_ref.shape[0], left_ref.shape[1]

    def fill(row, rows_ref):
        out_ref[0, 0] = left_ref[0, row]
        out_ref[1 : 1 + cells_x, 0] = rows_ref[...]
        out_ref[1 + cells_x, 0] = right_ref[0, row]

    is_low = choose(lax.div(me_ref[0], per_y))

    @pl.when(is_low)
    def _():
        fill(0, low_ref)

    @pl.when(jnp.logical_not(is_low))
    def _():
        fill(cells_y - 1, high_ref)


def y_edge(me, left, low, high, right, per_y, choose):
    cells_x, cells_z, channels = low.shape
    return pl.pallas_call(
        functools.partial(edge_kernel, choose, per_y),
        in_specs=[IN_SMEM] + in_vmem(4),
        out_specs=in_vmem(1)[0],
        out_shape=jax.ShapeDtypeStruct((cells_x + 2, 1, cells_z, channels), low.dtype),
        compiler_params=pltpu.CompilerParams(vmem_limit_bytes=4 << 20),
    )(me, left, low, high, right)


def preload_kernel(first, weight_ref, out_ref, sems):
    count = out_ref.shape[0]
    pieces = sems.shape[0] // count
    modes = out_ref.shape[1] // pieces
    copies = []
    for i in range(count * pieces):
        item, at = i // pieces, pl.ds(i % pieces * modes, modes)
        copies.append(
            pltpu.make_async_copy(
                weight_ref.at[first + item, at], out_ref.at[item, at], sems.at[i]
            )
        )
    for copy in copies:
        copy.start()
    for copy in copies:
        copy.wait()


def preload(weight, pair, count):
    shape = (2 * count, *weight.shape[1:])
    return pl.pallas_call(
        functools.partial(preload_kernel, 2 * pair),
        in_specs=[pl.BlockSpec(memory_space=pltpu.HBM)],
        out_specs=in_vmem(1)[0],
        out_shape=jax.ShapeDtypeStruct(shape, weight.dtype),
        scratch_shapes=[pltpu.SemaphoreType.DMA((2 * 2 * count,))],
        compiler_params=pltpu.CompilerParams(vmem_limit_bytes=36 << 20),
        cost_estimate=pl.CostEstimate(
            flops=0, bytes_accessed=2 * math.prod(shape), transcendentals=0
        ),
    )(weight)


def mixing_kernel(shards, loaded, me_ref, *refs):
    outer, inner = shards
    row_refs, refs = refs[:inner], refs[inner:]
    forward_ref, backward_ref, weight_ref, *refs = refs
    loaded_refs, refs = refs[:loaded], refs[loaded:]
    loaded = sum(ref.shape[0] // 2 for ref in loaded_refs)
    out_refs, (held, sems, wide, left, mixed) = refs[:inner], refs[inner:]

    channels = wide.shape[1]
    _, cells_x, item_rows, _ = row_refs[0].shape
    pairs = item_rows // 2
    full_x = outer * inner * cells_x
    half = channels // 2
    span = 2 * MX
    block = cells_x * item_rows
    _, own_outer, own_inner = place(me_ref[0], shards)

    def copy(pair):
        slot = pair - loaded
        return pltpu.make_async_copy(
            weight_ref.at[pl.ds(2 * pair, 2)], held.at[slot], sems.at[slot]
        )

    for pair in range(loaded, pairs):
        copy(pair).start()

    def rows_of(outer_index, inner_index):
        start = pl.multiple_of((outer_index * inner + inner_index) * block, block)
        return pl.ds(start, block)

    for step in range(inner):
        source = origin(own_inner, step, inner)
        for slot in range(outer):
            value = row_refs[step][slot].reshape(block, channels)
            at = rows_of(origin(own_outer, slot, outer), source)
            wide[at, :] = value.astype(jnp.float32)
    low = lax.broadcasted_iota(jnp.int32, (span, channels), 1) < half
    for pair in range(pairs):
        columns = [wide[pl.ds(2 * pair + p, full_x, stride=item_rows), :] for p in range(2)]
        columns = jnp.concatenate(columns, axis=0).astype(jnp.bfloat16)
        both = dot(forward_ref[...], columns)
        value, turned = both[:span], both[span:]
        first = jnp.where(low, value, pltpu.roll(turned, half, axis=1))
        second = jnp.where(low, pltpu.roll(value, half, axis=1), turned)
        left[pl.ds(pair * span, span), :channels] = first.astype(left.dtype)
        left[pl.ds(pair * span, span), channels:] = second.astype(left.dtype)

    group = 16
    row = lax.broadcasted_iota(jnp.int32, (group, channels), 0) // 2

    def mix(pair, tile_of):
        for step in range(span // group):
            start = pl.multiple_of(pair * span + step * group, group)
            lhs = left[pl.ds(start, group), :]
            gathered = jnp.zeros((group, channels), jnp.float32)
            for i in range(0, group // 2, 2):
                mode = step * (group // 2) + i
                tiles = [
                    jnp.concatenate([tile_of(h, mode + k) for h in range(2)], axis=0)
                    for k in range(2)
                ]
                product = dot(lhs, jnp.concatenate(tiles, axis=1))
                for k in range(2):
                    gathered = jnp.where(
                        row == i + k, product[:, k * channels : (k + 1) * channels], gathered
                    )
            mixed[pl.ds(start, group), :] = gathered.astype(mixed.dtype)

    pair = 0
    for ref in loaded_refs:
        count = ref.shape[0] // 2

        def ready(i, carry, ref=ref, pair=pair):
            mix(pair + i, lambda h, mode: ref[2 * i + h, mode])
            return carry

        lax.fori_loop(0, count, ready, 0)
        pair += count

    def streamed(pair, carry):
        copy(pair).wait()
        mix(pair, lambda h, mode: held[pair - loaded, h, mode])
        return carry

    lax.fori_loop(loaded, pairs, streamed, 0)

    for pair in range(pairs):
        result = dot(backward_ref[...], mixed[pl.ds(pair * span, span), :])
        for p in range(2):
            wide[pl.ds(2 * pair + p, full_x, stride=item_rows), :] = result[
                p * full_x : (p + 1) * full_x
            ]
    for step in range(inner):
        target = peer(own_inner, step, inner)
        for slot in range(outer):
            value = wide[rows_of(peer(own_outer, slot, outer), target), :]
            value = value.reshape(cells_x, item_rows, channels)
            out_refs[step][slot] = value.astype(out_refs[step].dtype)


def mixing(me, rows, forward_x, backward_x, weight, loaded, shards):
    outer, inner = shards
    _, cells_x, item_rows, channels = rows[0].shape
    pairs = item_rows // 2
    row_count = outer * inner * cells_x * item_rows
    streamed = pairs - sum(part.shape[0] // 2 for part in loaded)
    return pl.pallas_call(
        functools.partial(mixing_kernel, shards, len(loaded)),
        in_specs=[IN_SMEM]
        + in_vmem(inner + 2)
        + [pl.BlockSpec(memory_space=pltpu.HBM)]
        + in_vmem(len(loaded)),
        out_specs=in_vmem(inner),
        out_shape=[jax.ShapeDtypeStruct(rows[0].shape, jnp.bfloat16)] * inner,
        scratch_shapes=[
            pltpu.VMEM((streamed, 2, *weight.shape[1:]), weight.dtype),
            pltpu.SemaphoreType.DMA((streamed,)),
            pltpu.VMEM((row_count, channels), jnp.float32),
            pltpu.VMEM((pairs * 2 * MX, 2 * channels), jnp.bfloat16),
            pltpu.VMEM((pairs * 2 * MX, channels), jnp.bfloat16),
        ],
        compiler_params=pltpu.CompilerParams(vmem_limit_bytes=20 << 20),
        cost_estimate=pl.CostEstimate(
            flops=8 * weight.size, bytes_accessed=2 * weight.size, transcendentals=0
        ),
    )(me, *rows, forward_x, backward_x, weight, *loaded)


def convolution_kernel(x, width, shards_y, per_y, me_ref, *refs):
    *plane_refs, front_ref, back_ref, kernel_ref, out_ref, padded = refs
    _, cells_y, cells_z, channels = out_ref.shape
    own_y = lax.div(me_ref[0], per_y)
    for plane, ref in enumerate(plane_refs):
        padded[plane, 1 : cells_y + 1] = ref[0]
        edge = front_ref[x + plane, 0]
        padded[plane, 0] = jnp.where(own_y > 0, edge, jnp.zeros_like(edge))
        edge = back_ref[x + plane, 0]
        padded[plane, cells_y + 1] = jnp.where(own_y < shards_y - 1, edge, jnp.zeros_like(edge))

    rows = 4 if cells_y % 4 == 0 else 1
    columns = [(k, d) for k in range(width) for d in range(3)]
    columns = [columns[i : i + 2] for i in range(0, len(columns), 2)]
    none = jnp.zeros((channels, channels), kernel_ref.dtype)

    def chunk(index, carry):
        y = index * rows
        products = {}
        for group in columns:
            blocks, kernels = [], []
            for p in range(width + 2):
                if not any(0 <= p - k < 3 for k, _ in group):
                    continue
                for b in range(3):
                    part = padded[p, pl.ds(y + b, rows)]
                    blocks.append(part.reshape(rows * cells_z, channels))
                    parts = [
                        kernel_ref[p - k, b, d] if 0 <= p - k < 3 else none for k, d in group
                    ]
                    kernels.append(jnp.concatenate(parts, axis=1))
            product = dot(jnp.concatenate(blocks, axis=1), jnp.concatenate(kernels, axis=0))
            for i, column in enumerate(group):
                part = product[:, i * channels : (i + 1) * channels]
                products[column] = part.reshape(rows, cells_z, channels)
        z = lax.broadcasted_iota(jnp.int32, (rows, cells_z, channels), 1)
        for k in range(width):
            before = jnp.where(z == 0, 0.0, pltpu.roll(products[k, 0], 1, axis=1))
            after = pltpu.roll(products[k, 2], cells_z - 1, axis=1)
            after = jnp.where(z == cells_z - 1, 0.0, after)
            total = before + products[k, 1] + after
            out_ref[k, pl.ds(y, rows)] = total.astype(out_ref.dtype)
        return carry

    lax.fori_loop(0, cells_y // rows, chunk, 0)


def convolution(me, x, width, flow, left, right, front, back, kernel, shards_y, per_y):
    cells_x, cells_y, cells_z, channels = flow.shape
    specs, planes = [], []
    for p in range(x - 1, x + width + 1):
        inside = 0 <= p < cells_x
        planes.append(flow if inside else (left if p < 0 else right))
        at = p if inside else 0
        specs.append(
            pl.BlockSpec((1, cells_y, cells_z, channels), lambda i, at=at: (at, 0, 0, 0))
        )
    whole = lambda array: pl.BlockSpec(array.shape, lambda i: (0,) * array.ndim)
    shape = (width, cells_y, cells_z, channels)
    return pl.pallas_call(
        functools.partial(convolution_kernel, x, width, shards_y, per_y),
        grid=(1,),
        in_specs=[IN_SMEM] + specs + [whole(front), whole(back), whole(kernel)],
        out_specs=pl.BlockSpec(shape, lambda i: (0, 0, 0, 0)),
        out_shape=jax.ShapeDtypeStruct(shape, jnp.bfloat16),
        scratch_shapes=[pltpu.VMEM((width + 2, cells_y + 2, cells_z, channels), flow.dtype)],
        compiler_params=pltpu.CompilerParams(vmem_limit_bytes=14 << 20),
        cost_estimate=pl.CostEstimate(
            flops=3 * 27 * width * cells_y * cells_z * channels * channels,
            bytes_accessed=10 * cells_y * cells_z * channels,
            transcendentals=0,
        ),
    )(me, *planes, front, back, kernel)


def final_kernel(shards, shards_y, me_ref, table_ref, *refs):
    outer, inner = shards
    *piece_refs, bias_ref, out_ref, held = refs
    cells_x, cells_y, cells_z, channels = out_ref.shape
    width = 2 if cells_x % 2 == 0 else 1
    count = -(-cells_x // width)
    piece_refs, convolved_refs = piece_refs[:-count], piece_refs[-count:]
    own_y, own_outer, own_inner = place(me_ref[0], shards)
    rows = piece_refs[0].shape[2]

    @pl.when(pl.program_id(0) == 0)
    def _():
        for number, ref in enumerate(piece_refs):
            step, slot = divmod(number, outer)
            source_y = lax.rem(own_y + (shards_y - step), shards_y)
            source = source_y * outer + origin(own_outer, slot, outer)
            for part in range(inner):
                at = (source * inner + origin(own_inner, part, inner)) * rows
                for x in range(cells_x):
                    held[x, pl.ds(pl.multiple_of(at, rows), rows), :] = ref[part, x]

    bias = bias_ref[...]
    part = pl.program_id(0)
    count = cells_y * cells_z
    table = table_ref[own_y, pl.ds(pl.multiple_of(part * count, count), count), :]
    for x in range(0, cells_x, width):
        columns = [held[x + i] for i in range(width)]
        total = dot(table, jnp.concatenate(columns, axis=1))
        for i in range(width):
            spectral = total[:, i * channels : (i + 1) * channels]
            spectral = spectral.reshape(cells_y, cells_z, channels)
            convolved = convolved_refs[x // width][i, pl.ds(part * cells_y, cells_y)]
            value = spectral + convolved.astype(jnp.float32) + bias
            out_ref[x + i] = jax.nn.gelu(value, approximate=True).astype(out_ref.dtype)


def final(me, table, pieces, convolved, bias, shards, shards_y):
    width, cells_y, cells_z, channels = convolved[0].shape
    cells_x = width * len(convolved)
    parts = 4 if cells_y % 4 == 0 else 1
    block = (cells_x, cells_y // parts, cells_z, channels)
    depth = table.shape[2]
    return pl.pallas_call(
        functools.partial(final_kernel, shards, shards_y),
        grid_spec=pltpu.PrefetchScalarGridSpec(
            num_scalar_prefetch=1,
            grid=(parts,),
            in_specs=[
                *in_vmem(2 + len(pieces) + len(convolved)),
            ],
            out_specs=pl.BlockSpec(block, lambda i, me: (0, i, 0, 0)),
            scratch_shapes=[pltpu.VMEM((cells_x, depth, channels), jnp.bfloat16)],
        ),
        out_shape=jax.ShapeDtypeStruct((cells_x, cells_y, cells_z, channels), jnp.bfloat16),
        compiler_params=pltpu.CompilerParams(vmem_limit_bytes=10 << 20),
        cost_estimate=pl.CostEstimate(
            flops=2 * table.shape[1] * depth * cells_x * channels,
            bytes_accessed=6 * len(convolved) * convolved[0].size,
            transcendentals=len(convolved) * convolved[0].size,
        ),
    )(me, table, *pieces, *convolved, bias)


def with_halo(array, sides, width):
    for axis, dim in sides:
        size, length = (lax.axis_size(axis), array.shape[dim])
        up = [(i, (i + 1) % size) for i in range(size - 1)]
        down = [(j, i) for i, j in up]
        last = lax.slice_in_dim(array, length - width, length, axis=dim)
        initial = lax.slice_in_dim(array, 0, width, axis=dim)
        before = lax.ppermute(last, axis, up)
        after = lax.ppermute(initial, axis, down)
        array = jnp.concatenate([before, array, after], axis=dim)
    return array


def signed_modes(mode_count):
    position = jnp.arange(mode_count, dtype=jnp.int32)
    return jnp.where(position < mode_count // 2, position, position - mode_count)


def angle_grid(first, second, length):
    phase_turns = first[:, None] * second[None, :] % length
    return phase_turns.astype(jnp.float32) * (2.0 * math.pi / length)


def real_table(first, second, length, factor):
    angles = angle_grid(first, second, length)
    return jnp.stack([jnp.cos(angles) * factor, -jnp.sin(angles) * factor])


def complex_table(first, second, length, factor, direction):
    angles = angle_grid(first, second, length)
    cosine = jnp.cos(angles) * factor
    sine_part = jnp.sin(angles) * factor
    return jnp.stack(
        [jnp.stack([cosine, direction * sine_part]), jnp.stack([-direction * sine_part, cosine])]
    )


def split_pair_spectral(flow_field, spectral_weight):
    highest = lax.Precision.HIGHEST
    cells_x, cells_y, cells_z, channels = flow_field.shape
    count_x = lax.axis_size("gx")
    count_y = lax.axis_size("gy")
    full_x = cells_x * count_x
    full_y = cells_y * count_y
    item_count = spectral_weight.shape[0]
    local_y = lax.axis_index("gy") * cells_y + jnp.arange(cells_y, dtype=jnp.int32)
    grid_x = jnp.arange(full_x, dtype=jnp.int32)
    grid_z = jnp.arange(cells_z, dtype=jnp.int32)
    modes_z = jnp.arange(MZ, dtype=jnp.int32)
    forward_z = real_table(grid_z, modes_z, cells_z, cells_z ** (-0.5)).astype(jnp.bfloat16)
    z_spectrum = jnp.einsum(
        "xyzc,pzk->pxykc", flow_field, forward_z, preferred_element_type=jnp.float32
    )
    columns = lax.all_to_all(
        z_spectrum.astype(jnp.bfloat16), "gy", split_axis=4, concat_axis=2, tiled=True
    ).astype(z_spectrum.dtype)
    whole_y = jnp.arange(full_y, dtype=jnp.int32)
    forward_full = complex_table(whole_y, signed_modes(MY), full_y, full_y ** (-0.5), -1.0)
    y_spectrum = jnp.einsum("pxykc,pqyj->qxjkc", columns, forward_full, precision=highest)
    owned = lax.all_to_all(
        y_spectrum.astype(jnp.bfloat16), "gy", split_axis=2, concat_axis=4, tiled=True
    ).astype(y_spectrum.dtype)
    owned_modes = owned.reshape(2, cells_x, count_x, item_count, channels // 2)
    gathered_rows = lax.all_to_all(
        owned_modes.astype(jnp.bfloat16), "gx", split_axis=2, concat_axis=1, tiled=True
    ).astype(owned_modes.dtype)
    gathered_rows = gathered_rows.reshape(2, full_x, item_count, channels // 2)
    forward_x = complex_table(grid_x, signed_modes(MX), full_x, full_x ** (-0.5), -1.0)
    x_spectrum = jnp.einsum("pxjc,pqxm->qmjc", gathered_rows, forward_x, precision=highest).astype(
        jnp.bfloat16
    )
    products = jnp.einsum(
        "pmjc,jmqco->pqmjo", x_spectrum, spectral_weight, preferred_element_type=jnp.float32
    )
    mixed_modes = jnp.stack([products[0, 0] - products[1, 1], products[0, 1] + products[1, 0]])
    backward_x = complex_table(signed_modes(MX), grid_x, full_x, MX ** (-0.5), 1.0)
    inverse_x = jnp.einsum("pmjc,pqmx->qxjc", mixed_modes, backward_x, precision=highest)
    inverse_x = inverse_x.reshape(2, full_x, 1, item_count, channels)
    returned = lax.all_to_all(
        inverse_x.astype(jnp.bfloat16), "gx", split_axis=1, concat_axis=2, tiled=True
    ).astype(inverse_x.dtype)
    band_rows = MY // count_y
    summed = returned.reshape(2, cells_x, band_rows * MZ, 2, channels).sum(axis=3)
    summed = summed.reshape(2, cells_x, band_rows, MZ, channels)
    coefficients = lax.all_gather(summed.astype(jnp.bfloat16), "gy", axis=2, tiled=True).astype(
        summed.dtype
    )
    backward_y = complex_table(signed_modes(MY), local_y, full_y, MY ** (-0.5), 1.0)
    y_inverse = jnp.einsum("pxjkc,pqjy->qxykc", coefficients, backward_y, precision=highest).astype(
        jnp.bfloat16
    )
    backward_z = real_table(modes_z, grid_z, cells_z, MZ ** (-0.5)).astype(jnp.bfloat16)
    return jnp.einsum("pxykc,pkz->xyzc", y_inverse, backward_z, preferred_element_type=jnp.float32)


def split_pair_convolve(flow_field, conv_weight):
    cells_x, cells_y, cells_z, channels = flow_field.shape
    padded = with_halo(flow_field, (("gx", 0), ("gy", 1)), 1)
    padded = jnp.pad(padded, ((0, 0), (0, 0), (1, 1), (0, 0)))
    stacked = jnp.concatenate(
        [padded[:, :, 0:cells_z], padded[:, :, 1 : cells_z + 1], padded[:, :, 2 : cells_z + 2]],
        axis=3,
    )
    kernel = conv_weight.reshape(3, 3, 3 * channels, channels)
    accumulated = jnp.zeros((cells_x, cells_y, cells_z, channels), jnp.float32)
    for shift_x in range(3):
        for shift_y in range(3):
            accumulated = accumulated + jnp.dot(
                stacked[shift_x : shift_x + cells_x, shift_y : shift_y + cells_y],
                kernel[shift_x, shift_y],
                preferred_element_type=jnp.float32,
            )
    return accumulated


def neighbours(first, last, axis):
    size = lax.axis_size(axis)
    up = [(i, i + 1) for i in range(size - 1)]
    down = [(i + 1, i) for i in range(size - 1)]
    return lax.ppermute(last, axis, up), lax.ppermute(first, axis, down)


def exchange(array, step, shards, along_outer):
    outer, inner = shards
    pairs = []
    for i in range(outer * inner):
        a, b = divmod(i, inner)
        count, own = (outer, a) if along_outer else (inner, b)
        to = own ^ step if count & (count - 1) == 0 else (own + step) % count
        pairs.append((i, to * inner + b if along_outer else a * inner + to))
    return lax.ppermute(array, "gx", pairs)


def over_y(array, step, shards_y):
    return lax.ppermute(array, "gy", [(i, (i + step) % shards_y) for i in range(shards_y)])


def body(flow, spectral_weight, conv_weight, bias):
    cells_x, cells_y, cells_z, channels = flow.shape
    shards_x, shards_y = lax.axis_size("gx"), lax.axis_size("gy")
    items = spectral_weight.shape[0]
    pairs = items // 2
    if items % 2 or shards_y < 2:
        spectral = split_pair_spectral(flow, spectral_weight)
        convolved = split_pair_convolve(flow, conv_weight)
        return jax.nn.gelu(spectral + convolved + bias, approximate=True).astype(jnp.bfloat16)

    inner = max(d for d in range(1, shards_x + 1) if shards_x % d == 0 and d * d <= shards_x)
    shards = (shards_x // inner, inner)
    outer = shards[0]
    me = lax.axis_index(("gy", "gx")).astype(jnp.int32).reshape(1)
    sizes = (shards_x, shards_y, pairs, cells_y, cells_z)
    full_x = cells_x * shards_x

    weight = spectral_weight.reshape(items, MX, channels, channels)

    table = jnp.asarray(forward_yz_table(*sizes))
    columns = flow.reshape(cells_x, cells_y * cells_z, channels)
    order = list(range(outer - 1, -1, -1))
    cut = (outer + 1) // 2
    pieces = [piece for piece in (order[:cut], order[cut:]) if piece]
    arrived = [[] for _ in pieces]
    for step in range(1, shards_y):
        sent = forward_yz(me, table, columns, step, shards, shards_y, pieces, jnp.bfloat16)
        sent, columns, weight = lax.optimization_barrier((sent, columns, weight))
        for into, piece in zip(arrived, sent):
            into.append(over_y(piece, step, shards_y))
    *kept, first, last, low, high = forward_yz(
        me, table, columns, 0, shards, shards_y, pieces, jnp.float32, edges=cells_z
    )
    first, last = (x.reshape(1, cells_y, cells_z, channels) for x in (first, last))

    early = pairs // 4
    loaded = [preload(weight, 0, early)] if early else []
    loaded, arrived = lax.optimization_barrier((loaded, arrived))
    by_outer = [None] * outer
    for piece, own, parts in zip(pieces, kept, arrived):
        for step, total in zip(piece, add_pieces(own, parts)):
            by_outer[step] = exchange(total, step, shards, True) if step else total
    if early:
        loaded.append(preload(weight, early, early))
    by_outer, loaded = lax.optimization_barrier((by_outer, loaded))
    by_inner = regroup(me, by_outer, shards, True)
    by_inner, weight = lax.optimization_barrier((by_inner, weight))
    if early:
        loaded.append(preload(weight, 2 * early, 1))
    rows = [by_inner[0]] + [exchange(by_inner[s], s, shards, False) for s in range(1, inner)]
    rows, first, last = lax.optimization_barrier((rows, first, last))
    left, right = neighbours(first, last, "gx")


    returned = mixing(
        me,
        rows,
        jnp.asarray(forward_x_table(full_x)),
        jnp.asarray(backward_x_table(full_x)),
        weight,
        loaded,
        shards,
    )
    returned, left, right = lax.optimization_barrier((returned, left, right))
    if shards_y == 2:
        edge = y_edge(me, left, low, high, right, shards_x, lambda own: own > 0)
        front = back = over_y(edge, 1, shards_y)
    else:
        ends = [
            y_edge(me, left, low, high, right, shards_x, lambda own, use=use: own >= use)
            for use in (0, shards_y)
        ]
        front, back = neighbours(*ends, "gy")
    planes = (flow, left, right, front, back, conv_weight)
    width = 2 if cells_x % 2 == 0 else 1
    convolved = [
        convolution(me, x, width, *planes, shards_y, shards_x) for x in range(0, cells_x, width)
    ]

    returned = [returned[0]] + [
        exchange(returned[s], s, shards, False) for s in range(1, inner)
    ]
    returned = regroup(me, returned, shards, False)
    returned = [returned[0]] + [exchange(returned[s], s, shards, True) for s in range(1, outer)]
    coefficients = list(returned)
    for step in range(1, shards_y):
        coefficients += [over_y(part, step, shards_y) for part in returned]
    return final(
        me,
        jnp.asarray(backward_yz_table(*sizes)),
        coefficients,
        convolved,
        bias.reshape(1, channels),
        shards,
        shards_y,
    )


def solution(mesh):
    placed = (P("gx", "gy", None, None), P(("gy", "gx"), None, None, None, None), P(), P())
    return jax.shard_map(
        body, mesh=mesh, in_specs=placed, out_specs=P("gx", "gy", None, None), check_vma=False
    )
```

```python
import functools
import math

import jax
import jax.numpy as jnp
import numpy as np
from jax import lax
from jax.experimental import pallas as pl
from jax.experimental.pallas import tpu as pltpu
from jax.sharding import PartitionSpec as P

MX = 64
MY = 16
MZ = 16


def frequencies(mode_count):
    position = np.arange(mode_count)
    return np.where(position < mode_count // 2, position, position - mode_count)


def wave(first, second, length, factor):
    turns = (np.asarray(first)[:, None] * np.asarray(second)[None, :]) % length
    angles = turns * (2.0 * math.pi / length)
    return (np.cos(angles) + 1j * np.sin(angles)) * factor


def rounded(values):
    return values.astype(np.float32).astype(jnp.bfloat16).astype(np.float64)


def item_modes(shards_x, shards_y, pairs):
    index = np.arange(shards_y * shards_x * pairs).reshape(shards_y, shards_x, pairs)
    return index // MZ, index % MZ


def forward_yz_table(shards_x, shards_y, pairs, cells_y, cells_z):
    full_y = shards_y * cells_y
    turn_z = wave(np.arange(MZ), np.arange(cells_z), cells_z, cells_z**-0.5)
    turn_z = rounded(turn_z.real) - 1j * rounded(turn_z.imag)
    turn_y = np.conj(wave(frequencies(MY), np.arange(full_y), full_y, full_y**-0.5))
    mode_y, mode_z = item_modes(shards_x, shards_y, pairs)
    table = np.empty((shards_y, shards_y, shards_x, pairs, 2, cells_y, cells_z), np.float32)
    for own in range(shards_y):
        rows = turn_y[:, own * cells_y : (own + 1) * cells_y]
        product = rows[mode_y][..., :, None] * turn_z[mode_z][..., None, :]
        table[own, :, :, :, 0] = product.real
        table[own, :, :, :, 1] = product.imag
    return table.reshape(shards_y, -1, cells_y * cells_z).astype(jnp.bfloat16)


def backward_yz_table(shards_x, shards_y, pairs, cells_y, cells_z):
    full_y = shards_y * cells_y
    turn_z = wave(np.arange(MZ), np.arange(cells_z), cells_z, MZ**-0.5)
    turn_z = rounded(turn_z.real) + 1j * rounded(turn_z.imag)
    turn_y = wave(frequencies(MY), np.arange(full_y), full_y, MY**-0.5)
    mode_y, mode_z = item_modes(shards_x, shards_y, pairs)
    table = np.empty((shards_y, cells_y, cells_z, shards_y, shards_x, pairs, 2), np.float32)
    for own in range(shards_y):
        rows = turn_y[:, own * cells_y : (own + 1) * cells_y]
        product = rows[mode_y][..., :, None] * turn_z[mode_z][..., None, :]
        product = np.moveaxis(product, (3, 4), (0, 1))
        table[own, ..., 0] = product.real
        table[own, ..., 1] = -product.imag
    return table.reshape(shards_y, cells_y * cells_z, -1).astype(jnp.bfloat16)


def forward_x_table(full_x):
    turn = np.conj(wave(frequencies(MX), np.arange(full_x), full_x, full_x**-0.5))
    parts = np.empty((2, MX, 2, 2, full_x), np.float32)
    parts[0, :, 0, 0], parts[0, :, 0, 1] = turn.real, -turn.imag
    parts[0, :, 1, 0], parts[0, :, 1, 1] = turn.imag, turn.real
    parts[1, :, 0] = -parts[0, :, 1]
    parts[1, :, 1] = parts[0, :, 0]
    return parts.reshape(2 * MX * 2, 2 * full_x).astype(jnp.bfloat16)


def backward_x_table(full_x):
    turn = wave(frequencies(MX), np.arange(full_x), full_x, MX**-0.5).T
    parts = np.empty((2, full_x, MX, 2), np.float32)
    parts[0, :, :, 0], parts[0, :, :, 1] = turn.real, -turn.imag
    parts[1, :, :, 0], parts[1, :, :, 1] = turn.imag, turn.real
    return parts.reshape(2 * full_x, MX * 2).astype(jnp.bfloat16)


def dot(left, right):
    return jnp.dot(left, right, preferred_element_type=jnp.float32)


def peer(index, step, count):
    if count & (count - 1) == 0:
        return index ^ step
    return lax.rem(index + step, count)


def origin(index, step, count):
    if count & (count - 1) == 0:
        return index ^ step
    return lax.rem(index + (count - step), count)


def far_first(count):
    return list(range(count - 1, -1, -1))


def place(me, shards):
    outer, inner = shards
    across = lax.rem(me, outer * inner)
    return lax.div(me, outer * inner), lax.div(across, inner), lax.rem(across, inner)


def in_vmem(count):
    return [pl.BlockSpec(memory_space=pltpu.VMEM)] * count


IN_SMEM = pl.BlockSpec(memory_space=pltpu.SMEM)


def transform(table, flow_at, cells_x, refs, pieces):
    inner, _, rows, channels = refs[0].shape[1:]
    block = inner * rows
    width = 2 if cells_x % 2 == 0 else 1
    for x in range(0, cells_x, width):
        columns = [flow_at(x + i) for i in range(width)]
        result = dot(table, jnp.concatenate(columns, axis=1))
        for i in range(width):
            part = result[:, i * channels : (i + 1) * channels]
            at = 0
            for ref, piece in zip(refs, pieces):
                for slot in range(len(piece)):
                    value = part[at : at + block].reshape(inner, rows, channels)
                    ref[slot, :, x + i] = value.astype(ref.dtype)
                    at += block


def send_kernel(shards, shards_y, pieces, step, me_ref, table_ref, flow_ref, *refs):
    *refs, table, flow, table_sems, flow_sems = refs
    cells_x = flow.shape[0]
    outer, _ = shards
    block = refs[0].shape[1] * refs[0].shape[3]
    own_y, own, _ = place(me_ref[0], shards)
    owner = lax.rem(own_y + step, shards_y)
    copies = []
    for i, other in enumerate(step for piece in pieces for step in piece):
        start = (owner * outer + peer(own, other, outer)) * block
        source = table_ref.at[own_y, pl.ds(pl.multiple_of(start, block), block)]
        copies.append(
            pltpu.make_async_copy(source, table.at[pl.ds(i * block, block)], table_sems.at[i])
        )
    loads = [
        pltpu.make_async_copy(flow_ref.at[x], flow.at[x], flow_sems.at[x])
        for x in range(cells_x)
    ]
    for copy in copies + loads:
        copy.start()
    for copy in copies:
        copy.wait()

    def flow_at(x):
        loads[x].wait()
        return flow[x]

    transform(table[...], flow_at, cells_x, refs, pieces)


def keep_kernel(shards, shards_y, pieces, me_ref, table_ref, flow_ref, *refs):
    refs, (first, last, *rows) = refs[: len(pieces)], refs[len(pieces) :]
    cells_x, positions, _ = flow_ref.shape
    outer, _ = shards
    block = refs[0].shape[1] * refs[0].shape[3]
    own_y, own, _ = place(me_ref[0], shards)
    tables = []
    for other in (step for piece in pieces for step in piece):
        start = (own_y * outer + peer(own, other, outer)) * block
        tables.append(table_ref[own_y, pl.ds(pl.multiple_of(start, block), block), :])
    transform(
        jnp.concatenate(tables, axis=0), lambda x: flow_ref[x], cells_x, refs, pieces
    )
    first[...] = flow_ref[0]
    last[...] = flow_ref[cells_x - 1]
    cells_z = rows[0].shape[1]
    low, high = pl.ds(0, cells_z), pl.ds(positions - cells_z, cells_z)
    if len(rows) > 1:
        rows[0][...] = flow_ref[:, low]
        rows[1][...] = flow_ref[:, high]
    else:

        @pl.when(own_y > 0)
        def _():
            rows[0][...] = flow_ref[:, low]

        @pl.when(own_y == 0)
        def _():
            rows[0][...] = flow_ref[:, high]


def forward_yz(me, table, flow, step, shards, shards_y, pieces, cells_z=0):
    cells_x, positions, channels = flow.shape
    outer, inner = shards
    rows = table.shape[1] // shards_y
    unit = (inner, cells_x, rows // (outer * inner), channels)
    dtype = jnp.bfloat16 if step else jnp.float32
    shapes = [jax.ShapeDtypeStruct((len(piece), *unit), dtype) for piece in pieces]
    if step:
        kernel = functools.partial(send_kernel, shards, shards_y, pieces, step)
        specs = [pl.BlockSpec(memory_space=pltpu.HBM)] * 2
        scratch = [
            pltpu.VMEM((rows, positions), table.dtype),
            pltpu.VMEM(flow.shape, flow.dtype),
            pltpu.SemaphoreType.DMA((outer,)),
            pltpu.SemaphoreType.DMA((cells_x,)),
        ]
    else:
        kernel = functools.partial(keep_kernel, shards, shards_y, pieces)
        specs, scratch = in_vmem(2), []
        shapes += [jax.ShapeDtypeStruct((positions, channels), flow.dtype)] * 2
        edge = jax.ShapeDtypeStruct((cells_x, cells_z, channels), flow.dtype)
        shapes += [edge] * (1 if shards_y == 2 else 2)
    return pl.pallas_call(
        kernel,
        in_specs=[IN_SMEM] + specs,
        out_specs=in_vmem(len(shapes)),
        out_shape=shapes,
        scratch_shapes=scratch,
        compiler_params=pltpu.CompilerParams(vmem_limit_bytes=(56 if step else 10) << 20),
        cost_estimate=pl.CostEstimate(
            flops=2 * rows * positions * cells_x * channels,
            bytes_accessed=2 * positions * (rows + cells_x * channels),
            transcendentals=0,
        ),
    )(me, table, flow)


def add_kernel(count, *refs):
    out_refs = refs[count:]
    for slot, out_ref in enumerate(out_refs):
        total = refs[0][slot]
        for ref in refs[1:count]:
            total = total + ref[slot].astype(jnp.float32)
        out_ref[...] = total.astype(out_ref.dtype)


def add_pieces(own, arrived):
    slots, *unit = own.shape
    return pl.pallas_call(
        functools.partial(add_kernel, 1 + len(arrived)),
        in_specs=in_vmem(1 + len(arrived)),
        out_specs=in_vmem(slots),
        out_shape=[jax.ShapeDtypeStruct(unit, jnp.bfloat16)] * slots,
        cost_estimate=pl.CostEstimate(flops=own.size, bytes_accessed=0, transcendentals=0),
        compiler_params=pltpu.CompilerParams(vmem_limit_bytes=10 << 20),
    )(own, *arrived)


def regroup_kernel(shards, chosen, me_ref, *refs):
    _, _, own = place(me_ref[0], shards)
    count = refs[0].shape[0]
    in_refs, out_refs = refs[:-count], refs[-count:]
    for step, out_ref in enumerate(out_refs):
        at = peer(own, step, count) if chosen else step
        for number, in_ref in enumerate(in_refs):
            out_ref[far_first(len(in_refs))[number]] = in_ref[at]


def regroup(me, arrays, shards, chosen):
    count, *unit = arrays[0].shape
    return pl.pallas_call(
        functools.partial(regroup_kernel, shards, chosen),
        in_specs=[IN_SMEM] + in_vmem(len(arrays)),
        out_specs=in_vmem(count),
        out_shape=[jax.ShapeDtypeStruct((len(arrays), *unit), arrays[0].dtype)] * count,
        cost_estimate=pl.CostEstimate(
            flops=arrays[0].size, bytes_accessed=0, transcendentals=0
        ),
        compiler_params=pltpu.CompilerParams(vmem_limit_bytes=10 << 20),
    )(me, *arrays)


def halo_kernel(shards, shards_y, me_ref, first_ref, last_ref, front_ref, back_ref, *out_refs):
    own_y, own_outer, own_inner = place(me_ref[0], shards)
    even = lax.rem(own_outer * shards[1] + own_inner, 2) == 0
    cells_x, cells_z, _ = front_ref.shape
    cells_y = first_ref.shape[0] // cells_z

    def fill(out_ref, x, plane_ref):
        for y in range(cells_y):
            out_ref[y + 1] = plane_ref[pl.ds(y * cells_z, cells_z), :]
        row = front_ref[x]
        out_ref[0] = jnp.where(own_y > 0, row, jnp.zeros_like(row))
        row = back_ref[x]
        out_ref[cells_y + 1] = jnp.where(own_y < shards_y - 1, row, jnp.zeros_like(row))

    @pl.when(even)
    def _():
        fill(out_refs[0], cells_x - 1, last_ref)
        fill(out_refs[1], 0, first_ref)

    @pl.when(jnp.logical_not(even))
    def _():
        fill(out_refs[0], 0, first_ref)
        fill(out_refs[1], cells_x - 1, last_ref)


def halo_planes(me, first, last, front, back, shards, shards_y):
    cells_x, cells_z, channels = front.shape
    shape = (first.shape[0] // cells_z + 2, cells_z, channels)
    return pl.pallas_call(
        functools.partial(halo_kernel, shards, shards_y),
        in_specs=[IN_SMEM] + in_vmem(4),
        out_specs=in_vmem(2),
        out_shape=[jax.ShapeDtypeStruct(shape, first.dtype)] * 2,
        compiler_params=pltpu.CompilerParams(vmem_limit_bytes=10 << 20),
    )(me, first, last, front, back)


def preload_kernel(first, weight_ref, out_ref, sems):
    count = out_ref.shape[0]
    pieces = sems.shape[0] // count
    modes = out_ref.shape[1] // pieces
    copies = []
    for i in range(count * pieces):
        item, at = i // pieces, pl.ds(i % pieces * modes, modes)
        copies.append(
            pltpu.make_async_copy(
                weight_ref.at[first + item, at], out_ref.at[item, at], sems.at[i]
            )
        )
    for copy in copies:
        copy.start()
    for copy in copies:
        copy.wait()


def preload(weight, pair, count):
    shape = (2 * count, *weight.shape[1:])
    return pl.pallas_call(
        functools.partial(preload_kernel, 2 * pair),
        in_specs=[pl.BlockSpec(memory_space=pltpu.HBM)],
        out_specs=in_vmem(1)[0],
        out_shape=jax.ShapeDtypeStruct(shape, weight.dtype),
        scratch_shapes=[pltpu.SemaphoreType.DMA((2 * 2 * count,))],
        compiler_params=pltpu.CompilerParams(vmem_limit_bytes=36 << 20),
        cost_estimate=pl.CostEstimate(
            flops=0, bytes_accessed=2 * math.prod(shape), transcendentals=0
        ),
    )(weight)


def mixing_kernel(shards, loaded, me_ref, *refs):
    outer, inner = shards
    row_refs, refs = refs[:inner], refs[inner:]
    forward_ref, backward_ref, weight_ref, *refs = refs
    loaded_refs, refs = refs[:loaded], refs[loaded:]
    loaded = sum(ref.shape[0] // 2 for ref in loaded_refs)
    out_refs, (held, sems, wide, left, mixed) = refs[:inner], refs[inner:]

    channels = wide.shape[1]
    _, cells_x, item_rows, _ = row_refs[0].shape
    pairs = item_rows // 2
    full_x = outer * inner * cells_x
    half = channels // 2
    span = 2 * MX
    block = cells_x * item_rows
    _, own_outer, own_inner = place(me_ref[0], shards)

    def copy(pair):
        slot = pair - loaded
        return pltpu.make_async_copy(
            weight_ref.at[pl.ds(2 * pair, 2)], held.at[slot], sems.at[slot]
        )

    for pair in range(loaded, pairs):
        copy(pair).start()

    def rows_of(outer_index, inner_index):
        start = pl.multiple_of((outer_index * inner + inner_index) * block, block)
        return pl.ds(start, block)

    for number, step in enumerate(far_first(inner)):
        source = origin(own_inner, step, inner)
        for slot in range(outer):
            value = row_refs[number][slot].reshape(block, channels)
            at = rows_of(origin(own_outer, slot, outer), source)
            wide[at, :] = value.astype(jnp.float32)
    low = lax.broadcasted_iota(jnp.int32, (span, channels), 1) < half
    for pair in range(pairs):
        columns = [wide[pl.ds(2 * pair + p, full_x, stride=item_rows), :] for p in range(2)]
        columns = jnp.concatenate(columns, axis=0).astype(jnp.bfloat16)
        both = dot(forward_ref[...], columns)
        value, turned = both[:span], both[span:]
        first = jnp.where(low, value, pltpu.roll(turned, half, axis=1))
        second = jnp.where(low, pltpu.roll(value, half, axis=1), turned)
        left[pl.ds(pair * span, span), :channels] = first.astype(left.dtype)
        left[pl.ds(pair * span, span), channels:] = second.astype(left.dtype)

    group = 16
    row = lax.broadcasted_iota(jnp.int32, (group, channels), 0) // 2

    def mix(pair, tile_of):
        for step in range(span // group):
            start = pl.multiple_of(pair * span + step * group, group)
            lhs = left[pl.ds(start, group), :]
            gathered = jnp.zeros((group, channels), jnp.float32)
            for i in range(0, group // 2, 2):
                mode = step * (group // 2) + i
                tiles = [
                    jnp.concatenate([tile_of(h, mode + k) for h in range(2)], axis=0)
                    for k in range(2)
                ]
                product = dot(lhs, jnp.concatenate(tiles, axis=1))
                for k in range(2):
                    gathered = jnp.where(
                        row == i + k, product[:, k * channels : (k + 1) * channels], gathered
                    )
            mixed[pl.ds(start, group), :] = gathered.astype(mixed.dtype)

    pair = 0
    for ref in loaded_refs:
        count = ref.shape[0] // 2

        def ready(i, carry, ref=ref, pair=pair):
            mix(pair + i, lambda h, mode: ref[2 * i + h, mode])
            return carry

        lax.fori_loop(0, count, ready, 0)
        pair += count

    def streamed(pair, carry):
        copy(pair).wait()
        mix(pair, lambda h, mode: held[pair - loaded, h, mode])
        return carry

    lax.fori_loop(loaded, pairs, streamed, 0)

    for pair in range(pairs):
        result = dot(backward_ref[...], mixed[pl.ds(pair * span, span), :])
        for p in range(2):
            wide[pl.ds(2 * pair + p, full_x, stride=item_rows), :] = result[
                p * full_x : (p + 1) * full_x
            ]
    for step in range(inner):
        target = peer(own_inner, step, inner)
        for slot in range(outer):
            value = wide[rows_of(peer(own_outer, slot, outer), target), :]
            value = value.reshape(cells_x, item_rows, channels)
            out_refs[step][slot] = value.astype(out_refs[step].dtype)


def mixing(me, rows, forward_x, backward_x, weight, loaded, shards):
    outer, inner = shards
    _, cells_x, item_rows, channels = rows[0].shape
    pairs = item_rows // 2
    row_count = outer * inner * cells_x * item_rows
    streamed = pairs - sum(part.shape[0] // 2 for part in loaded)
    return pl.pallas_call(
        functools.partial(mixing_kernel, shards, len(loaded)),
        in_specs=[IN_SMEM]
        + in_vmem(inner + 2)
        + [pl.BlockSpec(memory_space=pltpu.HBM)]
        + in_vmem(len(loaded)),
        out_specs=in_vmem(inner),
        out_shape=[jax.ShapeDtypeStruct(rows[0].shape, jnp.bfloat16)] * inner,
        scratch_shapes=[
            pltpu.VMEM((streamed, 2, *weight.shape[1:]), weight.dtype),
            pltpu.SemaphoreType.DMA((streamed,)),
            pltpu.VMEM((row_count, channels), jnp.float32),
            pltpu.VMEM((pairs * 2 * MX, 2 * channels), jnp.bfloat16),
            pltpu.VMEM((pairs * 2 * MX, channels), jnp.bfloat16),
        ],
        compiler_params=pltpu.CompilerParams(vmem_limit_bytes=20 << 20),
        cost_estimate=pl.CostEstimate(
            flops=8 * weight.size, bytes_accessed=2 * weight.size, transcendentals=0
        ),
    )(me, *rows, forward_x, backward_x, weight, *loaded)


def convolution_kernel(x, cells_x, width, shards, shards_y, me_ref, *refs):
    flow_ref, paired_ref, other_ref, front_ref, back_ref, kernel_ref, out_ref, padded = refs
    _, cells_y, cells_z, channels = out_ref.shape
    own_y, own_outer, own_inner = place(me_ref[0], shards)
    even = lax.rem(own_outer * shards[1] + own_inner, 2) == 0
    for plane in range(width + 2):
        p = x + plane - 1
        if 0 <= p < cells_x:
            padded[plane, 1 : cells_y + 1] = flow_ref[p]
            row = front_ref[p]
            padded[plane, 0] = jnp.where(own_y > 0, row, jnp.zeros_like(row))
            row = back_ref[p]
            last = own_y == shards_y - 1
            padded[plane, cells_y + 1] = jnp.where(last, jnp.zeros_like(row), row)
        else:
            use_paired = jnp.logical_not(even) if p < 0 else even

            @pl.when(use_paired)
            def _(plane=plane):
                padded[plane] = paired_ref[...]

            @pl.when(jnp.logical_not(use_paired))
            def _(plane=plane):
                padded[plane] = other_ref[...]

    rows = 4 if cells_y % 4 == 0 else 1
    columns = [(k, d) for k in range(width) for d in range(3)]
    columns = [columns[i : i + 2] for i in range(0, len(columns), 2)]
    none = jnp.zeros((channels, channels), kernel_ref.dtype)

    def chunk(index, carry):
        y = index * rows
        products = {}
        for group in columns:
            blocks, kernels = [], []
            for p in range(width + 2):
                if not any(0 <= p - k < 3 for k, _ in group):
                    continue
                for b in range(3):
                    part = padded[p, pl.ds(y + b, rows)]
                    blocks.append(part.reshape(rows * cells_z, channels))
                    parts = [
                        kernel_ref[p - k, b, d] if 0 <= p - k < 3 else none for k, d in group
                    ]
                    kernels.append(jnp.concatenate(parts, axis=1))
            product = dot(jnp.concatenate(blocks, axis=1), jnp.concatenate(kernels, axis=0))
            for i, column in enumerate(group):
                part = product[:, i * channels : (i + 1) * channels]
                products[column] = part.reshape(rows, cells_z, channels)
        z = lax.broadcasted_iota(jnp.int32, (rows, cells_z, channels), 1)
        for k in range(width):
            before = jnp.where(z == 0, 0.0, pltpu.roll(products[k, 0], 1, axis=1))
            after = pltpu.roll(products[k, 2], cells_z - 1, axis=1)
            after = jnp.where(z == cells_z - 1, 0.0, after)
            total = before + products[k, 1] + after
            out_ref[k, pl.ds(y, rows)] = total.astype(out_ref.dtype)
        return carry

    lax.fori_loop(0, cells_y // rows, chunk, 0)


def convolution(me, x, width, flow, halos, kernel, shards, shards_y):
    cells_x, cells_y, cells_z, channels = flow.shape
    shape = (width, cells_y, cells_z, channels)
    return pl.pallas_call(
        functools.partial(convolution_kernel, x, cells_x, width, shards, shards_y),
        in_specs=[IN_SMEM] + in_vmem(2 + len(halos)),
        out_specs=in_vmem(1)[0],
        out_shape=jax.ShapeDtypeStruct(shape, jnp.bfloat16),
        scratch_shapes=[pltpu.VMEM((width + 2, cells_y + 2, cells_z, channels), flow.dtype)],
        compiler_params=pltpu.CompilerParams(vmem_limit_bytes=14 << 20),
        cost_estimate=pl.CostEstimate(
            flops=3 * 27 * width * cells_y * cells_z * channels * channels,
            bytes_accessed=10 * cells_y * cells_z * channels,
            transcendentals=0,
        ),
    )(me, flow, *halos, kernel)


def final_kernel(shards, shards_y, me_ref, table_ref, *refs):
    outer, inner = shards
    *piece_refs, bias_ref, out_ref, held = refs
    cells_x, cells_y, cells_z, channels = out_ref.shape
    width = 2 if cells_x % 2 == 0 else 1
    count = -(-cells_x // width)
    piece_refs, convolved_refs = piece_refs[:-count], piece_refs[-count:]
    own_y, own_outer, own_inner = place(me_ref[0], shards)
    rows = piece_refs[0].shape[2]

    @pl.when(pl.program_id(0) == 0)
    def _():
        for number, ref in enumerate(piece_refs):
            step, slot = divmod(number, outer)
            slot = far_first(outer)[slot]
            source_y = lax.rem(own_y + (shards_y - step), shards_y)
            source = source_y * outer + origin(own_outer, slot, outer)
            for part in range(inner):
                at = (source * inner + origin(own_inner, part, inner)) * rows
                for x in range(cells_x):
                    held[x, pl.ds(pl.multiple_of(at, rows), rows), :] = ref[part, x]

    bias = bias_ref[...]
    part = pl.program_id(0)
    count = cells_y * cells_z
    table = table_ref[own_y, pl.ds(pl.multiple_of(part * count, count), count), :]
    for x in range(0, cells_x, width):
        columns = [held[x + i] for i in range(width)]
        total = dot(table, jnp.concatenate(columns, axis=1))
        for i in range(width):
            spectral = total[:, i * channels : (i + 1) * channels]
            spectral = spectral.reshape(cells_y, cells_z, channels)
            convolved = convolved_refs[x // width][i, pl.ds(part * cells_y, cells_y)]
            value = spectral + convolved.astype(jnp.float32) + bias
            out_ref[x + i] = jax.nn.gelu(value, approximate=True).astype(out_ref.dtype)


def final(me, table, pieces, convolved, bias, shards, shards_y):
    width, cells_y, cells_z, channels = convolved[0].shape
    cells_x = width * len(convolved)
    parts = 4 if cells_y % 4 == 0 else 1
    block = (cells_x, cells_y // parts, cells_z, channels)
    depth = table.shape[2]
    return pl.pallas_call(
        functools.partial(final_kernel, shards, shards_y),
        grid_spec=pltpu.PrefetchScalarGridSpec(
            num_scalar_prefetch=1,
            grid=(parts,),
            in_specs=[
                *in_vmem(2 + len(pieces) + len(convolved)),
            ],
            out_specs=pl.BlockSpec(block, lambda i, me: (0, i, 0, 0)),
            scratch_shapes=[pltpu.VMEM((cells_x, depth, channels), jnp.bfloat16)],
        ),
        out_shape=jax.ShapeDtypeStruct((cells_x, cells_y, cells_z, channels), jnp.bfloat16),
        compiler_params=pltpu.CompilerParams(vmem_limit_bytes=10 << 20),
        cost_estimate=pl.CostEstimate(
            flops=2 * table.shape[1] * depth * cells_x * channels,
            bytes_accessed=6 * len(convolved) * convolved[0].size,
            transcendentals=len(convolved) * convolved[0].size,
        ),
    )(me, table, *pieces, *convolved, bias)


def with_halo(array, sides, width):
    for axis, dim in sides:
        size, length = (lax.axis_size(axis), array.shape[dim])
        up = [(i, (i + 1) % size) for i in range(size - 1)]
        down = [(j, i) for i, j in up]
        last = lax.slice_in_dim(array, length - width, length, axis=dim)
        initial = lax.slice_in_dim(array, 0, width, axis=dim)
        before = lax.ppermute(last, axis, up)
        after = lax.ppermute(initial, axis, down)
        array = jnp.concatenate([before, array, after], axis=dim)
    return array


def signed_modes(mode_count):
    position = jnp.arange(mode_count, dtype=jnp.int32)
    return jnp.where(position < mode_count // 2, position, position - mode_count)


def angle_grid(first, second, length):
    phase_turns = first[:, None] * second[None, :] % length
    return phase_turns.astype(jnp.float32) * (2.0 * math.pi / length)


def real_table(first, second, length, factor):
    angles = angle_grid(first, second, length)
    return jnp.stack([jnp.cos(angles) * factor, -jnp.sin(angles) * factor])


def complex_table(first, second, length, factor, direction):
    angles = angle_grid(first, second, length)
    cosine = jnp.cos(angles) * factor
    sine_part = jnp.sin(angles) * factor
    return jnp.stack(
        [jnp.stack([cosine, direction * sine_part]), jnp.stack([-direction * sine_part, cosine])]
    )


def split_pair_spectral(flow_field, spectral_weight):
    highest = lax.Precision.HIGHEST
    cells_x, cells_y, cells_z, channels = flow_field.shape
    count_x = lax.axis_size("gx")
    count_y = lax.axis_size("gy")
    full_x = cells_x * count_x
    full_y = cells_y * count_y
    item_count = spectral_weight.shape[0]
    local_y = lax.axis_index("gy") * cells_y + jnp.arange(cells_y, dtype=jnp.int32)
    grid_x = jnp.arange(full_x, dtype=jnp.int32)
    grid_z = jnp.arange(cells_z, dtype=jnp.int32)
    modes_z = jnp.arange(MZ, dtype=jnp.int32)
    forward_z = real_table(grid_z, modes_z, cells_z, cells_z ** (-0.5)).astype(jnp.bfloat16)
    z_spectrum = jnp.einsum(
        "xyzc,pzk->pxykc", flow_field, forward_z, preferred_element_type=jnp.float32
    )
    columns = lax.all_to_all(
        z_spectrum.astype(jnp.bfloat16), "gy", split_axis=4, concat_axis=2, tiled=True
    ).astype(z_spectrum.dtype)
    whole_y = jnp.arange(full_y, dtype=jnp.int32)
    forward_full = complex_table(whole_y, signed_modes(MY), full_y, full_y ** (-0.5), -1.0)
    y_spectrum = jnp.einsum("pxykc,pqyj->qxjkc", columns, forward_full, precision=highest)
    owned = lax.all_to_all(
        y_spectrum.astype(jnp.bfloat16), "gy", split_axis=2, concat_axis=4, tiled=True
    ).astype(y_spectrum.dtype)
    owned_modes = owned.reshape(2, cells_x, count_x, item_count, channels // 2)
    gathered_rows = lax.all_to_all(
        owned_modes.astype(jnp.bfloat16), "gx", split_axis=2, concat_axis=1, tiled=True
    ).astype(owned_modes.dtype)
    gathered_rows = gathered_rows.reshape(2, full_x, item_count, channels // 2)
    forward_x = complex_table(grid_x, signed_modes(MX), full_x, full_x ** (-0.5), -1.0)
    x_spectrum = jnp.einsum("pxjc,pqxm->qmjc", gathered_rows, forward_x, precision=highest).astype(
        jnp.bfloat16
    )
    products = jnp.einsum(
        "pmjc,jmqco->pqmjo", x_spectrum, spectral_weight, preferred_element_type=jnp.float32
    )
    mixed_modes = jnp.stack([products[0, 0] - products[1, 1], products[0, 1] + products[1, 0]])
    backward_x = complex_table(signed_modes(MX), grid_x, full_x, MX ** (-0.5), 1.0)
    inverse_x = jnp.einsum("pmjc,pqmx->qxjc", mixed_modes, backward_x, precision=highest)
    inverse_x = inverse_x.reshape(2, full_x, 1, item_count, channels)
    returned = lax.all_to_all(
        inverse_x.astype(jnp.bfloat16), "gx", split_axis=1, concat_axis=2, tiled=True
    ).astype(inverse_x.dtype)
    band_rows = MY // count_y
    summed = returned.reshape(2, cells_x, band_rows * MZ, 2, channels).sum(axis=3)
    summed = summed.reshape(2, cells_x, band_rows, MZ, channels)
    coefficients = lax.all_gather(summed.astype(jnp.bfloat16), "gy", axis=2, tiled=True).astype(
        summed.dtype
    )
    backward_y = complex_table(signed_modes(MY), local_y, full_y, MY ** (-0.5), 1.0)
    y_inverse = jnp.einsum("pxjkc,pqjy->qxykc", coefficients, backward_y, precision=highest).astype(
        jnp.bfloat16
    )
    backward_z = real_table(modes_z, grid_z, cells_z, MZ ** (-0.5)).astype(jnp.bfloat16)
    return jnp.einsum("pxykc,pkz->xyzc", y_inverse, backward_z, preferred_element_type=jnp.float32)


def split_pair_convolve(flow_field, conv_weight):
    cells_x, cells_y, cells_z, channels = flow_field.shape
    padded = with_halo(flow_field, (("gx", 0), ("gy", 1)), 1)
    padded = jnp.pad(padded, ((0, 0), (0, 0), (1, 1), (0, 0)))
    stacked = jnp.concatenate(
        [padded[:, :, 0:cells_z], padded[:, :, 1 : cells_z + 1], padded[:, :, 2 : cells_z + 2]],
        axis=3,
    )
    kernel = conv_weight.reshape(3, 3, 3 * channels, channels)
    accumulated = jnp.zeros((cells_x, cells_y, cells_z, channels), jnp.float32)
    for shift_x in range(3):
        for shift_y in range(3):
            accumulated = accumulated + jnp.dot(
                stacked[shift_x : shift_x + cells_x, shift_y : shift_y + cells_y],
                kernel[shift_x, shift_y],
                preferred_element_type=jnp.float32,
            )
    return accumulated


def neighbours(first, last, axis):
    size = lax.axis_size(axis)
    up = [(i, i + 1) for i in range(size - 1)]
    down = [(i + 1, i) for i in range(size - 1)]
    return lax.ppermute(last, axis, up), lax.ppermute(first, axis, down)


def with_neighbour(array, start, axis):
    size = lax.axis_size(axis)
    pairs = [(i, i + 1) for i in range(start, size - 1, 2)]
    return lax.ppermute(array, axis, pairs + [(j, i) for i, j in pairs])


def exchange(array, step, shards, along_outer):
    outer, inner = shards
    pairs = []
    for i in range(outer * inner):
        a, b = divmod(i, inner)
        count, own = (outer, a) if along_outer else (inner, b)
        to = own ^ step if count & (count - 1) == 0 else (own + step) % count
        pairs.append((i, to * inner + b if along_outer else a * inner + to))
    return lax.ppermute(array, "gx", pairs)


def over_y(array, step, shards_y):
    return lax.ppermute(array, "gy", [(i, (i + step) % shards_y) for i in range(shards_y)])


def body(flow, spectral_weight, conv_weight, bias):
    cells_x, cells_y, cells_z, channels = flow.shape
    shards_x, shards_y = lax.axis_size("gx"), lax.axis_size("gy")
    items = spectral_weight.shape[0]
    pairs = items // 2
    if items % 2 or shards_y < 2:
        spectral = split_pair_spectral(flow, spectral_weight)
        convolved = split_pair_convolve(flow, conv_weight)
        return jax.nn.gelu(spectral + convolved + bias, approximate=True).astype(jnp.bfloat16)

    barrier = lax.optimization_barrier
    inner = max(d for d in range(1, shards_x + 1) if shards_x % d == 0 and d * d <= shards_x)
    outer = shards_x // inner
    shards = (outer, inner)
    me = lax.axis_index(("gy", "gx")).astype(jnp.int32).reshape(1)
    sizes = (shards_x, shards_y, pairs, cells_y, cells_z)
    full_x = cells_x * shards_x
    weight = spectral_weight.reshape(items, MX, channels, channels)
    early = pairs // 4

    table = jnp.asarray(forward_yz_table(*sizes))
    columns = flow.reshape(cells_x, cells_y * cells_z, channels)
    order = far_first(outer)
    cut = (outer + 1) // 2
    pieces = [piece for piece in (order[:cut], order[cut:]) if piece]
    arrived = [[] for _ in pieces]
    for step in range(1, shards_y):
        sent = forward_yz(me, table, columns, step, shards, shards_y, pieces)
        sent, columns, weight = barrier((sent, columns, weight))
        for into, piece in zip(arrived, sent):
            into.append(over_y(piece, step, shards_y))
    kept = forward_yz(me, table, columns, 0, shards, shards_y, pieces, cells_z)
    kept, (first, last, *ends) = kept[: len(pieces)], kept[len(pieces) :]
    if shards_y == 2:
        front = back = over_y(ends[0], 1, shards_y)
    else:
        front, back = neighbours(*ends, "gy")
    loaded = [preload(weight, 0, early)] if early else []
    loaded, arrived[0] = barrier((loaded, arrived[0]))

    by_outer = []
    for piece, own, parts in zip(pieces, kept, arrived):
        for step, total in zip(piece, add_pieces(own, parts)):
            by_outer.append(exchange(total, step, shards, True) if step else total)
    if early:
        loaded.append(preload(weight, early, early))
    by_outer, loaded, weight = barrier((by_outer, loaded, weight))
    by_inner = regroup(me, by_outer, shards, True)
    by_inner, weight = barrier((by_inner, weight))
    rows = [
        exchange(by_inner[step], step, shards, False) if step else by_inner[0]
        for step in far_first(inner)
    ]
    if early:
        loaded.append(preload(weight, 2 * early, 1))

    rows, loaded, first, last, front, back = barrier((rows, loaded, first, last, front, back))
    planes = halo_planes(me, first, last, front, back, shards, shards_y)
    planes = [with_neighbour(plane, start, "gx") for start, plane in enumerate(planes)]
    returned = mixing(
        me,
        rows,
        jnp.asarray(forward_x_table(full_x)),
        jnp.asarray(backward_x_table(full_x)),
        weight,
        loaded,
        shards,
    )
    returned, planes = barrier((list(returned), planes))
    halos = (*planes, front, back)
    width = 2 if cells_x % 2 == 0 else 1
    convolved = [
        convolution(me, x, width, flow, halos, conv_weight, shards, shards_y)
        for x in range(0, cells_x, width)
    ]

    returned = [
        exchange(returned[step], step, shards, False) if step else returned[0]
        for step in far_first(inner)
    ]
    returned, convolved[0] = barrier((returned, convolved[0]))
    returned = regroup(me, returned, shards, False)
    returned = [
        exchange(returned[step], step, shards, True) if step else returned[0]
        for step in far_first(outer)
    ]
    coefficients = list(returned)
    for step in range(1, shards_y):
        coefficients += [over_y(part, step, shards_y) for part in returned]
    return final(
        me,
        jnp.asarray(backward_yz_table(*sizes)),
        coefficients,
        convolved,
        bias.reshape(1, channels),
        shards,
        shards_y,
    )


def solution(mesh):
    placed = (P("gx", "gy", None, None), P(("gy", "gx"), None, None, None, None), P(), P())
    return jax.shard_map(
        body, mesh=mesh, in_specs=placed, out_specs=P("gx", "gy", None, None), check_vma=False
    )
```

```python
import functools
import math

import jax
import jax.numpy as jnp
import numpy as np
from jax import lax
from jax.experimental import pallas as pl
from jax.experimental.pallas import tpu as pltpu
from jax.sharding import PartitionSpec as P

MX = 64
MY = 16
MZ = 16


def frequencies(mode_count):
    position = np.arange(mode_count)
    return np.where(position < mode_count // 2, position, position - mode_count)


def wave(first, second, length, factor):
    turns = (np.asarray(first)[:, None] * np.asarray(second)[None, :]) % length
    angles = turns * (2.0 * math.pi / length)
    return (np.cos(angles) + 1j * np.sin(angles)) * factor


def rounded(values):
    return values.astype(np.float32).astype(jnp.bfloat16).astype(np.float64)


def item_modes(shards_x, shards_y, pairs):
    index = np.arange(shards_y * shards_x * pairs).reshape(shards_y, shards_x, pairs)
    return index // MZ, index % MZ


def forward_yz_table(shards_x, shards_y, pairs, cells_y, cells_z):
    full_y = shards_y * cells_y
    turn_z = wave(np.arange(MZ), np.arange(cells_z), cells_z, cells_z**-0.5)
    turn_z = rounded(turn_z.real) - 1j * rounded(turn_z.imag)
    turn_y = np.conj(wave(frequencies(MY), np.arange(full_y), full_y, full_y**-0.5))
    mode_y, mode_z = item_modes(shards_x, shards_y, pairs)
    table = np.empty((shards_y, shards_y, shards_x, pairs, 2, cells_y, cells_z), np.float32)
    for own in range(shards_y):
        rows = turn_y[:, own * cells_y : (own + 1) * cells_y]
        product = rows[mode_y][..., :, None] * turn_z[mode_z][..., None, :]
        table[own, :, :, :, 0] = product.real
        table[own, :, :, :, 1] = product.imag
    return table.reshape(shards_y, -1, cells_y * cells_z).astype(jnp.bfloat16)


def backward_yz_table(shards_x, shards_y, pairs, cells_y, cells_z):
    full_y = shards_y * cells_y
    turn_z = wave(np.arange(MZ), np.arange(cells_z), cells_z, MZ**-0.5)
    turn_z = rounded(turn_z.real) + 1j * rounded(turn_z.imag)
    turn_y = wave(frequencies(MY), np.arange(full_y), full_y, MY**-0.5)
    mode_y, mode_z = item_modes(shards_x, shards_y, pairs)
    table = np.empty((shards_y, cells_y, cells_z, shards_y, shards_x, pairs, 2), np.float32)
    for own in range(shards_y):
        rows = turn_y[:, own * cells_y : (own + 1) * cells_y]
        product = rows[mode_y][..., :, None] * turn_z[mode_z][..., None, :]
        product = np.moveaxis(product, (3, 4), (0, 1))
        table[own, ..., 0] = product.real
        table[own, ..., 1] = -product.imag
    return table.reshape(shards_y, cells_y * cells_z, -1).astype(jnp.bfloat16)


def forward_x_table(full_x):
    turn = np.conj(wave(frequencies(MX), np.arange(full_x), full_x, full_x**-0.5))
    parts = np.empty((2, MX, 2, 2, full_x), np.float32)
    parts[0, :, 0, 0], parts[0, :, 0, 1] = turn.real, -turn.imag
    parts[0, :, 1, 0], parts[0, :, 1, 1] = turn.imag, turn.real
    parts[1, :, 0] = -parts[0, :, 1]
    parts[1, :, 1] = parts[0, :, 0]
    return parts.reshape(2 * MX * 2, 2 * full_x).astype(jnp.bfloat16)


def backward_x_table(full_x):
    turn = wave(frequencies(MX), np.arange(full_x), full_x, MX**-0.5).T
    parts = np.empty((2, full_x, MX, 2), np.float32)
    parts[0, :, :, 0], parts[0, :, :, 1] = turn.real, -turn.imag
    parts[1, :, :, 0], parts[1, :, :, 1] = turn.imag, turn.real
    return parts.reshape(2 * full_x, MX * 2).astype(jnp.bfloat16)


def dot(left, right):
    return jnp.dot(left, right, preferred_element_type=jnp.float32)


def peer(index, step, count):
    if count & (count - 1) == 0:
        return index ^ step
    return lax.rem(index + step, count)


def origin(index, step, count):
    if count & (count - 1) == 0:
        return index ^ step
    return lax.rem(index + (count - step), count)


def far_first(count):
    return list(range(count - 1, -1, -1))


def place(me, shards):
    outer, inner = shards
    across = lax.rem(me, outer * inner)
    return lax.div(me, outer * inner), lax.div(across, inner), lax.rem(across, inner)


def in_vmem(count):
    return [pl.BlockSpec(memory_space=pltpu.VMEM)] * count


IN_SMEM = pl.BlockSpec(memory_space=pltpu.SMEM)


def transform(table, flow_at, cells_x, refs, pieces):
    inner, _, rows, channels = refs[0].shape[1:]
    block = inner * rows
    width = 2 if cells_x % 2 == 0 else 1
    for x in range(0, cells_x, width):
        columns = [flow_at(x + i) for i in range(width)]
        result = dot(table, jnp.concatenate(columns, axis=1))
        for i in range(width):
            part = result[:, i * channels : (i + 1) * channels]
            at = 0
            for ref, piece in zip(refs, pieces):
                for slot in range(len(piece)):
                    value = part[at : at + block].reshape(inner, rows, channels)
                    ref[slot, :, x + i] = value.astype(ref.dtype)
                    at += block


def send_kernel(shards, shards_y, pieces, step, me_ref, table_ref, flow_ref, *refs):
    *refs, table, flow, table_sems, flow_sems = refs
    cells_x = flow.shape[0]
    outer, _ = shards
    block = refs[0].shape[1] * refs[0].shape[3]
    own_y, own, _ = place(me_ref[0], shards)
    owner = lax.rem(own_y + step, shards_y)
    copies = []
    for i, other in enumerate(step for piece in pieces for step in piece):
        start = (owner * outer + peer(own, other, outer)) * block
        source = table_ref.at[own_y, pl.ds(pl.multiple_of(start, block), block)]
        copies.append(
            pltpu.make_async_copy(source, table.at[pl.ds(i * block, block)], table_sems.at[i])
        )
    loads = [
        pltpu.make_async_copy(flow_ref.at[x], flow.at[x], flow_sems.at[x])
        for x in range(cells_x)
    ]
    for copy in copies + loads:
        copy.start()
    for copy in copies:
        copy.wait()

    def flow_at(x):
        loads[x].wait()
        return flow[x]

    transform(table[...], flow_at, cells_x, refs, pieces)


def is_even(me, shards):
    _, own_outer, own_inner = place(me, shards)
    return lax.rem(own_outer * shards[1] + own_inner, 2) == 0


def keep_kernel(shards, shards_y, pieces, me_ref, table_ref, flow_ref, *refs):
    refs, (to_paired, to_other, low, high) = refs[: len(pieces)], refs[len(pieces) :]
    cells_x, positions, _ = flow_ref.shape
    outer, _ = shards
    block = refs[0].shape[1] * refs[0].shape[3]
    own_y, own, _ = place(me_ref[0], shards)
    tables = []
    for other in (step for piece in pieces for step in piece):
        start = (own_y * outer + peer(own, other, outer)) * block
        tables.append(table_ref[own_y, pl.ds(pl.multiple_of(start, block), block), :])
    transform(
        jnp.concatenate(tables, axis=0), lambda x: flow_ref[x], cells_x, refs, pieces
    )
    even = is_even(me_ref[0], shards)
    to_paired[...] = flow_ref[jnp.where(even, cells_x - 1, 0)]
    to_other[...] = flow_ref[jnp.where(even, 0, cells_x - 1)]
    cells_z = low.shape[1]
    low[...] = flow_ref[:, pl.ds(0, cells_z)]
    high[...] = flow_ref[:, pl.ds(positions - cells_z, cells_z)]


def forward_yz(me, table, flow, step, shards, shards_y, pieces, cells_z=0):
    cells_x, positions, channels = flow.shape
    outer, inner = shards
    rows = table.shape[1] // shards_y
    unit = (inner, cells_x, rows // (outer * inner), channels)
    dtype = jnp.bfloat16 if step else jnp.float32
    shapes = [jax.ShapeDtypeStruct((len(piece), *unit), dtype) for piece in pieces]
    if step:
        kernel = functools.partial(send_kernel, shards, shards_y, pieces, step)
        specs = [pl.BlockSpec(memory_space=pltpu.HBM)] * 2
        scratch = [
            pltpu.VMEM((rows, positions), table.dtype),
            pltpu.VMEM(flow.shape, flow.dtype),
            pltpu.SemaphoreType.DMA((outer,)),
            pltpu.SemaphoreType.DMA((cells_x,)),
        ]
    else:
        kernel = functools.partial(keep_kernel, shards, shards_y, pieces)
        specs, scratch = in_vmem(2), []
        shapes += [jax.ShapeDtypeStruct((positions, channels), flow.dtype)] * 2
        edge = jax.ShapeDtypeStruct((cells_x, cells_z, channels), flow.dtype)
        shapes += [edge] * 2
    return pl.pallas_call(
        kernel,
        in_specs=[IN_SMEM] + specs,
        out_specs=in_vmem(len(shapes)),
        out_shape=shapes,
        scratch_shapes=scratch,
        compiler_params=pltpu.CompilerParams(vmem_limit_bytes=(56 if step else 10) << 20),
        cost_estimate=pl.CostEstimate(
            flops=2 * rows * positions * cells_x * channels,
            bytes_accessed=2 * positions * (rows + cells_x * channels),
            transcendentals=0,
        ),
    )(me, table, flow)


def add_kernel(count, *refs):
    out_refs = refs[count:]
    for slot, out_ref in enumerate(out_refs):
        total = refs[0][slot]
        for ref in refs[1:count]:
            total = total + ref[slot].astype(jnp.float32)
        out_ref[...] = total.astype(out_ref.dtype)


def add_pieces(own, arrived):
    slots, *unit = own.shape
    return pl.pallas_call(
        functools.partial(add_kernel, 1 + len(arrived)),
        in_specs=in_vmem(1 + len(arrived)),
        out_specs=in_vmem(slots),
        out_shape=[jax.ShapeDtypeStruct(unit, jnp.bfloat16)] * slots,
        cost_estimate=pl.CostEstimate(flops=own.size, bytes_accessed=0, transcendentals=0),
        compiler_params=pltpu.CompilerParams(vmem_limit_bytes=10 << 20),
    )(own, *arrived)


def regroup_kernel(shards, chosen, me_ref, *refs):
    _, _, own = place(me_ref[0], shards)
    count = refs[0].shape[0]
    in_refs, out_refs = refs[:-count], refs[-count:]
    for step, out_ref in enumerate(out_refs):
        at = peer(own, step, count) if chosen else step
        for number, in_ref in enumerate(in_refs):
            out_ref[far_first(len(in_refs))[number]] = in_ref[at]


def regroup(me, arrays, shards, chosen):
    count, *unit = arrays[0].shape
    return pl.pallas_call(
        functools.partial(regroup_kernel, shards, chosen),
        in_specs=[IN_SMEM] + in_vmem(len(arrays)),
        out_specs=in_vmem(count),
        out_shape=[jax.ShapeDtypeStruct((len(arrays), *unit), arrays[0].dtype)] * count,
        cost_estimate=pl.CostEstimate(
            flops=arrays[0].size, bytes_accessed=0, transcendentals=0
        ),
        compiler_params=pltpu.CompilerParams(vmem_limit_bytes=10 << 20),
    )(me, *arrays)


def edge_kernel(
    choose, shards, me_ref, paired_ref, other_ref, low_ref, high_ref, out_ref
):
    cells_x, cells_z, _ = low_ref.shape
    rows = paired_ref.shape[0]
    own_y, _, _ = place(me_ref[0], shards)
    is_low = choose(own_y)
    even = is_even(me_ref[0], shards)
    start = pl.multiple_of(jnp.where(is_low, 0, rows - cells_z), cells_z)
    paired, other = (ref[pl.ds(start, cells_z), :] for ref in (paired_ref, other_ref))
    out_ref[0] = jnp.where(even, other, paired)
    out_ref[1 + cells_x] = jnp.where(even, paired, other)

    @pl.when(is_low)
    def _():
        out_ref[1 : 1 + cells_x] = low_ref[...]

    @pl.when(jnp.logical_not(is_low))
    def _():
        out_ref[1 : 1 + cells_x] = high_ref[...]


def y_edge(me, paired, other, low, high, shards, choose):
    cells_x, cells_z, channels = low.shape
    return pl.pallas_call(
        functools.partial(edge_kernel, choose, shards),
        in_specs=[IN_SMEM] + in_vmem(4),
        out_specs=in_vmem(1)[0],
        out_shape=jax.ShapeDtypeStruct((cells_x + 2, cells_z, channels), low.dtype),
        compiler_params=pltpu.CompilerParams(vmem_limit_bytes=10 << 20),
    )(me, paired, other, low, high)


def preload_kernel(first, weight_ref, out_ref, sems):
    count = out_ref.shape[0]
    pieces = sems.shape[0] // count
    modes = out_ref.shape[1] // pieces
    copies = []
    for i in range(count * pieces):
        item, at = i // pieces, pl.ds(i % pieces * modes, modes)
        copies.append(
            pltpu.make_async_copy(
                weight_ref.at[first + item, at], out_ref.at[item, at], sems.at[i]
            )
        )
    for copy in copies:
        copy.start()
    for copy in copies:
        copy.wait()


def preload(weight, pair, count):
    shape = (2 * count, *weight.shape[1:])
    return pl.pallas_call(
        functools.partial(preload_kernel, 2 * pair),
        in_specs=[pl.BlockSpec(memory_space=pltpu.HBM)],
        out_specs=in_vmem(1)[0],
        out_shape=jax.ShapeDtypeStruct(shape, weight.dtype),
        scratch_shapes=[pltpu.SemaphoreType.DMA((2 * 2 * count,))],
        compiler_params=pltpu.CompilerParams(vmem_limit_bytes=36 << 20),
        cost_estimate=pl.CostEstimate(
            flops=0, bytes_accessed=2 * math.prod(shape), transcendentals=0
        ),
    )(weight)


def mixing_kernel(shards, loaded, me_ref, *refs):
    outer, inner = shards
    row_refs, refs = refs[:inner], refs[inner:]
    forward_ref, backward_ref, weight_ref, *refs = refs
    loaded_refs, refs = refs[:loaded], refs[loaded:]
    loaded = sum(ref.shape[0] // 2 for ref in loaded_refs)
    out_refs, (held, sems, wide, left, mixed) = refs[:inner], refs[inner:]

    channels = wide.shape[1]
    _, cells_x, item_rows, _ = row_refs[0].shape
    pairs = item_rows // 2
    full_x = outer * inner * cells_x
    half = channels // 2
    span = 2 * MX
    block = cells_x * item_rows
    _, own_outer, own_inner = place(me_ref[0], shards)

    def copy(pair):
        slot = pair - loaded
        return pltpu.make_async_copy(
            weight_ref.at[pl.ds(2 * pair, 2)], held.at[slot], sems.at[slot]
        )

    for pair in range(loaded, pairs):
        copy(pair).start()

    def rows_of(outer_index, inner_index):
        start = pl.multiple_of((outer_index * inner + inner_index) * block, block)
        return pl.ds(start, block)

    for number, step in enumerate(far_first(inner)):
        source = origin(own_inner, step, inner)
        for slot in range(outer):
            value = row_refs[number][slot].reshape(block, channels)
            at = rows_of(origin(own_outer, slot, outer), source)
            wide[at, :] = value.astype(jnp.float32)
    low = lax.broadcasted_iota(jnp.int32, (span, channels), 1) < half
    for pair in range(pairs):
        columns = [wide[pl.ds(2 * pair + p, full_x, stride=item_rows), :] for p in range(2)]
        columns = jnp.concatenate(columns, axis=0).astype(jnp.bfloat16)
        both = dot(forward_ref[...], columns)
        value, turned = both[:span], both[span:]
        first = jnp.where(low, value, pltpu.roll(turned, half, axis=1))
        second = jnp.where(low, pltpu.roll(value, half, axis=1), turned)
        left[pl.ds(pair * span, span), :channels] = first.astype(left.dtype)
        left[pl.ds(pair * span, span), channels:] = second.astype(left.dtype)

    group = 16
    row = lax.broadcasted_iota(jnp.int32, (group, channels), 0) // 2

    def mix(pair, tile_of):
        for step in range(span // group):
            start = pl.multiple_of(pair * span + step * group, group)
            lhs = left[pl.ds(start, group), :]
            gathered = jnp.zeros((group, channels), jnp.float32)
            for i in range(0, group // 2, 2):
                mode = step * (group // 2) + i
                tiles = [
                    jnp.concatenate([tile_of(h, mode + k) for h in range(2)], axis=0)
                    for k in range(2)
                ]
                product = dot(lhs, jnp.concatenate(tiles, axis=1))
                for k in range(2):
                    gathered = jnp.where(
                        row == i + k, product[:, k * channels : (k + 1) * channels], gathered
                    )
            mixed[pl.ds(start, group), :] = gathered.astype(mixed.dtype)

    pair = 0
    for ref in loaded_refs:
        count = ref.shape[0] // 2

        def ready(i, carry, ref=ref, pair=pair):
            mix(pair + i, lambda h, mode: ref[2 * i + h, mode])
            return carry

        lax.fori_loop(0, count, ready, 0)
        pair += count

    def streamed(pair, carry):
        copy(pair).wait()
        mix(pair, lambda h, mode: held[pair - loaded, h, mode])
        return carry

    lax.fori_loop(loaded, pairs, streamed, 0)

    for pair in range(pairs):
        result = dot(backward_ref[...], mixed[pl.ds(pair * span, span), :])
        for p in range(2):
            wide[pl.ds(2 * pair + p, full_x, stride=item_rows), :] = result[
                p * full_x : (p + 1) * full_x
            ]
    for step in range(inner):
        target = peer(own_inner, step, inner)
        for slot in range(outer):
            value = wide[rows_of(peer(own_outer, slot, outer), target), :]
            value = value.reshape(cells_x, item_rows, channels)
            out_refs[step][slot] = value.astype(out_refs[step].dtype)


def mixing(me, rows, forward_x, backward_x, weight, loaded, shards):
    outer, inner = shards
    _, cells_x, item_rows, channels = rows[0].shape
    pairs = item_rows // 2
    row_count = outer * inner * cells_x * item_rows
    streamed = pairs - sum(part.shape[0] // 2 for part in loaded)
    return pl.pallas_call(
        functools.partial(mixing_kernel, shards, len(loaded)),
        in_specs=[IN_SMEM]
        + in_vmem(inner + 2)
        + [pl.BlockSpec(memory_space=pltpu.HBM)]
        + in_vmem(len(loaded)),
        out_specs=in_vmem(inner),
        out_shape=[jax.ShapeDtypeStruct(rows[0].shape, jnp.bfloat16)] * inner,
        scratch_shapes=[
            pltpu.VMEM((streamed, 2, *weight.shape[1:]), weight.dtype),
            pltpu.SemaphoreType.DMA((streamed,)),
            pltpu.VMEM((row_count, channels), jnp.float32),
            pltpu.VMEM((pairs * 2 * MX, 2 * channels), jnp.bfloat16),
            pltpu.VMEM((pairs * 2 * MX, channels), jnp.bfloat16),
        ],
        compiler_params=pltpu.CompilerParams(vmem_limit_bytes=20 << 20),
        cost_estimate=pl.CostEstimate(
            flops=8 * weight.size, bytes_accessed=2 * weight.size, transcendentals=0
        ),
    )(me, *rows, forward_x, backward_x, weight, *loaded)


def convolution_kernel(x, cells_x, width, shards, shards_y, me_ref, *refs):
    flow_ref, paired_ref, other_ref, front_ref, back_ref, kernel_ref, out_ref, padded = refs
    _, cells_y, cells_z, channels = out_ref.shape
    own_y, _, _ = place(me_ref[0], shards)
    even = is_even(me_ref[0], shards)
    for plane in range(width + 2):
        p = x + plane - 1
        row = front_ref[p + 1]
        padded[plane, 0] = jnp.where(own_y > 0, row, jnp.zeros_like(row))
        row = back_ref[p + 1]
        last = own_y == shards_y - 1
        padded[plane, cells_y + 1] = jnp.where(last, jnp.zeros_like(row), row)
        if 0 <= p < cells_x:
            padded[plane, 1 : cells_y + 1] = flow_ref[p]
        else:
            use_paired = jnp.logical_not(even) if p < 0 else even

            @pl.when(use_paired)
            def _(plane=plane):
                padded[plane, 1 : cells_y + 1] = paired_ref[...]

            @pl.when(jnp.logical_not(use_paired))
            def _(plane=plane):
                padded[plane, 1 : cells_y + 1] = other_ref[...]

    rows = 4 if cells_y % 4 == 0 else 1
    columns = [(k, d) for k in range(width) for d in range(3)]
    columns = [columns[i : i + 2] for i in range(0, len(columns), 2)]
    none = jnp.zeros((channels, channels), kernel_ref.dtype)

    def chunk(index, carry):
        y = index * rows
        products = {}
        for group in columns:
            blocks, kernels = [], []
            for p in range(width + 2):
                if not any(0 <= p - k < 3 for k, _ in group):
                    continue
                for b in range(3):
                    part = padded[p, pl.ds(y + b, rows)]
                    blocks.append(part.reshape(rows * cells_z, channels))
                    parts = [
                        kernel_ref[p - k, b, d] if 0 <= p - k < 3 else none for k, d in group
                    ]
                    kernels.append(jnp.concatenate(parts, axis=1))
            product = dot(jnp.concatenate(blocks, axis=1), jnp.concatenate(kernels, axis=0))
            for i, column in enumerate(group):
                part = product[:, i * channels : (i + 1) * channels]
                products[column] = part.reshape(rows, cells_z, channels)
        z = lax.broadcasted_iota(jnp.int32, (rows, cells_z, channels), 1)
        for k in range(width):
            before = jnp.where(z == 0, 0.0, pltpu.roll(products[k, 0], 1, axis=1))
            after = pltpu.roll(products[k, 2], cells_z - 1, axis=1)
            after = jnp.where(z == cells_z - 1, 0.0, after)
            total = before + products[k, 1] + after
            out_ref[k, pl.ds(y, rows)] = total.astype(out_ref.dtype)
        return carry

    lax.fori_loop(0, cells_y // rows, chunk, 0)


def convolution(me, x, width, flow, halos, kernel, shards, shards_y):
    cells_x, cells_y, cells_z, channels = flow.shape
    shape = (width, cells_y, cells_z, channels)
    return pl.pallas_call(
        functools.partial(convolution_kernel, x, cells_x, width, shards, shards_y),
        in_specs=[IN_SMEM] + in_vmem(2 + len(halos)),
        out_specs=in_vmem(1)[0],
        out_shape=jax.ShapeDtypeStruct(shape, jnp.bfloat16),
        scratch_shapes=[pltpu.VMEM((width + 2, cells_y + 2, cells_z, channels), flow.dtype)],
        compiler_params=pltpu.CompilerParams(vmem_limit_bytes=14 << 20),
        cost_estimate=pl.CostEstimate(
            flops=3 * 27 * width * cells_y * cells_z * channels * channels,
            bytes_accessed=10 * cells_y * cells_z * channels,
            transcendentals=0,
        ),
    )(me, flow, *halos, kernel)


def final_kernel(shards, shards_y, me_ref, table_ref, *refs):
    outer, inner = shards
    *piece_refs, bias_ref, out_ref, held = refs
    cells_x, cells_y, cells_z, channels = out_ref.shape
    width = 2 if cells_x % 2 == 0 else 1
    count = -(-cells_x // width)
    piece_refs, convolved_refs = piece_refs[:-count], piece_refs[-count:]
    own_y, own_outer, own_inner = place(me_ref[0], shards)
    rows = piece_refs[0].shape[2]

    @pl.when(pl.program_id(0) == 0)
    def _():
        for number, ref in enumerate(piece_refs):
            step, slot = divmod(number, outer)
            slot = far_first(outer)[slot]
            source_y = lax.rem(own_y + (shards_y - step), shards_y)
            source = source_y * outer + origin(own_outer, slot, outer)
            for part in range(inner):
                at = (source * inner + origin(own_inner, part, inner)) * rows
                for x in range(cells_x):
                    held[x, pl.ds(pl.multiple_of(at, rows), rows), :] = ref[part, x]

    bias = bias_ref[...]
    part = pl.program_id(0)
    count = cells_y * cells_z
    table = table_ref[own_y, pl.ds(pl.multiple_of(part * count, count), count), :]
    for x in range(0, cells_x, width):
        columns = [held[x + i] for i in range(width)]
        total = dot(table, jnp.concatenate(columns, axis=1))
        for i in range(width):
            spectral = total[:, i * channels : (i + 1) * channels]
            spectral = spectral.reshape(cells_y, cells_z, channels)
            convolved = convolved_refs[x // width][i, pl.ds(part * cells_y, cells_y)]
            value = spectral + convolved.astype(jnp.float32) + bias
            out_ref[x + i] = jax.nn.gelu(value, approximate=True).astype(out_ref.dtype)


def final(me, table, pieces, convolved, bias, shards, shards_y):
    width, cells_y, cells_z, channels = convolved[0].shape
    cells_x = width * len(convolved)
    parts = 4 if cells_y % 4 == 0 else 1
    block = (cells_x, cells_y // parts, cells_z, channels)
    depth = table.shape[2]
    return pl.pallas_call(
        functools.partial(final_kernel, shards, shards_y),
        grid_spec=pltpu.PrefetchScalarGridSpec(
            num_scalar_prefetch=1,
            grid=(parts,),
            in_specs=[
                *in_vmem(2 + len(pieces) + len(convolved)),
            ],
            out_specs=pl.BlockSpec(block, lambda i, me: (0, i, 0, 0)),
            scratch_shapes=[pltpu.VMEM((cells_x, depth, channels), jnp.bfloat16)],
        ),
        out_shape=jax.ShapeDtypeStruct((cells_x, cells_y, cells_z, channels), jnp.bfloat16),
        compiler_params=pltpu.CompilerParams(vmem_limit_bytes=10 << 20),
        cost_estimate=pl.CostEstimate(
            flops=2 * table.shape[1] * depth * cells_x * channels,
            bytes_accessed=6 * len(convolved) * convolved[0].size,
            transcendentals=len(convolved) * convolved[0].size,
        ),
    )(me, table, *pieces, *convolved, bias)


def with_halo(array, sides, width):
    for axis, dim in sides:
        size, length = (lax.axis_size(axis), array.shape[dim])
        up = [(i, (i + 1) % size) for i in range(size - 1)]
        down = [(j, i) for i, j in up]
        last = lax.slice_in_dim(array, length - width, length, axis=dim)
        initial = lax.slice_in_dim(array, 0, width, axis=dim)
        before = lax.ppermute(last, axis, up)
        after = lax.ppermute(initial, axis, down)
        array = jnp.concatenate([before, array, after], axis=dim)
    return array


def signed_modes(mode_count):
    position = jnp.arange(mode_count, dtype=jnp.int32)
    return jnp.where(position < mode_count // 2, position, position - mode_count)


def angle_grid(first, second, length):
    phase_turns = first[:, None] * second[None, :] % length
    return phase_turns.astype(jnp.float32) * (2.0 * math.pi / length)


def real_table(first, second, length, factor):
    angles = angle_grid(first, second, length)
    return jnp.stack([jnp.cos(angles) * factor, -jnp.sin(angles) * factor])


def complex_table(first, second, length, factor, direction):
    angles = angle_grid(first, second, length)
    cosine = jnp.cos(angles) * factor
    sine_part = jnp.sin(angles) * factor
    return jnp.stack(
        [jnp.stack([cosine, direction * sine_part]), jnp.stack([-direction * sine_part, cosine])]
    )


def split_pair_spectral(flow_field, spectral_weight):
    highest = lax.Precision.HIGHEST
    cells_x, cells_y, cells_z, channels = flow_field.shape
    count_x = lax.axis_size("gx")
    count_y = lax.axis_size("gy")
    full_x = cells_x * count_x
    full_y = cells_y * count_y
    item_count = spectral_weight.shape[0]
    local_y = lax.axis_index("gy") * cells_y + jnp.arange(cells_y, dtype=jnp.int32)
    grid_x = jnp.arange(full_x, dtype=jnp.int32)
    grid_z = jnp.arange(cells_z, dtype=jnp.int32)
    modes_z = jnp.arange(MZ, dtype=jnp.int32)
    forward_z = real_table(grid_z, modes_z, cells_z, cells_z ** (-0.5)).astype(jnp.bfloat16)
    z_spectrum = jnp.einsum(
        "xyzc,pzk->pxykc", flow_field, forward_z, preferred_element_type=jnp.float32
    )
    columns = lax.all_to_all(
        z_spectrum.astype(jnp.bfloat16), "gy", split_axis=4, concat_axis=2, tiled=True
    ).astype(z_spectrum.dtype)
    whole_y = jnp.arange(full_y, dtype=jnp.int32)
    forward_full = complex_table(whole_y, signed_modes(MY), full_y, full_y ** (-0.5), -1.0)
    y_spectrum = jnp.einsum("pxykc,pqyj->qxjkc", columns, forward_full, precision=highest)
    owned = lax.all_to_all(
        y_spectrum.astype(jnp.bfloat16), "gy", split_axis=2, concat_axis=4, tiled=True
    ).astype(y_spectrum.dtype)
    owned_modes = owned.reshape(2, cells_x, count_x, item_count, channels // 2)
    gathered_rows = lax.all_to_all(
        owned_modes.astype(jnp.bfloat16), "gx", split_axis=2, concat_axis=1, tiled=True
    ).astype(owned_modes.dtype)
    gathered_rows = gathered_rows.reshape(2, full_x, item_count, channels // 2)
    forward_x = complex_table(grid_x, signed_modes(MX), full_x, full_x ** (-0.5), -1.0)
    x_spectrum = jnp.einsum("pxjc,pqxm->qmjc", gathered_rows, forward_x, precision=highest).astype(
        jnp.bfloat16
    )
    products = jnp.einsum(
        "pmjc,jmqco->pqmjo", x_spectrum, spectral_weight, preferred_element_type=jnp.float32
    )
    mixed_modes = jnp.stack([products[0, 0] - products[1, 1], products[0, 1] + products[1, 0]])
    backward_x = complex_table(signed_modes(MX), grid_x, full_x, MX ** (-0.5), 1.0)
    inverse_x = jnp.einsum("pmjc,pqmx->qxjc", mixed_modes, backward_x, precision=highest)
    inverse_x = inverse_x.reshape(2, full_x, 1, item_count, channels)
    returned = lax.all_to_all(
        inverse_x.astype(jnp.bfloat16), "gx", split_axis=1, concat_axis=2, tiled=True
    ).astype(inverse_x.dtype)
    band_rows = MY // count_y
    summed = returned.reshape(2, cells_x, band_rows * MZ, 2, channels).sum(axis=3)
    summed = summed.reshape(2, cells_x, band_rows, MZ, channels)
    coefficients = lax.all_gather(summed.astype(jnp.bfloat16), "gy", axis=2, tiled=True).astype(
        summed.dtype
    )
    backward_y = complex_table(signed_modes(MY), local_y, full_y, MY ** (-0.5), 1.0)
    y_inverse = jnp.einsum("pxjkc,pqjy->qxykc", coefficients, backward_y, precision=highest).astype(
        jnp.bfloat16
    )
    backward_z = real_table(modes_z, grid_z, cells_z, MZ ** (-0.5)).astype(jnp.bfloat16)
    return jnp.einsum("pxykc,pkz->xyzc", y_inverse, backward_z, preferred_element_type=jnp.float32)


def split_pair_convolve(flow_field, conv_weight):
    cells_x, cells_y, cells_z, channels = flow_field.shape
    padded = with_halo(flow_field, (("gx", 0), ("gy", 1)), 1)
    padded = jnp.pad(padded, ((0, 0), (0, 0), (1, 1), (0, 0)))
    stacked = jnp.concatenate(
        [padded[:, :, 0:cells_z], padded[:, :, 1 : cells_z + 1], padded[:, :, 2 : cells_z + 2]],
        axis=3,
    )
    kernel = conv_weight.reshape(3, 3, 3 * channels, channels)
    accumulated = jnp.zeros((cells_x, cells_y, cells_z, channels), jnp.float32)
    for shift_x in range(3):
        for shift_y in range(3):
            accumulated = accumulated + jnp.dot(
                stacked[shift_x : shift_x + cells_x, shift_y : shift_y + cells_y],
                kernel[shift_x, shift_y],
                preferred_element_type=jnp.float32,
            )
    return accumulated


def neighbours(first, last, axis):
    size = lax.axis_size(axis)
    up = [(i, i + 1) for i in range(size - 1)]
    down = [(i + 1, i) for i in range(size - 1)]
    return lax.ppermute(last, axis, up), lax.ppermute(first, axis, down)


def with_neighbour(array, start, axis):
    size = lax.axis_size(axis)
    pairs = [(i, i + 1) for i in range(start, size - 1, 2)]
    return lax.ppermute(array, axis, pairs + [(j, i) for i, j in pairs])


def exchange(array, step, shards, along_outer):
    outer, inner = shards
    pairs = []
    for i in range(outer * inner):
        a, b = divmod(i, inner)
        count, own = (outer, a) if along_outer else (inner, b)
        to = own ^ step if count & (count - 1) == 0 else (own + step) % count
        pairs.append((i, to * inner + b if along_outer else a * inner + to))
    return lax.ppermute(array, "gx", pairs)


def over_y(array, step, shards_y):
    return lax.ppermute(array, "gy", [(i, (i + step) % shards_y) for i in range(shards_y)])


def body(flow, spectral_weight, conv_weight, bias):
    cells_x, cells_y, cells_z, channels = flow.shape
    shards_x, shards_y = lax.axis_size("gx"), lax.axis_size("gy")
    items = spectral_weight.shape[0]
    pairs = items // 2
    if items % 2 or shards_y < 2:
        spectral = split_pair_spectral(flow, spectral_weight)
        convolved = split_pair_convolve(flow, conv_weight)
        return jax.nn.gelu(spectral + convolved + bias, approximate=True).astype(jnp.bfloat16)

    barrier = lax.optimization_barrier
    inner = max(d for d in range(1, shards_x + 1) if shards_x % d == 0 and d * d <= shards_x)
    outer = shards_x // inner
    shards = (outer, inner)
    me = lax.axis_index(("gy", "gx")).astype(jnp.int32).reshape(1)
    sizes = (shards_x, shards_y, pairs, cells_y, cells_z)
    full_x = cells_x * shards_x
    weight = spectral_weight.reshape(items, MX, channels, channels)
    early = pairs // 4

    table = jnp.asarray(forward_yz_table(*sizes))
    columns = flow.reshape(cells_x, cells_y * cells_z, channels)
    order = far_first(outer)
    cut = (outer + 1) // 2
    pieces = [piece for piece in (order[:cut], order[cut:]) if piece]
    arrived = [[] for _ in pieces]
    for step in range(1, shards_y):
        sent = forward_yz(me, table, columns, step, shards, shards_y, pieces)
        sent, columns, weight = barrier((sent, columns, weight))
        for into, piece in zip(arrived, sent):
            into.append(over_y(piece, step, shards_y))
    loaded = [preload(weight, 0, early // 2)] if early > 1 else []
    loaded, columns = barrier((loaded, columns))
    kept = forward_yz(me, table, columns, 0, shards, shards_y, pieces, cells_z)
    kept, (*ends, low, high) = kept[: len(pieces)], kept[len(pieces) :]
    planes = [with_neighbour(end, start, "gx") for start, end in enumerate(ends)]

    by_outer = []
    for piece, own, parts in zip(pieces, kept, arrived):
        for step, total in zip(piece, add_pieces(own, parts)):
            by_outer.append(exchange(total, step, shards, True) if step else total)
    if early:
        loaded.append(preload(weight, early // 2, early))
    by_outer, loaded, weight = barrier((by_outer[::-1], loaded, weight))
    by_inner = regroup(me, by_outer[::-1], shards, True)
    by_inner, weight = barrier((by_inner, weight))
    rows = [
        exchange(by_inner[step], step, shards, False) if step else by_inner[0]
        for step in far_first(inner)
    ]
    if early:
        loaded.append(preload(weight, early + early // 2, early))

    rows, loaded, planes = barrier((rows, loaded, planes))
    if shards_y == 2:
        edge = y_edge(me, *planes, low, high, shards, lambda own: own > 0)
        front = back = over_y(edge, 1, shards_y)
    else:
        ends = [
            y_edge(me, *planes, low, high, shards, lambda own, limit=limit: own < limit)
            for limit in (shards_y, 0)
        ]
        front, back = neighbours(*ends, "gy")
    returned = mixing(
        me,
        rows,
        jnp.asarray(forward_x_table(full_x)),
        jnp.asarray(backward_x_table(full_x)),
        weight,
        loaded,
        shards,
    )
    returned, front, back = barrier((list(returned), front, back))
    planes = [plane.reshape(cells_y, cells_z, channels) for plane in planes]
    halos = (*planes, front, back)
    width = 2 if cells_x % 2 == 0 else 1
    convolved = [
        convolution(me, x, width, flow, halos, conv_weight, shards, shards_y)
        for x in range(0, cells_x, width)
    ]

    returned = [
        exchange(returned[step], step, shards, False) if step else returned[0]
        for step in far_first(inner)
    ]
    returned, convolved[0] = barrier((returned, convolved[0]))
    returned = regroup(me, returned, shards, False)
    returned = [
        exchange(returned[step], step, shards, True) if step else returned[0]
        for step in far_first(outer)
    ]
    coefficients = list(returned)
    for step in range(1, shards_y):
        coefficients += [over_y(part, step, shards_y) for part in returned]
    return final(
        me,
        jnp.asarray(backward_yz_table(*sizes)),
        coefficients,
        convolved,
        bias.reshape(1, channels),
        shards,
        shards_y,
    )


def solution(mesh):
    placed = (P("gx", "gy", None, None), P(("gy", "gx"), None, None, None, None), P(), P())
    return jax.shard_map(
        body, mesh=mesh, in_specs=placed, out_specs=P("gx", "gy", None, None), check_vma=False
    )
```

```python
import functools
import math

import jax
import jax.numpy as jnp
import numpy as np
from jax import lax
from jax.experimental import pallas as pl
from jax.experimental.pallas import tpu as pltpu
from jax.sharding import PartitionSpec as P

MX = 64
MY = 16
MZ = 16


def frequencies(mode_count):
    position = np.arange(mode_count)
    return np.where(position < mode_count // 2, position, position - mode_count)


def wave(first, second, length, factor):
    turns = (np.asarray(first)[:, None] * np.asarray(second)[None, :]) % length
    angles = turns * (2.0 * math.pi / length)
    return (np.cos(angles) + 1j * np.sin(angles)) * factor


def rounded(values):
    return values.astype(np.float32).astype(jnp.bfloat16).astype(np.float64)


def item_modes(shards_x, shards_y, pairs):
    index = np.arange(shards_y * shards_x * pairs).reshape(shards_y, shards_x, pairs)
    return index // MZ, index % MZ


def forward_yz_table(shards_x, shards_y, pairs, cells_y, cells_z):
    full_y = shards_y * cells_y
    turn_z = wave(np.arange(MZ), np.arange(cells_z), cells_z, cells_z**-0.5)
    turn_z = rounded(turn_z.real) - 1j * rounded(turn_z.imag)
    turn_y = np.conj(wave(frequencies(MY), np.arange(full_y), full_y, full_y**-0.5))
    mode_y, mode_z = item_modes(shards_x, shards_y, pairs)
    table = np.empty((shards_y, shards_y, shards_x, pairs, 2, cells_y, cells_z), np.float32)
    for own in range(shards_y):
        rows = turn_y[:, own * cells_y : (own + 1) * cells_y]
        product = rows[mode_y][..., :, None] * turn_z[mode_z][..., None, :]
        table[own, :, :, :, 0] = product.real
        table[own, :, :, :, 1] = product.imag
    return table.reshape(shards_y, -1, cells_y * cells_z).astype(jnp.bfloat16)


def backward_yz_table(shards_x, shards_y, pairs, cells_y, cells_z):
    full_y = shards_y * cells_y
    turn_z = wave(np.arange(MZ), np.arange(cells_z), cells_z, MZ**-0.5)
    turn_z = rounded(turn_z.real) + 1j * rounded(turn_z.imag)
    turn_y = wave(frequencies(MY), np.arange(full_y), full_y, MY**-0.5)
    mode_y, mode_z = item_modes(shards_x, shards_y, pairs)
    table = np.empty((shards_y, shards_y, cells_y, cells_z, shards_x, pairs, 2), np.float32)
    for own in range(shards_y):
        rows = turn_y[:, own * cells_y : (own + 1) * cells_y]
        product = rows[mode_y][..., :, None] * turn_z[mode_z][..., None, :]
        product = np.moveaxis(product, (3, 4), (1, 2))
        table[own, ..., 0] = product.real
        table[own, ..., 1] = -product.imag
    return table.reshape(shards_y**2, cells_y * cells_z, -1).astype(jnp.bfloat16)


def forward_x_table(full_x):
    turn = np.conj(wave(frequencies(MX), np.arange(full_x), full_x, full_x**-0.5))
    parts = np.empty((2, MX, 2, 2, full_x), np.float32)
    parts[0, :, 0, 0], parts[0, :, 0, 1] = turn.real, -turn.imag
    parts[0, :, 1, 0], parts[0, :, 1, 1] = turn.imag, turn.real
    parts[1, :, 0] = -parts[0, :, 1]
    parts[1, :, 1] = parts[0, :, 0]
    return parts.reshape(2 * MX * 2, 2 * full_x).astype(jnp.bfloat16)


def backward_x_table(full_x):
    turn = wave(frequencies(MX), np.arange(full_x), full_x, MX**-0.5).T
    parts = np.empty((2, full_x, MX, 2), np.float32)
    parts[0, :, :, 0], parts[0, :, :, 1] = turn.real, -turn.imag
    parts[1, :, :, 0], parts[1, :, :, 1] = turn.imag, turn.real
    return parts.reshape(2 * full_x, MX * 2).astype(jnp.bfloat16)


def dot(left, right):
    return jnp.dot(left, right, preferred_element_type=jnp.float32)


def peer(index, step, count):
    if count & (count - 1) == 0:
        return index ^ step
    return lax.rem(index + step, count)


def origin(index, step, count):
    if count & (count - 1) == 0:
        return index ^ step
    return lax.rem(index + (count - step), count)


def far_first(count):
    return list(range(count - 1, -1, -1))


def place(me, shards):
    outer, inner = shards
    across = lax.rem(me, outer * inner)
    return lax.div(me, outer * inner), lax.div(across, inner), lax.rem(across, inner)


def in_vmem(count):
    return [pl.BlockSpec(memory_space=pltpu.VMEM)] * count


IN_SMEM = pl.BlockSpec(memory_space=pltpu.SMEM)


def transform(table, flow_at, cells_x, refs, pieces):
    inner, _, rows, channels = refs[0].shape[1:]
    block = inner * rows
    width = 2 if cells_x % 2 == 0 else 1
    for x in range(0, cells_x, width):
        columns = [flow_at(x + i) for i in range(width)]
        result = dot(table, jnp.concatenate(columns, axis=1))
        for i in range(width):
            part = result[:, i * channels : (i + 1) * channels]
            at = 0
            for ref, piece in zip(refs, pieces):
                for slot in range(len(piece)):
                    value = part[at : at + block].reshape(inner, rows, channels)
                    ref[slot, :, x + i] = value.astype(ref.dtype)
                    at += block


def send_kernel(shards, shards_y, pieces, step, me_ref, table_ref, flow_ref, *refs):
    *refs, table, flow, table_sems, flow_sems = refs
    refs, plane_refs = refs[: len(pieces)], refs[len(pieces) :]
    cells_x = flow.shape[0]
    outer, _ = shards
    block = refs[0].shape[1] * refs[0].shape[3]
    own_y, own, _ = place(me_ref[0], shards)
    owner = lax.rem(own_y + step, shards_y)
    copies = []
    for i, other in enumerate(step for piece in pieces for step in piece):
        start = (owner * outer + peer(own, other, outer)) * block
        source = table_ref.at[own_y, pl.ds(pl.multiple_of(start, block), block)]
        copies.append(
            pltpu.make_async_copy(source, table.at[pl.ds(i * block, block)], table_sems.at[i])
        )
    loads = [
        pltpu.make_async_copy(flow_ref.at[x], flow.at[x], flow_sems.at[x])
        for x in range(cells_x)
    ]
    for copy in copies + loads:
        copy.start()
    for copy in copies:
        copy.wait()

    def flow_at(x):
        loads[x].wait()
        return flow[x]

    transform(table[...], flow_at, cells_x, refs, pieces)
    if plane_refs:
        even = is_even(me_ref[0], shards)
        plane_refs[0][...] = flow[jnp.where(even, cells_x - 1, 0)]
        plane_refs[1][...] = flow[jnp.where(even, 0, cells_x - 1)]


def is_even(me, shards):
    _, own_outer, own_inner = place(me, shards)
    return lax.rem(own_outer * shards[1] + own_inner, 2) == 0


def keep_kernel(shards, shards_y, pieces, me_ref, table_ref, flow_ref, *refs):
    refs, (low, high) = refs[: len(pieces)], refs[len(pieces) :]
    cells_x, positions, _ = flow_ref.shape
    outer, _ = shards
    block = refs[0].shape[1] * refs[0].shape[3]
    own_y, own, _ = place(me_ref[0], shards)
    tables = []
    for other in (step for piece in pieces for step in piece):
        start = (own_y * outer + peer(own, other, outer)) * block
        tables.append(table_ref[own_y, pl.ds(pl.multiple_of(start, block), block), :])
    transform(
        jnp.concatenate(tables, axis=0), lambda x: flow_ref[x], cells_x, refs, pieces
    )
    cells_z = low.shape[1]
    low[...] = flow_ref[:, pl.ds(0, cells_z)]
    high[...] = flow_ref[:, pl.ds(positions - cells_z, cells_z)]


def forward_yz(me, table, flow, step, shards, shards_y, pieces, cells_z=0):
    cells_x, positions, channels = flow.shape
    outer, inner = shards
    rows = table.shape[1] // shards_y
    unit = (inner, cells_x, rows // (outer * inner), channels)
    dtype = jnp.bfloat16 if step else jnp.float32
    shapes = [jax.ShapeDtypeStruct((len(piece), *unit), dtype) for piece in pieces]
    if step == 1:
        shapes += [jax.ShapeDtypeStruct((positions, channels), flow.dtype)] * 2
    if step:
        kernel = functools.partial(send_kernel, shards, shards_y, pieces, step)
        specs = [pl.BlockSpec(memory_space=pltpu.HBM)] * 2
        scratch = [
            pltpu.VMEM((rows, positions), table.dtype),
            pltpu.VMEM(flow.shape, flow.dtype),
            pltpu.SemaphoreType.DMA((outer,)),
            pltpu.SemaphoreType.DMA((cells_x,)),
        ]
    else:
        kernel = functools.partial(keep_kernel, shards, shards_y, pieces)
        specs, scratch = in_vmem(2), []
        edge = jax.ShapeDtypeStruct((cells_x, cells_z, channels), flow.dtype)
        shapes += [edge] * 2
    return pl.pallas_call(
        kernel,
        in_specs=[IN_SMEM] + specs,
        out_specs=in_vmem(len(shapes)),
        out_shape=shapes,
        scratch_shapes=scratch,
        compiler_params=pltpu.CompilerParams(vmem_limit_bytes=(56 if step else 10) << 20),
        cost_estimate=pl.CostEstimate(
            flops=2 * rows * positions * cells_x * channels,
            bytes_accessed=2 * positions * (rows + cells_x * channels),
            transcendentals=0,
        ),
    )(me, table, flow)


def add_kernel(count, *refs):
    out_refs = refs[count:]
    for slot, out_ref in enumerate(out_refs):
        total = refs[0][slot]
        for ref in refs[1:count]:
            total = total + ref[slot].astype(jnp.float32)
        out_ref[...] = total.astype(out_ref.dtype)


def add_pieces(own, arrived):
    slots, *unit = own.shape
    return pl.pallas_call(
        functools.partial(add_kernel, 1 + len(arrived)),
        in_specs=in_vmem(1 + len(arrived)),
        out_specs=in_vmem(slots),
        out_shape=[jax.ShapeDtypeStruct(unit, jnp.bfloat16)] * slots,
        cost_estimate=pl.CostEstimate(flops=own.size, bytes_accessed=0, transcendentals=0),
        compiler_params=pltpu.CompilerParams(vmem_limit_bytes=10 << 20),
    )(own, *arrived)


def regroup_kernel(shards, chosen, me_ref, *refs):
    _, _, own = place(me_ref[0], shards)
    count = refs[0].shape[0]
    in_refs, out_refs = refs[:-count], refs[-count:]
    for step, out_ref in enumerate(out_refs):
        at = peer(own, step, count) if chosen else step
        for number, in_ref in enumerate(in_refs):
            out_ref[far_first(len(in_refs))[number]] = in_ref[at]


def regroup(me, arrays, shards, chosen):
    count, *unit = arrays[0].shape
    return pl.pallas_call(
        functools.partial(regroup_kernel, shards, chosen),
        in_specs=[IN_SMEM] + in_vmem(len(arrays)),
        out_specs=in_vmem(count),
        out_shape=[jax.ShapeDtypeStruct((len(arrays), *unit), arrays[0].dtype)] * count,
        cost_estimate=pl.CostEstimate(
            flops=arrays[0].size, bytes_accessed=0, transcendentals=0
        ),
        compiler_params=pltpu.CompilerParams(vmem_limit_bytes=10 << 20),
    )(me, *arrays)


def edge_kernel(
    choose, shards, me_ref, paired_ref, other_ref, low_ref, high_ref, out_ref
):
    cells_x, cells_z, _ = low_ref.shape
    rows = paired_ref.shape[0]
    own_y, _, _ = place(me_ref[0], shards)
    is_low = choose(own_y)
    even = is_even(me_ref[0], shards)
    start = pl.multiple_of(jnp.where(is_low, 0, rows - cells_z), cells_z)
    paired, other = (ref[pl.ds(start, cells_z), :] for ref in (paired_ref, other_ref))
    out_ref[0] = jnp.where(even, other, paired)
    out_ref[1 + cells_x] = jnp.where(even, paired, other)

    @pl.when(is_low)
    def _():
        out_ref[1 : 1 + cells_x] = low_ref[...]

    @pl.when(jnp.logical_not(is_low))
    def _():
        out_ref[1 : 1 + cells_x] = high_ref[...]


def y_edge(me, paired, other, low, high, shards, choose):
    cells_x, cells_z, channels = low.shape
    return pl.pallas_call(
        functools.partial(edge_kernel, choose, shards),
        in_specs=[IN_SMEM] + in_vmem(4),
        out_specs=in_vmem(1)[0],
        out_shape=jax.ShapeDtypeStruct((cells_x + 2, cells_z, channels), low.dtype),
        compiler_params=pltpu.CompilerParams(vmem_limit_bytes=10 << 20),
    )(me, paired, other, low, high)


def preload_kernel(first, weight_ref, out_ref, sems):
    count = out_ref.shape[0]
    pieces = sems.shape[0] // count
    modes = out_ref.shape[1] // pieces
    copies = []
    for i in range(count * pieces):
        item, at = i // pieces, pl.ds(i % pieces * modes, modes)
        copies.append(
            pltpu.make_async_copy(
                weight_ref.at[first + item, at], out_ref.at[item, at], sems.at[i]
            )
        )
    for copy in copies:
        copy.start()
    for copy in copies:
        copy.wait()


def preload(weight, pair, count):
    shape = (2 * count, *weight.shape[1:])
    return pl.pallas_call(
        functools.partial(preload_kernel, 2 * pair),
        in_specs=[pl.BlockSpec(memory_space=pltpu.HBM)],
        out_specs=in_vmem(1)[0],
        out_shape=jax.ShapeDtypeStruct(shape, weight.dtype),
        scratch_shapes=[pltpu.SemaphoreType.DMA((2 * 2 * count,))],
        compiler_params=pltpu.CompilerParams(vmem_limit_bytes=36 << 20),
        cost_estimate=pl.CostEstimate(
            flops=0, bytes_accessed=2 * math.prod(shape), transcendentals=0
        ),
    )(weight)


def mixing_kernel(shards, loaded, me_ref, *refs):
    outer, inner = shards
    row_refs, refs = refs[:inner], refs[inner:]
    forward_ref, backward_ref, weight_ref, *refs = refs
    loaded_refs, refs = refs[:loaded], refs[loaded:]
    loaded = sum(ref.shape[0] // 2 for ref in loaded_refs)
    out_refs, (held, sems, wide, left, mixed) = refs[:inner], refs[inner:]

    channels = wide.shape[1]
    _, cells_x, item_rows, _ = row_refs[0].shape
    pairs = item_rows // 2
    full_x = outer * inner * cells_x
    half = channels // 2
    span = 2 * MX
    block = cells_x * item_rows
    _, own_outer, own_inner = place(me_ref[0], shards)

    def copy(pair):
        slot = pair - loaded
        return pltpu.make_async_copy(
            weight_ref.at[pl.ds(2 * pair, 2)], held.at[slot], sems.at[slot]
        )

    for pair in range(loaded, pairs):
        copy(pair).start()

    def rows_of(outer_index, inner_index):
        start = pl.multiple_of((outer_index * inner + inner_index) * block, block)
        return pl.ds(start, block)

    for number, step in enumerate(far_first(inner)):
        source = origin(own_inner, step, inner)
        for slot in range(outer):
            value = row_refs[number][slot].reshape(block, channels)
            at = rows_of(origin(own_outer, slot, outer), source)
            wide[at, :] = value.astype(jnp.float32)
    low = lax.broadcasted_iota(jnp.int32, (span, channels), 1) < half
    for pair in range(pairs):
        columns = [wide[pl.ds(2 * pair + p, full_x, stride=item_rows), :] for p in range(2)]
        columns = jnp.concatenate(columns, axis=0).astype(jnp.bfloat16)
        both = dot(forward_ref[...], columns)
        value, turned = both[:span], both[span:]
        first = jnp.where(low, value, pltpu.roll(turned, half, axis=1))
        second = jnp.where(low, pltpu.roll(value, half, axis=1), turned)
        left[pl.ds(pair * span, span), :channels] = first.astype(left.dtype)
        left[pl.ds(pair * span, span), channels:] = second.astype(left.dtype)

    group = 16
    row = lax.broadcasted_iota(jnp.int32, (group, channels), 0) // 2

    def mix(pair, tile_of):
        for step in range(span // group):
            start = pl.multiple_of(pair * span + step * group, group)
            lhs = left[pl.ds(start, group), :]
            gathered = jnp.zeros((group, channels), jnp.float32)
            for i in range(0, group // 2, 2):
                mode = step * (group // 2) + i
                tiles = [
                    jnp.concatenate([tile_of(h, mode + k) for h in range(2)], axis=0)
                    for k in range(2)
                ]
                product = dot(lhs, jnp.concatenate(tiles, axis=1))
                for k in range(2):
                    gathered = jnp.where(
                        row == i + k, product[:, k * channels : (k + 1) * channels], gathered
                    )
            mixed[pl.ds(start, group), :] = gathered.astype(mixed.dtype)

    pair = 0
    for ref in loaded_refs:
        count = ref.shape[0] // 2

        def ready(i, carry, ref=ref, pair=pair):
            mix(pair + i, lambda h, mode: ref[2 * i + h, mode])
            return carry

        lax.fori_loop(0, count, ready, 0)
        pair += count

    def streamed(pair, carry):
        copy(pair).wait()
        mix(pair, lambda h, mode: held[pair - loaded, h, mode])
        return carry

    lax.fori_loop(loaded, pairs, streamed, 0)

    for pair in range(pairs):
        result = dot(backward_ref[...], mixed[pl.ds(pair * span, span), :])
        for p in range(2):
            wide[pl.ds(2 * pair + p, full_x, stride=item_rows), :] = result[
                p * full_x : (p + 1) * full_x
            ]
    for step in range(inner):
        target = peer(own_inner, step, inner)
        for slot in range(outer):
            value = wide[rows_of(peer(own_outer, slot, outer), target), :]
            value = value.reshape(cells_x, item_rows, channels)
            out_refs[step][slot] = value.astype(out_refs[step].dtype)


def mixing(me, rows, forward_x, backward_x, weight, loaded, shards):
    outer, inner = shards
    _, cells_x, item_rows, channels = rows[0].shape
    pairs = item_rows // 2
    row_count = outer * inner * cells_x * item_rows
    streamed = pairs - sum(part.shape[0] // 2 for part in loaded)
    return pl.pallas_call(
        functools.partial(mixing_kernel, shards, len(loaded)),
        in_specs=[IN_SMEM]
        + in_vmem(inner + 2)
        + [pl.BlockSpec(memory_space=pltpu.HBM)]
        + in_vmem(len(loaded)),
        out_specs=in_vmem(inner),
        out_shape=[jax.ShapeDtypeStruct(rows[0].shape, jnp.bfloat16)] * inner,
        scratch_shapes=[
            pltpu.VMEM((streamed, 2, *weight.shape[1:]), weight.dtype),
            pltpu.SemaphoreType.DMA((streamed,)),
            pltpu.VMEM((row_count, channels), jnp.float32),
            pltpu.VMEM((pairs * 2 * MX, 2 * channels), jnp.bfloat16),
            pltpu.VMEM((pairs * 2 * MX, channels), jnp.bfloat16),
        ],
        compiler_params=pltpu.CompilerParams(vmem_limit_bytes=20 << 20),
        cost_estimate=pl.CostEstimate(
            flops=8 * weight.size, bytes_accessed=2 * weight.size, transcendentals=0
        ),
    )(me, *rows, forward_x, backward_x, weight, *loaded)


def convolution_kernel(x, cells_x, width, shards, shards_y, me_ref, *refs):
    flow_ref, paired_ref, other_ref, front_ref, back_ref, kernel_ref, out_ref, padded = refs
    _, cells_y, cells_z, channels = out_ref.shape
    own_y, _, _ = place(me_ref[0], shards)
    even = is_even(me_ref[0], shards)
    for plane in range(width + 2):
        p = x + plane - 1
        row = front_ref[p + 1]
        padded[plane, 0] = jnp.where(own_y > 0, row, jnp.zeros_like(row))
        row = back_ref[p + 1]
        last = own_y == shards_y - 1
        padded[plane, cells_y + 1] = jnp.where(last, jnp.zeros_like(row), row)
        if 0 <= p < cells_x:
            padded[plane, 1 : cells_y + 1] = flow_ref[p]
        else:
            use_paired = jnp.logical_not(even) if p < 0 else even

            @pl.when(use_paired)
            def _(plane=plane):
                padded[plane, 1 : cells_y + 1] = paired_ref[...]

            @pl.when(jnp.logical_not(use_paired))
            def _(plane=plane):
                padded[plane, 1 : cells_y + 1] = other_ref[...]

    rows = 4 if cells_y % 4 == 0 else 1
    columns = [(k, d) for k in range(width) for d in range(3)]
    columns = [columns[i : i + 2] for i in range(0, len(columns), 2)]
    none = jnp.zeros((channels, channels), kernel_ref.dtype)

    def chunk(index, carry):
        y = index * rows
        products = {}
        for group in columns:
            blocks, kernels = [], []
            for p in range(width + 2):
                if not any(0 <= p - k < 3 for k, _ in group):
                    continue
                for b in range(3):
                    part = padded[p, pl.ds(y + b, rows)]
                    blocks.append(part.reshape(rows * cells_z, channels))
                    parts = [
                        kernel_ref[p - k, b, d] if 0 <= p - k < 3 else none for k, d in group
                    ]
                    kernels.append(jnp.concatenate(parts, axis=1))
            product = dot(jnp.concatenate(blocks, axis=1), jnp.concatenate(kernels, axis=0))
            for i, column in enumerate(group):
                part = product[:, i * channels : (i + 1) * channels]
                products[column] = part.reshape(rows, cells_z, channels)
        z = lax.broadcasted_iota(jnp.int32, (rows, cells_z, channels), 1)
        for k in range(width):
            before = jnp.where(z == 0, 0.0, pltpu.roll(products[k, 0], 1, axis=1))
            after = pltpu.roll(products[k, 2], cells_z - 1, axis=1)
            after = jnp.where(z == cells_z - 1, 0.0, after)
            total = before + products[k, 1] + after
            out_ref[k, pl.ds(y, rows)] = total.astype(out_ref.dtype)
        return carry

    lax.fori_loop(0, cells_y // rows, chunk, 0)


def convolution(me, x, width, flow, halos, kernel, shards, shards_y):
    cells_x, cells_y, cells_z, channels = flow.shape
    shape = (width, cells_y, cells_z, channels)
    return pl.pallas_call(
        functools.partial(convolution_kernel, x, cells_x, width, shards, shards_y),
        in_specs=[IN_SMEM] + in_vmem(2 + len(halos)),
        out_specs=in_vmem(1)[0],
        out_shape=jax.ShapeDtypeStruct(shape, jnp.bfloat16),
        scratch_shapes=[pltpu.VMEM((width + 2, cells_y + 2, cells_z, channels), flow.dtype)],
        compiler_params=pltpu.CompilerParams(vmem_limit_bytes=14 << 20),
        cost_estimate=pl.CostEstimate(
            flops=3 * 27 * width * cells_y * cells_z * channels * channels,
            bytes_accessed=10 * cells_y * cells_z * channels,
            transcendentals=0,
        ),
    )(me, flow, *halos, kernel)


def bundled_slots(count):
    slots = [0] + far_first(count)[:-1]
    cut = (count + 1) // 2
    return [part for part in (slots[:cut], slots[cut:]) if part]


def bundle_kernel(*refs):
    *in_refs, out_ref = refs
    for i, ref in enumerate(in_refs):
        out_ref[i] = ref[...]


def bundle(arrays):
    shape = (len(arrays), *arrays[0].shape)
    return pl.pallas_call(
        bundle_kernel,
        in_specs=in_vmem(len(arrays)),
        out_specs=in_vmem(1)[0],
        out_shape=jax.ShapeDtypeStruct(shape, arrays[0].dtype),
        cost_estimate=pl.CostEstimate(
            flops=math.prod(shape), bytes_accessed=0, transcendentals=0
        ),
        compiler_params=pltpu.CompilerParams(vmem_limit_bytes=10 << 20),
    )(*arrays)


def gather_pieces(me, shards, pieces, held):
    outer, inner = shards
    _, own_outer, own_inner = place(me, shards)
    for number, slot, ref in pieces:
        cells_x, rows = ref.shape[1:3]
        source = (number * outer + origin(own_outer, slot, outer)) * inner
        for part in range(inner):
            at = (source + origin(own_inner, part, inner)) * rows
            for x in range(cells_x):
                held[x, pl.ds(pl.multiple_of(at, rows), rows), :] = ref[part, x]


def inverse(me, shards, shards_y, steps, table_ref, held, part, x, width, positions):
    own_y, _, _ = place(me, shards)
    columns = [held[x + i] for i in range(width)]
    depth = table_ref.shape[2]
    total = None
    for number, step in enumerate(steps):
        source = lax.rem(own_y + (shards_y - step), shards_y)
        rows = pl.ds(pl.multiple_of(part * positions, positions), positions)
        table = table_ref[own_y * shards_y + source, rows, :]
        block = [column[number * depth : (number + 1) * depth] for column in columns]
        product = dot(table, jnp.concatenate(block, axis=1))
        total = product if total is None else total + product
    return total


def own_part_kernel(shards, shards_y, me_ref, table_ref, *refs):
    *piece_refs, bias_ref, out_ref, held = refs
    cells_x, cells_y, cells_z, channels = out_ref.shape
    width = 2 if cells_x % 2 == 0 else 1
    count = -(-cells_x // width)
    piece_refs, convolved_refs = piece_refs[:-count], piece_refs[-count:]
    slots = far_first(shards[0])
    gather_pieces(me_ref[0], shards, [(0, *p) for p in zip(slots, piece_refs)], held)
    bias = bias_ref[...]
    rows = 4 if cells_y % 4 == 0 else 1
    positions = rows * cells_z

    def chunk(part, carry):
        for x in range(0, cells_x, width):
            total = inverse(
                me_ref[0], shards, shards_y, [0], table_ref, held, part, x, width, positions
            )
            for i in range(width):
                spectral = total[:, i * channels : (i + 1) * channels]
                convolved = convolved_refs[x // width][i, pl.ds(part * rows, rows)]
                value = spectral.reshape(rows, cells_z, channels) + convolved + bias
                out_ref[x + i, pl.ds(part * rows, rows)] = value
        return carry

    lax.fori_loop(0, cells_y // rows, chunk, 0)


def last_part_kernel(shards, shards_y, me_ref, table_ref, *refs):
    *bundle_refs, partial_ref, out_ref, held = refs
    cells_x, cells_y, cells_z, channels = out_ref.shape
    bundles = bundled_slots(shards[0])
    steps = list(range(1, shards_y))
    width = 2 if cells_x % 2 == 0 else 1
    part = pl.program_id(0)

    @pl.when(part == 0)
    def _():
        pieces = []
        for i, ref in enumerate(bundle_refs):
            number, bundle = divmod(i, len(bundles))
            pieces += [(number, slot, ref.at[j]) for j, slot in enumerate(bundles[bundle])]
        gather_pieces(me_ref[0], shards, pieces, held)

    for x in range(0, cells_x, width):
        total = inverse(
            me_ref[0], shards, shards_y, steps, table_ref, held, part, x, width,
            cells_y * cells_z,
        )
        for i in range(width):
            spectral = total[:, i * channels : (i + 1) * channels]
            value = partial_ref[x + i, pl.ds(part * cells_y, cells_y)]
            value = value + spectral.reshape(cells_y, cells_z, channels)
            out_ref[x + i] = jax.nn.gelu(value, approximate=True).astype(out_ref.dtype)


def own_part(me, table, pieces, convolved, bias, shards, shards_y):
    width, cells_y, cells_z, channels = convolved[0].shape
    shape = (width * len(convolved), cells_y, cells_z, channels)
    depth = table.shape[2]
    return pl.pallas_call(
        functools.partial(own_part_kernel, shards, shards_y),
        in_specs=[IN_SMEM] + in_vmem(2 + len(pieces) + len(convolved)),
        out_specs=in_vmem(1)[0],
        out_shape=jax.ShapeDtypeStruct(shape, jnp.float32),
        scratch_shapes=[pltpu.VMEM((shape[0], depth, channels), jnp.bfloat16)],
        compiler_params=pltpu.CompilerParams(vmem_limit_bytes=14 << 20),
        cost_estimate=pl.CostEstimate(
            flops=2 * math.prod(shape) * depth,
            bytes_accessed=6 * math.prod(shape),
            transcendentals=0,
        ),
    )(me, table, *pieces, *convolved, bias)


def last_part(me, table, pieces, partial, shards, shards_y):
    cells_x, cells_y, cells_z, channels = partial.shape
    parts = 4 if cells_y % 4 == 0 else 1
    block = (cells_x, cells_y // parts, cells_z, channels)
    depth = table.shape[2] * (shards_y - 1)
    return pl.pallas_call(
        functools.partial(last_part_kernel, shards, shards_y),
        grid_spec=pltpu.PrefetchScalarGridSpec(
            num_scalar_prefetch=1,
            grid=(parts,),
            in_specs=in_vmem(2 + len(pieces)),
            out_specs=pl.BlockSpec(block, lambda i, me: (0, i, 0, 0)),
            scratch_shapes=[pltpu.VMEM((cells_x, depth, channels), jnp.bfloat16)],
        ),
        out_shape=jax.ShapeDtypeStruct(partial.shape, jnp.bfloat16),
        compiler_params=pltpu.CompilerParams(vmem_limit_bytes=14 << 20),
        cost_estimate=pl.CostEstimate(
            flops=2 * partial.size * depth,
            bytes_accessed=6 * partial.size,
            transcendentals=partial.size,
        ),
    )(me, table, *pieces, partial)


def with_halo(array, sides, width):
    for axis, dim in sides:
        size, length = (lax.axis_size(axis), array.shape[dim])
        up = [(i, (i + 1) % size) for i in range(size - 1)]
        down = [(j, i) for i, j in up]
        last = lax.slice_in_dim(array, length - width, length, axis=dim)
        initial = lax.slice_in_dim(array, 0, width, axis=dim)
        before = lax.ppermute(last, axis, up)
        after = lax.ppermute(initial, axis, down)
        array = jnp.concatenate([before, array, after], axis=dim)
    return array


def signed_modes(mode_count):
    position = jnp.arange(mode_count, dtype=jnp.int32)
    return jnp.where(position < mode_count // 2, position, position - mode_count)


def angle_grid(first, second, length):
    phase_turns = first[:, None] * second[None, :] % length
    return phase_turns.astype(jnp.float32) * (2.0 * math.pi / length)


def real_table(first, second, length, factor):
    angles = angle_grid(first, second, length)
    return jnp.stack([jnp.cos(angles) * factor, -jnp.sin(angles) * factor])


def complex_table(first, second, length, factor, direction):
    angles = angle_grid(first, second, length)
    cosine = jnp.cos(angles) * factor
    sine_part = jnp.sin(angles) * factor
    return jnp.stack(
        [jnp.stack([cosine, direction * sine_part]), jnp.stack([-direction * sine_part, cosine])]
    )


def split_pair_spectral(flow_field, spectral_weight):
    highest = lax.Precision.HIGHEST
    cells_x, cells_y, cells_z, channels = flow_field.shape
    count_x = lax.axis_size("gx")
    count_y = lax.axis_size("gy")
    full_x = cells_x * count_x
    full_y = cells_y * count_y
    item_count = spectral_weight.shape[0]
    local_y = lax.axis_index("gy") * cells_y + jnp.arange(cells_y, dtype=jnp.int32)
    grid_x = jnp.arange(full_x, dtype=jnp.int32)
    grid_z = jnp.arange(cells_z, dtype=jnp.int32)
    modes_z = jnp.arange(MZ, dtype=jnp.int32)
    forward_z = real_table(grid_z, modes_z, cells_z, cells_z ** (-0.5)).astype(jnp.bfloat16)
    z_spectrum = jnp.einsum(
        "xyzc,pzk->pxykc", flow_field, forward_z, preferred_element_type=jnp.float32
    )
    columns = lax.all_to_all(
        z_spectrum.astype(jnp.bfloat16), "gy", split_axis=4, concat_axis=2, tiled=True
    ).astype(z_spectrum.dtype)
    whole_y = jnp.arange(full_y, dtype=jnp.int32)
    forward_full = complex_table(whole_y, signed_modes(MY), full_y, full_y ** (-0.5), -1.0)
    y_spectrum = jnp.einsum("pxykc,pqyj->qxjkc", columns, forward_full, precision=highest)
    owned = lax.all_to_all(
        y_spectrum.astype(jnp.bfloat16), "gy", split_axis=2, concat_axis=4, tiled=True
    ).astype(y_spectrum.dtype)
    owned_modes = owned.reshape(2, cells_x, count_x, item_count, channels // 2)
    gathered_rows = lax.all_to_all(
        owned_modes.astype(jnp.bfloat16), "gx", split_axis=2, concat_axis=1, tiled=True
    ).astype(owned_modes.dtype)
    gathered_rows = gathered_rows.reshape(2, full_x, item_count, channels // 2)
    forward_x = complex_table(grid_x, signed_modes(MX), full_x, full_x ** (-0.5), -1.0)
    x_spectrum = jnp.einsum("pxjc,pqxm->qmjc", gathered_rows, forward_x, precision=highest).astype(
        jnp.bfloat16
    )
    products = jnp.einsum(
        "pmjc,jmqco->pqmjo", x_spectrum, spectral_weight, preferred_element_type=jnp.float32
    )
    mixed_modes = jnp.stack([products[0, 0] - products[1, 1], products[0, 1] + products[1, 0]])
    backward_x = complex_table(signed_modes(MX), grid_x, full_x, MX ** (-0.5), 1.0)
    inverse_x = jnp.einsum("pmjc,pqmx->qxjc", mixed_modes, backward_x, precision=highest)
    inverse_x = inverse_x.reshape(2, full_x, 1, item_count, channels)
    returned = lax.all_to_all(
        inverse_x.astype(jnp.bfloat16), "gx", split_axis=1, concat_axis=2, tiled=True
    ).astype(inverse_x.dtype)
    band_rows = MY // count_y
    summed = returned.reshape(2, cells_x, band_rows * MZ, 2, channels).sum(axis=3)
    summed = summed.reshape(2, cells_x, band_rows, MZ, channels)
    coefficients = lax.all_gather(summed.astype(jnp.bfloat16), "gy", axis=2, tiled=True).astype(
        summed.dtype
    )
    backward_y = complex_table(signed_modes(MY), local_y, full_y, MY ** (-0.5), 1.0)
    y_inverse = jnp.einsum("pxjkc,pqjy->qxykc", coefficients, backward_y, precision=highest).astype(
        jnp.bfloat16
    )
    backward_z = real_table(modes_z, grid_z, cells_z, MZ ** (-0.5)).astype(jnp.bfloat16)
    return jnp.einsum("pxykc,pkz->xyzc", y_inverse, backward_z, preferred_element_type=jnp.float32)


def split_pair_convolve(flow_field, conv_weight):
    cells_x, cells_y, cells_z, channels = flow_field.shape
    padded = with_halo(flow_field, (("gx", 0), ("gy", 1)), 1)
    padded = jnp.pad(padded, ((0, 0), (0, 0), (1, 1), (0, 0)))
    stacked = jnp.concatenate(
        [padded[:, :, 0:cells_z], padded[:, :, 1 : cells_z + 1], padded[:, :, 2 : cells_z + 2]],
        axis=3,
    )
    kernel = conv_weight.reshape(3, 3, 3 * channels, channels)
    accumulated = jnp.zeros((cells_x, cells_y, cells_z, channels), jnp.float32)
    for shift_x in range(3):
        for shift_y in range(3):
            accumulated = accumulated + jnp.dot(
                stacked[shift_x : shift_x + cells_x, shift_y : shift_y + cells_y],
                kernel[shift_x, shift_y],
                preferred_element_type=jnp.float32,
            )
    return accumulated


def neighbours(first, last, axis):
    size = lax.axis_size(axis)
    up = [(i, i + 1) for i in range(size - 1)]
    down = [(i + 1, i) for i in range(size - 1)]
    return lax.ppermute(last, axis, up), lax.ppermute(first, axis, down)


def with_neighbour(array, start, axis):
    size = lax.axis_size(axis)
    pairs = [(i, i + 1) for i in range(start, size - 1, 2)]
    return lax.ppermute(array, axis, pairs + [(j, i) for i, j in pairs])


def exchange(array, step, shards, along_outer):
    outer, inner = shards
    pairs = []
    for i in range(outer * inner):
        a, b = divmod(i, inner)
        count, own = (outer, a) if along_outer else (inner, b)
        to = own ^ step if count & (count - 1) == 0 else (own + step) % count
        pairs.append((i, to * inner + b if along_outer else a * inner + to))
    return lax.ppermute(array, "gx", pairs)


def over_y(array, step, shards_y):
    return lax.ppermute(array, "gy", [(i, (i + step) % shards_y) for i in range(shards_y)])


def body(flow, spectral_weight, conv_weight, bias):
    cells_x, cells_y, cells_z, channels = flow.shape
    shards_x, shards_y = lax.axis_size("gx"), lax.axis_size("gy")
    items = spectral_weight.shape[0]
    pairs = items // 2
    if items % 2 or shards_y < 2:
        spectral = split_pair_spectral(flow, spectral_weight)
        convolved = split_pair_convolve(flow, conv_weight)
        return jax.nn.gelu(spectral + convolved + bias, approximate=True).astype(jnp.bfloat16)

    barrier = lax.optimization_barrier
    inner = max(d for d in range(1, shards_x + 1) if shards_x % d == 0 and d * d <= shards_x)
    outer = shards_x // inner
    shards = (outer, inner)
    me = lax.axis_index(("gy", "gx")).astype(jnp.int32).reshape(1)
    sizes = (shards_x, shards_y, pairs, cells_y, cells_z)
    full_x = cells_x * shards_x
    weight = spectral_weight.reshape(items, MX, channels, channels)
    early = pairs // 4

    table = jnp.asarray(forward_yz_table(*sizes))
    columns = flow.reshape(cells_x, cells_y * cells_z, channels)
    order = far_first(outer)
    cut = (outer + 1) // 2
    pieces = [piece for piece in (order[:cut], order[cut:]) if piece]
    arrived = [[] for _ in pieces]
    for step in range(1, shards_y):
        sent = forward_yz(me, table, columns, step, shards, shards_y, pieces)
        sent, columns, weight = barrier((sent, columns, weight))
        for into, piece in zip(arrived, sent):
            into.append(over_y(piece, step, shards_y))
        if step == 1:
            ends = sent[len(pieces) :]
            planes = [with_neighbour(end, start, "gx") for start, end in enumerate(ends)]
    loaded = [preload(weight, 0, early // 2)] if early > 1 else []
    loaded, columns = barrier((loaded, columns))
    kept = forward_yz(me, table, columns, 0, shards, shards_y, pieces, cells_z)
    kept, (low, high) = kept[: len(pieces)], kept[len(pieces) :]

    by_outer = []
    for piece, own, parts in zip(pieces, kept, arrived):
        for step, total in zip(piece, add_pieces(own, parts)):
            by_outer.append(exchange(total, step, shards, True) if step else total)
    if early:
        loaded.append(preload(weight, early // 2, early))
    by_outer, loaded, weight = barrier((by_outer[::-1], loaded, weight))
    by_inner = regroup(me, by_outer[::-1], shards, True)
    by_inner, weight = barrier((by_inner, weight))
    rows = [
        exchange(by_inner[step], step, shards, False) if step else by_inner[0]
        for step in far_first(inner)
    ]
    if early:
        loaded.append(preload(weight, early + early // 2, early))

    rows, loaded, planes = barrier((rows, loaded, planes))
    if shards_y == 2:
        edge = y_edge(me, *planes, low, high, shards, lambda own: own > 0)
        front = back = over_y(edge, 1, shards_y)
    else:
        ends = [
            y_edge(me, *planes, low, high, shards, lambda own, limit=limit: own < limit)
            for limit in (shards_y, 0)
        ]
        front, back = neighbours(*ends, "gy")
    returned = mixing(
        me,
        rows,
        jnp.asarray(forward_x_table(full_x)),
        jnp.asarray(backward_x_table(full_x)),
        weight,
        loaded,
        shards,
    )
    returned, front, back = barrier((list(returned), front, back))
    planes = [plane.reshape(cells_y, cells_z, channels) for plane in planes]
    halos = (*planes, front, back)
    width = 2 if cells_x % 2 == 0 else 1
    convolved = [
        convolution(me, x, width, flow, halos, conv_weight, shards, shards_y)
        for x in range(0, cells_x, width)
    ]

    returned = [
        exchange(returned[step], step, shards, False) if step else returned[0]
        for step in far_first(inner)
    ]
    returned, convolved[0] = barrier((returned, convolved[0]))
    returned = regroup(me, returned, shards, False)
    returned = [
        exchange(returned[step], step, shards, True) if step else returned[0]
        for step in far_first(outer)
    ]
    returned[0], convolved[-1] = barrier((returned[0], convolved[-1]))
    by_slot = dict(zip(far_first(outer), returned))
    bundles = [bundle([by_slot[slot] for slot in slots]) for slots in bundled_slots(outer)]
    others = []
    for step in range(1, shards_y):
        others += [over_y(part, step, shards_y) for part in bundles]
    table = jnp.asarray(backward_yz_table(*sizes))
    bias = bias.reshape(1, channels)
    partial = own_part(me, table, returned, convolved, bias, shards, shards_y)
    return last_part(me, table, others, partial, shards, shards_y)


def solution(mesh):
    placed = (P("gx", "gy", None, None), P(("gy", "gx"), None, None, None, None), P(), P())
    return jax.shard_map(
        body, mesh=mesh, in_specs=placed, out_specs=P("gx", "gy", None, None), check_vma=False
    )
```

```python
import functools
import math

import jax
import jax.numpy as jnp
import numpy as np
from jax import lax
from jax.experimental import pallas as pl
from jax.experimental.pallas import tpu as pltpu
from jax.sharding import PartitionSpec as P

MX = 64
MY = 16
MZ = 16


def frequencies(mode_count):
    position = np.arange(mode_count)
    return np.where(position < mode_count // 2, position, position - mode_count)


def wave(first, second, length, factor):
    turns = (np.asarray(first)[:, None] * np.asarray(second)[None, :]) % length
    angles = turns * (2.0 * math.pi / length)
    return (np.cos(angles) + 1j * np.sin(angles)) * factor


def rounded(values):
    return values.astype(np.float32).astype(jnp.bfloat16).astype(np.float64)


def item_modes(shards_x, shards_y, pairs):
    index = np.arange(shards_y * shards_x * pairs).reshape(shards_y, shards_x, pairs)
    return index // MZ, index % MZ


def forward_yz_table(shards_x, shards_y, pairs, cells_y, cells_z):
    full_y = shards_y * cells_y
    turn_z = wave(np.arange(MZ), np.arange(cells_z), cells_z, cells_z**-0.5)
    turn_z = rounded(turn_z.real) - 1j * rounded(turn_z.imag)
    turn_y = np.conj(wave(frequencies(MY), np.arange(full_y), full_y, full_y**-0.5))
    mode_y, mode_z = item_modes(shards_x, shards_y, pairs)
    table = np.empty((shards_y, shards_y, shards_x, pairs, 2, cells_y, cells_z), np.float32)
    for own in range(shards_y):
        rows = turn_y[:, own * cells_y : (own + 1) * cells_y]
        product = rows[mode_y][..., :, None] * turn_z[mode_z][..., None, :]
        table[own, :, :, :, 0] = product.real
        table[own, :, :, :, 1] = product.imag
    return table.reshape(shards_y, -1, cells_y * cells_z).astype(jnp.bfloat16)


def backward_yz_table(shards_x, shards_y, pairs, cells_y, cells_z):
    full_y = shards_y * cells_y
    turn_z = wave(np.arange(MZ), np.arange(cells_z), cells_z, MZ**-0.5)
    turn_z = rounded(turn_z.real) + 1j * rounded(turn_z.imag)
    turn_y = wave(frequencies(MY), np.arange(full_y), full_y, MY**-0.5)
    mode_y, mode_z = item_modes(shards_x, shards_y, pairs)
    table = np.empty((shards_y, shards_y, cells_y, cells_z, shards_x, pairs, 2), np.float32)
    for own in range(shards_y):
        rows = turn_y[:, own * cells_y : (own + 1) * cells_y]
        product = rows[mode_y][..., :, None] * turn_z[mode_z][..., None, :]
        product = np.moveaxis(product, (3, 4), (1, 2))
        table[own, ..., 0] = product.real
        table[own, ..., 1] = -product.imag
    return table.reshape(shards_y**2, cells_y * cells_z, -1).astype(jnp.bfloat16)


def forward_x_table(full_x):
    turn = np.conj(wave(frequencies(MX), np.arange(full_x), full_x, full_x**-0.5))
    parts = np.empty((2, MX, 2, 2, full_x), np.float32)
    parts[0, :, 0, 0], parts[0, :, 0, 1] = turn.real, -turn.imag
    parts[0, :, 1, 0], parts[0, :, 1, 1] = turn.imag, turn.real
    parts[1, :, 0] = -parts[0, :, 1]
    parts[1, :, 1] = parts[0, :, 0]
    return parts.reshape(2 * MX * 2, 2 * full_x).astype(jnp.bfloat16)


def backward_x_table(full_x):
    turn = wave(frequencies(MX), np.arange(full_x), full_x, MX**-0.5).T
    parts = np.empty((2, full_x, MX, 2), np.float32)
    parts[0, :, :, 0], parts[0, :, :, 1] = turn.real, -turn.imag
    parts[1, :, :, 0], parts[1, :, :, 1] = turn.imag, turn.real
    return parts.reshape(2 * full_x, MX * 2).astype(jnp.bfloat16)


def dot(left, right):
    return jnp.dot(left, right, preferred_element_type=jnp.float32)


def peer(index, step, count):
    if count & (count - 1) == 0:
        return index ^ step
    return lax.rem(index + step, count)


def origin(index, step, count):
    if count & (count - 1) == 0:
        return index ^ step
    return lax.rem(index + (count - step), count)


def far_first(count):
    return list(range(count - 1, -1, -1))


def place(me, shards):
    outer, inner = shards
    across = lax.rem(me, outer * inner)
    return lax.div(me, outer * inner), lax.div(across, inner), lax.rem(across, inner)


def in_vmem(count):
    return [pl.BlockSpec(memory_space=pltpu.VMEM)] * count


IN_SMEM = pl.BlockSpec(memory_space=pltpu.SMEM)


def transform(table, flow_at, cells_x, refs, pieces):
    inner, _, rows, channels = refs[0].shape[1:]
    block = inner * rows
    width = 2 if cells_x % 2 == 0 else 1
    for x in range(0, cells_x, width):
        columns = [flow_at(x + i) for i in range(width)]
        result = dot(table, jnp.concatenate(columns, axis=1))
        for i in range(width):
            part = result[:, i * channels : (i + 1) * channels]
            at = 0
            for ref, piece in zip(refs, pieces):
                for slot in range(len(piece)):
                    value = part[at : at + block].reshape(inner, rows, channels)
                    ref[slot, :, x + i] = value.astype(ref.dtype)
                    at += block


def send_kernel(shards, shards_y, pieces, step, me_ref, table_ref, flow_ref, *refs):
    *refs, table, flow, table_sems, flow_sems = refs
    refs, plane_refs = refs[: len(pieces)], refs[len(pieces) :]
    cells_x = flow.shape[0]
    outer, _ = shards
    block = refs[0].shape[1] * refs[0].shape[3]
    own_y, own, _ = place(me_ref[0], shards)
    owner = lax.rem(own_y + step, shards_y)
    copies = []
    for i, other in enumerate(step for piece in pieces for step in piece):
        start = (owner * outer + peer(own, other, outer)) * block
        source = table_ref.at[own_y, pl.ds(pl.multiple_of(start, block), block)]
        copies.append(
            pltpu.make_async_copy(source, table.at[pl.ds(i * block, block)], table_sems.at[i])
        )
    loads = [
        pltpu.make_async_copy(flow_ref.at[x], flow.at[x], flow_sems.at[x])
        for x in range(cells_x)
    ]
    for copy in copies + loads:
        copy.start()
    for copy in copies:
        copy.wait()

    def flow_at(x):
        loads[x].wait()
        return flow[x]

    transform(table[...], flow_at, cells_x, refs, pieces)
    if plane_refs:
        even = is_even(me_ref[0], shards)
        plane_refs[0][...] = flow[jnp.where(even, cells_x - 1, 0)]
        plane_refs[1][...] = flow[jnp.where(even, 0, cells_x - 1)]


def is_even(me, shards):
    _, own_outer, own_inner = place(me, shards)
    return lax.rem(own_outer * shards[1] + own_inner, 2) == 0


def keep_kernel(shards, shards_y, pieces, me_ref, table_ref, flow_ref, *refs):
    refs, (low, high) = refs[: len(pieces)], refs[len(pieces) :]
    cells_x, positions, _ = flow_ref.shape
    outer, _ = shards
    block = refs[0].shape[1] * refs[0].shape[3]
    own_y, own, _ = place(me_ref[0], shards)
    tables = []
    for other in (step for piece in pieces for step in piece):
        start = (own_y * outer + peer(own, other, outer)) * block
        tables.append(table_ref[own_y, pl.ds(pl.multiple_of(start, block), block), :])
    transform(
        jnp.concatenate(tables, axis=0), lambda x: flow_ref[x], cells_x, refs, pieces
    )
    cells_z = low.shape[1]
    low[...] = flow_ref[:, pl.ds(0, cells_z)]
    high[...] = flow_ref[:, pl.ds(positions - cells_z, cells_z)]


def forward_yz(me, table, flow, step, shards, shards_y, pieces, cells_z=0):
    cells_x, positions, channels = flow.shape
    outer, inner = shards
    rows = table.shape[1] // shards_y
    unit = (inner, cells_x, rows // (outer * inner), channels)
    dtype = jnp.bfloat16 if step else jnp.float32
    shapes = [jax.ShapeDtypeStruct((len(piece), *unit), dtype) for piece in pieces]
    if step == 1:
        shapes += [jax.ShapeDtypeStruct((positions, channels), flow.dtype)] * 2
    if step:
        kernel = functools.partial(send_kernel, shards, shards_y, pieces, step)
        specs = [pl.BlockSpec(memory_space=pltpu.HBM)] * 2
        scratch = [
            pltpu.VMEM((rows, positions), table.dtype),
            pltpu.VMEM(flow.shape, flow.dtype),
            pltpu.SemaphoreType.DMA((outer,)),
            pltpu.SemaphoreType.DMA((cells_x,)),
        ]
    else:
        kernel = functools.partial(keep_kernel, shards, shards_y, pieces)
        specs, scratch = in_vmem(2), []
        edge = jax.ShapeDtypeStruct((cells_x, cells_z, channels), flow.dtype)
        shapes += [edge] * 2
    return pl.pallas_call(
        kernel,
        in_specs=[IN_SMEM] + specs,
        out_specs=in_vmem(len(shapes)),
        out_shape=shapes,
        scratch_shapes=scratch,
        compiler_params=pltpu.CompilerParams(vmem_limit_bytes=(56 if step else 10) << 20),
        cost_estimate=pl.CostEstimate(
            flops=2 * rows * positions * cells_x * channels,
            bytes_accessed=2 * positions * (rows + cells_x * channels),
            transcendentals=0,
        ),
    )(me, table, flow)


def add_kernel(count, *refs):
    out_refs = refs[count:]
    for slot, out_ref in enumerate(out_refs):
        total = refs[0][slot]
        for ref in refs[1:count]:
            total = total + ref[slot].astype(jnp.float32)
        out_ref[...] = total.astype(out_ref.dtype)


def add_pieces(own, arrived):
    slots, *unit = own.shape
    return pl.pallas_call(
        functools.partial(add_kernel, 1 + len(arrived)),
        in_specs=in_vmem(1 + len(arrived)),
        out_specs=in_vmem(slots),
        out_shape=[jax.ShapeDtypeStruct(unit, jnp.bfloat16)] * slots,
        cost_estimate=pl.CostEstimate(flops=own.size, bytes_accessed=0, transcendentals=0),
        compiler_params=pltpu.CompilerParams(vmem_limit_bytes=10 << 20),
    )(own, *arrived)


def regroup_kernel(shards, chosen, me_ref, *refs):
    _, _, own = place(me_ref[0], shards)
    count = refs[0].shape[0]
    in_refs, out_refs = refs[:-count], refs[-count:]
    for step, out_ref in enumerate(out_refs):
        at = peer(own, step, count) if chosen else step
        for number, in_ref in enumerate(in_refs):
            out_ref[far_first(len(in_refs))[number]] = in_ref[at]


def regroup(me, arrays, shards, chosen):
    count, *unit = arrays[0].shape
    return pl.pallas_call(
        functools.partial(regroup_kernel, shards, chosen),
        in_specs=[IN_SMEM] + in_vmem(len(arrays)),
        out_specs=in_vmem(count),
        out_shape=[jax.ShapeDtypeStruct((len(arrays), *unit), arrays[0].dtype)] * count,
        cost_estimate=pl.CostEstimate(
            flops=arrays[0].size, bytes_accessed=0, transcendentals=0
        ),
        compiler_params=pltpu.CompilerParams(vmem_limit_bytes=10 << 20),
    )(me, *arrays)


def edge_kernel(
    choose, shards, me_ref, paired_ref, other_ref, low_ref, high_ref, out_ref
):
    cells_x, cells_z, _ = low_ref.shape
    rows = paired_ref.shape[0]
    own_y, _, _ = place(me_ref[0], shards)
    is_low = choose(own_y)
    even = is_even(me_ref[0], shards)
    start = pl.multiple_of(jnp.where(is_low, 0, rows - cells_z), cells_z)
    paired, other = (ref[pl.ds(start, cells_z), :] for ref in (paired_ref, other_ref))
    out_ref[0] = jnp.where(even, other, paired)
    out_ref[1 + cells_x] = jnp.where(even, paired, other)

    @pl.when(is_low)
    def _():
        out_ref[1 : 1 + cells_x] = low_ref[...]

    @pl.when(jnp.logical_not(is_low))
    def _():
        out_ref[1 : 1 + cells_x] = high_ref[...]


def y_edge(me, paired, other, low, high, shards, choose):
    cells_x, cells_z, channels = low.shape
    return pl.pallas_call(
        functools.partial(edge_kernel, choose, shards),
        in_specs=[IN_SMEM] + in_vmem(4),
        out_specs=in_vmem(1)[0],
        out_shape=jax.ShapeDtypeStruct((cells_x + 2, cells_z, channels), low.dtype),
        compiler_params=pltpu.CompilerParams(vmem_limit_bytes=10 << 20),
    )(me, paired, other, low, high)


def preload_kernel(first, weight_ref, out_ref, sems):
    count = out_ref.shape[0]
    pieces = sems.shape[0] // count
    modes = out_ref.shape[1] // pieces
    copies = []
    for i in range(count * pieces):
        item, at = i // pieces, pl.ds(i % pieces * modes, modes)
        copies.append(
            pltpu.make_async_copy(
                weight_ref.at[first + item, at], out_ref.at[item, at], sems.at[i]
            )
        )
    for copy in copies:
        copy.start()
    for copy in copies:
        copy.wait()


def preload(weight, pair, count):
    shape = (2 * count, *weight.shape[1:])
    return pl.pallas_call(
        functools.partial(preload_kernel, 2 * pair),
        in_specs=[pl.BlockSpec(memory_space=pltpu.HBM)],
        out_specs=in_vmem(1)[0],
        out_shape=jax.ShapeDtypeStruct(shape, weight.dtype),
        scratch_shapes=[pltpu.SemaphoreType.DMA((2 * 2 * count,))],
        compiler_params=pltpu.CompilerParams(vmem_limit_bytes=36 << 20),
        cost_estimate=pl.CostEstimate(
            flops=0, bytes_accessed=2 * math.prod(shape), transcendentals=0
        ),
    )(weight)


def mixing_kernel(shards, loaded, me_ref, *refs):
    outer, inner = shards
    row_refs, refs = refs[:inner], refs[inner:]
    forward_ref, backward_ref, weight_ref, *refs = refs
    loaded_refs, refs = refs[:loaded], refs[loaded:]
    loaded = sum(ref.shape[0] // 2 for ref in loaded_refs)
    out_refs, (held, sems, wide, left, mixed) = refs[:inner], refs[inner:]

    channels = wide.shape[1]
    _, cells_x, item_rows, _ = row_refs[0].shape
    pairs = item_rows // 2
    full_x = outer * inner * cells_x
    half = channels // 2
    span = 2 * MX
    block = cells_x * item_rows
    _, own_outer, own_inner = place(me_ref[0], shards)

    def copy(pair):
        slot = pair - loaded
        return pltpu.make_async_copy(
            weight_ref.at[pl.ds(2 * pair, 2)], held.at[slot], sems.at[slot]
        )

    for pair in range(loaded, pairs):
        copy(pair).start()

    def rows_of(outer_index, inner_index):
        start = pl.multiple_of((outer_index * inner + inner_index) * block, block)
        return pl.ds(start, block)

    for number, step in enumerate(far_first(inner)):
        source = origin(own_inner, step, inner)
        for slot in range(outer):
            value = row_refs[number][slot].reshape(block, channels)
            at = rows_of(origin(own_outer, slot, outer), source)
            wide[at, :] = value.astype(jnp.float32)
    low = lax.broadcasted_iota(jnp.int32, (span, channels), 1) < half
    for pair in range(pairs):
        columns = [wide[pl.ds(2 * pair + p, full_x, stride=item_rows), :] for p in range(2)]
        columns = jnp.concatenate(columns, axis=0).astype(jnp.bfloat16)
        both = dot(forward_ref[...], columns)
        value, turned = both[:span], both[span:]
        first = jnp.where(low, value, pltpu.roll(turned, half, axis=1))
        second = jnp.where(low, pltpu.roll(value, half, axis=1), turned)
        left[pl.ds(pair * span, span), :channels] = first.astype(left.dtype)
        left[pl.ds(pair * span, span), channels:] = second.astype(left.dtype)

    group = 16
    row = lax.broadcasted_iota(jnp.int32, (group, channels), 0) // 2

    def mix(pair, tile_of):
        for step in range(span // group):
            start = pl.multiple_of(pair * span + step * group, group)
            lhs = left[pl.ds(start, group), :]
            gathered = jnp.zeros((group, channels), jnp.float32)
            for i in range(0, group // 2, 2):
                mode = step * (group // 2) + i
                tiles = [
                    jnp.concatenate([tile_of(h, mode + k) for h in range(2)], axis=0)
                    for k in range(2)
                ]
                product = dot(lhs, jnp.concatenate(tiles, axis=1))
                for k in range(2):
                    gathered = jnp.where(
                        row == i + k, product[:, k * channels : (k + 1) * channels], gathered
                    )
            mixed[pl.ds(start, group), :] = gathered.astype(mixed.dtype)

    pair = 0
    for ref in loaded_refs:
        count = ref.shape[0] // 2

        def ready(i, carry, ref=ref, pair=pair):
            mix(pair + i, lambda h, mode: ref[2 * i + h, mode])
            return carry

        lax.fori_loop(0, count, ready, 0)
        pair += count

    def streamed(pair, carry):
        copy(pair).wait()
        mix(pair, lambda h, mode: held[pair - loaded, h, mode])
        return carry

    lax.fori_loop(loaded, pairs, streamed, 0)

    for pair in range(pairs):
        result = dot(backward_ref[...], mixed[pl.ds(pair * span, span), :])
        for p in range(2):
            wide[pl.ds(2 * pair + p, full_x, stride=item_rows), :] = result[
                p * full_x : (p + 1) * full_x
            ]
    for step in range(inner):
        target = peer(own_inner, step, inner)
        for slot in range(outer):
            value = wide[rows_of(peer(own_outer, slot, outer), target), :]
            value = value.reshape(cells_x, item_rows, channels)
            out_refs[step][slot] = value.astype(out_refs[step].dtype)


def mixing(me, rows, forward_x, backward_x, weight, loaded, shards):
    outer, inner = shards
    _, cells_x, item_rows, channels = rows[0].shape
    pairs = item_rows // 2
    row_count = outer * inner * cells_x * item_rows
    streamed = pairs - sum(part.shape[0] // 2 for part in loaded)
    return pl.pallas_call(
        functools.partial(mixing_kernel, shards, len(loaded)),
        in_specs=[IN_SMEM]
        + in_vmem(inner + 2)
        + [pl.BlockSpec(memory_space=pltpu.HBM)]
        + in_vmem(len(loaded)),
        out_specs=in_vmem(inner),
        out_shape=[jax.ShapeDtypeStruct(rows[0].shape, jnp.bfloat16)] * inner,
        scratch_shapes=[
            pltpu.VMEM((streamed, 2, *weight.shape[1:]), weight.dtype),
            pltpu.SemaphoreType.DMA((streamed,)),
            pltpu.VMEM((row_count, channels), jnp.float32),
            pltpu.VMEM((pairs * 2 * MX, 2 * channels), jnp.bfloat16),
            pltpu.VMEM((pairs * 2 * MX, channels), jnp.bfloat16),
        ],
        compiler_params=pltpu.CompilerParams(vmem_limit_bytes=20 << 20),
        cost_estimate=pl.CostEstimate(
            flops=8 * weight.size, bytes_accessed=2 * weight.size, transcendentals=0
        ),
    )(me, *rows, forward_x, backward_x, weight, *loaded)


def convolution_kernel(x, cells_x, width, shards, shards_y, me_ref, *refs):
    flow_ref, paired_ref, other_ref, front_ref, back_ref, kernel_ref, out_ref, padded = refs
    _, cells_y, cells_z, channels = out_ref.shape
    own_y, _, _ = place(me_ref[0], shards)
    even = is_even(me_ref[0], shards)
    for plane in range(width + 2):
        p = x + plane - 1
        row = front_ref[p + 1]
        padded[plane, 0] = jnp.where(own_y > 0, row, jnp.zeros_like(row))
        row = back_ref[p + 1]
        last = own_y == shards_y - 1
        padded[plane, cells_y + 1] = jnp.where(last, jnp.zeros_like(row), row)
        if 0 <= p < cells_x:
            padded[plane, 1 : cells_y + 1] = flow_ref[p]
        else:
            use_paired = jnp.logical_not(even) if p < 0 else even

            @pl.when(use_paired)
            def _(plane=plane):
                padded[plane, 1 : cells_y + 1] = paired_ref[...]

            @pl.when(jnp.logical_not(use_paired))
            def _(plane=plane):
                padded[plane, 1 : cells_y + 1] = other_ref[...]

    rows = 8 if cells_y % 8 == 0 else 1
    columns = [(k, d) for k in range(width) for d in range(3)]
    columns = [columns[i : i + 2] for i in range(0, len(columns), 2)]
    none = jnp.zeros((channels, channels), kernel_ref.dtype)

    def chunk(index, carry):
        y = index * rows
        products = {}
        for group in columns:
            blocks, kernels = [], []
            for p in range(width + 2):
                if not any(0 <= p - k < 3 for k, _ in group):
                    continue
                for b in range(3):
                    part = padded[p, pl.ds(y + b, rows)]
                    blocks.append(part.reshape(rows * cells_z, channels))
                    parts = [
                        kernel_ref[p - k, b, d] if 0 <= p - k < 3 else none for k, d in group
                    ]
                    kernels.append(jnp.concatenate(parts, axis=1))
            product = dot(jnp.concatenate(blocks, axis=1), jnp.concatenate(kernels, axis=0))
            for i, column in enumerate(group):
                part = product[:, i * channels : (i + 1) * channels]
                products[column] = part.reshape(rows, cells_z, channels)
        z = lax.broadcasted_iota(jnp.int32, (rows, cells_z, channels), 1)
        for k in range(width):
            before = jnp.where(z == 0, 0.0, pltpu.roll(products[k, 0], 1, axis=1))
            after = pltpu.roll(products[k, 2], cells_z - 1, axis=1)
            after = jnp.where(z == cells_z - 1, 0.0, after)
            total = before + products[k, 1] + after
            out_ref[k, pl.ds(y, rows)] = total.astype(out_ref.dtype)
        return carry

    lax.fori_loop(0, cells_y // rows, chunk, 0)


def convolution(me, x, width, flow, halos, kernel, shards, shards_y):
    cells_x, cells_y, cells_z, channels = flow.shape
    shape = (width, cells_y, cells_z, channels)
    return pl.pallas_call(
        functools.partial(convolution_kernel, x, cells_x, width, shards, shards_y),
        in_specs=[IN_SMEM] + in_vmem(2 + len(halos)),
        out_specs=in_vmem(1)[0],
        out_shape=jax.ShapeDtypeStruct(shape, jnp.bfloat16),
        scratch_shapes=[pltpu.VMEM((width + 2, cells_y + 2, cells_z, channels), flow.dtype)],
        compiler_params=pltpu.CompilerParams(vmem_limit_bytes=14 << 20),
        cost_estimate=pl.CostEstimate(
            flops=3 * 27 * width * cells_y * cells_z * channels * channels,
            bytes_accessed=10 * cells_y * cells_z * channels,
            transcendentals=0,
        ),
    )(me, flow, *halos, kernel)


def bundled_slots(count):
    parts = ([0], [count - 1], far_first(count)[1:-1]) if count > 1 else ([0],)
    return [part for part in parts if part]


def bundle_kernel(*refs):
    *in_refs, out_ref = refs
    for i, ref in enumerate(in_refs):
        out_ref[i] = ref[...]


def bundle(arrays):
    shape = (len(arrays), *arrays[0].shape)
    return pl.pallas_call(
        bundle_kernel,
        in_specs=in_vmem(len(arrays)),
        out_specs=in_vmem(1)[0],
        out_shape=jax.ShapeDtypeStruct(shape, arrays[0].dtype),
        cost_estimate=pl.CostEstimate(
            flops=math.prod(shape), bytes_accessed=0, transcendentals=0
        ),
        compiler_params=pltpu.CompilerParams(vmem_limit_bytes=10 << 20),
    )(*arrays)


def gather_pieces(me, shards, pieces, held):
    outer, inner = shards
    _, own_outer, own_inner = place(me, shards)
    for number, slot, ref in pieces:
        cells_x, rows = ref.shape[1:3]
        source = (number * outer + origin(own_outer, slot, outer)) * inner
        for part in range(inner):
            at = (source + origin(own_inner, part, inner)) * rows
            for x in range(cells_x):
                held[x, pl.ds(pl.multiple_of(at, rows), rows), :] = ref[part, x]


def inverse(me, shards, shards_y, steps, table_ref, held, part, x, width, positions):
    own_y, _, _ = place(me, shards)
    columns = [held[x + i] for i in range(width)]
    depth = table_ref.shape[2]
    total = None
    for number, step in enumerate(steps):
        source = lax.rem(own_y + (shards_y - step), shards_y)
        rows = pl.ds(pl.multiple_of(part * positions, positions), positions)
        table = table_ref[own_y * shards_y + source, rows, :]
        block = [column[number * depth : (number + 1) * depth] for column in columns]
        product = dot(table, jnp.concatenate(block, axis=1))
        total = product if total is None else total + product
    return total


def own_part_kernel(shards, shards_y, me_ref, table_ref, *refs):
    *piece_refs, bias_ref, out_ref, held = refs
    cells_x, cells_y, cells_z, channels = out_ref.shape
    width = 2 if cells_x % 2 == 0 else 1
    count = -(-cells_x // width)
    piece_refs, convolved_refs = piece_refs[:-count], piece_refs[-count:]
    slots = far_first(shards[0])
    gather_pieces(me_ref[0], shards, [(0, *p) for p in zip(slots, piece_refs)], held)
    bias = bias_ref[...]
    rows = 4 if cells_y % 4 == 0 else 1
    positions = rows * cells_z

    def chunk(part, carry):
        for x in range(0, cells_x, width):
            total = inverse(
                me_ref[0], shards, shards_y, [0], table_ref, held, part, x, width, positions
            )
            for i in range(width):
                spectral = total[:, i * channels : (i + 1) * channels]
                convolved = convolved_refs[x // width][i, pl.ds(part * rows, rows)]
                value = spectral.reshape(rows, cells_z, channels) + convolved + bias
                out_ref[x + i, pl.ds(part * rows, rows)] = value
        return carry

    lax.fori_loop(0, cells_y // rows, chunk, 0)


def last_part_kernel(shards, shards_y, me_ref, table_ref, *refs):
    *bundle_refs, partial_ref, out_ref, held = refs
    cells_x, cells_y, cells_z, channels = out_ref.shape
    bundles = bundled_slots(shards[0])
    steps = list(range(1, shards_y))
    width = 2 if cells_x % 2 == 0 else 1
    part = pl.program_id(0)

    @pl.when(part == 0)
    def _():
        pieces = []
        for i, ref in enumerate(bundle_refs):
            number, bundle = divmod(i, len(bundles))
            pieces += [(number, slot, ref.at[j]) for j, slot in enumerate(bundles[bundle])]
        gather_pieces(me_ref[0], shards, pieces, held)

    for x in range(0, cells_x, width):
        total = inverse(
            me_ref[0], shards, shards_y, steps, table_ref, held, part, x, width,
            cells_y * cells_z,
        )
        for i in range(width):
            spectral = total[:, i * channels : (i + 1) * channels]
            value = partial_ref[x + i, pl.ds(part * cells_y, cells_y)]
            value = value + spectral.reshape(cells_y, cells_z, channels)
            out_ref[x + i] = jax.nn.gelu(value, approximate=True).astype(out_ref.dtype)


def own_part(me, table, pieces, convolved, bias, shards, shards_y):
    width, cells_y, cells_z, channels = convolved[0].shape
    shape = (width * len(convolved), cells_y, cells_z, channels)
    depth = table.shape[2]
    return pl.pallas_call(
        functools.partial(own_part_kernel, shards, shards_y),
        in_specs=[IN_SMEM] + in_vmem(2 + len(pieces) + len(convolved)),
        out_specs=in_vmem(1)[0],
        out_shape=jax.ShapeDtypeStruct(shape, jnp.float32),
        scratch_shapes=[pltpu.VMEM((shape[0], depth, channels), jnp.bfloat16)],
        compiler_params=pltpu.CompilerParams(vmem_limit_bytes=14 << 20),
        cost_estimate=pl.CostEstimate(
            flops=2 * math.prod(shape) * depth,
            bytes_accessed=6 * math.prod(shape),
            transcendentals=0,
        ),
    )(me, table, *pieces, *convolved, bias)


def last_part(me, table, pieces, partial, shards, shards_y):
    cells_x, cells_y, cells_z, channels = partial.shape
    parts = 4 if cells_y % 4 == 0 else 1
    block = (cells_x, cells_y // parts, cells_z, channels)
    depth = table.shape[2] * (shards_y - 1)
    return pl.pallas_call(
        functools.partial(last_part_kernel, shards, shards_y),
        grid_spec=pltpu.PrefetchScalarGridSpec(
            num_scalar_prefetch=1,
            grid=(parts,),
            in_specs=in_vmem(2 + len(pieces)),
            out_specs=pl.BlockSpec(block, lambda i, me: (0, i, 0, 0)),
            scratch_shapes=[pltpu.VMEM((cells_x, depth, channels), jnp.bfloat16)],
        ),
        out_shape=jax.ShapeDtypeStruct(partial.shape, jnp.bfloat16),
        compiler_params=pltpu.CompilerParams(vmem_limit_bytes=14 << 20),
        cost_estimate=pl.CostEstimate(
            flops=2 * partial.size * depth,
            bytes_accessed=6 * partial.size,
            transcendentals=partial.size,
        ),
    )(me, table, *pieces, partial)


def with_halo(array, sides, width):
    for axis, dim in sides:
        size, length = (lax.axis_size(axis), array.shape[dim])
        up = [(i, (i + 1) % size) for i in range(size - 1)]
        down = [(j, i) for i, j in up]
        last = lax.slice_in_dim(array, length - width, length, axis=dim)
        initial = lax.slice_in_dim(array, 0, width, axis=dim)
        before = lax.ppermute(last, axis, up)
        after = lax.ppermute(initial, axis, down)
        array = jnp.concatenate([before, array, after], axis=dim)
    return array


def signed_modes(mode_count):
    position = jnp.arange(mode_count, dtype=jnp.int32)
    return jnp.where(position < mode_count // 2, position, position - mode_count)


def angle_grid(first, second, length):
    phase_turns = first[:, None] * second[None, :] % length
    return phase_turns.astype(jnp.float32) * (2.0 * math.pi / length)


def real_table(first, second, length, factor):
    angles = angle_grid(first, second, length)
    return jnp.stack([jnp.cos(angles) * factor, -jnp.sin(angles) * factor])


def complex_table(first, second, length, factor, direction):
    angles = angle_grid(first, second, length)
    cosine = jnp.cos(angles) * factor
    sine_part = jnp.sin(angles) * factor
    return jnp.stack(
        [jnp.stack([cosine, direction * sine_part]), jnp.stack([-direction * sine_part, cosine])]
    )


def split_pair_spectral(flow_field, spectral_weight):
    highest = lax.Precision.HIGHEST
    cells_x, cells_y, cells_z, channels = flow_field.shape
    count_x = lax.axis_size("gx")
    count_y = lax.axis_size("gy")
    full_x = cells_x * count_x
    full_y = cells_y * count_y
    item_count = spectral_weight.shape[0]
    local_y = lax.axis_index("gy") * cells_y + jnp.arange(cells_y, dtype=jnp.int32)
    grid_x = jnp.arange(full_x, dtype=jnp.int32)
    grid_z = jnp.arange(cells_z, dtype=jnp.int32)
    modes_z = jnp.arange(MZ, dtype=jnp.int32)
    forward_z = real_table(grid_z, modes_z, cells_z, cells_z ** (-0.5)).astype(jnp.bfloat16)
    z_spectrum = jnp.einsum(
        "xyzc,pzk->pxykc", flow_field, forward_z, preferred_element_type=jnp.float32
    )
    columns = lax.all_to_all(
        z_spectrum.astype(jnp.bfloat16), "gy", split_axis=4, concat_axis=2, tiled=True
    ).astype(z_spectrum.dtype)
    whole_y = jnp.arange(full_y, dtype=jnp.int32)
    forward_full = complex_table(whole_y, signed_modes(MY), full_y, full_y ** (-0.5), -1.0)
    y_spectrum = jnp.einsum("pxykc,pqyj->qxjkc", columns, forward_full, precision=highest)
    owned = lax.all_to_all(
        y_spectrum.astype(jnp.bfloat16), "gy", split_axis=2, concat_axis=4, tiled=True
    ).astype(y_spectrum.dtype)
    owned_modes = owned.reshape(2, cells_x, count_x, item_count, channels // 2)
    gathered_rows = lax.all_to_all(
        owned_modes.astype(jnp.bfloat16), "gx", split_axis=2, concat_axis=1, tiled=True
    ).astype(owned_modes.dtype)
    gathered_rows = gathered_rows.reshape(2, full_x, item_count, channels // 2)
    forward_x = complex_table(grid_x, signed_modes(MX), full_x, full_x ** (-0.5), -1.0)
    x_spectrum = jnp.einsum("pxjc,pqxm->qmjc", gathered_rows, forward_x, precision=highest).astype(
        jnp.bfloat16
    )
    products = jnp.einsum(
        "pmjc,jmqco->pqmjo", x_spectrum, spectral_weight, preferred_element_type=jnp.float32
    )
    mixed_modes = jnp.stack([products[0, 0] - products[1, 1], products[0, 1] + products[1, 0]])
    backward_x = complex_table(signed_modes(MX), grid_x, full_x, MX ** (-0.5), 1.0)
    inverse_x = jnp.einsum("pmjc,pqmx->qxjc", mixed_modes, backward_x, precision=highest)
    inverse_x = inverse_x.reshape(2, full_x, 1, item_count, channels)
    returned = lax.all_to_all(
        inverse_x.astype(jnp.bfloat16), "gx", split_axis=1, concat_axis=2, tiled=True
    ).astype(inverse_x.dtype)
    band_rows = MY // count_y
    summed = returned.reshape(2, cells_x, band_rows * MZ, 2, channels).sum(axis=3)
    summed = summed.reshape(2, cells_x, band_rows, MZ, channels)
    coefficients = lax.all_gather(summed.astype(jnp.bfloat16), "gy", axis=2, tiled=True).astype(
        summed.dtype
    )
    backward_y = complex_table(signed_modes(MY), local_y, full_y, MY ** (-0.5), 1.0)
    y_inverse = jnp.einsum("pxjkc,pqjy->qxykc", coefficients, backward_y, precision=highest).astype(
        jnp.bfloat16
    )
    backward_z = real_table(modes_z, grid_z, cells_z, MZ ** (-0.5)).astype(jnp.bfloat16)
    return jnp.einsum("pxykc,pkz->xyzc", y_inverse, backward_z, preferred_element_type=jnp.float32)


def split_pair_convolve(flow_field, conv_weight):
    cells_x, cells_y, cells_z, channels = flow_field.shape
    padded = with_halo(flow_field, (("gx", 0), ("gy", 1)), 1)
    padded = jnp.pad(padded, ((0, 0), (0, 0), (1, 1), (0, 0)))
    stacked = jnp.concatenate(
        [padded[:, :, 0:cells_z], padded[:, :, 1 : cells_z + 1], padded[:, :, 2 : cells_z + 2]],
        axis=3,
    )
    kernel = conv_weight.reshape(3, 3, 3 * channels, channels)
    accumulated = jnp.zeros((cells_x, cells_y, cells_z, channels), jnp.float32)
    for shift_x in range(3):
        for shift_y in range(3):
            accumulated = accumulated + jnp.dot(
                stacked[shift_x : shift_x + cells_x, shift_y : shift_y + cells_y],
                kernel[shift_x, shift_y],
                preferred_element_type=jnp.float32,
            )
    return accumulated


def neighbours(first, last, axis):
    size = lax.axis_size(axis)
    up = [(i, i + 1) for i in range(size - 1)]
    down = [(i + 1, i) for i in range(size - 1)]
    return lax.ppermute(last, axis, up), lax.ppermute(first, axis, down)


def with_neighbour(array, start, axis):
    size = lax.axis_size(axis)
    pairs = [(i, i + 1) for i in range(start, size - 1, 2)]
    return lax.ppermute(array, axis, pairs + [(j, i) for i, j in pairs])


def exchange(array, step, shards, along_outer):
    outer, inner = shards
    pairs = []
    for i in range(outer * inner):
        a, b = divmod(i, inner)
        count, own = (outer, a) if along_outer else (inner, b)
        to = own ^ step if count & (count - 1) == 0 else (own + step) % count
        pairs.append((i, to * inner + b if along_outer else a * inner + to))
    return lax.ppermute(array, "gx", pairs)


def over_y(array, step, shards_y):
    return lax.ppermute(array, "gy", [(i, (i + step) % shards_y) for i in range(shards_y)])


def body(flow, spectral_weight, conv_weight, bias):
    cells_x, cells_y, cells_z, channels = flow.shape
    shards_x, shards_y = lax.axis_size("gx"), lax.axis_size("gy")
    items = spectral_weight.shape[0]
    pairs = items // 2
    if items % 2 or shards_y < 2:
        spectral = split_pair_spectral(flow, spectral_weight)
        convolved = split_pair_convolve(flow, conv_weight)
        return jax.nn.gelu(spectral + convolved + bias, approximate=True).astype(jnp.bfloat16)

    barrier = lax.optimization_barrier
    inner = max(d for d in range(1, shards_x + 1) if shards_x % d == 0 and d * d <= shards_x)
    outer = shards_x // inner
    shards = (outer, inner)
    me = lax.axis_index(("gy", "gx")).astype(jnp.int32).reshape(1)
    sizes = (shards_x, shards_y, pairs, cells_y, cells_z)
    full_x = cells_x * shards_x
    weight = spectral_weight.reshape(items, MX, channels, channels)
    early = pairs // 4

    table = jnp.asarray(forward_yz_table(*sizes))
    columns = flow.reshape(cells_x, cells_y * cells_z, channels)
    order = far_first(outer)
    cut = (outer + 1) // 2
    pieces = [piece for piece in (order[:cut], order[cut:]) if piece]
    arrived = [[] for _ in pieces]
    for step in range(1, shards_y):
        sent = forward_yz(me, table, columns, step, shards, shards_y, pieces)
        sent, columns, weight = barrier((sent, columns, weight))
        for into, piece in zip(arrived, sent):
            into.append(over_y(piece, step, shards_y))
        if step == 1:
            ends = sent[len(pieces) :]
            planes = [with_neighbour(end, start, "gx") for start, end in enumerate(ends)]
    loaded = []
    kept = forward_yz(me, table, columns, 0, shards, shards_y, pieces, cells_z)
    kept, (low, high) = kept[: len(pieces)], kept[len(pieces) :]

    by_outer = []
    for piece, own, parts in zip(pieces, kept, arrived):
        for step, total in zip(piece, add_pieces(own, parts)):
            by_outer.append(exchange(total, step, shards, True) if step else total)
    if early:
        loaded.append(preload(weight, 0, early))
    by_outer, loaded, weight = barrier((by_outer[::-1], loaded, weight))
    by_inner = regroup(me, by_outer[::-1], shards, True)
    by_inner, weight = barrier((by_inner, weight))
    rows = [
        exchange(by_inner[step], step, shards, False) if step else by_inner[0]
        for step in far_first(inner)
    ]
    if early:
        loaded.append(preload(weight, early, early))

    rows, loaded, planes = barrier((rows, loaded, planes[::-1]))
    planes = planes[::-1]
    if shards_y == 2:
        edge = y_edge(me, *planes, low, high, shards, lambda own: own > 0)
        front = back = over_y(edge, 1, shards_y)
    else:
        ends = [
            y_edge(me, *planes, low, high, shards, lambda own, limit=limit: own < limit)
            for limit in (shards_y, 0)
        ]
        front, back = neighbours(*ends, "gy")
    returned = mixing(
        me,
        rows,
        jnp.asarray(forward_x_table(full_x)),
        jnp.asarray(backward_x_table(full_x)),
        weight,
        loaded,
        shards,
    )
    returned, front, back = barrier((list(returned), front, back))
    planes = [plane.reshape(cells_y, cells_z, channels) for plane in planes]
    halos = (*planes, front, back)
    width = 2 if cells_x % 2 == 0 else 1
    convolved = [
        convolution(me, x, width, flow, halos, conv_weight, shards, shards_y)
        for x in range(0, cells_x, width)
    ]

    returned = [
        exchange(returned[step], step, shards, False) if step else returned[0]
        for step in far_first(inner)
    ]
    returned, convolved[0] = barrier((returned, convolved[0]))
    returned = regroup(me, returned, shards, False)
    returned = [
        exchange(returned[step], step, shards, True) if step else returned[0]
        for step in far_first(outer)
    ]
    by_slot = dict(zip(far_first(outer), returned))
    bundles = [
        bundle([by_slot[slot] for slot in slots]) if slots[1:] else by_slot[slots[0]][None]
        for slots in bundled_slots(outer)
    ]
    others = []
    for step in range(1, shards_y):
        others += [over_y(part, step, shards_y) for part in bundles]
    table = jnp.asarray(backward_yz_table(*sizes))
    bias = bias.reshape(1, channels)
    partial = own_part(me, table, returned, convolved, bias, shards, shards_y)
    return last_part(me, table, others, partial, shards, shards_y)


def solution(mesh):
    placed = (P("gx", "gy", None, None), P(("gy", "gx"), None, None, None, None), P(), P())
    return jax.shard_map(
        body, mesh=mesh, in_specs=placed, out_specs=P("gx", "gy", None, None), check_vma=False
    )
```

```python
import functools
import math

import jax
import jax.numpy as jnp
import numpy as np
from jax import lax
from jax.experimental import pallas as pl
from jax.experimental.pallas import tpu as pltpu
from jax.sharding import PartitionSpec as P

MX = 64
MY = 16
MZ = 16


def frequencies(mode_count):
    position = np.arange(mode_count)
    return np.where(position < mode_count // 2, position, position - mode_count)


def wave(first, second, length, factor):
    turns = (np.asarray(first)[:, None] * np.asarray(second)[None, :]) % length
    angles = turns * (2.0 * math.pi / length)
    return (np.cos(angles) + 1j * np.sin(angles)) * factor


def rounded(values):
    return values.astype(np.float32).astype(jnp.bfloat16).astype(np.float64)


def item_modes(shards_x, shards_y, pairs):
    index = np.arange(shards_y * shards_x * pairs).reshape(shards_y, shards_x, pairs)
    return index // MZ, index % MZ


def forward_yz_table(shards_x, shards_y, pairs, cells_y, cells_z):
    full_y = shards_y * cells_y
    turn_z = wave(np.arange(MZ), np.arange(cells_z), cells_z, cells_z**-0.5)
    turn_z = rounded(turn_z.real) - 1j * rounded(turn_z.imag)
    turn_y = np.conj(wave(frequencies(MY), np.arange(full_y), full_y, full_y**-0.5))
    mode_y, mode_z = item_modes(shards_x, shards_y, pairs)
    table = np.empty((shards_y, shards_y, shards_x, pairs, 2, cells_y, cells_z), np.float32)
    for own in range(shards_y):
        rows = turn_y[:, own * cells_y : (own + 1) * cells_y]
        product = rows[mode_y][..., :, None] * turn_z[mode_z][..., None, :]
        table[own, :, :, :, 0] = product.real
        table[own, :, :, :, 1] = product.imag
    return table.reshape(shards_y, -1, cells_y * cells_z).astype(jnp.bfloat16)


def backward_yz_table(shards_x, shards_y, pairs, cells_y, cells_z):
    full_y = shards_y * cells_y
    turn_z = wave(np.arange(MZ), np.arange(cells_z), cells_z, MZ**-0.5)
    turn_z = rounded(turn_z.real) + 1j * rounded(turn_z.imag)
    turn_y = wave(frequencies(MY), np.arange(full_y), full_y, MY**-0.5)
    mode_y, mode_z = item_modes(shards_x, shards_y, pairs)
    table = np.empty((shards_y, shards_y, cells_y, cells_z, shards_x, pairs, 2), np.float32)
    for own in range(shards_y):
        rows = turn_y[:, own * cells_y : (own + 1) * cells_y]
        product = rows[mode_y][..., :, None] * turn_z[mode_z][..., None, :]
        product = np.moveaxis(product, (3, 4), (1, 2))
        table[own, ..., 0] = product.real
        table[own, ..., 1] = -product.imag
    return table.reshape(shards_y**2, cells_y * cells_z, -1).astype(jnp.bfloat16)


def forward_x_table(full_x):
    turn = np.conj(wave(frequencies(MX), np.arange(full_x), full_x, full_x**-0.5))
    parts = np.empty((2, MX, 2, 2, full_x), np.float32)
    parts[0, :, 0, 0], parts[0, :, 0, 1] = turn.real, -turn.imag
    parts[0, :, 1, 0], parts[0, :, 1, 1] = turn.imag, turn.real
    parts[1, :, 0] = -parts[0, :, 1]
    parts[1, :, 1] = parts[0, :, 0]
    return parts.reshape(2 * MX * 2, 2 * full_x).astype(jnp.bfloat16)


def backward_x_table(full_x):
    turn = wave(frequencies(MX), np.arange(full_x), full_x, MX**-0.5).T
    parts = np.empty((2, full_x, MX, 2), np.float32)
    parts[0, :, :, 0], parts[0, :, :, 1] = turn.real, -turn.imag
    parts[1, :, :, 0], parts[1, :, :, 1] = turn.imag, turn.real
    return parts.reshape(2 * full_x, MX * 2).astype(jnp.bfloat16)


def dot(left, right):
    return jnp.dot(left, right, preferred_element_type=jnp.float32)


def peer(index, step, count):
    if count & (count - 1) == 0:
        return index ^ step
    return lax.rem(index + step, count)


def origin(index, step, count):
    if count & (count - 1) == 0:
        return index ^ step
    return lax.rem(index + (count - step), count)


def far_first(count):
    return list(range(count - 1, -1, -1))


def place(me, shards):
    outer, inner = shards
    across = lax.rem(me, outer * inner)
    return lax.div(me, outer * inner), lax.div(across, inner), lax.rem(across, inner)


def in_vmem(count):
    return [pl.BlockSpec(memory_space=pltpu.VMEM)] * count


IN_SMEM = pl.BlockSpec(memory_space=pltpu.SMEM)


def transform(table, flow_at, cells_x, refs, pieces):
    inner, _, rows, channels = refs[0].shape[1:]
    block = inner * rows
    width = 2 if cells_x % 2 == 0 else 1
    for x in range(0, cells_x, width):
        columns = [flow_at(x + i) for i in range(width)]
        result = dot(table, jnp.concatenate(columns, axis=1))
        for i in range(width):
            part = result[:, i * channels : (i + 1) * channels]
            at = 0
            for ref, piece in zip(refs, pieces):
                for slot in range(len(piece)):
                    value = part[at : at + block].reshape(inner, rows, channels)
                    ref[slot, :, x + i] = value.astype(ref.dtype)
                    at += block


def send_kernel(shards, shards_y, pieces, step, me_ref, table_ref, flow_ref, *refs):
    *refs, table, flow, table_sems, flow_sems = refs
    cells_x = flow.shape[0]
    outer, _ = shards
    block = refs[0].shape[1] * refs[0].shape[3]
    own_y, own, _ = place(me_ref[0], shards)
    owner = lax.rem(own_y + step, shards_y)
    copies = []
    for i, other in enumerate(step for piece in pieces for step in piece):
        start = (owner * outer + peer(own, other, outer)) * block
        source = table_ref.at[own_y, pl.ds(pl.multiple_of(start, block), block)]
        copies.append(
            pltpu.make_async_copy(source, table.at[pl.ds(i * block, block)], table_sems.at[i])
        )
    loads = [
        pltpu.make_async_copy(flow_ref.at[x], flow.at[x], flow_sems.at[x])
        for x in range(cells_x)
    ]
    for copy in copies + loads:
        copy.start()
    for copy in copies:
        copy.wait()

    def flow_at(x):
        loads[x].wait()
        return flow[x]

    transform(table[...], flow_at, cells_x, refs, pieces)


def is_even(me, shards):
    _, own_outer, own_inner = place(me, shards)
    return lax.rem(own_outer * shards[1] + own_inner, 2) == 0


def keep_kernel(shards, shards_y, pieces, me_ref, table_ref, flow_ref, *refs):
    refs, (first, last, *edges) = refs[: len(pieces)], refs[len(pieces) :]
    cells_x, positions, _ = flow_ref.shape
    outer, _ = shards
    block = refs[0].shape[1] * refs[0].shape[3]
    own_y, own, _ = place(me_ref[0], shards)
    tables = []
    for other in (step for piece in pieces for step in piece):
        start = (own_y * outer + peer(own, other, outer)) * block
        tables.append(table_ref[own_y, pl.ds(pl.multiple_of(start, block), block), :])
    transform(
        jnp.concatenate(tables, axis=0), lambda x: flow_ref[x], cells_x, refs, pieces
    )
    first[...] = flow_ref[0]
    last[...] = flow_ref[cells_x - 1]
    cells_z = edges[0].shape[1]
    low, high = pl.ds(0, cells_z), pl.ds(positions - cells_z, cells_z)
    if len(edges) > 1:
        edges[0][...] = flow_ref[:, low]
        edges[1][...] = flow_ref[:, high]
    else:

        @pl.when(own_y > 0)
        def _():
            edges[0][...] = flow_ref[:, low]

        @pl.when(own_y == 0)
        def _():
            edges[0][...] = flow_ref[:, high]


def forward_yz(me, table, flow, step, shards, shards_y, pieces, cells_z=0):
    cells_x, positions, channels = flow.shape
    outer, inner = shards
    rows = table.shape[1] // shards_y
    unit = (inner, cells_x, rows // (outer * inner), channels)
    dtype = jnp.bfloat16 if step else jnp.float32
    shapes = [jax.ShapeDtypeStruct((len(piece), *unit), dtype) for piece in pieces]
    if step:
        kernel = functools.partial(send_kernel, shards, shards_y, pieces, step)
        specs = [pl.BlockSpec(memory_space=pltpu.HBM)] * 2
        scratch = [
            pltpu.VMEM((rows, positions), table.dtype),
            pltpu.VMEM(flow.shape, flow.dtype),
            pltpu.SemaphoreType.DMA((outer,)),
            pltpu.SemaphoreType.DMA((cells_x,)),
        ]
    else:
        kernel = functools.partial(keep_kernel, shards, shards_y, pieces)
        specs, scratch = in_vmem(2), []
        shapes += [jax.ShapeDtypeStruct((positions, channels), flow.dtype)] * 2
        edge = jax.ShapeDtypeStruct((cells_x, cells_z, channels), flow.dtype)
        shapes += [edge] * (1 if shards_y == 2 else 2)
    return pl.pallas_call(
        kernel,
        in_specs=[IN_SMEM] + specs,
        out_specs=in_vmem(len(shapes)),
        out_shape=shapes,
        scratch_shapes=scratch,
        compiler_params=pltpu.CompilerParams(vmem_limit_bytes=(56 if step else 10) << 20),
        cost_estimate=pl.CostEstimate(
            flops=2 * rows * positions * cells_x * channels,
            bytes_accessed=2 * positions * (rows + cells_x * channels),
            transcendentals=0,
        ),
    )(me, table, flow)


def add_kernel(count, *refs):
    out_refs = refs[count:]
    for slot, out_ref in enumerate(out_refs):
        total = refs[0][slot]
        for ref in refs[1:count]:
            total = total + ref[slot].astype(jnp.float32)
        out_ref[...] = total.astype(out_ref.dtype)


def add_pieces(own, arrived):
    slots, *unit = own.shape
    return pl.pallas_call(
        functools.partial(add_kernel, 1 + len(arrived)),
        in_specs=in_vmem(1 + len(arrived)),
        out_specs=in_vmem(slots),
        out_shape=[jax.ShapeDtypeStruct(unit, jnp.bfloat16)] * slots,
        cost_estimate=pl.CostEstimate(flops=own.size, bytes_accessed=0, transcendentals=0),
        compiler_params=pltpu.CompilerParams(vmem_limit_bytes=10 << 20),
    )(own, *arrived)


def regroup_kernel(shards, chosen, me_ref, *refs):
    _, _, own = place(me_ref[0], shards)
    count = refs[0].shape[0]
    in_refs, out_refs = refs[:-count], refs[-count:]
    for step, out_ref in enumerate(out_refs):
        at = peer(own, step, count) if chosen else step
        for number, in_ref in enumerate(in_refs):
            out_ref[far_first(len(in_refs))[number]] = in_ref[at]


def regroup(me, arrays, shards, chosen):
    count, *unit = arrays[0].shape
    return pl.pallas_call(
        functools.partial(regroup_kernel, shards, chosen),
        in_specs=[IN_SMEM] + in_vmem(len(arrays)),
        out_specs=in_vmem(count),
        out_shape=[jax.ShapeDtypeStruct((len(arrays), *unit), arrays[0].dtype)] * count,
        cost_estimate=pl.CostEstimate(
            flops=arrays[0].size, bytes_accessed=0, transcendentals=0
        ),
        compiler_params=pltpu.CompilerParams(vmem_limit_bytes=10 << 20),
    )(me, *arrays)


def halo_kernel(shards, shards_y, me_ref, first_ref, last_ref, front_ref, back_ref, *out_refs):
    own_y, _, _ = place(me_ref[0], shards)
    even = is_even(me_ref[0], shards)
    cells_x, cells_z, _ = front_ref.shape
    cells_y = first_ref.shape[0] // cells_z

    def fill(out_ref, x, plane_ref):
        for y in range(cells_y):
            out_ref[y + 1] = plane_ref[pl.ds(y * cells_z, cells_z), :]
        row = front_ref[x]
        out_ref[0] = jnp.where(own_y > 0, row, jnp.zeros_like(row))
        row = back_ref[x]
        out_ref[cells_y + 1] = jnp.where(own_y < shards_y - 1, row, jnp.zeros_like(row))

    @pl.when(even)
    def _():
        fill(out_refs[0], cells_x - 1, last_ref)
        fill(out_refs[1], 0, first_ref)

    @pl.when(jnp.logical_not(even))
    def _():
        fill(out_refs[0], 0, first_ref)
        fill(out_refs[1], cells_x - 1, last_ref)


def halo_planes(me, first, last, front, back, shards, shards_y):
    cells_x, cells_z, channels = front.shape
    shape = (first.shape[0] // cells_z + 2, cells_z, channels)
    return pl.pallas_call(
        functools.partial(halo_kernel, shards, shards_y),
        in_specs=[IN_SMEM] + in_vmem(4),
        out_specs=in_vmem(2),
        out_shape=[jax.ShapeDtypeStruct(shape, first.dtype)] * 2,
        compiler_params=pltpu.CompilerParams(vmem_limit_bytes=10 << 20),
    )(me, first, last, front, back)


def preload_kernel(first, weight_ref, out_ref, sems):
    count = out_ref.shape[0]
    pieces = sems.shape[0] // count
    modes = out_ref.shape[1] // pieces
    copies = []
    for i in range(count * pieces):
        item, at = i // pieces, pl.ds(i % pieces * modes, modes)
        copies.append(
            pltpu.make_async_copy(
                weight_ref.at[first + item, at], out_ref.at[item, at], sems.at[i]
            )
        )
    for copy in copies:
        copy.start()
    for copy in copies:
        copy.wait()


def preload(weight, pair, count):
    shape = (2 * count, *weight.shape[1:])
    return pl.pallas_call(
        functools.partial(preload_kernel, 2 * pair),
        in_specs=[pl.BlockSpec(memory_space=pltpu.HBM)],
        out_specs=in_vmem(1)[0],
        out_shape=jax.ShapeDtypeStruct(shape, weight.dtype),
        scratch_shapes=[pltpu.SemaphoreType.DMA((2 * 2 * count,))],
        compiler_params=pltpu.CompilerParams(vmem_limit_bytes=34 << 20),
        cost_estimate=pl.CostEstimate(
            flops=0, bytes_accessed=2 * math.prod(shape), transcendentals=0
        ),
    )(weight)


def mixing_kernel(shards, loaded, me_ref, *refs):
    outer, inner = shards
    row_refs, refs = refs[:inner], refs[inner:]
    forward_ref, backward_ref, weight_ref, *refs = refs
    loaded_refs, refs = refs[:loaded], refs[loaded:]
    loaded = sum(ref.shape[0] // 2 for ref in loaded_refs)
    out_refs, (held, sems, wide, left, mixed) = refs[:inner], refs[inner:]

    channels = wide.shape[1]
    _, cells_x, item_rows, _ = row_refs[0].shape
    pairs = item_rows // 2
    full_x = outer * inner * cells_x
    half = channels // 2
    span = 2 * MX
    block = cells_x * item_rows
    _, own_outer, own_inner = place(me_ref[0], shards)

    def copy(pair):
        slot = pair - loaded
        return pltpu.make_async_copy(
            weight_ref.at[pl.ds(2 * pair, 2)], held.at[slot], sems.at[slot]
        )

    for pair in range(loaded, pairs):
        copy(pair).start()

    def rows_of(outer_index, inner_index):
        start = pl.multiple_of((outer_index * inner + inner_index) * block, block)
        return pl.ds(start, block)

    for number, step in enumerate(far_first(inner)):
        source = origin(own_inner, step, inner)
        for slot in range(outer):
            value = row_refs[number][slot].reshape(block, channels)
            at = rows_of(origin(own_outer, slot, outer), source)
            wide[at, :] = value.astype(jnp.float32)
    low = lax.broadcasted_iota(jnp.int32, (span, channels), 1) < half
    for pair in range(pairs):
        columns = [wide[pl.ds(2 * pair + p, full_x, stride=item_rows), :] for p in range(2)]
        columns = jnp.concatenate(columns, axis=0).astype(jnp.bfloat16)
        both = dot(forward_ref[...], columns)
        value, turned = both[:span], both[span:]
        first = jnp.where(low, value, pltpu.roll(turned, half, axis=1))
        second = jnp.where(low, pltpu.roll(value, half, axis=1), turned)
        left[pl.ds(pair * span, span), :channels] = first.astype(left.dtype)
        left[pl.ds(pair * span, span), channels:] = second.astype(left.dtype)

    group = 16
    row = lax.broadcasted_iota(jnp.int32, (group, channels), 0) // 2

    def mix(pair, tile_of):
        for step in range(span // group):
            start = pl.multiple_of(pair * span + step * group, group)
            lhs = left[pl.ds(start, group), :]
            gathered = jnp.zeros((group, channels), jnp.float32)
            for i in range(0, group // 2, 2):
                mode = step * (group // 2) + i
                tiles = [
                    jnp.concatenate([tile_of(h, mode + k) for h in range(2)], axis=0)
                    for k in range(2)
                ]
                product = dot(lhs, jnp.concatenate(tiles, axis=1))
                for k in range(2):
                    gathered = jnp.where(
                        row == i + k, product[:, k * channels : (k + 1) * channels], gathered
                    )
            mixed[pl.ds(start, group), :] = gathered.astype(mixed.dtype)

    pair = 0
    for ref in loaded_refs:
        count = ref.shape[0] // 2

        def ready(i, carry, ref=ref, pair=pair):
            mix(pair + i, lambda h, mode: ref[2 * i + h, mode])
            return carry

        lax.fori_loop(0, count, ready, 0)
        pair += count

    def streamed(pair, carry):
        copy(pair).wait()
        mix(pair, lambda h, mode: held[pair - loaded, h, mode])
        return carry

    lax.fori_loop(loaded, pairs, streamed, 0)

    for pair in range(pairs):
        result = dot(backward_ref[...], mixed[pl.ds(pair * span, span), :])
        for p in range(2):
            wide[pl.ds(2 * pair + p, full_x, stride=item_rows), :] = result[
                p * full_x : (p + 1) * full_x
            ]
    for step in range(inner):
        target = peer(own_inner, step, inner)
        for slot in range(outer):
            value = wide[rows_of(peer(own_outer, slot, outer), target), :]
            value = value.reshape(cells_x, item_rows, channels)
            out_refs[step][slot] = value.astype(out_refs[step].dtype)


def mixing(me, rows, forward_x, backward_x, weight, loaded, shards):
    outer, inner = shards
    _, cells_x, item_rows, channels = rows[0].shape
    pairs = item_rows // 2
    row_count = outer * inner * cells_x * item_rows
    streamed = pairs - sum(part.shape[0] // 2 for part in loaded)
    return pl.pallas_call(
        functools.partial(mixing_kernel, shards, len(loaded)),
        in_specs=[IN_SMEM]
        + in_vmem(inner + 2)
        + [pl.BlockSpec(memory_space=pltpu.HBM)]
        + in_vmem(len(loaded)),
        out_specs=in_vmem(inner),
        out_shape=[jax.ShapeDtypeStruct(rows[0].shape, jnp.bfloat16)] * inner,
        scratch_shapes=[
            pltpu.VMEM((streamed, 2, *weight.shape[1:]), weight.dtype),
            pltpu.SemaphoreType.DMA((streamed,)),
            pltpu.VMEM((row_count, channels), jnp.float32),
            pltpu.VMEM((pairs * 2 * MX, 2 * channels), jnp.bfloat16),
            pltpu.VMEM((pairs * 2 * MX, channels), jnp.bfloat16),
        ],
        compiler_params=pltpu.CompilerParams(vmem_limit_bytes=20 << 20),
        cost_estimate=pl.CostEstimate(
            flops=8 * weight.size, bytes_accessed=2 * weight.size, transcendentals=0
        ),
    )(me, *rows, forward_x, backward_x, weight, *loaded)


def convolution_kernel(x, cells_x, width, shards, shards_y, me_ref, *refs):
    flow_ref, paired_ref, other_ref, front_ref, back_ref, kernel_ref, out_ref, padded = refs
    _, cells_y, cells_z, channels = out_ref.shape
    own_y, _, _ = place(me_ref[0], shards)
    even = is_even(me_ref[0], shards)
    for plane in range(width + 2):
        p = x + plane - 1
        if 0 <= p < cells_x:
            padded[plane, 1 : cells_y + 1] = flow_ref[p]
            row = front_ref[p]
            padded[plane, 0] = jnp.where(own_y > 0, row, jnp.zeros_like(row))
            row = back_ref[p]
            last = own_y == shards_y - 1
            padded[plane, cells_y + 1] = jnp.where(last, jnp.zeros_like(row), row)
        else:
            use_paired = jnp.logical_not(even) if p < 0 else even

            @pl.when(use_paired)
            def _(plane=plane):
                padded[plane] = paired_ref[...]

            @pl.when(jnp.logical_not(use_paired))
            def _(plane=plane):
                padded[plane] = other_ref[...]

    rows = 8 if cells_y % 8 == 0 else 1
    columns = [(k, d) for k in range(width) for d in range(3)]
    columns = [columns[i : i + 2] for i in range(0, len(columns), 2)]
    none = jnp.zeros((channels, channels), kernel_ref.dtype)

    def chunk(index, carry):
        y = index * rows
        products = {}
        for group in columns:
            blocks, kernels = [], []
            for p in range(width + 2):
                if not any(0 <= p - k < 3 for k, _ in group):
                    continue
                for b in range(3):
                    part = padded[p, pl.ds(y + b, rows)]
                    blocks.append(part.reshape(rows * cells_z, channels))
                    parts = [
                        kernel_ref[p - k, b, d] if 0 <= p - k < 3 else none for k, d in group
                    ]
                    kernels.append(jnp.concatenate(parts, axis=1))
            product = dot(jnp.concatenate(blocks, axis=1), jnp.concatenate(kernels, axis=0))
            for i, column in enumerate(group):
                part = product[:, i * channels : (i + 1) * channels]
                products[column] = part.reshape(rows, cells_z, channels)
        z = lax.broadcasted_iota(jnp.int32, (rows, cells_z, channels), 1)
        for k in range(width):
            before = jnp.where(z == 0, 0.0, pltpu.roll(products[k, 0], 1, axis=1))
            after = pltpu.roll(products[k, 2], cells_z - 1, axis=1)
            after = jnp.where(z == cells_z - 1, 0.0, after)
            total = before + products[k, 1] + after
            out_ref[k, pl.ds(y, rows)] = total.astype(out_ref.dtype)
        return carry

    lax.fori_loop(0, cells_y // rows, chunk, 0)


def convolution(me, x, width, flow, halos, kernel, shards, shards_y):
    cells_x, cells_y, cells_z, channels = flow.shape
    shape = (width, cells_y, cells_z, channels)
    return pl.pallas_call(
        functools.partial(convolution_kernel, x, cells_x, width, shards, shards_y),
        in_specs=[IN_SMEM] + in_vmem(2 + len(halos)),
        out_specs=in_vmem(1)[0],
        out_shape=jax.ShapeDtypeStruct(shape, jnp.bfloat16),
        scratch_shapes=[pltpu.VMEM((width + 2, cells_y + 2, cells_z, channels), flow.dtype)],
        compiler_params=pltpu.CompilerParams(vmem_limit_bytes=14 << 20),
        cost_estimate=pl.CostEstimate(
            flops=3 * 27 * width * cells_y * cells_z * channels * channels,
            bytes_accessed=10 * cells_y * cells_z * channels,
            transcendentals=0,
        ),
    )(me, flow, *halos, kernel)


def bundled_slots(count):
    return [[0] + far_first(count)[:-1]]


def bundle_kernel(*refs):
    *in_refs, out_ref = refs
    for i, ref in enumerate(in_refs):
        out_ref[i] = ref[...]


def bundle(arrays):
    shape = (len(arrays), *arrays[0].shape)
    return pl.pallas_call(
        bundle_kernel,
        in_specs=in_vmem(len(arrays)),
        out_specs=in_vmem(1)[0],
        out_shape=jax.ShapeDtypeStruct(shape, arrays[0].dtype),
        cost_estimate=pl.CostEstimate(
            flops=math.prod(shape), bytes_accessed=0, transcendentals=0
        ),
        compiler_params=pltpu.CompilerParams(vmem_limit_bytes=10 << 20),
    )(*arrays)


def gather_pieces(me, shards, pieces, held):
    outer, inner = shards
    _, own_outer, own_inner = place(me, shards)
    for number, slot, ref in pieces:
        cells_x, rows = ref.shape[1:3]
        source = (number * outer + origin(own_outer, slot, outer)) * inner
        for part in range(inner):
            at = (source + origin(own_inner, part, inner)) * rows
            for x in range(cells_x):
                held[x, pl.ds(pl.multiple_of(at, rows), rows), :] = ref[part, x]


def inverse(me, shards, shards_y, steps, table_ref, held, part, x, width, positions):
    own_y, _, _ = place(me, shards)
    columns = [held[x + i] for i in range(width)]
    depth = table_ref.shape[2]
    total = None
    for number, step in enumerate(steps):
        source = lax.rem(own_y + (shards_y - step), shards_y)
        rows = pl.ds(pl.multiple_of(part * positions, positions), positions)
        table = table_ref[own_y * shards_y + source, rows, :]
        block = [column[number * depth : (number + 1) * depth] for column in columns]
        product = dot(table, jnp.concatenate(block, axis=1))
        total = product if total is None else total + product
    return total


def own_part_kernel(shards, shards_y, me_ref, table_ref, *refs):
    *piece_refs, bias_ref, out_ref, held = refs
    cells_x, cells_y, cells_z, channels = out_ref.shape
    width = 2 if cells_x % 2 == 0 else 1
    count = -(-cells_x // width)
    piece_refs, convolved_refs = piece_refs[:-count], piece_refs[-count:]
    slots = far_first(shards[0])
    gather_pieces(me_ref[0], shards, [(0, *p) for p in zip(slots, piece_refs)], held)
    bias = bias_ref[...]
    rows = 4 if cells_y % 4 == 0 else 1
    positions = rows * cells_z

    def chunk(part, carry):
        for x in range(0, cells_x, width):
            total = inverse(
                me_ref[0], shards, shards_y, [0], table_ref, held, part, x, width, positions
            )
            for i in range(width):
                spectral = total[:, i * channels : (i + 1) * channels]
                convolved = convolved_refs[x // width][i, pl.ds(part * rows, rows)]
                value = spectral.reshape(rows, cells_z, channels) + convolved + bias
                out_ref[x + i, pl.ds(part * rows, rows)] = value
        return carry

    lax.fori_loop(0, cells_y // rows, chunk, 0)


def last_part_kernel(shards, shards_y, me_ref, table_ref, *refs):
    *bundle_refs, partial_ref, out_ref, held = refs
    cells_x, cells_y, cells_z, channels = out_ref.shape
    bundles = bundled_slots(shards[0])
    steps = list(range(1, shards_y))
    width = 2 if cells_x % 2 == 0 else 1
    part = pl.program_id(0)

    @pl.when(part == 0)
    def _():
        pieces = []
        for i, ref in enumerate(bundle_refs):
            number, bundle = divmod(i, len(bundles))
            pieces += [(number, slot, ref.at[j]) for j, slot in enumerate(bundles[bundle])]
        gather_pieces(me_ref[0], shards, pieces, held)

    for x in range(0, cells_x, width):
        total = inverse(
            me_ref[0], shards, shards_y, steps, table_ref, held, part, x, width,
            cells_y * cells_z,
        )
        for i in range(width):
            spectral = total[:, i * channels : (i + 1) * channels]
            value = partial_ref[x + i, pl.ds(part * cells_y, cells_y)]
            value = value + spectral.reshape(cells_y, cells_z, channels)
            out_ref[x + i] = jax.nn.gelu(value, approximate=True).astype(out_ref.dtype)


def own_part(me, table, pieces, convolved, bias, shards, shards_y):
    width, cells_y, cells_z, channels = convolved[0].shape
    shape = (width * len(convolved), cells_y, cells_z, channels)
    depth = table.shape[2]
    return pl.pallas_call(
        functools.partial(own_part_kernel, shards, shards_y),
        in_specs=[IN_SMEM] + in_vmem(2 + len(pieces) + len(convolved)),
        out_specs=in_vmem(1)[0],
        out_shape=jax.ShapeDtypeStruct(shape, jnp.float32),
        scratch_shapes=[pltpu.VMEM((shape[0], depth, channels), jnp.bfloat16)],
        compiler_params=pltpu.CompilerParams(vmem_limit_bytes=14 << 20),
        cost_estimate=pl.CostEstimate(
            flops=2 * math.prod(shape) * depth,
            bytes_accessed=6 * math.prod(shape),
            transcendentals=0,
        ),
    )(me, table, *pieces, *convolved, bias)


def last_part(me, table, pieces, partial, shards, shards_y):
    cells_x, cells_y, cells_z, channels = partial.shape
    parts = 4 if cells_y % 4 == 0 else 1
    block = (cells_x, cells_y // parts, cells_z, channels)
    depth = table.shape[2] * (shards_y - 1)
    return pl.pallas_call(
        functools.partial(last_part_kernel, shards, shards_y),
        grid_spec=pltpu.PrefetchScalarGridSpec(
            num_scalar_prefetch=1,
            grid=(parts,),
            in_specs=in_vmem(2 + len(pieces)),
            out_specs=pl.BlockSpec(block, lambda i, me: (0, i, 0, 0)),
            scratch_shapes=[pltpu.VMEM((cells_x, depth, channels), jnp.bfloat16)],
        ),
        out_shape=jax.ShapeDtypeStruct(partial.shape, jnp.bfloat16),
        compiler_params=pltpu.CompilerParams(vmem_limit_bytes=14 << 20),
        cost_estimate=pl.CostEstimate(
            flops=2 * partial.size * depth,
            bytes_accessed=6 * partial.size,
            transcendentals=partial.size,
        ),
    )(me, table, *pieces, partial)


def with_halo(array, sides, width):
    for axis, dim in sides:
        size, length = (lax.axis_size(axis), array.shape[dim])
        up = [(i, (i + 1) % size) for i in range(size - 1)]
        down = [(j, i) for i, j in up]
        last = lax.slice_in_dim(array, length - width, length, axis=dim)
        initial = lax.slice_in_dim(array, 0, width, axis=dim)
        before = lax.ppermute(last, axis, up)
        after = lax.ppermute(initial, axis, down)
        array = jnp.concatenate([before, array, after], axis=dim)
    return array


def signed_modes(mode_count):
    position = jnp.arange(mode_count, dtype=jnp.int32)
    return jnp.where(position < mode_count // 2, position, position - mode_count)


def angle_grid(first, second, length):
    phase_turns = first[:, None] * second[None, :] % length
    return phase_turns.astype(jnp.float32) * (2.0 * math.pi / length)


def real_table(first, second, length, factor):
    angles = angle_grid(first, second, length)
    return jnp.stack([jnp.cos(angles) * factor, -jnp.sin(angles) * factor])


def complex_table(first, second, length, factor, direction):
    angles = angle_grid(first, second, length)
    cosine = jnp.cos(angles) * factor
    sine_part = jnp.sin(angles) * factor
    return jnp.stack(
        [jnp.stack([cosine, direction * sine_part]), jnp.stack([-direction * sine_part, cosine])]
    )


def split_pair_spectral(flow_field, spectral_weight):
    highest = lax.Precision.HIGHEST
    cells_x, cells_y, cells_z, channels = flow_field.shape
    count_x = lax.axis_size("gx")
    count_y = lax.axis_size("gy")
    full_x = cells_x * count_x
    full_y = cells_y * count_y
    item_count = spectral_weight.shape[0]
    local_y = lax.axis_index("gy") * cells_y + jnp.arange(cells_y, dtype=jnp.int32)
    grid_x = jnp.arange(full_x, dtype=jnp.int32)
    grid_z = jnp.arange(cells_z, dtype=jnp.int32)
    modes_z = jnp.arange(MZ, dtype=jnp.int32)
    forward_z = real_table(grid_z, modes_z, cells_z, cells_z ** (-0.5)).astype(jnp.bfloat16)
    z_spectrum = jnp.einsum(
        "xyzc,pzk->pxykc", flow_field, forward_z, preferred_element_type=jnp.float32
    )
    columns = lax.all_to_all(
        z_spectrum.astype(jnp.bfloat16), "gy", split_axis=4, concat_axis=2, tiled=True
    ).astype(z_spectrum.dtype)
    whole_y = jnp.arange(full_y, dtype=jnp.int32)
    forward_full = complex_table(whole_y, signed_modes(MY), full_y, full_y ** (-0.5), -1.0)
    y_spectrum = jnp.einsum("pxykc,pqyj->qxjkc", columns, forward_full, precision=highest)
    owned = lax.all_to_all(
        y_spectrum.astype(jnp.bfloat16), "gy", split_axis=2, concat_axis=4, tiled=True
    ).astype(y_spectrum.dtype)
    owned_modes = owned.reshape(2, cells_x, count_x, item_count, channels // 2)
    gathered_rows = lax.all_to_all(
        owned_modes.astype(jnp.bfloat16), "gx", split_axis=2, concat_axis=1, tiled=True
    ).astype(owned_modes.dtype)
    gathered_rows = gathered_rows.reshape(2, full_x, item_count, channels // 2)
    forward_x = complex_table(grid_x, signed_modes(MX), full_x, full_x ** (-0.5), -1.0)
    x_spectrum = jnp.einsum("pxjc,pqxm->qmjc", gathered_rows, forward_x, precision=highest).astype(
        jnp.bfloat16
    )
    products = jnp.einsum(
        "pmjc,jmqco->pqmjo", x_spectrum, spectral_weight, preferred_element_type=jnp.float32
    )
    mixed_modes = jnp.stack([products[0, 0] - products[1, 1], products[0, 1] + products[1, 0]])
    backward_x = complex_table(signed_modes(MX), grid_x, full_x, MX ** (-0.5), 1.0)
    inverse_x = jnp.einsum("pmjc,pqmx->qxjc", mixed_modes, backward_x, precision=highest)
    inverse_x = inverse_x.reshape(2, full_x, 1, item_count, channels)
    returned = lax.all_to_all(
        inverse_x.astype(jnp.bfloat16), "gx", split_axis=1, concat_axis=2, tiled=True
    ).astype(inverse_x.dtype)
    band_rows = MY // count_y
    summed = returned.reshape(2, cells_x, band_rows * MZ, 2, channels).sum(axis=3)
    summed = summed.reshape(2, cells_x, band_rows, MZ, channels)
    coefficients = lax.all_gather(summed.astype(jnp.bfloat16), "gy", axis=2, tiled=True).astype(
        summed.dtype
    )
    backward_y = complex_table(signed_modes(MY), local_y, full_y, MY ** (-0.5), 1.0)
    y_inverse = jnp.einsum("pxjkc,pqjy->qxykc", coefficients, backward_y, precision=highest).astype(
        jnp.bfloat16
    )
    backward_z = real_table(modes_z, grid_z, cells_z, MZ ** (-0.5)).astype(jnp.bfloat16)
    return jnp.einsum("pxykc,pkz->xyzc", y_inverse, backward_z, preferred_element_type=jnp.float32)


def split_pair_convolve(flow_field, conv_weight):
    cells_x, cells_y, cells_z, channels = flow_field.shape
    padded = with_halo(flow_field, (("gx", 0), ("gy", 1)), 1)
    padded = jnp.pad(padded, ((0, 0), (0, 0), (1, 1), (0, 0)))
    stacked = jnp.concatenate(
        [padded[:, :, 0:cells_z], padded[:, :, 1 : cells_z + 1], padded[:, :, 2 : cells_z + 2]],
        axis=3,
    )
    kernel = conv_weight.reshape(3, 3, 3 * channels, channels)
    accumulated = jnp.zeros((cells_x, cells_y, cells_z, channels), jnp.float32)
    for shift_x in range(3):
        for shift_y in range(3):
            accumulated = accumulated + jnp.dot(
                stacked[shift_x : shift_x + cells_x, shift_y : shift_y + cells_y],
                kernel[shift_x, shift_y],
                preferred_element_type=jnp.float32,
            )
    return accumulated


def neighbours(first, last, axis):
    size = lax.axis_size(axis)
    up = [(i, i + 1) for i in range(size - 1)]
    down = [(i + 1, i) for i in range(size - 1)]
    return lax.ppermute(last, axis, up), lax.ppermute(first, axis, down)


def with_neighbour(array, start, axis):
    size = lax.axis_size(axis)
    pairs = [(i, i + 1) for i in range(start, size - 1, 2)]
    return lax.ppermute(array, axis, pairs + [(j, i) for i, j in pairs])


def exchange(array, step, shards, along_outer):
    outer, inner = shards
    pairs = []
    for i in range(outer * inner):
        a, b = divmod(i, inner)
        count, own = (outer, a) if along_outer else (inner, b)
        to = own ^ step if count & (count - 1) == 0 else (own + step) % count
        pairs.append((i, to * inner + b if along_outer else a * inner + to))
    return lax.ppermute(array, "gx", pairs)


def over_y(array, step, shards_y):
    return lax.ppermute(array, "gy", [(i, (i + step) % shards_y) for i in range(shards_y)])


def body(flow, spectral_weight, conv_weight, bias):
    cells_x, cells_y, cells_z, channels = flow.shape
    shards_x, shards_y = lax.axis_size("gx"), lax.axis_size("gy")
    items = spectral_weight.shape[0]
    pairs = items // 2
    if items % 2 or shards_y < 2:
        spectral = split_pair_spectral(flow, spectral_weight)
        convolved = split_pair_convolve(flow, conv_weight)
        return jax.nn.gelu(spectral + convolved + bias, approximate=True).astype(jnp.bfloat16)

    barrier = lax.optimization_barrier
    inner = max(d for d in range(1, shards_x + 1) if shards_x % d == 0 and d * d <= shards_x)
    outer = shards_x // inner
    shards = (outer, inner)
    me = lax.axis_index(("gy", "gx")).astype(jnp.int32).reshape(1)
    sizes = (shards_x, shards_y, pairs, cells_y, cells_z)
    full_x = cells_x * shards_x
    weight = spectral_weight.reshape(items, MX, channels, channels)
    early = pairs // 4

    table = jnp.asarray(forward_yz_table(*sizes))
    columns = flow.reshape(cells_x, cells_y * cells_z, channels)
    order = far_first(outer)
    cut = (outer + 1) // 2
    pieces = [piece for piece in (order[:cut], order[cut:]) if piece]
    arrived = [[] for _ in pieces]
    for step in range(1, shards_y):
        sent = forward_yz(me, table, columns, step, shards, shards_y, pieces)
        sent, columns, weight = barrier((sent, columns, weight))
        for into, piece in zip(arrived, sent):
            into.append(over_y(piece, step, shards_y))
    loaded = [preload(weight, 0, early)] if early else []
    loaded, columns = barrier((loaded, columns))
    kept = forward_yz(me, table, columns, 0, shards, shards_y, pieces, cells_z)
    kept, (first, last, *ends) = kept[: len(pieces)], kept[len(pieces) :]
    if shards_y == 2:
        front = back = over_y(ends[0], 1, shards_y)
    else:
        front, back = neighbours(*ends, "gy")

    by_outer = []
    for piece, own, parts in zip(pieces, kept, arrived):
        for step, total in zip(piece, add_pieces(own, parts)):
            by_outer.append(exchange(total, step, shards, True) if step else total)
    if early:
        loaded.append(preload(weight, early, early))
    by_outer, loaded, weight = barrier((by_outer[::-1], loaded, weight))
    by_inner = regroup(me, by_outer[::-1], shards, True)
    by_inner, weight = barrier((by_inner, weight))
    rows = [
        exchange(by_inner[step], step, shards, False) if step else by_inner[0]
        for step in far_first(inner)
    ]
    if early:
        loaded.append(preload(weight, 2 * early, early))

    rows, loaded, first, last, front, back = barrier((rows, loaded, first, last, front, back))
    paired, other = halo_planes(me, first, last, front, back, shards, shards_y)
    paired, other = with_neighbour(paired, 0, "gx"), with_neighbour(other, 1, "gx")
    returned = mixing(
        me,
        rows,
        jnp.asarray(forward_x_table(full_x)),
        jnp.asarray(backward_x_table(full_x)),
        weight,
        loaded,
        shards,
    )
    returned, paired, other = barrier((list(returned), paired, other))
    halos = (paired, other, front, back)
    width = 2 if cells_x % 2 == 0 else 1
    convolved = [
        convolution(me, x, width, flow, halos, conv_weight, shards, shards_y)
        for x in range(0, cells_x, width)
    ]

    returned = [
        exchange(returned[step], step, shards, False) if step else returned[0]
        for step in far_first(inner)
    ]
    returned, convolved[0] = barrier((returned, convolved[0]))
    returned = regroup(me, returned, shards, False)
    returned = [
        exchange(returned[step], step, shards, True) if step else returned[0]
        for step in far_first(outer)
    ]
    by_slot = dict(zip(far_first(outer), returned))
    bundles = [bundle([by_slot[slot] for slot in slots]) for slots in bundled_slots(outer)]
    others = []
    for step in range(1, shards_y):
        others += [over_y(part, step, shards_y) for part in bundles]
    table = jnp.asarray(backward_yz_table(*sizes))
    bias = bias.reshape(1, channels)
    partial = own_part(me, table, returned, convolved, bias, shards, shards_y)
    return last_part(me, table, others, partial, shards, shards_y)


def solution(mesh):
    placed = (P("gx", "gy", None, None), P(("gy", "gx"), None, None, None, None), P(), P())
    return jax.shard_map(
        body, mesh=mesh, in_specs=placed, out_specs=P("gx", "gy", None, None), check_vma=False
    )
```

```python
import functools
import math

import jax
import jax.numpy as jnp
import numpy as np
from jax import lax
from jax.experimental import pallas as pl
from jax.experimental.pallas import tpu as pltpu
from jax.sharding import PartitionSpec as P

MX = 64
MY = 16
MZ = 16


def frequencies(mode_count):
    position = np.arange(mode_count)
    return np.where(position < mode_count // 2, position, position - mode_count)


def wave(first, second, length, factor):
    turns = (np.asarray(first)[:, None] * np.asarray(second)[None, :]) % length
    angles = turns * (2.0 * math.pi / length)
    return (np.cos(angles) + 1j * np.sin(angles)) * factor


def rounded(values):
    return values.astype(np.float32).astype(jnp.bfloat16).astype(np.float64)


def item_modes(shards_x, shards_y, pairs):
    index = np.arange(shards_y * shards_x * pairs).reshape(shards_y, shards_x, pairs)
    return index // MZ, index % MZ


def forward_yz_table(shards_x, shards_y, pairs, cells_y, cells_z):
    full_y = shards_y * cells_y
    turn_z = wave(np.arange(MZ), np.arange(cells_z), cells_z, cells_z**-0.5)
    turn_z = rounded(turn_z.real) - 1j * rounded(turn_z.imag)
    turn_y = np.conj(wave(frequencies(MY), np.arange(full_y), full_y, full_y**-0.5))
    mode_y, mode_z = item_modes(shards_x, shards_y, pairs)
    table = np.empty((shards_y, shards_y, shards_x, pairs, 2, cells_y, cells_z), np.float32)
    for own in range(shards_y):
        rows = turn_y[:, own * cells_y : (own + 1) * cells_y]
        product = rows[mode_y][..., :, None] * turn_z[mode_z][..., None, :]
        table[own, :, :, :, 0] = product.real
        table[own, :, :, :, 1] = product.imag
    return table.reshape(shards_y, -1, cells_y * cells_z).astype(jnp.bfloat16)


def backward_yz_table(shards_x, shards_y, pairs, cells_y, cells_z):
    full_y = shards_y * cells_y
    turn_z = wave(np.arange(MZ), np.arange(cells_z), cells_z, MZ**-0.5)
    turn_z = rounded(turn_z.real) + 1j * rounded(turn_z.imag)
    turn_y = wave(frequencies(MY), np.arange(full_y), full_y, MY**-0.5)
    mode_y, mode_z = item_modes(shards_x, shards_y, pairs)
    table = np.empty((shards_y, shards_y, cells_y, cells_z, shards_x, pairs, 2), np.float32)
    for own in range(shards_y):
        rows = turn_y[:, own * cells_y : (own + 1) * cells_y]
        product = rows[mode_y][..., :, None] * turn_z[mode_z][..., None, :]
        product = np.moveaxis(product, (3, 4), (1, 2))
        table[own, ..., 0] = product.real
        table[own, ..., 1] = -product.imag
    return table.reshape(shards_y**2, cells_y * cells_z, -1).astype(jnp.bfloat16)


def forward_x_table(full_x):
    turn = np.conj(wave(frequencies(MX), np.arange(full_x), full_x, full_x**-0.5))
    parts = np.empty((2, MX, 2, 2, full_x), np.float32)
    parts[0, :, 0, 0], parts[0, :, 0, 1] = turn.real, -turn.imag
    parts[0, :, 1, 0], parts[0, :, 1, 1] = turn.imag, turn.real
    parts[1, :, 0] = -parts[0, :, 1]
    parts[1, :, 1] = parts[0, :, 0]
    return parts.reshape(2 * MX * 2, 2 * full_x).astype(jnp.bfloat16)


def backward_x_table(full_x):
    turn = wave(frequencies(MX), np.arange(full_x), full_x, MX**-0.5).T
    parts = np.empty((2, full_x, MX, 2), np.float32)
    parts[0, :, :, 0], parts[0, :, :, 1] = turn.real, -turn.imag
    parts[1, :, :, 0], parts[1, :, :, 1] = turn.imag, turn.real
    return parts.reshape(2 * full_x, MX * 2).astype(jnp.bfloat16)


def dot(left, right):
    return jnp.dot(left, right, preferred_element_type=jnp.float32)


def peer(index, step, count):
    if count & (count - 1) == 0:
        return index ^ step
    return lax.rem(index + step, count)


def origin(index, step, count):
    if count & (count - 1) == 0:
        return index ^ step
    return lax.rem(index + (count - step), count)


def far_first(count):
    return list(range(count - 1, -1, -1))


def place(me, shards):
    outer, inner = shards
    across = lax.rem(me, outer * inner)
    return lax.div(me, outer * inner), lax.div(across, inner), lax.rem(across, inner)


def in_vmem(count):
    return [pl.BlockSpec(memory_space=pltpu.VMEM)] * count


IN_SMEM = pl.BlockSpec(memory_space=pltpu.SMEM)


def transform(table, flow_at, cells_x, refs, pieces):
    inner, _, rows, channels = refs[0].shape[1:]
    block = inner * rows
    width = 2 if cells_x % 2 == 0 else 1
    for x in range(0, cells_x, width):
        columns = [flow_at(x + i) for i in range(width)]
        result = dot(table, jnp.concatenate(columns, axis=1))
        for i in range(width):
            part = result[:, i * channels : (i + 1) * channels]
            at = 0
            for ref, piece in zip(refs, pieces):
                for slot in range(len(piece)):
                    value = part[at : at + block].reshape(inner, rows, channels)
                    ref[slot, :, x + i] = value.astype(ref.dtype)
                    at += block


def send_kernel(shards, shards_y, pieces, step, me_ref, table_ref, flow_ref, *refs):
    *refs, table, flow, table_sems, flow_sems = refs
    cells_x = flow.shape[0]
    outer, _ = shards
    block = refs[0].shape[1] * refs[0].shape[3]
    own_y, own, _ = place(me_ref[0], shards)
    owner = lax.rem(own_y + step, shards_y)
    copies = []
    for i, other in enumerate(step for piece in pieces for step in piece):
        start = (owner * outer + peer(own, other, outer)) * block
        source = table_ref.at[own_y, pl.ds(pl.multiple_of(start, block), block)]
        copies.append(
            pltpu.make_async_copy(source, table.at[pl.ds(i * block, block)], table_sems.at[i])
        )
    loads = [
        pltpu.make_async_copy(flow_ref.at[x], flow.at[x], flow_sems.at[x])
        for x in range(cells_x)
    ]
    for copy in copies + loads:
        copy.start()
    for copy in copies:
        copy.wait()

    def flow_at(x):
        loads[x].wait()
        return flow[x]

    transform(table[...], flow_at, cells_x, refs, pieces)


def is_even(me, shards):
    _, own_outer, own_inner = place(me, shards)
    return lax.rem(own_outer * shards[1] + own_inner, 2) == 0


def keep_kernel(shards, shards_y, pieces, me_ref, table_ref, flow_ref, *refs):
    refs, (first, last, *edges) = refs[: len(pieces)], refs[len(pieces) :]
    cells_x, positions, _ = flow_ref.shape
    outer, _ = shards
    block = refs[0].shape[1] * refs[0].shape[3]
    own_y, own, _ = place(me_ref[0], shards)
    tables = []
    for other in (step for piece in pieces for step in piece):
        start = (own_y * outer + peer(own, other, outer)) * block
        tables.append(table_ref[own_y, pl.ds(pl.multiple_of(start, block), block), :])
    transform(
        jnp.concatenate(tables, axis=0), lambda x: flow_ref[x], cells_x, refs, pieces
    )
    first[...] = flow_ref[0]
    last[...] = flow_ref[cells_x - 1]
    cells_z = edges[0].shape[1]
    low, high = pl.ds(0, cells_z), pl.ds(positions - cells_z, cells_z)
    if len(edges) > 1:
        edges[0][...] = flow_ref[:, low]
        edges[1][...] = flow_ref[:, high]
    else:

        @pl.when(own_y > 0)
        def _():
            edges[0][...] = flow_ref[:, low]

        @pl.when(own_y == 0)
        def _():
            edges[0][...] = flow_ref[:, high]


def forward_yz(me, table, flow, step, shards, shards_y, pieces, cells_z=0):
    cells_x, positions, channels = flow.shape
    outer, inner = shards
    rows = table.shape[1] // shards_y
    unit = (inner, cells_x, rows // (outer * inner), channels)
    dtype = jnp.bfloat16 if step else jnp.float32
    shapes = [jax.ShapeDtypeStruct((len(piece), *unit), dtype) for piece in pieces]
    if step:
        kernel = functools.partial(send_kernel, shards, shards_y, pieces, step)
        specs = [pl.BlockSpec(memory_space=pltpu.HBM)] * 2
        scratch = [
            pltpu.VMEM((rows, positions), table.dtype),
            pltpu.VMEM(flow.shape, flow.dtype),
            pltpu.SemaphoreType.DMA((outer,)),
            pltpu.SemaphoreType.DMA((cells_x,)),
        ]
    else:
        kernel = functools.partial(keep_kernel, shards, shards_y, pieces)
        specs, scratch = in_vmem(2), []
        shapes += [jax.ShapeDtypeStruct((positions, channels), flow.dtype)] * 2
        edge = jax.ShapeDtypeStruct((cells_x, cells_z, channels), flow.dtype)
        shapes += [edge] * (1 if shards_y == 2 else 2)
    return pl.pallas_call(
        kernel,
        in_specs=[IN_SMEM] + specs,
        out_specs=in_vmem(len(shapes)),
        out_shape=shapes,
        scratch_shapes=scratch,
        compiler_params=pltpu.CompilerParams(vmem_limit_bytes=(56 if step else 10) << 20),
        cost_estimate=pl.CostEstimate(
            flops=2 * rows * positions * cells_x * channels,
            bytes_accessed=2 * positions * (rows + cells_x * channels),
            transcendentals=0,
        ),
    )(me, table, flow)


def add_kernel(count, *refs):
    out_refs = refs[count:]
    for slot, out_ref in enumerate(out_refs):
        total = refs[0][slot]
        for ref in refs[1:count]:
            total = total + ref[slot].astype(jnp.float32)
        out_ref[...] = total.astype(out_ref.dtype)


def add_pieces(own, arrived):
    slots, *unit = own.shape
    return pl.pallas_call(
        functools.partial(add_kernel, 1 + len(arrived)),
        in_specs=in_vmem(1 + len(arrived)),
        out_specs=in_vmem(slots),
        out_shape=[jax.ShapeDtypeStruct(unit, jnp.bfloat16)] * slots,
        cost_estimate=pl.CostEstimate(flops=own.size, bytes_accessed=0, transcendentals=0),
        compiler_params=pltpu.CompilerParams(vmem_limit_bytes=10 << 20),
    )(own, *arrived)


def regroup_kernel(shards, chosen, me_ref, *refs):
    _, _, own = place(me_ref[0], shards)
    count = refs[0].shape[0]
    in_refs, out_refs = refs[:-count], refs[-count:]
    for step, out_ref in enumerate(out_refs):
        at = peer(own, step, count) if chosen else step
        for number, in_ref in enumerate(in_refs):
            out_ref[far_first(len(in_refs))[number]] = in_ref[at]


def regroup(me, arrays, shards, chosen):
    count, *unit = arrays[0].shape
    return pl.pallas_call(
        functools.partial(regroup_kernel, shards, chosen),
        in_specs=[IN_SMEM] + in_vmem(len(arrays)),
        out_specs=in_vmem(count),
        out_shape=[jax.ShapeDtypeStruct((len(arrays), *unit), arrays[0].dtype)] * count,
        cost_estimate=pl.CostEstimate(
            flops=arrays[0].size, bytes_accessed=0, transcendentals=0
        ),
        compiler_params=pltpu.CompilerParams(vmem_limit_bytes=10 << 20),
    )(me, *arrays)


def halo_kernel(shards, shards_y, me_ref, first_ref, last_ref, front_ref, back_ref, *out_refs):
    own_y, _, _ = place(me_ref[0], shards)
    even = is_even(me_ref[0], shards)
    cells_x, cells_z, _ = front_ref.shape
    cells_y = first_ref.shape[0] // cells_z

    def fill(out_ref, x, plane_ref):
        for y in range(cells_y):
            out_ref[y + 1] = plane_ref[pl.ds(y * cells_z, cells_z), :]
        row = front_ref[x]
        out_ref[0] = jnp.where(own_y > 0, row, jnp.zeros_like(row))
        row = back_ref[x]
        out_ref[cells_y + 1] = jnp.where(own_y < shards_y - 1, row, jnp.zeros_like(row))

    @pl.when(even)
    def _():
        fill(out_refs[0], cells_x - 1, last_ref)
        fill(out_refs[1], 0, first_ref)

    @pl.when(jnp.logical_not(even))
    def _():
        fill(out_refs[0], 0, first_ref)
        fill(out_refs[1], cells_x - 1, last_ref)


def halo_planes(me, first, last, front, back, shards, shards_y):
    cells_x, cells_z, channels = front.shape
    shape = (first.shape[0] // cells_z + 2, cells_z, channels)
    return pl.pallas_call(
        functools.partial(halo_kernel, shards, shards_y),
        in_specs=[IN_SMEM] + in_vmem(4),
        out_specs=in_vmem(2),
        out_shape=[jax.ShapeDtypeStruct(shape, first.dtype)] * 2,
        compiler_params=pltpu.CompilerParams(vmem_limit_bytes=10 << 20),
    )(me, first, last, front, back)


def preload_kernel(first, weight_ref, out_ref, sems):
    count = out_ref.shape[0]
    pieces = sems.shape[0] // count
    modes = out_ref.shape[1] // pieces
    copies = []
    for i in range(count * pieces):
        item, at = i // pieces, pl.ds(i % pieces * modes, modes)
        copies.append(
            pltpu.make_async_copy(
                weight_ref.at[first + item, at], out_ref.at[item, at], sems.at[i]
            )
        )
    for copy in copies:
        copy.start()
    for copy in copies:
        copy.wait()


def preload(weight, pair, count):
    shape = (2 * count, *weight.shape[1:])
    return pl.pallas_call(
        functools.partial(preload_kernel, 2 * pair),
        in_specs=[pl.BlockSpec(memory_space=pltpu.HBM)],
        out_specs=in_vmem(1)[0],
        out_shape=jax.ShapeDtypeStruct(shape, weight.dtype),
        scratch_shapes=[pltpu.SemaphoreType.DMA((2 * 2 * count,))],
        compiler_params=pltpu.CompilerParams(vmem_limit_bytes=34 << 20),
        cost_estimate=pl.CostEstimate(
            flops=0, bytes_accessed=2 * math.prod(shape), transcendentals=0
        ),
    )(weight)


def mixing_kernel(shards, loaded, me_ref, *refs):
    outer, inner = shards
    row_refs, refs = refs[:inner], refs[inner:]
    forward_ref, backward_ref, weight_ref, *refs = refs
    loaded_refs, refs = refs[:loaded], refs[loaded:]
    loaded = sum(ref.shape[0] // 2 for ref in loaded_refs)
    out_refs, (held, sems, wide, left, mixed) = refs[:inner], refs[inner:]

    channels = wide.shape[1]
    _, cells_x, item_rows, _ = row_refs[0].shape
    pairs = item_rows // 2
    full_x = outer * inner * cells_x
    half = channels // 2
    span = 2 * MX
    block = cells_x * item_rows
    _, own_outer, own_inner = place(me_ref[0], shards)

    def copy(pair):
        slot = pair - loaded
        return pltpu.make_async_copy(
            weight_ref.at[pl.ds(2 * pair, 2)], held.at[slot], sems.at[slot]
        )

    for pair in range(loaded, pairs):
        copy(pair).start()

    def rows_of(outer_index, inner_index):
        start = pl.multiple_of((outer_index * inner + inner_index) * block, block)
        return pl.ds(start, block)

    for number, step in enumerate(far_first(inner)):
        source = origin(own_inner, step, inner)
        for slot in range(outer):
            value = row_refs[number][slot].reshape(block, channels)
            at = rows_of(origin(own_outer, slot, outer), source)
            wide[at, :] = value.astype(jnp.float32)
    low = lax.broadcasted_iota(jnp.int32, (span, channels), 1) < half
    for pair in range(pairs):
        columns = [wide[pl.ds(2 * pair + p, full_x, stride=item_rows), :] for p in range(2)]
        columns = jnp.concatenate(columns, axis=0).astype(jnp.bfloat16)
        both = dot(forward_ref[...], columns)
        value, turned = both[:span], both[span:]
        first = jnp.where(low, value, pltpu.roll(turned, half, axis=1))
        second = jnp.where(low, pltpu.roll(value, half, axis=1), turned)
        left[pl.ds(pair * span, span), :channels] = first.astype(left.dtype)
        left[pl.ds(pair * span, span), channels:] = second.astype(left.dtype)

    group = 16
    row = lax.broadcasted_iota(jnp.int32, (group, channels), 0) // 2

    def mix(pair, tile_of):
        for step in range(span // group):
            start = pl.multiple_of(pair * span + step * group, group)
            lhs = left[pl.ds(start, group), :]
            gathered = jnp.zeros((group, channels), jnp.float32)
            for i in range(0, group // 2, 2):
                mode = step * (group // 2) + i
                tiles = [
                    jnp.concatenate([tile_of(h, mode + k) for h in range(2)], axis=0)
                    for k in range(2)
                ]
                product = dot(lhs, jnp.concatenate(tiles, axis=1))
                for k in range(2):
                    gathered = jnp.where(
                        row == i + k, product[:, k * channels : (k + 1) * channels], gathered
                    )
            mixed[pl.ds(start, group), :] = gathered.astype(mixed.dtype)

    pair = 0
    for ref in loaded_refs:
        count = ref.shape[0] // 2

        def ready(i, carry, ref=ref, pair=pair):
            mix(pair + i, lambda h, mode: ref[2 * i + h, mode])
            return carry

        lax.fori_loop(0, count, ready, 0)
        pair += count

    def streamed(pair, carry):
        copy(pair).wait()
        mix(pair, lambda h, mode: held[pair - loaded, h, mode])
        return carry

    lax.fori_loop(loaded, pairs, streamed, 0)

    for pair in range(pairs):
        result = dot(backward_ref[...], mixed[pl.ds(pair * span, span), :])
        for p in range(2):
            wide[pl.ds(2 * pair + p, full_x, stride=item_rows), :] = result[
                p * full_x : (p + 1) * full_x
            ]
    for step in range(inner):
        target = peer(own_inner, step, inner)
        for slot in range(outer):
            value = wide[rows_of(peer(own_outer, slot, outer), target), :]
            value = value.reshape(cells_x, item_rows, channels)
            out_refs[step][slot] = value.astype(out_refs[step].dtype)


def mixing(me, rows, forward_x, backward_x, weight, loaded, shards):
    outer, inner = shards
    _, cells_x, item_rows, channels = rows[0].shape
    pairs = item_rows // 2
    row_count = outer * inner * cells_x * item_rows
    streamed = pairs - sum(part.shape[0] // 2 for part in loaded)
    return pl.pallas_call(
        functools.partial(mixing_kernel, shards, len(loaded)),
        in_specs=[IN_SMEM]
        + in_vmem(inner + 2)
        + [pl.BlockSpec(memory_space=pltpu.HBM)]
        + in_vmem(len(loaded)),
        out_specs=in_vmem(inner),
        out_shape=[jax.ShapeDtypeStruct(rows[0].shape, jnp.bfloat16)] * inner,
        scratch_shapes=[
            pltpu.VMEM((streamed, 2, *weight.shape[1:]), weight.dtype),
            pltpu.SemaphoreType.DMA((streamed,)),
            pltpu.VMEM((row_count, channels), jnp.float32),
            pltpu.VMEM((pairs * 2 * MX, 2 * channels), jnp.bfloat16),
            pltpu.VMEM((pairs * 2 * MX, channels), jnp.bfloat16),
        ],
        compiler_params=pltpu.CompilerParams(vmem_limit_bytes=20 << 20),
        cost_estimate=pl.CostEstimate(
            flops=8 * weight.size, bytes_accessed=2 * weight.size, transcendentals=0
        ),
    )(me, *rows, forward_x, backward_x, weight, *loaded)


def convolution_kernel(x, cells_x, width, shards, shards_y, me_ref, *refs):
    flow_ref, paired_ref, other_ref, front_ref, back_ref, kernel_ref, out_ref, padded = refs
    _, cells_y, cells_z, channels = out_ref.shape
    own_y, _, _ = place(me_ref[0], shards)
    even = is_even(me_ref[0], shards)
    for plane in range(width + 2):
        p = x + plane - 1
        if 0 <= p < cells_x:
            padded[plane, 1 : cells_y + 1] = flow_ref[p]
            row = front_ref[p]
            padded[plane, 0] = jnp.where(own_y > 0, row, jnp.zeros_like(row))
            row = back_ref[p]
            last = own_y == shards_y - 1
            padded[plane, cells_y + 1] = jnp.where(last, jnp.zeros_like(row), row)
        else:
            use_paired = jnp.logical_not(even) if p < 0 else even

            @pl.when(use_paired)
            def _(plane=plane):
                padded[plane] = paired_ref[...]

            @pl.when(jnp.logical_not(use_paired))
            def _(plane=plane):
                padded[plane] = other_ref[...]

    rows = 8 if cells_y % 8 == 0 else 1
    columns = [(k, d) for k in range(width) for d in range(3)]
    columns = [columns[i : i + 2] for i in range(0, len(columns), 2)]
    none = jnp.zeros((channels, channels), kernel_ref.dtype)

    def chunk(index, carry):
        y = index * rows
        products = {}
        for group in columns:
            blocks, kernels = [], []
            for p in range(width + 2):
                if not any(0 <= p - k < 3 for k, _ in group):
                    continue
                for b in range(3):
                    part = padded[p, pl.ds(y + b, rows)]
                    blocks.append(part.reshape(rows * cells_z, channels))
                    parts = [
                        kernel_ref[p - k, b, d] if 0 <= p - k < 3 else none for k, d in group
                    ]
                    kernels.append(jnp.concatenate(parts, axis=1))
            product = dot(jnp.concatenate(blocks, axis=1), jnp.concatenate(kernels, axis=0))
            for i, column in enumerate(group):
                part = product[:, i * channels : (i + 1) * channels]
                products[column] = part.reshape(rows, cells_z, channels)
        z = lax.broadcasted_iota(jnp.int32, (rows, cells_z, channels), 1)
        for k in range(width):
            before = jnp.where(z == 0, 0.0, pltpu.roll(products[k, 0], 1, axis=1))
            after = pltpu.roll(products[k, 2], cells_z - 1, axis=1)
            after = jnp.where(z == cells_z - 1, 0.0, after)
            total = before + products[k, 1] + after
            out_ref[k, pl.ds(y, rows)] = total.astype(out_ref.dtype)
        return carry

    lax.fori_loop(0, cells_y // rows, chunk, 0)


def convolution(me, x, width, flow, halos, kernel, shards, shards_y):
    cells_x, cells_y, cells_z, channels = flow.shape
    shape = (width, cells_y, cells_z, channels)
    return pl.pallas_call(
        functools.partial(convolution_kernel, x, cells_x, width, shards, shards_y),
        in_specs=[IN_SMEM] + in_vmem(2 + len(halos)),
        out_specs=in_vmem(1)[0],
        out_shape=jax.ShapeDtypeStruct(shape, jnp.bfloat16),
        scratch_shapes=[pltpu.VMEM((width + 2, cells_y + 2, cells_z, channels), flow.dtype)],
        compiler_params=pltpu.CompilerParams(vmem_limit_bytes=14 << 20),
        cost_estimate=pl.CostEstimate(
            flops=3 * 27 * width * cells_y * cells_z * channels * channels,
            bytes_accessed=10 * cells_y * cells_z * channels,
            transcendentals=0,
        ),
    )(me, flow, *halos, kernel)


def bundled_slots(count):
    parts = ([0], [count - 1], far_first(count)[1:-1]) if count > 1 else ([0],)
    return [part for part in parts if part]


def bundle_kernel(*refs):
    *in_refs, out_ref = refs
    for i, ref in enumerate(in_refs):
        out_ref[i] = ref[...]


def bundle(arrays):
    shape = (len(arrays), *arrays[0].shape)
    return pl.pallas_call(
        bundle_kernel,
        in_specs=in_vmem(len(arrays)),
        out_specs=in_vmem(1)[0],
        out_shape=jax.ShapeDtypeStruct(shape, arrays[0].dtype),
        cost_estimate=pl.CostEstimate(
            flops=math.prod(shape), bytes_accessed=0, transcendentals=0
        ),
        compiler_params=pltpu.CompilerParams(vmem_limit_bytes=10 << 20),
    )(*arrays)


def gather_pieces(me, shards, pieces, held):
    outer, inner = shards
    _, own_outer, own_inner = place(me, shards)
    for number, slot, ref in pieces:
        cells_x, rows = ref.shape[1:3]
        source = (number * outer + origin(own_outer, slot, outer)) * inner
        for part in range(inner):
            at = (source + origin(own_inner, part, inner)) * rows
            for x in range(cells_x):
                held[x, pl.ds(pl.multiple_of(at, rows), rows), :] = ref[part, x]


def inverse(me, shards, shards_y, steps, table_ref, held, part, x, width, positions):
    own_y, _, _ = place(me, shards)
    columns = [held[x + i] for i in range(width)]
    depth = table_ref.shape[2]
    total = None
    for number, step in enumerate(steps):
        source = lax.rem(own_y + (shards_y - step), shards_y)
        rows = pl.ds(pl.multiple_of(part * positions, positions), positions)
        table = table_ref[own_y * shards_y + source, rows, :]
        block = [column[number * depth : (number + 1) * depth] for column in columns]
        product = dot(table, jnp.concatenate(block, axis=1))
        total = product if total is None else total + product
    return total


def own_part_kernel(shards, shards_y, me_ref, table_ref, *refs):
    *piece_refs, bias_ref, out_ref, held = refs
    cells_x, cells_y, cells_z, channels = out_ref.shape
    width = 2 if cells_x % 2 == 0 else 1
    count = -(-cells_x // width)
    piece_refs, convolved_refs = piece_refs[:-count], piece_refs[-count:]
    slots = far_first(shards[0])
    gather_pieces(me_ref[0], shards, [(0, *p) for p in zip(slots, piece_refs)], held)
    bias = bias_ref[...]
    rows = 4 if cells_y % 4 == 0 else 1
    positions = rows * cells_z

    def chunk(part, carry):
        for x in range(0, cells_x, width):
            total = inverse(
                me_ref[0], shards, shards_y, [0], table_ref, held, part, x, width, positions
            )
            for i in range(width):
                spectral = total[:, i * channels : (i + 1) * channels]
                convolved = convolved_refs[x // width][i, pl.ds(part * rows, rows)]
                value = spectral.reshape(rows, cells_z, channels) + convolved + bias
                out_ref[x + i, pl.ds(part * rows, rows)] = value
        return carry

    lax.fori_loop(0, cells_y // rows, chunk, 0)


def last_part_kernel(shards, shards_y, me_ref, table_ref, *refs):
    *bundle_refs, partial_ref, out_ref, held = refs
    cells_x, cells_y, cells_z, channels = out_ref.shape
    bundles = bundled_slots(shards[0])
    steps = list(range(1, shards_y))
    width = 2 if cells_x % 2 == 0 else 1
    part = pl.program_id(0)

    @pl.when(part == 0)
    def _():
        pieces = []
        for i, ref in enumerate(bundle_refs):
            number, bundle = divmod(i, len(bundles))
            pieces += [(number, slot, ref.at[j]) for j, slot in enumerate(bundles[bundle])]
        gather_pieces(me_ref[0], shards, pieces, held)

    for x in range(0, cells_x, width):
        total = inverse(
            me_ref[0], shards, shards_y, steps, table_ref, held, part, x, width,
            cells_y * cells_z,
        )
        for i in range(width):
            spectral = total[:, i * channels : (i + 1) * channels]
            value = partial_ref[x + i, pl.ds(part * cells_y, cells_y)]
            value = value + spectral.reshape(cells_y, cells_z, channels)
            out_ref[x + i] = jax.nn.gelu(value, approximate=True).astype(out_ref.dtype)


def own_part(me, table, pieces, convolved, bias, shards, shards_y):
    width, cells_y, cells_z, channels = convolved[0].shape
    shape = (width * len(convolved), cells_y, cells_z, channels)
    depth = table.shape[2]
    return pl.pallas_call(
        functools.partial(own_part_kernel, shards, shards_y),
        in_specs=[IN_SMEM] + in_vmem(2 + len(pieces) + len(convolved)),
        out_specs=in_vmem(1)[0],
        out_shape=jax.ShapeDtypeStruct(shape, jnp.float32),
        scratch_shapes=[pltpu.VMEM((shape[0], depth, channels), jnp.bfloat16)],
        compiler_params=pltpu.CompilerParams(vmem_limit_bytes=14 << 20),
        cost_estimate=pl.CostEstimate(
            flops=2 * math.prod(shape) * depth,
            bytes_accessed=6 * math.prod(shape),
            transcendentals=0,
        ),
    )(me, table, *pieces, *convolved, bias)


def last_part(me, table, pieces, partial, shards, shards_y):
    cells_x, cells_y, cells_z, channels = partial.shape
    parts = 4 if cells_y % 4 == 0 else 1
    block = (cells_x, cells_y // parts, cells_z, channels)
    depth = table.shape[2] * (shards_y - 1)
    return pl.pallas_call(
        functools.partial(last_part_kernel, shards, shards_y),
        grid_spec=pltpu.PrefetchScalarGridSpec(
            num_scalar_prefetch=1,
            grid=(parts,),
            in_specs=in_vmem(2 + len(pieces)),
            out_specs=pl.BlockSpec(block, lambda i, me: (0, i, 0, 0)),
            scratch_shapes=[pltpu.VMEM((cells_x, depth, channels), jnp.bfloat16)],
        ),
        out_shape=jax.ShapeDtypeStruct(partial.shape, jnp.bfloat16),
        compiler_params=pltpu.CompilerParams(vmem_limit_bytes=14 << 20),
        cost_estimate=pl.CostEstimate(
            flops=2 * partial.size * depth,
            bytes_accessed=6 * partial.size,
            transcendentals=partial.size,
        ),
    )(me, table, *pieces, partial)


def with_halo(array, sides, width):
    for axis, dim in sides:
        size, length = (lax.axis_size(axis), array.shape[dim])
        up = [(i, (i + 1) % size) for i in range(size - 1)]
        down = [(j, i) for i, j in up]
        last = lax.slice_in_dim(array, length - width, length, axis=dim)
        initial = lax.slice_in_dim(array, 0, width, axis=dim)
        before = lax.ppermute(last, axis, up)
        after = lax.ppermute(initial, axis, down)
        array = jnp.concatenate([before, array, after], axis=dim)
    return array


def signed_modes(mode_count):
    position = jnp.arange(mode_count, dtype=jnp.int32)
    return jnp.where(position < mode_count // 2, position, position - mode_count)


def angle_grid(first, second, length):
    phase_turns = first[:, None] * second[None, :] % length
    return phase_turns.astype(jnp.float32) * (2.0 * math.pi / length)


def real_table(first, second, length, factor):
    angles = angle_grid(first, second, length)
    return jnp.stack([jnp.cos(angles) * factor, -jnp.sin(angles) * factor])


def complex_table(first, second, length, factor, direction):
    angles = angle_grid(first, second, length)
    cosine = jnp.cos(angles) * factor
    sine_part = jnp.sin(angles) * factor
    return jnp.stack(
        [jnp.stack([cosine, direction * sine_part]), jnp.stack([-direction * sine_part, cosine])]
    )


def split_pair_spectral(flow_field, spectral_weight):
    highest = lax.Precision.HIGHEST
    cells_x, cells_y, cells_z, channels = flow_field.shape
    count_x = lax.axis_size("gx")
    count_y = lax.axis_size("gy")
    full_x = cells_x * count_x
    full_y = cells_y * count_y
    item_count = spectral_weight.shape[0]
    local_y = lax.axis_index("gy") * cells_y + jnp.arange(cells_y, dtype=jnp.int32)
    grid_x = jnp.arange(full_x, dtype=jnp.int32)
    grid_z = jnp.arange(cells_z, dtype=jnp.int32)
    modes_z = jnp.arange(MZ, dtype=jnp.int32)
    forward_z = real_table(grid_z, modes_z, cells_z, cells_z ** (-0.5)).astype(jnp.bfloat16)
    z_spectrum = jnp.einsum(
        "xyzc,pzk->pxykc", flow_field, forward_z, preferred_element_type=jnp.float32
    )
    columns = lax.all_to_all(
        z_spectrum.astype(jnp.bfloat16), "gy", split_axis=4, concat_axis=2, tiled=True
    ).astype(z_spectrum.dtype)
    whole_y = jnp.arange(full_y, dtype=jnp.int32)
    forward_full = complex_table(whole_y, signed_modes(MY), full_y, full_y ** (-0.5), -1.0)
    y_spectrum = jnp.einsum("pxykc,pqyj->qxjkc", columns, forward_full, precision=highest)
    owned = lax.all_to_all(
        y_spectrum.astype(jnp.bfloat16), "gy", split_axis=2, concat_axis=4, tiled=True
    ).astype(y_spectrum.dtype)
    owned_modes = owned.reshape(2, cells_x, count_x, item_count, channels // 2)
    gathered_rows = lax.all_to_all(
        owned_modes.astype(jnp.bfloat16), "gx", split_axis=2, concat_axis=1, tiled=True
    ).astype(owned_modes.dtype)
    gathered_rows = gathered_rows.reshape(2, full_x, item_count, channels // 2)
    forward_x = complex_table(grid_x, signed_modes(MX), full_x, full_x ** (-0.5), -1.0)
    x_spectrum = jnp.einsum("pxjc,pqxm->qmjc", gathered_rows, forward_x, precision=highest).astype(
        jnp.bfloat16
    )
    products = jnp.einsum(
        "pmjc,jmqco->pqmjo", x_spectrum, spectral_weight, preferred_element_type=jnp.float32
    )
    mixed_modes = jnp.stack([products[0, 0] - products[1, 1], products[0, 1] + products[1, 0]])
    backward_x = complex_table(signed_modes(MX), grid_x, full_x, MX ** (-0.5), 1.0)
    inverse_x = jnp.einsum("pmjc,pqmx->qxjc", mixed_modes, backward_x, precision=highest)
    inverse_x = inverse_x.reshape(2, full_x, 1, item_count, channels)
    returned = lax.all_to_all(
        inverse_x.astype(jnp.bfloat16), "gx", split_axis=1, concat_axis=2, tiled=True
    ).astype(inverse_x.dtype)
    band_rows = MY // count_y
    summed = returned.reshape(2, cells_x, band_rows * MZ, 2, channels).sum(axis=3)
    summed = summed.reshape(2, cells_x, band_rows, MZ, channels)
    coefficients = lax.all_gather(summed.astype(jnp.bfloat16), "gy", axis=2, tiled=True).astype(
        summed.dtype
    )
    backward_y = complex_table(signed_modes(MY), local_y, full_y, MY ** (-0.5), 1.0)
    y_inverse = jnp.einsum("pxjkc,pqjy->qxykc", coefficients, backward_y, precision=highest).astype(
        jnp.bfloat16
    )
    backward_z = real_table(modes_z, grid_z, cells_z, MZ ** (-0.5)).astype(jnp.bfloat16)
    return jnp.einsum("pxykc,pkz->xyzc", y_inverse, backward_z, preferred_element_type=jnp.float32)


def split_pair_convolve(flow_field, conv_weight):
    cells_x, cells_y, cells_z, channels = flow_field.shape
    padded = with_halo(flow_field, (("gx", 0), ("gy", 1)), 1)
    padded = jnp.pad(padded, ((0, 0), (0, 0), (1, 1), (0, 0)))
    stacked = jnp.concatenate(
        [padded[:, :, 0:cells_z], padded[:, :, 1 : cells_z + 1], padded[:, :, 2 : cells_z + 2]],
        axis=3,
    )
    kernel = conv_weight.reshape(3, 3, 3 * channels, channels)
    accumulated = jnp.zeros((cells_x, cells_y, cells_z, channels), jnp.float32)
    for shift_x in range(3):
        for shift_y in range(3):
            accumulated = accumulated + jnp.dot(
                stacked[shift_x : shift_x + cells_x, shift_y : shift_y + cells_y],
                kernel[shift_x, shift_y],
                preferred_element_type=jnp.float32,
            )
    return accumulated


def neighbours(first, last, axis):
    size = lax.axis_size(axis)
    up = [(i, i + 1) for i in range(size - 1)]
    down = [(i + 1, i) for i in range(size - 1)]
    return lax.ppermute(last, axis, up), lax.ppermute(first, axis, down)


def with_neighbour(array, start, axis):
    size = lax.axis_size(axis)
    pairs = [(i, i + 1) for i in range(start, size - 1, 2)]
    return lax.ppermute(array, axis, pairs + [(j, i) for i, j in pairs])


def exchange(array, step, shards, along_outer):
    outer, inner = shards
    pairs = []
    for i in range(outer * inner):
        a, b = divmod(i, inner)
        count, own = (outer, a) if along_outer else (inner, b)
        to = own ^ step if count & (count - 1) == 0 else (own + step) % count
        pairs.append((i, to * inner + b if along_outer else a * inner + to))
    return lax.ppermute(array, "gx", pairs)


def over_y(array, step, shards_y):
    return lax.ppermute(array, "gy", [(i, (i + step) % shards_y) for i in range(shards_y)])


def body(flow, spectral_weight, conv_weight, bias):
    cells_x, cells_y, cells_z, channels = flow.shape
    shards_x, shards_y = lax.axis_size("gx"), lax.axis_size("gy")
    items = spectral_weight.shape[0]
    pairs = items // 2
    if items % 2 or shards_y < 2:
        spectral = split_pair_spectral(flow, spectral_weight)
        convolved = split_pair_convolve(flow, conv_weight)
        return jax.nn.gelu(spectral + convolved + bias, approximate=True).astype(jnp.bfloat16)

    barrier = lax.optimization_barrier
    inner = max(d for d in range(1, shards_x + 1) if shards_x % d == 0 and d * d <= shards_x)
    outer = shards_x // inner
    shards = (outer, inner)
    me = lax.axis_index(("gy", "gx")).astype(jnp.int32).reshape(1)
    sizes = (shards_x, shards_y, pairs, cells_y, cells_z)
    full_x = cells_x * shards_x
    weight = spectral_weight.reshape(items, MX, channels, channels)
    early = pairs // 4

    table = jnp.asarray(forward_yz_table(*sizes))
    columns = flow.reshape(cells_x, cells_y * cells_z, channels)
    order = far_first(outer)
    cut = (outer + 1) // 2
    pieces = [piece for piece in (order[:cut], order[cut:]) if piece]
    arrived = [[] for _ in pieces]
    for step in range(1, shards_y):
        sent = forward_yz(me, table, columns, step, shards, shards_y, pieces)
        sent, columns, weight = barrier((sent, columns, weight))
        for into, piece in zip(arrived, sent):
            into.append(over_y(piece, step, shards_y))
    loaded = [preload(weight, 0, early)] if early else []
    loaded, columns = barrier((loaded, columns))
    kept = forward_yz(me, table, columns, 0, shards, shards_y, pieces, cells_z)
    kept, (first, last, *ends) = kept[: len(pieces)], kept[len(pieces) :]
    if shards_y == 2:
        front = back = over_y(ends[0], 1, shards_y)
    else:
        front, back = neighbours(*ends, "gy")

    by_outer = []
    for piece, own, parts in zip(pieces, kept, arrived):
        for step, total in zip(piece, add_pieces(own, parts)):
            by_outer.append(exchange(total, step, shards, True) if step else total)
    if early:
        loaded.append(preload(weight, early, early))
    by_outer, loaded, weight = barrier((by_outer[::-1], loaded, weight))
    by_inner = regroup(me, by_outer[::-1], shards, True)
    by_inner, weight = barrier((by_inner, weight))
    rows = [
        exchange(by_inner[step], step, shards, False) if step else by_inner[0]
        for step in far_first(inner)
    ]
    if early:
        loaded.append(preload(weight, 2 * early, max(early // 2, 1)))

    rows, loaded, first, last, front, back = barrier((rows, loaded, first, last, front, back))
    paired, other = halo_planes(me, first, last, front, back, shards, shards_y)
    paired, other = with_neighbour(paired, 0, "gx"), with_neighbour(other, 1, "gx")
    returned = mixing(
        me,
        rows,
        jnp.asarray(forward_x_table(full_x)),
        jnp.asarray(backward_x_table(full_x)),
        weight,
        loaded,
        shards,
    )
    returned, other, paired = barrier((list(returned), other, paired))
    halos = (paired, other, front, back)
    width = 2 if cells_x % 2 == 0 else 1
    convolved = [
        convolution(me, x, width, flow, halos, conv_weight, shards, shards_y)
        for x in range(0, cells_x, width)
    ]

    returned = [
        exchange(returned[step], step, shards, False) if step else returned[0]
        for step in far_first(inner)
    ]
    returned, convolved[0] = barrier((returned, convolved[0]))
    returned = regroup(me, returned, shards, False)
    returned = [
        exchange(returned[step], step, shards, True) if step else returned[0]
        for step in far_first(outer)
    ]
    by_slot = dict(zip(far_first(outer), returned))
    bundles = [
        bundle([by_slot[slot] for slot in slots]) if slots[1:] else by_slot[slots[0]][None]
        for slots in bundled_slots(outer)
    ]
    others = []
    for step in range(1, shards_y):
        others += [over_y(part, step, shards_y) for part in bundles]
    table = jnp.asarray(backward_yz_table(*sizes))
    bias = bias.reshape(1, channels)
    partial = own_part(me, table, returned, convolved, bias, shards, shards_y)
    return last_part(me, table, others, partial, shards, shards_y)


def solution(mesh):
    placed = (P("gx", "gy", None, None), P(("gy", "gx"), None, None, None, None), P(), P())
    return jax.shard_map(
        body, mesh=mesh, in_specs=placed, out_specs=P("gx", "gy", None, None), check_vma=False
    )
```

```python
import functools
import math

import jax
import jax.numpy as jnp
import numpy as np
from jax import lax
from jax.experimental import pallas as pl
from jax.experimental.pallas import tpu as pltpu
from jax.sharding import PartitionSpec as P

MX = 64
MY = 16
MZ = 16


def frequencies(mode_count):
    position = np.arange(mode_count)
    return np.where(position < mode_count // 2, position, position - mode_count)


def wave(first, second, length, factor):
    turns = (np.asarray(first)[:, None] * np.asarray(second)[None, :]) % length
    angles = turns * (2.0 * math.pi / length)
    return (np.cos(angles) + 1j * np.sin(angles)) * factor


def rounded(values):
    return values.astype(np.float32).astype(jnp.bfloat16).astype(np.float64)


def item_modes(shards_x, shards_y, pairs):
    index = np.arange(shards_y * shards_x * pairs).reshape(shards_y, shards_x, pairs)
    return index // MZ, index % MZ


def forward_yz_table(shards_x, shards_y, pairs, cells_y, cells_z):
    full_y = shards_y * cells_y
    turn_z = wave(np.arange(MZ), np.arange(cells_z), cells_z, cells_z**-0.5)
    turn_z = rounded(turn_z.real) - 1j * rounded(turn_z.imag)
    turn_y = np.conj(wave(frequencies(MY), np.arange(full_y), full_y, full_y**-0.5))
    mode_y, mode_z = item_modes(shards_x, shards_y, pairs)
    table = np.empty((shards_y, shards_y, shards_x, pairs, 2, cells_y, cells_z), np.float32)
    for own in range(shards_y):
        rows = turn_y[:, own * cells_y : (own + 1) * cells_y]
        product = rows[mode_y][..., :, None] * turn_z[mode_z][..., None, :]
        table[own, :, :, :, 0] = product.real
        table[own, :, :, :, 1] = product.imag
    return table.reshape(shards_y, -1, cells_y * cells_z).astype(jnp.bfloat16)


def backward_yz_table(shards_x, shards_y, pairs, cells_y, cells_z):
    full_y = shards_y * cells_y
    turn_z = wave(np.arange(MZ), np.arange(cells_z), cells_z, MZ**-0.5)
    turn_z = rounded(turn_z.real) + 1j * rounded(turn_z.imag)
    turn_y = wave(frequencies(MY), np.arange(full_y), full_y, MY**-0.5)
    mode_y, mode_z = item_modes(shards_x, shards_y, pairs)
    table = np.empty((shards_y, shards_y, cells_y, cells_z, shards_x, pairs, 2), np.float32)
    for own in range(shards_y):
        rows = turn_y[:, own * cells_y : (own + 1) * cells_y]
        product = rows[mode_y][..., :, None] * turn_z[mode_z][..., None, :]
        product = np.moveaxis(product, (3, 4), (1, 2))
        table[own, ..., 0] = product.real
        table[own, ..., 1] = -product.imag
    return table.reshape(shards_y**2, cells_y * cells_z, -1).astype(jnp.bfloat16)


def forward_x_table(full_x):
    turn = np.conj(wave(frequencies(MX), np.arange(full_x), full_x, full_x**-0.5))
    parts = np.empty((2, MX, 2, 2, full_x), np.float32)
    parts[0, :, 0, 0], parts[0, :, 0, 1] = turn.real, -turn.imag
    parts[0, :, 1, 0], parts[0, :, 1, 1] = turn.imag, turn.real
    parts[1, :, 0] = -parts[0, :, 1]
    parts[1, :, 1] = parts[0, :, 0]
    return parts.reshape(2 * MX * 2, 2 * full_x).astype(jnp.bfloat16)


def backward_x_table(full_x):
    turn = wave(frequencies(MX), np.arange(full_x), full_x, MX**-0.5).T
    parts = np.empty((2, full_x, MX, 2), np.float32)
    parts[0, :, :, 0], parts[0, :, :, 1] = turn.real, -turn.imag
    parts[1, :, :, 0], parts[1, :, :, 1] = turn.imag, turn.real
    return parts.reshape(2 * full_x, MX * 2).astype(jnp.bfloat16)


def dot(left, right):
    return jnp.dot(left, right, preferred_element_type=jnp.float32)


def peer(index, step, count):
    if count & (count - 1) == 0:
        return index ^ step
    return lax.rem(index + step, count)


def origin(index, step, count):
    if count & (count - 1) == 0:
        return index ^ step
    return lax.rem(index + (count - step), count)


def far_first(count):
    return list(range(count - 1, -1, -1))


def place(me, shards):
    outer, inner = shards
    across = lax.rem(me, outer * inner)
    return lax.div(me, outer * inner), lax.div(across, inner), lax.rem(across, inner)


def in_vmem(count):
    return [pl.BlockSpec(memory_space=pltpu.VMEM)] * count


IN_SMEM = pl.BlockSpec(memory_space=pltpu.SMEM)


def transform(table, flow_at, cells_x, refs, pieces):
    inner, _, rows, channels = refs[0].shape[1:]
    block = inner * rows
    width = 2 if cells_x % 2 == 0 else 1
    for x in range(0, cells_x, width):
        columns = [flow_at(x + i) for i in range(width)]
        result = dot(table, jnp.concatenate(columns, axis=1))
        for i in range(width):
            part = result[:, i * channels : (i + 1) * channels]
            at = 0
            for ref, piece in zip(refs, pieces):
                for slot in range(len(piece)):
                    value = part[at : at + block].reshape(inner, rows, channels)
                    ref[slot, :, x + i] = value.astype(ref.dtype)
                    at += block


def send_kernel(shards, shards_y, pieces, step, me_ref, table_ref, flow_ref, *refs):
    *refs, table, flow, table_sems, flow_sems = refs
    cells_x = flow.shape[0]
    outer, _ = shards
    block = refs[0].shape[1] * refs[0].shape[3]
    own_y, own, _ = place(me_ref[0], shards)
    owner = lax.rem(own_y + step, shards_y)
    copies = []
    for i, other in enumerate(step for piece in pieces for step in piece):
        start = (owner * outer + peer(own, other, outer)) * block
        source = table_ref.at[own_y, pl.ds(pl.multiple_of(start, block), block)]
        copies.append(
            pltpu.make_async_copy(source, table.at[pl.ds(i * block, block)], table_sems.at[i])
        )
    loads = [
        pltpu.make_async_copy(flow_ref.at[x], flow.at[x], flow_sems.at[x])
        for x in range(cells_x)
    ]
    for copy in copies + loads:
        copy.start()
    for copy in copies:
        copy.wait()

    def flow_at(x):
        loads[x].wait()
        return flow[x]

    transform(table[...], flow_at, cells_x, refs, pieces)


def is_even(me, shards):
    _, own_outer, own_inner = place(me, shards)
    return lax.rem(own_outer * shards[1] + own_inner, 2) == 0


def keep_kernel(shards, shards_y, pieces, me_ref, table_ref, flow_ref, *refs):
    refs, (first, last, *edges) = refs[: len(pieces)], refs[len(pieces) :]
    cells_x, positions, _ = flow_ref.shape
    outer, _ = shards
    block = refs[0].shape[1] * refs[0].shape[3]
    own_y, own, _ = place(me_ref[0], shards)
    tables = []
    for other in (step for piece in pieces for step in piece):
        start = (own_y * outer + peer(own, other, outer)) * block
        tables.append(table_ref[own_y, pl.ds(pl.multiple_of(start, block), block), :])
    transform(
        jnp.concatenate(tables, axis=0), lambda x: flow_ref[x], cells_x, refs, pieces
    )
    first[...] = flow_ref[0]
    last[...] = flow_ref[cells_x - 1]
    cells_z = edges[0].shape[1]
    low, high = pl.ds(0, cells_z), pl.ds(positions - cells_z, cells_z)
    if len(edges) > 1:
        edges[0][...] = flow_ref[:, low]
        edges[1][...] = flow_ref[:, high]
    else:

        @pl.when(own_y > 0)
        def _():
            edges[0][...] = flow_ref[:, low]

        @pl.when(own_y == 0)
        def _():
            edges[0][...] = flow_ref[:, high]


def forward_yz(me, table, flow, step, shards, shards_y, pieces, cells_z=0):
    cells_x, positions, channels = flow.shape
    outer, inner = shards
    rows = table.shape[1] // shards_y
    unit = (inner, cells_x, rows // (outer * inner), channels)
    dtype = jnp.bfloat16 if step else jnp.float32
    shapes = [jax.ShapeDtypeStruct((len(piece), *unit), dtype) for piece in pieces]
    if step:
        kernel = functools.partial(send_kernel, shards, shards_y, pieces, step)
        specs = [pl.BlockSpec(memory_space=pltpu.HBM)] * 2
        scratch = [
            pltpu.VMEM((rows, positions), table.dtype),
            pltpu.VMEM(flow.shape, flow.dtype),
            pltpu.SemaphoreType.DMA((outer,)),
            pltpu.SemaphoreType.DMA((cells_x,)),
        ]
    else:
        kernel = functools.partial(keep_kernel, shards, shards_y, pieces)
        specs, scratch = in_vmem(2), []
        shapes += [jax.ShapeDtypeStruct((positions, channels), flow.dtype)] * 2
        edge = jax.ShapeDtypeStruct((cells_x, cells_z, channels), flow.dtype)
        shapes += [edge] * (1 if shards_y == 2 else 2)
    return pl.pallas_call(
        kernel,
        in_specs=[IN_SMEM] + specs,
        out_specs=in_vmem(len(shapes)),
        out_shape=shapes,
        scratch_shapes=scratch,
        compiler_params=pltpu.CompilerParams(vmem_limit_bytes=(56 if step else 10) << 20),
        cost_estimate=pl.CostEstimate(
            flops=2 * rows * positions * cells_x * channels,
            bytes_accessed=2 * positions * (rows + cells_x * channels),
            transcendentals=0,
        ),
    )(me, table, flow)


def add_kernel(count, *refs):
    out_refs = refs[count:]
    for slot, out_ref in enumerate(out_refs):
        total = refs[0][slot]
        for ref in refs[1:count]:
            total = total + ref[slot].astype(jnp.float32)
        out_ref[...] = total.astype(out_ref.dtype)


def add_pieces(own, arrived):
    slots, *unit = own.shape
    return pl.pallas_call(
        functools.partial(add_kernel, 1 + len(arrived)),
        in_specs=in_vmem(1 + len(arrived)),
        out_specs=in_vmem(slots),
        out_shape=[jax.ShapeDtypeStruct(unit, jnp.bfloat16)] * slots,
        cost_estimate=pl.CostEstimate(flops=own.size, bytes_accessed=0, transcendentals=0),
        compiler_params=pltpu.CompilerParams(vmem_limit_bytes=10 << 20),
    )(own, *arrived)


def regroup_kernel(shards, chosen, me_ref, *refs):
    _, _, own = place(me_ref[0], shards)
    count = refs[0].shape[0]
    in_refs, out_refs = refs[:-count], refs[-count:]
    for step, out_ref in enumerate(out_refs):
        at = peer(own, step, count) if chosen else step
        for number, in_ref in enumerate(in_refs):
            out_ref[far_first(len(in_refs))[number]] = in_ref[at]


def regroup(me, arrays, shards, chosen):
    count, *unit = arrays[0].shape
    return pl.pallas_call(
        functools.partial(regroup_kernel, shards, chosen),
        in_specs=[IN_SMEM] + in_vmem(len(arrays)),
        out_specs=in_vmem(count),
        out_shape=[jax.ShapeDtypeStruct((len(arrays), *unit), arrays[0].dtype)] * count,
        cost_estimate=pl.CostEstimate(
            flops=arrays[0].size, bytes_accessed=0, transcendentals=0
        ),
        compiler_params=pltpu.CompilerParams(vmem_limit_bytes=10 << 20),
    )(me, *arrays)


def halo_kernel(shards, shards_y, me_ref, first_ref, last_ref, front_ref, back_ref, *out_refs):
    own_y, _, _ = place(me_ref[0], shards)
    even = is_even(me_ref[0], shards)
    cells_x, cells_z, _ = front_ref.shape
    cells_y = first_ref.shape[0] // cells_z

    def fill(out_ref, x, plane_ref):
        for y in range(cells_y):
            out_ref[y + 1] = plane_ref[pl.ds(y * cells_z, cells_z), :]
        row = front_ref[x]
        out_ref[0] = jnp.where(own_y > 0, row, jnp.zeros_like(row))
        row = back_ref[x]
        out_ref[cells_y + 1] = jnp.where(own_y < shards_y - 1, row, jnp.zeros_like(row))

    @pl.when(even)
    def _():
        fill(out_refs[0], cells_x - 1, last_ref)
        fill(out_refs[1], 0, first_ref)

    @pl.when(jnp.logical_not(even))
    def _():
        fill(out_refs[0], 0, first_ref)
        fill(out_refs[1], cells_x - 1, last_ref)


def halo_planes(me, first, last, front, back, shards, shards_y):
    cells_x, cells_z, channels = front.shape
    shape = (first.shape[0] // cells_z + 2, cells_z, channels)
    return pl.pallas_call(
        functools.partial(halo_kernel, shards, shards_y),
        in_specs=[IN_SMEM] + in_vmem(4),
        out_specs=in_vmem(2),
        out_shape=[jax.ShapeDtypeStruct(shape, first.dtype)] * 2,
        compiler_params=pltpu.CompilerParams(vmem_limit_bytes=10 << 20),
    )(me, first, last, front, back)


def preload_kernel(first, weight_ref, out_ref, sems):
    count = out_ref.shape[0]
    pieces = sems.shape[0] // count
    modes = out_ref.shape[1] // pieces
    copies = []
    for i in range(count * pieces):
        item, at = i // pieces, pl.ds(i % pieces * modes, modes)
        copies.append(
            pltpu.make_async_copy(
                weight_ref.at[first + item, at], out_ref.at[item, at], sems.at[i]
            )
        )
    for copy in copies:
        copy.start()
    for copy in copies:
        copy.wait()


def preload(weight, pair, count):
    shape = (2 * count, *weight.shape[1:])
    return pl.pallas_call(
        functools.partial(preload_kernel, 2 * pair),
        in_specs=[pl.BlockSpec(memory_space=pltpu.HBM)],
        out_specs=in_vmem(1)[0],
        out_shape=jax.ShapeDtypeStruct(shape, weight.dtype),
        scratch_shapes=[pltpu.SemaphoreType.DMA((2 * 2 * count,))],
        compiler_params=pltpu.CompilerParams(vmem_limit_bytes=34 << 20),
        cost_estimate=pl.CostEstimate(
            flops=0, bytes_accessed=2 * math.prod(shape), transcendentals=0
        ),
    )(weight)


def mixing_kernel(shards, loaded, me_ref, *refs):
    outer, inner = shards
    row_refs, refs = refs[:inner], refs[inner:]
    forward_ref, backward_ref, weight_ref, *refs = refs
    loaded_refs, refs = refs[:loaded], refs[loaded:]
    loaded = sum(ref.shape[0] // 2 for ref in loaded_refs)
    out_refs, (held, sems, wide, left, mixed) = refs[:inner], refs[inner:]

    channels = wide.shape[1]
    _, cells_x, item_rows, _ = row_refs[0].shape
    pairs = item_rows // 2
    full_x = outer * inner * cells_x
    half = channels // 2
    span = 2 * MX
    block = cells_x * item_rows
    _, own_outer, own_inner = place(me_ref[0], shards)

    def copy(pair):
        slot = pair - loaded
        return pltpu.make_async_copy(
            weight_ref.at[pl.ds(2 * pair, 2)], held.at[slot], sems.at[slot]
        )

    for pair in range(loaded, pairs):
        copy(pair).start()

    def rows_of(outer_index, inner_index):
        start = pl.multiple_of((outer_index * inner + inner_index) * block, block)
        return pl.ds(start, block)

    for number, step in enumerate(far_first(inner)):
        source = origin(own_inner, step, inner)
        for slot in range(outer):
            value = row_refs[number][slot].reshape(block, channels)
            at = rows_of(origin(own_outer, slot, outer), source)
            wide[at, :] = value.astype(jnp.float32)
    low = lax.broadcasted_iota(jnp.int32, (span, channels), 1) < half
    for pair in range(pairs):
        columns = [wide[pl.ds(2 * pair + p, full_x, stride=item_rows), :] for p in range(2)]
        columns = jnp.concatenate(columns, axis=0).astype(jnp.bfloat16)
        both = dot(forward_ref[...], columns)
        value, turned = both[:span], both[span:]
        first = jnp.where(low, value, pltpu.roll(turned, half, axis=1))
        second = jnp.where(low, pltpu.roll(value, half, axis=1), turned)
        left[pl.ds(pair * span, span), :channels] = first.astype(left.dtype)
        left[pl.ds(pair * span, span), channels:] = second.astype(left.dtype)

    group = 16
    row = lax.broadcasted_iota(jnp.int32, (group, channels), 0) // 2

    def mix(pair, tile_of):
        for step in range(span // group):
            start = pl.multiple_of(pair * span + step * group, group)
            lhs = left[pl.ds(start, group), :]
            gathered = jnp.zeros((group, channels), jnp.float32)
            for i in range(0, group // 2, 2):
                mode = step * (group // 2) + i
                tiles = [
                    jnp.concatenate([tile_of(h, mode + k) for h in range(2)], axis=0)
                    for k in range(2)
                ]
                product = dot(lhs, jnp.concatenate(tiles, axis=1))
                for k in range(2):
                    gathered = jnp.where(
                        row == i + k, product[:, k * channels : (k + 1) * channels], gathered
                    )
            mixed[pl.ds(start, group), :] = gathered.astype(mixed.dtype)

    pair = 0
    for ref in loaded_refs:
        count = ref.shape[0] // 2

        def ready(i, carry, ref=ref, pair=pair):
            mix(pair + i, lambda h, mode: ref[2 * i + h, mode])
            return carry

        lax.fori_loop(0, count, ready, 0)
        pair += count

    def streamed(pair, carry):
        copy(pair).wait()
        mix(pair, lambda h, mode: held[pair - loaded, h, mode])
        return carry

    lax.fori_loop(loaded, pairs, streamed, 0)

    for pair in range(pairs):
        result = dot(backward_ref[...], mixed[pl.ds(pair * span, span), :])
        for p in range(2):
            wide[pl.ds(2 * pair + p, full_x, stride=item_rows), :] = result[
                p * full_x : (p + 1) * full_x
            ]
    for step in range(inner):
        target = peer(own_inner, step, inner)
        for slot in range(outer):
            value = wide[rows_of(peer(own_outer, slot, outer), target), :]
            value = value.reshape(cells_x, item_rows, channels)
            out_refs[step][slot] = value.astype(out_refs[step].dtype)


def mixing(me, rows, forward_x, backward_x, weight, loaded, shards):
    outer, inner = shards
    _, cells_x, item_rows, channels = rows[0].shape
    pairs = item_rows // 2
    row_count = outer * inner * cells_x * item_rows
    streamed = pairs - sum(part.shape[0] // 2 for part in loaded)
    return pl.pallas_call(
        functools.partial(mixing_kernel, shards, len(loaded)),
        in_specs=[IN_SMEM]
        + in_vmem(inner + 2)
        + [pl.BlockSpec(memory_space=pltpu.HBM)]
        + in_vmem(len(loaded)),
        out_specs=in_vmem(inner),
        out_shape=[jax.ShapeDtypeStruct(rows[0].shape, jnp.bfloat16)] * inner,
        scratch_shapes=[
            pltpu.VMEM((streamed, 2, *weight.shape[1:]), weight.dtype),
            pltpu.SemaphoreType.DMA((streamed,)),
            pltpu.VMEM((row_count, channels), jnp.float32),
            pltpu.VMEM((pairs * 2 * MX, 2 * channels), jnp.bfloat16),
            pltpu.VMEM((pairs * 2 * MX, channels), jnp.bfloat16),
        ],
        compiler_params=pltpu.CompilerParams(vmem_limit_bytes=20 << 20),
        cost_estimate=pl.CostEstimate(
            flops=8 * weight.size, bytes_accessed=2 * weight.size, transcendentals=0
        ),
    )(me, *rows, forward_x, backward_x, weight, *loaded)


def convolution_kernel(x, cells_x, width, shards, shards_y, me_ref, *refs):
    flow_ref, paired_ref, other_ref, front_ref, back_ref, kernel_ref, out_ref, padded = refs
    _, cells_y, cells_z, channels = out_ref.shape
    own_y, own_outer, own_inner = place(me_ref[0], shards)
    own_x = own_outer * shards[1] + own_inner
    even = is_even(me_ref[0], shards)
    for plane in range(width + 2):
        p = x + plane - 1
        if 0 <= p < cells_x:
            padded[plane, 1 : cells_y + 1] = flow_ref[p]
            row = front_ref[p]
            padded[plane, 0] = jnp.where(own_y > 0, row, jnp.zeros_like(row))
            row = back_ref[p]
            last = own_y == shards_y - 1
            padded[plane, cells_y + 1] = jnp.where(last, jnp.zeros_like(row), row)
        else:
            use_paired = jnp.logical_not(even) if p < 0 else even
            outside = own_x == (0 if p < 0 else shards[0] * shards[1] - 1)

            @pl.when(outside)
            def _(plane=plane):
                padded[plane] = jnp.zeros(padded.shape[1:], padded.dtype)

            @pl.when(jnp.logical_and(jnp.logical_not(outside), use_paired))
            def _(plane=plane):
                padded[plane] = paired_ref[...]

            @pl.when(jnp.logical_not(jnp.logical_or(outside, use_paired)))
            def _(plane=plane):
                padded[plane] = other_ref[...]

    rows = 8 if cells_y % 8 == 0 else 1
    columns = [(k, d) for k in range(width) for d in range(3)]
    columns = [columns[i : i + 2] for i in range(0, len(columns), 2)]
    none = jnp.zeros((channels, channels), kernel_ref.dtype)

    def chunk(index, carry):
        y = index * rows
        products = {}
        for group in columns:
            blocks, kernels = [], []
            for p in range(width + 2):
                if not any(0 <= p - k < 3 for k, _ in group):
                    continue
                for b in range(3):
                    part = padded[p, pl.ds(y + b, rows)]
                    blocks.append(part.reshape(rows * cells_z, channels))
                    parts = [
                        kernel_ref[p - k, b, d] if 0 <= p - k < 3 else none for k, d in group
                    ]
                    kernels.append(jnp.concatenate(parts, axis=1))
            product = dot(jnp.concatenate(blocks, axis=1), jnp.concatenate(kernels, axis=0))
            for i, column in enumerate(group):
                part = product[:, i * channels : (i + 1) * channels]
                products[column] = part.reshape(rows, cells_z, channels)
        z = lax.broadcasted_iota(jnp.int32, (rows, cells_z, channels), 1)
        for k in range(width):
            before = jnp.where(z == 0, 0.0, pltpu.roll(products[k, 0], 1, axis=1))
            after = pltpu.roll(products[k, 2], cells_z - 1, axis=1)
            after = jnp.where(z == cells_z - 1, 0.0, after)
            total = before + products[k, 1] + after
            out_ref[k, pl.ds(y, rows)] = total.astype(out_ref.dtype)
        return carry

    lax.fori_loop(0, cells_y // rows, chunk, 0)


def convolution(me, x, width, flow, halos, kernel, shards, shards_y):
    cells_x, cells_y, cells_z, channels = flow.shape
    shape = (width, cells_y, cells_z, channels)
    return pl.pallas_call(
        functools.partial(convolution_kernel, x, cells_x, width, shards, shards_y),
        in_specs=[IN_SMEM] + in_vmem(2 + len(halos)),
        out_specs=in_vmem(1)[0],
        out_shape=jax.ShapeDtypeStruct(shape, jnp.bfloat16),
        scratch_shapes=[pltpu.VMEM((width + 2, cells_y + 2, cells_z, channels), flow.dtype)],
        compiler_params=pltpu.CompilerParams(vmem_limit_bytes=14 << 20),
        cost_estimate=pl.CostEstimate(
            flops=3 * 27 * width * cells_y * cells_z * channels * channels,
            bytes_accessed=10 * cells_y * cells_z * channels,
            transcendentals=0,
        ),
    )(me, flow, *halos, kernel)


def bundled_slots(count):
    parts = ([0], [count - 1], far_first(count)[1:-1]) if count > 1 else ([0],)
    return [part for part in parts if part]


def bundle_kernel(*refs):
    *in_refs, out_ref = refs
    for i, ref in enumerate(in_refs):
        out_ref[i] = ref[...]


def bundle(arrays):
    shape = (len(arrays), *arrays[0].shape)
    return pl.pallas_call(
        bundle_kernel,
        in_specs=in_vmem(len(arrays)),
        out_specs=in_vmem(1)[0],
        out_shape=jax.ShapeDtypeStruct(shape, arrays[0].dtype),
        cost_estimate=pl.CostEstimate(
            flops=math.prod(shape), bytes_accessed=0, transcendentals=0
        ),
        compiler_params=pltpu.CompilerParams(vmem_limit_bytes=10 << 20),
    )(*arrays)


def gather_pieces(me, shards, pieces, held):
    outer, inner = shards
    _, own_outer, own_inner = place(me, shards)
    for number, slot, ref in pieces:
        cells_x, rows = ref.shape[1:3]
        source = (number * outer + origin(own_outer, slot, outer)) * inner
        for part in range(inner):
            at = (source + origin(own_inner, part, inner)) * rows
            for x in range(cells_x):
                held[x, pl.ds(pl.multiple_of(at, rows), rows), :] = ref[part, x]


def inverse(me, shards, shards_y, steps, table_ref, held, part, x, width, positions):
    own_y, _, _ = place(me, shards)
    columns = [held[x + i] for i in range(width)]
    depth = table_ref.shape[2]
    total = None
    for number, step in enumerate(steps):
        source = lax.rem(own_y + (shards_y - step), shards_y)
        rows = pl.ds(pl.multiple_of(part * positions, positions), positions)
        table = table_ref[own_y * shards_y + source, rows, :]
        block = [column[number * depth : (number + 1) * depth] for column in columns]
        product = dot(table, jnp.concatenate(block, axis=1))
        total = product if total is None else total + product
    return total


def own_part_kernel(shards, shards_y, me_ref, table_ref, *refs):
    *piece_refs, bias_ref, out_ref, held = refs
    cells_x, cells_y, cells_z, channels = out_ref.shape
    width = 2 if cells_x % 2 == 0 else 1
    count = -(-cells_x // width)
    piece_refs, convolved_refs = piece_refs[:-count], piece_refs[-count:]
    slots = far_first(shards[0])
    gather_pieces(me_ref[0], shards, [(0, *p) for p in zip(slots, piece_refs)], held)
    bias = bias_ref[...]
    rows = 4 if cells_y % 4 == 0 else 1
    positions = rows * cells_z

    def chunk(part, carry):
        for x in range(0, cells_x, width):
            total = inverse(
                me_ref[0], shards, shards_y, [0], table_ref, held, part, x, width, positions
            )
            for i in range(width):
                spectral = total[:, i * channels : (i + 1) * channels]
                convolved = convolved_refs[x // width][i, pl.ds(part * rows, rows)]
                value = spectral.reshape(rows, cells_z, channels) + convolved + bias
                out_ref[x + i, pl.ds(part * rows, rows)] = value
        return carry

    lax.fori_loop(0, cells_y // rows, chunk, 0)


def last_part_kernel(shards, shards_y, me_ref, table_ref, *refs):
    *bundle_refs, partial_ref, out_ref, held = refs
    cells_x, cells_y, cells_z, channels = out_ref.shape
    bundles = bundled_slots(shards[0])
    steps = list(range(1, shards_y))
    width = 2 if cells_x % 2 == 0 else 1
    part = pl.program_id(0)

    @pl.when(part == 0)
    def _():
        pieces = []
        for i, ref in enumerate(bundle_refs):
            number, bundle = divmod(i, len(bundles))
            pieces += [(number, slot, ref.at[j]) for j, slot in enumerate(bundles[bundle])]
        gather_pieces(me_ref[0], shards, pieces, held)

    for x in range(0, cells_x, width):
        total = inverse(
            me_ref[0], shards, shards_y, steps, table_ref, held, part, x, width,
            cells_y * cells_z,
        )
        for i in range(width):
            spectral = total[:, i * channels : (i + 1) * channels]
            value = partial_ref[x + i, pl.ds(part * cells_y, cells_y)]
            value = value + spectral.reshape(cells_y, cells_z, channels)
            out_ref[x + i] = jax.nn.gelu(value, approximate=True).astype(out_ref.dtype)


def own_part(me, table, pieces, convolved, bias, shards, shards_y):
    width, cells_y, cells_z, channels = convolved[0].shape
    shape = (width * len(convolved), cells_y, cells_z, channels)
    depth = table.shape[2]
    return pl.pallas_call(
        functools.partial(own_part_kernel, shards, shards_y),
        in_specs=[IN_SMEM] + in_vmem(2 + len(pieces) + len(convolved)),
        out_specs=in_vmem(1)[0],
        out_shape=jax.ShapeDtypeStruct(shape, jnp.float32),
        scratch_shapes=[pltpu.VMEM((shape[0], depth, channels), jnp.bfloat16)],
        compiler_params=pltpu.CompilerParams(vmem_limit_bytes=14 << 20),
        cost_estimate=pl.CostEstimate(
            flops=2 * math.prod(shape) * depth,
            bytes_accessed=6 * math.prod(shape),
            transcendentals=0,
        ),
    )(me, table, *pieces, *convolved, bias)


def last_part(me, table, pieces, partial, shards, shards_y):
    cells_x, cells_y, cells_z, channels = partial.shape
    parts = 4 if cells_y % 4 == 0 else 1
    block = (cells_x, cells_y // parts, cells_z, channels)
    depth = table.shape[2] * (shards_y - 1)
    return pl.pallas_call(
        functools.partial(last_part_kernel, shards, shards_y),
        grid_spec=pltpu.PrefetchScalarGridSpec(
            num_scalar_prefetch=1,
            grid=(parts,),
            in_specs=in_vmem(2 + len(pieces)),
            out_specs=pl.BlockSpec(block, lambda i, me: (0, i, 0, 0)),
            scratch_shapes=[pltpu.VMEM((cells_x, depth, channels), jnp.bfloat16)],
        ),
        out_shape=jax.ShapeDtypeStruct(partial.shape, jnp.bfloat16),
        compiler_params=pltpu.CompilerParams(vmem_limit_bytes=14 << 20),
        cost_estimate=pl.CostEstimate(
            flops=2 * partial.size * depth,
            bytes_accessed=6 * partial.size,
            transcendentals=partial.size,
        ),
    )(me, table, *pieces, partial)


def with_halo(array, sides, width):
    for axis, dim in sides:
        size, length = (lax.axis_size(axis), array.shape[dim])
        up = [(i, (i + 1) % size) for i in range(size - 1)]
        down = [(j, i) for i, j in up]
        last = lax.slice_in_dim(array, length - width, length, axis=dim)
        initial = lax.slice_in_dim(array, 0, width, axis=dim)
        before = lax.ppermute(last, axis, up)
        after = lax.ppermute(initial, axis, down)
        array = jnp.concatenate([before, array, after], axis=dim)
    return array


def signed_modes(mode_count):
    position = jnp.arange(mode_count, dtype=jnp.int32)
    return jnp.where(position < mode_count // 2, position, position - mode_count)


def angle_grid(first, second, length):
    phase_turns = first[:, None] * second[None, :] % length
    return phase_turns.astype(jnp.float32) * (2.0 * math.pi / length)


def real_table(first, second, length, factor):
    angles = angle_grid(first, second, length)
    return jnp.stack([jnp.cos(angles) * factor, -jnp.sin(angles) * factor])


def complex_table(first, second, length, factor, direction):
    angles = angle_grid(first, second, length)
    cosine = jnp.cos(angles) * factor
    sine_part = jnp.sin(angles) * factor
    return jnp.stack(
        [jnp.stack([cosine, direction * sine_part]), jnp.stack([-direction * sine_part, cosine])]
    )


def split_pair_spectral(flow_field, spectral_weight):
    highest = lax.Precision.HIGHEST
    cells_x, cells_y, cells_z, channels = flow_field.shape
    count_x = lax.axis_size("gx")
    count_y = lax.axis_size("gy")
    full_x = cells_x * count_x
    full_y = cells_y * count_y
    item_count = spectral_weight.shape[0]
    local_y = lax.axis_index("gy") * cells_y + jnp.arange(cells_y, dtype=jnp.int32)
    grid_x = jnp.arange(full_x, dtype=jnp.int32)
    grid_z = jnp.arange(cells_z, dtype=jnp.int32)
    modes_z = jnp.arange(MZ, dtype=jnp.int32)
    forward_z = real_table(grid_z, modes_z, cells_z, cells_z ** (-0.5)).astype(jnp.bfloat16)
    z_spectrum = jnp.einsum(
        "xyzc,pzk->pxykc", flow_field, forward_z, preferred_element_type=jnp.float32
    )
    columns = lax.all_to_all(
        z_spectrum.astype(jnp.bfloat16), "gy", split_axis=4, concat_axis=2, tiled=True
    ).astype(z_spectrum.dtype)
    whole_y = jnp.arange(full_y, dtype=jnp.int32)
    forward_full = complex_table(whole_y, signed_modes(MY), full_y, full_y ** (-0.5), -1.0)
    y_spectrum = jnp.einsum("pxykc,pqyj->qxjkc", columns, forward_full, precision=highest)
    owned = lax.all_to_all(
        y_spectrum.astype(jnp.bfloat16), "gy", split_axis=2, concat_axis=4, tiled=True
    ).astype(y_spectrum.dtype)
    owned_modes = owned.reshape(2, cells_x, count_x, item_count, channels // 2)
    gathered_rows = lax.all_to_all(
        owned_modes.astype(jnp.bfloat16), "gx", split_axis=2, concat_axis=1, tiled=True
    ).astype(owned_modes.dtype)
    gathered_rows = gathered_rows.reshape(2, full_x, item_count, channels // 2)
    forward_x = complex_table(grid_x, signed_modes(MX), full_x, full_x ** (-0.5), -1.0)
    x_spectrum = jnp.einsum("pxjc,pqxm->qmjc", gathered_rows, forward_x, precision=highest).astype(
        jnp.bfloat16
    )
    products = jnp.einsum(
        "pmjc,jmqco->pqmjo", x_spectrum, spectral_weight, preferred_element_type=jnp.float32
    )
    mixed_modes = jnp.stack([products[0, 0] - products[1, 1], products[0, 1] + products[1, 0]])
    backward_x = complex_table(signed_modes(MX), grid_x, full_x, MX ** (-0.5), 1.0)
    inverse_x = jnp.einsum("pmjc,pqmx->qxjc", mixed_modes, backward_x, precision=highest)
    inverse_x = inverse_x.reshape(2, full_x, 1, item_count, channels)
    returned = lax.all_to_all(
        inverse_x.astype(jnp.bfloat16), "gx", split_axis=1, concat_axis=2, tiled=True
    ).astype(inverse_x.dtype)
    band_rows = MY // count_y
    summed = returned.reshape(2, cells_x, band_rows * MZ, 2, channels).sum(axis=3)
    summed = summed.reshape(2, cells_x, band_rows, MZ, channels)
    coefficients = lax.all_gather(summed.astype(jnp.bfloat16), "gy", axis=2, tiled=True).astype(
        summed.dtype
    )
    backward_y = complex_table(signed_modes(MY), local_y, full_y, MY ** (-0.5), 1.0)
    y_inverse = jnp.einsum("pxjkc,pqjy->qxykc", coefficients, backward_y, precision=highest).astype(
        jnp.bfloat16
    )
    backward_z = real_table(modes_z, grid_z, cells_z, MZ ** (-0.5)).astype(jnp.bfloat16)
    return jnp.einsum("pxykc,pkz->xyzc", y_inverse, backward_z, preferred_element_type=jnp.float32)


def split_pair_convolve(flow_field, conv_weight):
    cells_x, cells_y, cells_z, channels = flow_field.shape
    padded = with_halo(flow_field, (("gx", 0), ("gy", 1)), 1)
    padded = jnp.pad(padded, ((0, 0), (0, 0), (1, 1), (0, 0)))
    stacked = jnp.concatenate(
        [padded[:, :, 0:cells_z], padded[:, :, 1 : cells_z + 1], padded[:, :, 2 : cells_z + 2]],
        axis=3,
    )
    kernel = conv_weight.reshape(3, 3, 3 * channels, channels)
    accumulated = jnp.zeros((cells_x, cells_y, cells_z, channels), jnp.float32)
    for shift_x in range(3):
        for shift_y in range(3):
            accumulated = accumulated + jnp.dot(
                stacked[shift_x : shift_x + cells_x, shift_y : shift_y + cells_y],
                kernel[shift_x, shift_y],
                preferred_element_type=jnp.float32,
            )
    return accumulated


def neighbours(first, last, axis):
    size = lax.axis_size(axis)
    up = [(i, i + 1) for i in range(size - 1)]
    down = [(i + 1, i) for i in range(size - 1)]
    return lax.ppermute(last, axis, up), lax.ppermute(first, axis, down)


def with_neighbour(array, start, axis):
    size = lax.axis_size(axis)
    pairs = [(i, i + 1) for i in range(start, size - 1, 2)]
    alone = set(range(size)) - {i for pair in pairs for i in pair}
    pairs += [(j, i) for i, j in pairs] + [(i, i) for i in sorted(alone)]
    return lax.ppermute(array, axis, pairs)


def exchange(array, step, shards, along_outer):
    outer, inner = shards
    pairs = []
    for i in range(outer * inner):
        a, b = divmod(i, inner)
        count, own = (outer, a) if along_outer else (inner, b)
        to = own ^ step if count & (count - 1) == 0 else (own + step) % count
        pairs.append((i, to * inner + b if along_outer else a * inner + to))
    return lax.ppermute(array, "gx", pairs)


def over_y(array, step, shards_y):
    return lax.ppermute(array, "gy", [(i, (i + step) % shards_y) for i in range(shards_y)])


def body(flow, spectral_weight, conv_weight, bias):
    cells_x, cells_y, cells_z, channels = flow.shape
    shards_x, shards_y = lax.axis_size("gx"), lax.axis_size("gy")
    items = spectral_weight.shape[0]
    pairs = items // 2
    if items % 2 or shards_y < 2:
        spectral = split_pair_spectral(flow, spectral_weight)
        convolved = split_pair_convolve(flow, conv_weight)
        return jax.nn.gelu(spectral + convolved + bias, approximate=True).astype(jnp.bfloat16)

    barrier = lax.optimization_barrier
    inner = max(d for d in range(1, shards_x + 1) if shards_x % d == 0 and d * d <= shards_x)
    outer = shards_x // inner
    shards = (outer, inner)
    me = lax.axis_index(("gy", "gx")).astype(jnp.int32).reshape(1)
    sizes = (shards_x, shards_y, pairs, cells_y, cells_z)
    full_x = cells_x * shards_x
    weight = spectral_weight.reshape(items, MX, channels, channels)
    early = pairs // 4

    table = jnp.asarray(forward_yz_table(*sizes))
    columns = flow.reshape(cells_x, cells_y * cells_z, channels)
    order = far_first(outer)
    cut = (outer + 1) // 2
    pieces = [piece for piece in (order[:cut], order[cut:]) if piece]
    arrived = [[] for _ in pieces]
    for step in range(1, shards_y):
        sent = forward_yz(me, table, columns, step, shards, shards_y, pieces)
        sent, columns, weight = barrier((sent, columns, weight))
        for into, piece in zip(arrived, sent):
            into.append(over_y(piece, step, shards_y))
    loaded = [preload(weight, 0, early)] if early else []
    loaded, columns = barrier((loaded, columns))
    kept = forward_yz(me, table, columns, 0, shards, shards_y, pieces, cells_z)
    kept, (first, last, *ends) = kept[: len(pieces)], kept[len(pieces) :]
    if shards_y == 2:
        front = back = over_y(ends[0], 1, shards_y)
    else:
        front, back = neighbours(*ends, "gy")

    by_outer = []
    for piece, own, parts in zip(pieces, kept, arrived):
        for step, total in zip(piece, add_pieces(own, parts)):
            by_outer.append(exchange(total, step, shards, True) if step else total)
    if early:
        loaded.append(preload(weight, early, early))
    by_outer, loaded, weight = barrier((by_outer[::-1], loaded, weight))
    by_inner = regroup(me, by_outer[::-1], shards, True)
    by_inner, weight = barrier((by_inner, weight))
    rows = [
        exchange(by_inner[step], step, shards, False) if step else by_inner[0]
        for step in far_first(inner)
    ]
    if early:
        loaded.append(preload(weight, 2 * early, max(early // 2, 1)))

    rows, loaded, first, last, front, back = barrier((rows, loaded, first, last, front, back))
    paired, other = halo_planes(me, first, last, front, back, shards, shards_y)
    paired, other = with_neighbour(paired, 0, "gx"), with_neighbour(other, 1, "gx")
    returned = mixing(
        me,
        rows,
        jnp.asarray(forward_x_table(full_x)),
        jnp.asarray(backward_x_table(full_x)),
        weight,
        loaded,
        shards,
    )
    returned, other, paired = barrier((list(returned), other, paired))
    halos = (paired, other, front, back)
    width = 2 if cells_x % 2 == 0 else 1
    convolved = [
        convolution(me, x, width, flow, halos, conv_weight, shards, shards_y)
        for x in range(0, cells_x, width)
    ]

    returned = [
        exchange(returned[step], step, shards, False) if step else returned[0]
        for step in far_first(inner)
    ]
    returned, convolved[0] = barrier((returned, convolved[0]))
    returned = regroup(me, returned, shards, False)
    returned = [
        exchange(returned[step], step, shards, True) if step else returned[0]
        for step in far_first(outer)
    ]
    by_slot = dict(zip(far_first(outer), returned))
    bundles = [
        bundle([by_slot[slot] for slot in slots]) if slots[1:] else by_slot[slots[0]][None]
        for slots in bundled_slots(outer)
    ]
    others = []
    for step in range(1, shards_y):
        others += [over_y(part, step, shards_y) for part in bundles]
    table = jnp.asarray(backward_yz_table(*sizes))
    bias = bias.reshape(1, channels)
    partial = own_part(me, table, returned, convolved, bias, shards, shards_y)
    return last_part(me, table, others, partial, shards, shards_y)


def solution(mesh):
    placed = (P("gx", "gy", None, None), P(("gy", "gx"), None, None, None, None), P(), P())
    return jax.shard_map(
        body, mesh=mesh, in_specs=placed, out_specs=P("gx", "gy", None, None), check_vma=False
    )
```

```python
import functools
import math

import jax
import jax.numpy as jnp
import numpy as np
from jax import lax
from jax.experimental import pallas as pl
from jax.experimental.pallas import tpu as pltpu
from jax.sharding import PartitionSpec as P

MX = 64
MY = 16
MZ = 16


def frequencies(mode_count):
    position = np.arange(mode_count)
    return np.where(position < mode_count // 2, position, position - mode_count)


def wave(first, second, length, factor):
    turns = (np.asarray(first)[:, None] * np.asarray(second)[None, :]) % length
    angles = turns * (2.0 * math.pi / length)
    return (np.cos(angles) + 1j * np.sin(angles)) * factor


def rounded(values):
    return values.astype(np.float32).astype(jnp.bfloat16).astype(np.float64)


def item_modes(shards_x, shards_y, pairs):
    index = np.arange(shards_y * shards_x * pairs).reshape(shards_y, shards_x, pairs)
    return index // MZ, index % MZ


def forward_yz_table(shards_x, shards_y, pairs, cells_y, cells_z):
    full_y = shards_y * cells_y
    turn_z = wave(np.arange(MZ), np.arange(cells_z), cells_z, cells_z**-0.5)
    turn_z = rounded(turn_z.real) - 1j * rounded(turn_z.imag)
    turn_y = np.conj(wave(frequencies(MY), np.arange(full_y), full_y, full_y**-0.5))
    mode_y, mode_z = item_modes(shards_x, shards_y, pairs)
    table = np.empty((shards_y, shards_y, shards_x, pairs, 2, cells_y, cells_z), np.float32)
    for own in range(shards_y):
        rows = turn_y[:, own * cells_y : (own + 1) * cells_y]
        product = rows[mode_y][..., :, None] * turn_z[mode_z][..., None, :]
        table[own, :, :, :, 0] = product.real
        table[own, :, :, :, 1] = product.imag
    return table.reshape(shards_y, -1, cells_y * cells_z).astype(jnp.bfloat16)


def backward_yz_table(shards_x, shards_y, pairs, cells_y, cells_z):
    full_y = shards_y * cells_y
    turn_z = wave(np.arange(MZ), np.arange(cells_z), cells_z, MZ**-0.5)
    turn_z = rounded(turn_z.real) + 1j * rounded(turn_z.imag)
    turn_y = wave(frequencies(MY), np.arange(full_y), full_y, MY**-0.5)
    mode_y, mode_z = item_modes(shards_x, shards_y, pairs)
    table = np.empty((shards_y, shards_y, cells_y, cells_z, shards_x, pairs, 2), np.float32)
    for own in range(shards_y):
        rows = turn_y[:, own * cells_y : (own + 1) * cells_y]
        product = rows[mode_y][..., :, None] * turn_z[mode_z][..., None, :]
        product = np.moveaxis(product, (3, 4), (1, 2))
        table[own, ..., 0] = product.real
        table[own, ..., 1] = -product.imag
    return table.reshape(shards_y**2, cells_y * cells_z, -1).astype(jnp.bfloat16)


def forward_x_table(full_x):
    turn = np.conj(wave(frequencies(MX), np.arange(full_x), full_x, full_x**-0.5))
    parts = np.empty((2, MX, 2, 2, full_x), np.float32)
    parts[0, :, 0, 0], parts[0, :, 0, 1] = turn.real, -turn.imag
    parts[0, :, 1, 0], parts[0, :, 1, 1] = turn.imag, turn.real
    parts[1, :, 0] = -parts[0, :, 1]
    parts[1, :, 1] = parts[0, :, 0]
    return parts.reshape(2 * MX * 2, 2 * full_x).astype(jnp.bfloat16)


def backward_x_table(full_x):
    turn = wave(frequencies(MX), np.arange(full_x), full_x, MX**-0.5).T
    parts = np.empty((2, full_x, MX, 2), np.float32)
    parts[0, :, :, 0], parts[0, :, :, 1] = turn.real, -turn.imag
    parts[1, :, :, 0], parts[1, :, :, 1] = turn.imag, turn.real
    return parts.reshape(2 * full_x, MX * 2).astype(jnp.bfloat16)


def dot(left, right):
    return jnp.dot(left, right, preferred_element_type=jnp.float32)


def peer(index, step, count):
    if count & (count - 1) == 0:
        return index ^ step
    return lax.rem(index + step, count)


def origin(index, step, count):
    if count & (count - 1) == 0:
        return index ^ step
    return lax.rem(index + (count - step), count)


def far_first(count):
    return list(range(count - 1, -1, -1))


def place(me, shards):
    outer, inner = shards
    across = lax.rem(me, outer * inner)
    return lax.div(me, outer * inner), lax.div(across, inner), lax.rem(across, inner)


def in_vmem(count):
    return [pl.BlockSpec(memory_space=pltpu.VMEM)] * count


IN_SMEM = pl.BlockSpec(memory_space=pltpu.SMEM)


def transform(table, flow_at, cells_x, refs, pieces):
    inner, _, rows, channels = refs[0].shape[1:]
    block = inner * rows
    width = 2 if cells_x % 2 == 0 else 1
    for x in range(0, cells_x, width):
        columns = [flow_at(x + i) for i in range(width)]
        result = dot(table, jnp.concatenate(columns, axis=1))
        for i in range(width):
            part = result[:, i * channels : (i + 1) * channels]
            at = 0
            for ref, piece in zip(refs, pieces):
                for slot in range(len(piece)):
                    value = part[at : at + block].reshape(inner, rows, channels)
                    ref[slot, :, x + i] = value.astype(ref.dtype)
                    at += block


def send_kernel(shards, shards_y, pieces, step, me_ref, table_ref, flow_ref, *refs):
    *refs, table, flow, table_sems, flow_sems = refs
    cells_x = flow.shape[0]
    outer, _ = shards
    block = refs[0].shape[1] * refs[0].shape[3]
    own_y, own, _ = place(me_ref[0], shards)
    owner = lax.rem(own_y + step, shards_y)
    copies = []
    for i, other in enumerate(step for piece in pieces for step in piece):
        start = (owner * outer + peer(own, other, outer)) * block
        source = table_ref.at[own_y, pl.ds(pl.multiple_of(start, block), block)]
        copies.append(
            pltpu.make_async_copy(source, table.at[pl.ds(i * block, block)], table_sems.at[i])
        )
    loads = [
        pltpu.make_async_copy(flow_ref.at[x], flow.at[x], flow_sems.at[x])
        for x in range(cells_x)
    ]
    for copy in copies + loads:
        copy.start()
    for copy in copies:
        copy.wait()

    def flow_at(x):
        loads[x].wait()
        return flow[x]

    transform(table[...], flow_at, cells_x, refs, pieces)


def is_even(me, shards):
    _, own_outer, own_inner = place(me, shards)
    return lax.rem(own_outer * shards[1] + own_inner, 2) == 0


def keep_kernel(shards, shards_y, pieces, me_ref, table_ref, flow_ref, *refs):
    refs, (first, last, *edges) = refs[: len(pieces)], refs[len(pieces) :]
    cells_x, positions, _ = flow_ref.shape
    outer, _ = shards
    block = refs[0].shape[1] * refs[0].shape[3]
    own_y, own, _ = place(me_ref[0], shards)
    tables = []
    for other in (step for piece in pieces for step in piece):
        start = (own_y * outer + peer(own, other, outer)) * block
        tables.append(table_ref[own_y, pl.ds(pl.multiple_of(start, block), block), :])
    transform(
        jnp.concatenate(tables, axis=0), lambda x: flow_ref[x], cells_x, refs, pieces
    )
    first[...] = flow_ref[0]
    last[...] = flow_ref[cells_x - 1]
    cells_z = edges[0].shape[1]
    low, high = pl.ds(0, cells_z), pl.ds(positions - cells_z, cells_z)
    if len(edges) > 1:
        edges[0][...] = flow_ref[:, low]
        edges[1][...] = flow_ref[:, high]
    else:

        @pl.when(own_y > 0)
        def _():
            edges[0][...] = flow_ref[:, low]

        @pl.when(own_y == 0)
        def _():
            edges[0][...] = flow_ref[:, high]


def forward_yz(me, table, flow, step, shards, shards_y, pieces, cells_z=0):
    cells_x, positions, channels = flow.shape
    outer, inner = shards
    rows = table.shape[1] // shards_y
    unit = (inner, cells_x, rows // (outer * inner), channels)
    dtype = jnp.bfloat16 if step else jnp.float32
    shapes = [jax.ShapeDtypeStruct((len(piece), *unit), dtype) for piece in pieces]
    if step:
        kernel = functools.partial(send_kernel, shards, shards_y, pieces, step)
        specs = [pl.BlockSpec(memory_space=pltpu.HBM)] * 2
        scratch = [
            pltpu.VMEM((rows, positions), table.dtype),
            pltpu.VMEM(flow.shape, flow.dtype),
            pltpu.SemaphoreType.DMA((outer,)),
            pltpu.SemaphoreType.DMA((cells_x,)),
        ]
    else:
        kernel = functools.partial(keep_kernel, shards, shards_y, pieces)
        specs, scratch = in_vmem(2), []
        shapes += [jax.ShapeDtypeStruct((positions, channels), flow.dtype)] * 2
        edge = jax.ShapeDtypeStruct((cells_x, cells_z, channels), flow.dtype)
        shapes += [edge] * (1 if shards_y == 2 else 2)
    return pl.pallas_call(
        kernel,
        in_specs=[IN_SMEM] + specs,
        out_specs=in_vmem(len(shapes)),
        out_shape=shapes,
        scratch_shapes=scratch,
        compiler_params=pltpu.CompilerParams(vmem_limit_bytes=(56 if step else 10) << 20),
        cost_estimate=pl.CostEstimate(
            flops=2 * rows * positions * cells_x * channels,
            bytes_accessed=2 * positions * (rows + cells_x * channels),
            transcendentals=0,
        ),
    )(me, table, flow)


def add_kernel(count, *refs):
    out_refs = refs[count:]
    for slot, out_ref in enumerate(out_refs):
        total = refs[0][slot]
        for ref in refs[1:count]:
            total = total + ref[slot].astype(jnp.float32)
        out_ref[...] = total.astype(out_ref.dtype)


def add_pieces(own, arrived):
    slots, *unit = own.shape
    return pl.pallas_call(
        functools.partial(add_kernel, 1 + len(arrived)),
        in_specs=in_vmem(1 + len(arrived)),
        out_specs=in_vmem(slots),
        out_shape=[jax.ShapeDtypeStruct(unit, jnp.bfloat16)] * slots,
        cost_estimate=pl.CostEstimate(flops=own.size, bytes_accessed=0, transcendentals=0),
        compiler_params=pltpu.CompilerParams(vmem_limit_bytes=10 << 20),
    )(own, *arrived)


def regroup_kernel(shards, chosen, me_ref, *refs):
    _, _, own = place(me_ref[0], shards)
    count = refs[0].shape[0]
    in_refs, out_refs = refs[:-count], refs[-count:]
    for step, out_ref in enumerate(out_refs):
        at = peer(own, step, count) if chosen else step
        for number, in_ref in enumerate(in_refs):
            out_ref[far_first(len(in_refs))[number]] = in_ref[at]


def regroup(me, arrays, shards, chosen):
    count, *unit = arrays[0].shape
    return pl.pallas_call(
        functools.partial(regroup_kernel, shards, chosen),
        in_specs=[IN_SMEM] + in_vmem(len(arrays)),
        out_specs=in_vmem(count),
        out_shape=[jax.ShapeDtypeStruct((len(arrays), *unit), arrays[0].dtype)] * count,
        cost_estimate=pl.CostEstimate(
            flops=arrays[0].size, bytes_accessed=0, transcendentals=0
        ),
        compiler_params=pltpu.CompilerParams(vmem_limit_bytes=10 << 20),
    )(me, *arrays)


def halo_kernel(shards, shards_y, me_ref, first_ref, last_ref, front_ref, back_ref, *out_refs):
    own_y, _, _ = place(me_ref[0], shards)
    even = is_even(me_ref[0], shards)
    cells_x, cells_z, _ = front_ref.shape
    cells_y = first_ref.shape[0] // cells_z

    def fill(out_ref, x, plane_ref):
        for y in range(cells_y):
            out_ref[y + 1] = plane_ref[pl.ds(y * cells_z, cells_z), :]
        row = front_ref[x]
        out_ref[0] = jnp.where(own_y > 0, row, jnp.zeros_like(row))
        row = back_ref[x]
        out_ref[cells_y + 1] = jnp.where(own_y < shards_y - 1, row, jnp.zeros_like(row))

    @pl.when(even)
    def _():
        fill(out_refs[0], cells_x - 1, last_ref)
        fill(out_refs[1], 0, first_ref)

    @pl.when(jnp.logical_not(even))
    def _():
        fill(out_refs[0], 0, first_ref)
        fill(out_refs[1], cells_x - 1, last_ref)


def halo_planes(me, first, last, front, back, shards, shards_y):
    cells_x, cells_z, channels = front.shape
    shape = (first.shape[0] // cells_z + 2, cells_z, channels)
    return pl.pallas_call(
        functools.partial(halo_kernel, shards, shards_y),
        in_specs=[IN_SMEM] + in_vmem(4),
        out_specs=in_vmem(2),
        out_shape=[jax.ShapeDtypeStruct(shape, first.dtype)] * 2,
        compiler_params=pltpu.CompilerParams(vmem_limit_bytes=10 << 20),
    )(me, first, last, front, back)


def preload_kernel(first, weight_ref, out_ref, sems):
    count = out_ref.shape[0]
    pieces = sems.shape[0] // count
    modes = out_ref.shape[1] // pieces
    copies = []
    for i in range(count * pieces):
        item, at = i // pieces, pl.ds(i % pieces * modes, modes)
        copies.append(
            pltpu.make_async_copy(
                weight_ref.at[first + item, at], out_ref.at[item, at], sems.at[i]
            )
        )
    for copy in copies:
        copy.start()
    for copy in copies:
        copy.wait()


def preload(weight, pair, count):
    shape = (2 * count, *weight.shape[1:])
    return pl.pallas_call(
        functools.partial(preload_kernel, 2 * pair),
        in_specs=[pl.BlockSpec(memory_space=pltpu.HBM)],
        out_specs=in_vmem(1)[0],
        out_shape=jax.ShapeDtypeStruct(shape, weight.dtype),
        scratch_shapes=[pltpu.SemaphoreType.DMA((2 * 2 * count,))],
        compiler_params=pltpu.CompilerParams(vmem_limit_bytes=34 << 20),
        cost_estimate=pl.CostEstimate(
            flops=0, bytes_accessed=2 * math.prod(shape), transcendentals=0
        ),
    )(weight)


def mixing_kernel(shards, loaded, me_ref, *refs):
    outer, inner = shards
    row_refs, refs = refs[:inner], refs[inner:]
    forward_ref, backward_ref, weight_ref, *refs = refs
    loaded_refs, refs = refs[:loaded], refs[loaded:]
    loaded = sum(ref.shape[0] // 2 for ref in loaded_refs)
    out_refs, (held, sems, wide, left, mixed) = refs[:inner], refs[inner:]

    channels = wide.shape[1]
    _, cells_x, item_rows, _ = row_refs[0].shape
    pairs = item_rows // 2
    full_x = outer * inner * cells_x
    half = channels // 2
    span = 2 * MX
    block = cells_x * item_rows
    _, own_outer, own_inner = place(me_ref[0], shards)

    def copy(pair):
        slot = pair - loaded
        return pltpu.make_async_copy(
            weight_ref.at[pl.ds(2 * pair, 2)], held.at[slot], sems.at[slot]
        )

    for pair in range(loaded, pairs):
        copy(pair).start()

    def rows_of(outer_index, inner_index):
        start = pl.multiple_of((outer_index * inner + inner_index) * block, block)
        return pl.ds(start, block)

    for number, step in enumerate(far_first(inner)):
        source = origin(own_inner, step, inner)
        for slot in range(outer):
            value = row_refs[number][slot].reshape(block, channels)
            at = rows_of(origin(own_outer, slot, outer), source)
            wide[at, :] = value.astype(jnp.float32)
    low = lax.broadcasted_iota(jnp.int32, (span, channels), 1) < half
    for pair in range(pairs):
        columns = [wide[pl.ds(2 * pair + p, full_x, stride=item_rows), :] for p in range(2)]
        columns = jnp.concatenate(columns, axis=0).astype(jnp.bfloat16)
        both = dot(forward_ref[...], columns)
        value, turned = both[:span], both[span:]
        first = jnp.where(low, value, pltpu.roll(turned, half, axis=1))
        second = jnp.where(low, pltpu.roll(value, half, axis=1), turned)
        left[pl.ds(pair * span, span), :channels] = first.astype(left.dtype)
        left[pl.ds(pair * span, span), channels:] = second.astype(left.dtype)

    group = 16
    row = lax.broadcasted_iota(jnp.int32, (group, channels), 0) // 2

    def mix(pair, tile_of):
        for step in range(span // group):
            start = pl.multiple_of(pair * span + step * group, group)
            lhs = left[pl.ds(start, group), :]
            gathered = jnp.zeros((group, channels), jnp.float32)
            for i in range(0, group // 2, 2):
                mode = step * (group // 2) + i
                tiles = [
                    jnp.concatenate([tile_of(h, mode + k) for h in range(2)], axis=0)
                    for k in range(2)
                ]
                product = dot(lhs, jnp.concatenate(tiles, axis=1))
                for k in range(2):
                    gathered = jnp.where(
                        row == i + k, product[:, k * channels : (k + 1) * channels], gathered
                    )
            mixed[pl.ds(start, group), :] = gathered.astype(mixed.dtype)

    pair = 0
    for ref in loaded_refs:
        count = ref.shape[0] // 2

        def ready(i, carry, ref=ref, pair=pair):
            mix(pair + i, lambda h, mode: ref[2 * i + h, mode])
            return carry

        lax.fori_loop(0, count, ready, 0)
        pair += count

    def streamed(pair, carry):
        copy(pair).wait()
        mix(pair, lambda h, mode: held[pair - loaded, h, mode])
        return carry

    lax.fori_loop(loaded, pairs, streamed, 0)

    for pair in range(pairs):
        result = dot(backward_ref[...], mixed[pl.ds(pair * span, span), :])
        for p in range(2):
            wide[pl.ds(2 * pair + p, full_x, stride=item_rows), :] = result[
                p * full_x : (p + 1) * full_x
            ]
    for step in range(inner):
        target = peer(own_inner, step, inner)
        for slot in range(outer):
            value = wide[rows_of(peer(own_outer, slot, outer), target), :]
            value = value.reshape(cells_x, item_rows, channels)
            out_refs[step][slot] = value.astype(out_refs[step].dtype)


def mixing(me, rows, forward_x, backward_x, weight, loaded, shards):
    outer, inner = shards
    _, cells_x, item_rows, channels = rows[0].shape
    pairs = item_rows // 2
    row_count = outer * inner * cells_x * item_rows
    streamed = pairs - sum(part.shape[0] // 2 for part in loaded)
    return pl.pallas_call(
        functools.partial(mixing_kernel, shards, len(loaded)),
        in_specs=[IN_SMEM]
        + in_vmem(inner + 2)
        + [pl.BlockSpec(memory_space=pltpu.HBM)]
        + in_vmem(len(loaded)),
        out_specs=in_vmem(inner),
        out_shape=[jax.ShapeDtypeStruct(rows[0].shape, jnp.bfloat16)] * inner,
        scratch_shapes=[
            pltpu.VMEM((streamed, 2, *weight.shape[1:]), weight.dtype),
            pltpu.SemaphoreType.DMA((streamed,)),
            pltpu.VMEM((row_count, channels), jnp.float32),
            pltpu.VMEM((pairs * 2 * MX, 2 * channels), jnp.bfloat16),
            pltpu.VMEM((pairs * 2 * MX, channels), jnp.bfloat16),
        ],
        compiler_params=pltpu.CompilerParams(vmem_limit_bytes=20 << 20),
        cost_estimate=pl.CostEstimate(
            flops=8 * weight.size, bytes_accessed=2 * weight.size, transcendentals=0
        ),
    )(me, *rows, forward_x, backward_x, weight, *loaded)


def convolution_kernel(x, cells_x, width, shards, shards_y, me_ref, *refs):
    flow_ref, paired_ref, other_ref, front_ref, back_ref, kernel_ref, out_ref, padded = refs
    _, cells_y, cells_z, channels = out_ref.shape
    own_y, _, _ = place(me_ref[0], shards)
    even = is_even(me_ref[0], shards)
    for plane in range(width + 2):
        p = x + plane - 1
        if 0 <= p < cells_x:
            padded[plane, 1 : cells_y + 1] = flow_ref[p]
            row = front_ref[p]
            padded[plane, 0] = jnp.where(own_y > 0, row, jnp.zeros_like(row))
            row = back_ref[p]
            last = own_y == shards_y - 1
            padded[plane, cells_y + 1] = jnp.where(last, jnp.zeros_like(row), row)
        else:
            use_paired = jnp.logical_not(even) if p < 0 else even

            @pl.when(use_paired)
            def _(plane=plane):
                padded[plane] = paired_ref[...]

            @pl.when(jnp.logical_not(use_paired))
            def _(plane=plane):
                padded[plane] = other_ref[...]

    rows = 16 if cells_y % 16 == 0 else 1
    columns = [(k, d) for k in range(width) for d in range(3)]
    columns = [columns[i : i + 2] for i in range(0, len(columns), 2)]
    none = jnp.zeros((channels, channels), kernel_ref.dtype)

    def chunk(index, carry):
        y = index * rows
        products = {}
        for group in columns:
            blocks, kernels = [], []
            for p in range(width + 2):
                if not any(0 <= p - k < 3 for k, _ in group):
                    continue
                for b in range(3):
                    part = padded[p, pl.ds(y + b, rows)]
                    blocks.append(part.reshape(rows * cells_z, channels))
                    parts = [
                        kernel_ref[p - k, b, d] if 0 <= p - k < 3 else none for k, d in group
                    ]
                    kernels.append(jnp.concatenate(parts, axis=1))
            product = dot(jnp.concatenate(blocks, axis=1), jnp.concatenate(kernels, axis=0))
            for i, column in enumerate(group):
                part = product[:, i * channels : (i + 1) * channels]
                products[column] = part.reshape(rows, cells_z, channels)
        z = lax.broadcasted_iota(jnp.int32, (rows, cells_z, channels), 1)
        for k in range(width):
            before = jnp.where(z == 0, 0.0, pltpu.roll(products[k, 0], 1, axis=1))
            after = pltpu.roll(products[k, 2], cells_z - 1, axis=1)
            after = jnp.where(z == cells_z - 1, 0.0, after)
            total = before + products[k, 1] + after
            out_ref[k, pl.ds(y, rows)] = total.astype(out_ref.dtype)
        return carry

    lax.fori_loop(0, cells_y // rows, chunk, 0)


def convolution(me, x, width, flow, halos, kernel, shards, shards_y):
    cells_x, cells_y, cells_z, channels = flow.shape
    shape = (width, cells_y, cells_z, channels)
    return pl.pallas_call(
        functools.partial(convolution_kernel, x, cells_x, width, shards, shards_y),
        in_specs=[IN_SMEM] + in_vmem(2 + len(halos)),
        out_specs=in_vmem(1)[0],
        out_shape=jax.ShapeDtypeStruct(shape, jnp.bfloat16),
        scratch_shapes=[pltpu.VMEM((width + 2, cells_y + 2, cells_z, channels), flow.dtype)],
        compiler_params=pltpu.CompilerParams(vmem_limit_bytes=14 << 20),
        cost_estimate=pl.CostEstimate(
            flops=3 * 27 * width * cells_y * cells_z * channels * channels,
            bytes_accessed=10 * cells_y * cells_z * channels,
            transcendentals=0,
        ),
    )(me, flow, *halos, kernel)


def bundled_slots(count):
    parts = ([0], [count - 1], far_first(count)[1:-1]) if count > 1 else ([0],)
    return [part for part in parts if part]


def bundle_kernel(*refs):
    *in_refs, out_ref = refs
    for i, ref in enumerate(in_refs):
        out_ref[i] = ref[...]


def bundle(arrays):
    shape = (len(arrays), *arrays[0].shape)
    return pl.pallas_call(
        bundle_kernel,
        in_specs=in_vmem(len(arrays)),
        out_specs=in_vmem(1)[0],
        out_shape=jax.ShapeDtypeStruct(shape, arrays[0].dtype),
        cost_estimate=pl.CostEstimate(
            flops=math.prod(shape), bytes_accessed=0, transcendentals=0
        ),
        compiler_params=pltpu.CompilerParams(vmem_limit_bytes=10 << 20),
    )(*arrays)


def gather_pieces(me, shards, pieces, held):
    outer, inner = shards
    _, own_outer, own_inner = place(me, shards)
    for number, slot, ref in pieces:
        cells_x, rows = ref.shape[1:3]
        source = (number * outer + origin(own_outer, slot, outer)) * inner
        for part in range(inner):
            at = (source + origin(own_inner, part, inner)) * rows
            for x in range(cells_x):
                held[x, pl.ds(pl.multiple_of(at, rows), rows), :] = ref[part, x]


def inverse(me, shards, shards_y, steps, table_ref, held, part, x, width, positions):
    own_y, _, _ = place(me, shards)
    columns = [held[x + i] for i in range(width)]
    depth = table_ref.shape[2]
    total = None
    for number, step in enumerate(steps):
        source = lax.rem(own_y + (shards_y - step), shards_y)
        rows = pl.ds(pl.multiple_of(part * positions, positions), positions)
        table = table_ref[own_y * shards_y + source, rows, :]
        block = [column[number * depth : (number + 1) * depth] for column in columns]
        product = dot(table, jnp.concatenate(block, axis=1))
        total = product if total is None else total + product
    return total


def final_kernel(shards, shards_y, me_ref, table_ref, *refs):
    outer, _ = shards
    *piece_refs, bias_ref, out_ref, held = refs
    cells_x, cells_y, cells_z, channels = out_ref.shape
    width = 2 if cells_x % 2 == 0 else 1
    count = -(-cells_x // width)
    piece_refs, convolved_refs = piece_refs[:-count], piece_refs[-count:]
    bundles = bundled_slots(outer)
    steps = list(range(shards_y))
    part = pl.program_id(0)

    @pl.when(part == 0)
    def _():
        pieces = [(0, *piece) for piece in zip(far_first(outer), piece_refs)]
        for i, ref in enumerate(piece_refs[outer:]):
            number, place_in = divmod(i, len(bundles))
            for j, slot in enumerate(bundles[place_in]):
                pieces.append((number + 1, slot, ref.at[j]))
        gather_pieces(me_ref[0], shards, pieces, held)

    bias = bias_ref[...]
    for x in range(0, cells_x, width):
        total = inverse(
            me_ref[0], shards, shards_y, steps, table_ref, held, part, x, width,
            cells_y * cells_z,
        )
        for i in range(width):
            spectral = total[:, i * channels : (i + 1) * channels]
            convolved = convolved_refs[x // width][i, pl.ds(part * cells_y, cells_y)]
            value = spectral.reshape(cells_y, cells_z, channels) + convolved + bias
            out_ref[x + i] = jax.nn.gelu(value, approximate=True).astype(out_ref.dtype)


def final(me, table, pieces, convolved, bias, shards, shards_y):
    width, cells_y, cells_z, channels = convolved[0].shape
    cells_x = width * len(convolved)
    parts = 4 if cells_y % 4 == 0 else 1
    block = (cells_x, cells_y // parts, cells_z, channels)
    shape = (cells_x, cells_y, cells_z, channels)
    depth = table.shape[2] * shards_y
    return pl.pallas_call(
        functools.partial(final_kernel, shards, shards_y),
        grid_spec=pltpu.PrefetchScalarGridSpec(
            num_scalar_prefetch=1,
            grid=(parts,),
            in_specs=in_vmem(2 + len(pieces) + len(convolved)),
            out_specs=pl.BlockSpec(block, lambda i, me: (0, i, 0, 0)),
            scratch_shapes=[pltpu.VMEM((cells_x, depth, channels), jnp.bfloat16)],
        ),
        out_shape=jax.ShapeDtypeStruct(shape, jnp.bfloat16),
        compiler_params=pltpu.CompilerParams(vmem_limit_bytes=14 << 20),
        cost_estimate=pl.CostEstimate(
            flops=2 * math.prod(shape) * depth,
            bytes_accessed=6 * math.prod(shape),
            transcendentals=math.prod(shape),
        ),
    )(me, table, *pieces, *convolved, bias)


def with_halo(array, sides, width):
    for axis, dim in sides:
        size, length = (lax.axis_size(axis), array.shape[dim])
        up = [(i, (i + 1) % size) for i in range(size - 1)]
        down = [(j, i) for i, j in up]
        last = lax.slice_in_dim(array, length - width, length, axis=dim)
        initial = lax.slice_in_dim(array, 0, width, axis=dim)
        before = lax.ppermute(last, axis, up)
        after = lax.ppermute(initial, axis, down)
        array = jnp.concatenate([before, array, after], axis=dim)
    return array


def signed_modes(mode_count):
    position = jnp.arange(mode_count, dtype=jnp.int32)
    return jnp.where(position < mode_count // 2, position, position - mode_count)


def angle_grid(first, second, length):
    phase_turns = first[:, None] * second[None, :] % length
    return phase_turns.astype(jnp.float32) * (2.0 * math.pi / length)


def real_table(first, second, length, factor):
    angles = angle_grid(first, second, length)
    return jnp.stack([jnp.cos(angles) * factor, -jnp.sin(angles) * factor])


def complex_table(first, second, length, factor, direction):
    angles = angle_grid(first, second, length)
    cosine = jnp.cos(angles) * factor
    sine_part = jnp.sin(angles) * factor
    return jnp.stack(
        [jnp.stack([cosine, direction * sine_part]), jnp.stack([-direction * sine_part, cosine])]
    )


def split_pair_spectral(flow_field, spectral_weight):
    highest = lax.Precision.HIGHEST
    cells_x, cells_y, cells_z, channels = flow_field.shape
    count_x = lax.axis_size("gx")
    count_y = lax.axis_size("gy")
    full_x = cells_x * count_x
    full_y = cells_y * count_y
    item_count = spectral_weight.shape[0]
    local_y = lax.axis_index("gy") * cells_y + jnp.arange(cells_y, dtype=jnp.int32)
    grid_x = jnp.arange(full_x, dtype=jnp.int32)
    grid_z = jnp.arange(cells_z, dtype=jnp.int32)
    modes_z = jnp.arange(MZ, dtype=jnp.int32)
    forward_z = real_table(grid_z, modes_z, cells_z, cells_z ** (-0.5)).astype(jnp.bfloat16)
    z_spectrum = jnp.einsum(
        "xyzc,pzk->pxykc", flow_field, forward_z, preferred_element_type=jnp.float32
    )
    columns = lax.all_to_all(
        z_spectrum.astype(jnp.bfloat16), "gy", split_axis=4, concat_axis=2, tiled=True
    ).astype(z_spectrum.dtype)
    whole_y = jnp.arange(full_y, dtype=jnp.int32)
    forward_full = complex_table(whole_y, signed_modes(MY), full_y, full_y ** (-0.5), -1.0)
    y_spectrum = jnp.einsum("pxykc,pqyj->qxjkc", columns, forward_full, precision=highest)
    owned = lax.all_to_all(
        y_spectrum.astype(jnp.bfloat16), "gy", split_axis=2, concat_axis=4, tiled=True
    ).astype(y_spectrum.dtype)
    owned_modes = owned.reshape(2, cells_x, count_x, item_count, channels // 2)
    gathered_rows = lax.all_to_all(
        owned_modes.astype(jnp.bfloat16), "gx", split_axis=2, concat_axis=1, tiled=True
    ).astype(owned_modes.dtype)
    gathered_rows = gathered_rows.reshape(2, full_x, item_count, channels // 2)
    forward_x = complex_table(grid_x, signed_modes(MX), full_x, full_x ** (-0.5), -1.0)
    x_spectrum = jnp.einsum("pxjc,pqxm->qmjc", gathered_rows, forward_x, precision=highest).astype(
        jnp.bfloat16
    )
    products = jnp.einsum(
        "pmjc,jmqco->pqmjo", x_spectrum, spectral_weight, preferred_element_type=jnp.float32
    )
    mixed_modes = jnp.stack([products[0, 0] - products[1, 1], products[0, 1] + products[1, 0]])
    backward_x = complex_table(signed_modes(MX), grid_x, full_x, MX ** (-0.5), 1.0)
    inverse_x = jnp.einsum("pmjc,pqmx->qxjc", mixed_modes, backward_x, precision=highest)
    inverse_x = inverse_x.reshape(2, full_x, 1, item_count, channels)
    returned = lax.all_to_all(
        inverse_x.astype(jnp.bfloat16), "gx", split_axis=1, concat_axis=2, tiled=True
    ).astype(inverse_x.dtype)
    band_rows = MY // count_y
    summed = returned.reshape(2, cells_x, band_rows * MZ, 2, channels).sum(axis=3)
    summed = summed.reshape(2, cells_x, band_rows, MZ, channels)
    coefficients = lax.all_gather(summed.astype(jnp.bfloat16), "gy", axis=2, tiled=True).astype(
        summed.dtype
    )
    backward_y = complex_table(signed_modes(MY), local_y, full_y, MY ** (-0.5), 1.0)
    y_inverse = jnp.einsum("pxjkc,pqjy->qxykc", coefficients, backward_y, precision=highest).astype(
        jnp.bfloat16
    )
    backward_z = real_table(modes_z, grid_z, cells_z, MZ ** (-0.5)).astype(jnp.bfloat16)
    return jnp.einsum("pxykc,pkz->xyzc", y_inverse, backward_z, preferred_element_type=jnp.float32)


def split_pair_convolve(flow_field, conv_weight):
    cells_x, cells_y, cells_z, channels = flow_field.shape
    padded = with_halo(flow_field, (("gx", 0), ("gy", 1)), 1)
    padded = jnp.pad(padded, ((0, 0), (0, 0), (1, 1), (0, 0)))
    stacked = jnp.concatenate(
        [padded[:, :, 0:cells_z], padded[:, :, 1 : cells_z + 1], padded[:, :, 2 : cells_z + 2]],
        axis=3,
    )
    kernel = conv_weight.reshape(3, 3, 3 * channels, channels)
    accumulated = jnp.zeros((cells_x, cells_y, cells_z, channels), jnp.float32)
    for shift_x in range(3):
        for shift_y in range(3):
            accumulated = accumulated + jnp.dot(
                stacked[shift_x : shift_x + cells_x, shift_y : shift_y + cells_y],
                kernel[shift_x, shift_y],
                preferred_element_type=jnp.float32,
            )
    return accumulated


def neighbours(first, last, axis):
    size = lax.axis_size(axis)
    up = [(i, i + 1) for i in range(size - 1)]
    down = [(i + 1, i) for i in range(size - 1)]
    return lax.ppermute(last, axis, up), lax.ppermute(first, axis, down)


def with_neighbour(array, start, axis):
    size = lax.axis_size(axis)
    pairs = [(i, i + 1) for i in range(start, size - 1, 2)]
    return lax.ppermute(array, axis, pairs + [(j, i) for i, j in pairs])


def exchange(array, step, shards, along_outer):
    outer, inner = shards
    pairs = []
    for i in range(outer * inner):
        a, b = divmod(i, inner)
        count, own = (outer, a) if along_outer else (inner, b)
        to = own ^ step if count & (count - 1) == 0 else (own + step) % count
        pairs.append((i, to * inner + b if along_outer else a * inner + to))
    return lax.ppermute(array, "gx", pairs)


def over_y(array, step, shards_y):
    return lax.ppermute(array, "gy", [(i, (i + step) % shards_y) for i in range(shards_y)])


def body(flow, spectral_weight, conv_weight, bias):
    cells_x, cells_y, cells_z, channels = flow.shape
    shards_x, shards_y = lax.axis_size("gx"), lax.axis_size("gy")
    items = spectral_weight.shape[0]
    pairs = items // 2
    if items % 2 or shards_y < 2:
        spectral = split_pair_spectral(flow, spectral_weight)
        convolved = split_pair_convolve(flow, conv_weight)
        return jax.nn.gelu(spectral + convolved + bias, approximate=True).astype(jnp.bfloat16)

    barrier = lax.optimization_barrier
    inner = max(d for d in range(1, shards_x + 1) if shards_x % d == 0 and d * d <= shards_x)
    outer = shards_x // inner
    shards = (outer, inner)
    me = lax.axis_index(("gy", "gx")).astype(jnp.int32).reshape(1)
    sizes = (shards_x, shards_y, pairs, cells_y, cells_z)
    full_x = cells_x * shards_x
    weight = spectral_weight.reshape(items, MX, channels, channels)
    early = pairs // 4

    table = jnp.asarray(forward_yz_table(*sizes))
    columns = flow.reshape(cells_x, cells_y * cells_z, channels)
    order = far_first(outer)
    cut = (outer + 1) // 2
    pieces = [piece for piece in (order[:cut], order[cut:]) if piece]
    arrived = [[] for _ in pieces]
    for step in range(1, shards_y):
        sent = forward_yz(me, table, columns, step, shards, shards_y, pieces)
        sent, columns, weight = barrier((sent, columns, weight))
        for into, piece in zip(arrived, sent):
            into.append(over_y(piece, step, shards_y))
    loaded = [preload(weight, 0, early)] if early else []
    loaded, columns = barrier((loaded, columns))
    kept = forward_yz(me, table, columns, 0, shards, shards_y, pieces, cells_z)
    kept, (first, last, *ends) = kept[: len(pieces)], kept[len(pieces) :]
    if shards_y == 2:
        front = back = over_y(ends[0], 1, shards_y)
    else:
        front, back = neighbours(*ends, "gy")

    by_outer = []
    for piece, own, parts in zip(pieces, kept, arrived):
        for step, total in zip(piece, add_pieces(own, parts)):
            by_outer.append(exchange(total, step, shards, True) if step else total)
    if early:
        loaded.append(preload(weight, early, early))
    by_outer, loaded, weight = barrier((by_outer[::-1], loaded, weight))
    by_inner = regroup(me, by_outer[::-1], shards, True)
    by_inner, weight = barrier((by_inner, weight))
    rows = [
        exchange(by_inner[step], step, shards, False) if step else by_inner[0]
        for step in far_first(inner)
    ]
    if early:
        loaded.append(preload(weight, 2 * early, max(early // 2, 1)))

    rows, loaded, first, last, front, back = barrier((rows, loaded, first, last, front, back))
    paired, other = halo_planes(me, first, last, front, back, shards, shards_y)
    paired, other = with_neighbour(paired, 0, "gx"), with_neighbour(other, 1, "gx")
    returned = mixing(
        me,
        rows,
        jnp.asarray(forward_x_table(full_x)),
        jnp.asarray(backward_x_table(full_x)),
        weight,
        loaded,
        shards,
    )
    returned, other, paired = barrier((list(returned), other, paired))
    halos = (paired, other, front, back)
    width = 2 if cells_x % 2 == 0 else 1
    convolved = [
        convolution(me, x, width, flow, halos, conv_weight, shards, shards_y)
        for x in range(0, cells_x, width)
    ]

    returned = [
        exchange(returned[step], step, shards, False) if step else returned[0]
        for step in far_first(inner)
    ]
    returned, convolved[0] = barrier((returned, convolved[0]))
    returned = regroup(me, returned, shards, False)
    returned = [
        exchange(returned[step], step, shards, True) if step else returned[0]
        for step in far_first(outer)
    ]
    by_slot = dict(zip(far_first(outer), returned))
    bundles = [
        bundle([by_slot[slot] for slot in slots]) if slots[1:] else by_slot[slots[0]][None]
        for slots in bundled_slots(outer)
    ]
    others = []
    for step in range(1, shards_y):
        others += [over_y(part, step, shards_y) for part in bundles]
    table = jnp.asarray(backward_yz_table(*sizes))
    bias = bias.reshape(1, channels)
    return final(me, table, [*returned, *others], convolved, bias, shards, shards_y)


def solution(mesh):
    placed = (P("gx", "gy", None, None), P(("gy", "gx"), None, None, None, None), P(), P())
    return jax.shard_map(
        body, mesh=mesh, in_specs=placed, out_specs=P("gx", "gy", None, None), check_vma=False
    )
```

```python
import functools
import math

import jax
import jax.numpy as jnp
import numpy as np
from jax import lax
from jax.experimental import pallas as pl
from jax.experimental.pallas import tpu as pltpu
from jax.sharding import PartitionSpec as P

MX = 64
MY = 16
MZ = 16


def frequencies(mode_count):
    position = np.arange(mode_count)
    return np.where(position < mode_count // 2, position, position - mode_count)


def wave(first, second, length, factor):
    turns = (np.asarray(first)[:, None] * np.asarray(second)[None, :]) % length
    angles = turns * (2.0 * math.pi / length)
    return (np.cos(angles) + 1j * np.sin(angles)) * factor


def rounded(values):
    return values.astype(np.float32).astype(jnp.bfloat16).astype(np.float64)


def item_modes(shards_x, shards_y, pairs):
    index = np.arange(shards_y * shards_x * pairs).reshape(shards_y, shards_x, pairs)
    return index // MZ, index % MZ


def forward_yz_table(shards_x, shards_y, pairs, cells_y, cells_z):
    full_y = shards_y * cells_y
    turn_z = wave(np.arange(MZ), np.arange(cells_z), cells_z, cells_z**-0.5)
    turn_z = rounded(turn_z.real) - 1j * rounded(turn_z.imag)
    turn_y = np.conj(wave(frequencies(MY), np.arange(full_y), full_y, full_y**-0.5))
    mode_y, mode_z = item_modes(shards_x, shards_y, pairs)
    table = np.empty((shards_y, shards_y, shards_x, pairs, 2, cells_y, cells_z), np.float32)
    for own in range(shards_y):
        rows = turn_y[:, own * cells_y : (own + 1) * cells_y]
        product = rows[mode_y][..., :, None] * turn_z[mode_z][..., None, :]
        table[own, :, :, :, 0] = product.real
        table[own, :, :, :, 1] = product.imag
    return table.reshape(shards_y, -1, cells_y * cells_z).astype(jnp.bfloat16)


def backward_yz_table(shards_x, shards_y, pairs, cells_y, cells_z):
    full_y = shards_y * cells_y
    turn_z = wave(np.arange(MZ), np.arange(cells_z), cells_z, MZ**-0.5)
    turn_z = rounded(turn_z.real) + 1j * rounded(turn_z.imag)
    turn_y = wave(frequencies(MY), np.arange(full_y), full_y, MY**-0.5)
    mode_y, mode_z = item_modes(shards_x, shards_y, pairs)
    table = np.empty((shards_y, shards_y, cells_y, cells_z, shards_x, pairs, 2), np.float32)
    for own in range(shards_y):
        rows = turn_y[:, own * cells_y : (own + 1) * cells_y]
        product = rows[mode_y][..., :, None] * turn_z[mode_z][..., None, :]
        product = np.moveaxis(product, (3, 4), (1, 2))
        table[own, ..., 0] = product.real
        table[own, ..., 1] = -product.imag
    return table.reshape(shards_y**2, cells_y * cells_z, -1).astype(jnp.bfloat16)


def forward_x_table(full_x):
    turn = np.conj(wave(frequencies(MX), np.arange(full_x), full_x, full_x**-0.5))
    parts = np.empty((2, MX, 2, 2, full_x), np.float32)
    parts[0, :, 0, 0], parts[0, :, 0, 1] = turn.real, -turn.imag
    parts[0, :, 1, 0], parts[0, :, 1, 1] = turn.imag, turn.real
    parts[1, :, 0] = -parts[0, :, 1]
    parts[1, :, 1] = parts[0, :, 0]
    return parts.reshape(2 * MX * 2, 2 * full_x).astype(jnp.bfloat16)


def backward_x_table(full_x):
    turn = wave(frequencies(MX), np.arange(full_x), full_x, MX**-0.5).T
    parts = np.empty((2, full_x, MX, 2), np.float32)
    parts[0, :, :, 0], parts[0, :, :, 1] = turn.real, -turn.imag
    parts[1, :, :, 0], parts[1, :, :, 1] = turn.imag, turn.real
    return parts.reshape(2 * full_x, MX * 2).astype(jnp.bfloat16)


def dot(left, right):
    return jnp.dot(left, right, preferred_element_type=jnp.float32)


def peer(index, step, count):
    if count & (count - 1) == 0:
        return index ^ step
    return lax.rem(index + step, count)


def origin(index, step, count):
    if count & (count - 1) == 0:
        return index ^ step
    return lax.rem(index + (count - step), count)


def far_first(count):
    return list(range(count - 1, -1, -1))


def place(me, shards):
    outer, inner = shards
    across = lax.rem(me, outer * inner)
    return lax.div(me, outer * inner), lax.div(across, inner), lax.rem(across, inner)


def in_vmem(count):
    return [pl.BlockSpec(memory_space=pltpu.VMEM)] * count


IN_SMEM = pl.BlockSpec(memory_space=pltpu.SMEM)


def transform(table, flow_at, cells_x, refs, pieces):
    inner, _, rows, channels = refs[0].shape[1:]
    block = inner * rows
    width = 2 if cells_x % 2 == 0 else 1
    for x in range(0, cells_x, width):
        columns = [flow_at(x + i) for i in range(width)]
        result = dot(table, jnp.concatenate(columns, axis=1))
        for i in range(width):
            part = result[:, i * channels : (i + 1) * channels]
            at = 0
            for ref, piece in zip(refs, pieces):
                for slot in range(len(piece)):
                    value = part[at : at + block].reshape(inner, rows, channels)
                    ref[slot, :, x + i] = value.astype(ref.dtype)
                    at += block


def send_kernel(shards, shards_y, pieces, step, me_ref, table_ref, flow_ref, *refs):
    *refs, table, flow, table_sems, flow_sems = refs
    refs, plane_refs = refs[: len(pieces)], refs[len(pieces) :]
    cells_x = flow.shape[0]
    outer, _ = shards
    block = refs[0].shape[1] * refs[0].shape[3]
    own_y, own, _ = place(me_ref[0], shards)
    owner = lax.rem(own_y + step, shards_y)
    copies = []
    for i, other in enumerate(step for piece in pieces for step in piece):
        start = (owner * outer + peer(own, other, outer)) * block
        source = table_ref.at[own_y, pl.ds(pl.multiple_of(start, block), block)]
        copies.append(
            pltpu.make_async_copy(source, table.at[pl.ds(i * block, block)], table_sems.at[i])
        )
    loads = [
        pltpu.make_async_copy(flow_ref.at[x], flow.at[x], flow_sems.at[x])
        for x in range(cells_x)
    ]
    for copy in copies + loads:
        copy.start()
    for copy in copies:
        copy.wait()

    def flow_at(x):
        loads[x].wait()
        return flow[x]

    transform(table[...], flow_at, cells_x, refs, pieces)
    if plane_refs:
        even = is_even(me_ref[0], shards)
        plane_refs[0][...] = flow[jnp.where(even, cells_x - 1, 0)]
        plane_refs[1][...] = flow[jnp.where(even, 0, cells_x - 1)]


def is_even(me, shards):
    _, own_outer, own_inner = place(me, shards)
    return lax.rem(own_outer * shards[1] + own_inner, 2) == 0


def keep_kernel(shards, shards_y, pieces, me_ref, table_ref, flow_ref, *refs):
    refs, (low, high) = refs[: len(pieces)], refs[len(pieces) :]
    cells_x, positions, _ = flow_ref.shape
    outer, _ = shards
    block = refs[0].shape[1] * refs[0].shape[3]
    own_y, own, _ = place(me_ref[0], shards)
    tables = []
    for other in (step for piece in pieces for step in piece):
        start = (own_y * outer + peer(own, other, outer)) * block
        tables.append(table_ref[own_y, pl.ds(pl.multiple_of(start, block), block), :])
    transform(
        jnp.concatenate(tables, axis=0), lambda x: flow_ref[x], cells_x, refs, pieces
    )
    cells_z = low.shape[1]
    low[...] = flow_ref[:, pl.ds(0, cells_z)]
    high[...] = flow_ref[:, pl.ds(positions - cells_z, cells_z)]


def forward_yz(me, table, flow, step, shards, shards_y, pieces, cells_z=0):
    cells_x, positions, channels = flow.shape
    outer, inner = shards
    rows = table.shape[1] // shards_y
    unit = (inner, cells_x, rows // (outer * inner), channels)
    dtype = jnp.bfloat16 if step else jnp.float32
    shapes = [jax.ShapeDtypeStruct((len(piece), *unit), dtype) for piece in pieces]
    if step == 1:
        shapes += [jax.ShapeDtypeStruct((positions, channels), flow.dtype)] * 2
    if step:
        kernel = functools.partial(send_kernel, shards, shards_y, pieces, step)
        specs = [pl.BlockSpec(memory_space=pltpu.HBM)] * 2
        scratch = [
            pltpu.VMEM((rows, positions), table.dtype),
            pltpu.VMEM(flow.shape, flow.dtype),
            pltpu.SemaphoreType.DMA((outer,)),
            pltpu.SemaphoreType.DMA((cells_x,)),
        ]
    else:
        kernel = functools.partial(keep_kernel, shards, shards_y, pieces)
        specs, scratch = in_vmem(2), []
        edge = jax.ShapeDtypeStruct((cells_x, cells_z, channels), flow.dtype)
        shapes += [edge] * 2
    return pl.pallas_call(
        kernel,
        in_specs=[IN_SMEM] + specs,
        out_specs=in_vmem(len(shapes)),
        out_shape=shapes,
        scratch_shapes=scratch,
        compiler_params=pltpu.CompilerParams(vmem_limit_bytes=(56 if step else 10) << 20),
        cost_estimate=pl.CostEstimate(
            flops=2 * rows * positions * cells_x * channels,
            bytes_accessed=2 * positions * (rows + cells_x * channels),
            transcendentals=0,
        ),
    )(me, table, flow)


def add_kernel(count, *refs):
    out_refs = refs[count:]
    for slot, out_ref in enumerate(out_refs):
        total = refs[0][slot]
        for ref in refs[1:count]:
            total = total + ref[slot].astype(jnp.float32)
        out_ref[...] = total.astype(out_ref.dtype)


def add_pieces(own, arrived):
    slots, *unit = own.shape
    return pl.pallas_call(
        functools.partial(add_kernel, 1 + len(arrived)),
        in_specs=in_vmem(1 + len(arrived)),
        out_specs=in_vmem(slots),
        out_shape=[jax.ShapeDtypeStruct(unit, jnp.bfloat16)] * slots,
        cost_estimate=pl.CostEstimate(flops=own.size, bytes_accessed=0, transcendentals=0),
        compiler_params=pltpu.CompilerParams(vmem_limit_bytes=10 << 20),
    )(own, *arrived)


def regroup_kernel(shards, chosen, me_ref, *refs):
    _, _, own = place(me_ref[0], shards)
    count = refs[0].shape[0]
    in_refs, out_refs = refs[:-count], refs[-count:]
    for step, out_ref in enumerate(out_refs):
        at = peer(own, step, count) if chosen else step
        for number, in_ref in enumerate(in_refs):
            out_ref[far_first(len(in_refs))[number]] = in_ref[at]


def regroup(me, arrays, shards, chosen):
    count, *unit = arrays[0].shape
    return pl.pallas_call(
        functools.partial(regroup_kernel, shards, chosen),
        in_specs=[IN_SMEM] + in_vmem(len(arrays)),
        out_specs=in_vmem(count),
        out_shape=[jax.ShapeDtypeStruct((len(arrays), *unit), arrays[0].dtype)] * count,
        cost_estimate=pl.CostEstimate(
            flops=arrays[0].size, bytes_accessed=0, transcendentals=0
        ),
        compiler_params=pltpu.CompilerParams(vmem_limit_bytes=10 << 20),
    )(me, *arrays)


def edge_kernel(
    choose, shards, me_ref, paired_ref, other_ref, low_ref, high_ref, out_ref
):
    cells_x, cells_z, _ = low_ref.shape
    rows = paired_ref.shape[0]
    own_y, _, _ = place(me_ref[0], shards)
    is_low = choose(own_y)
    even = is_even(me_ref[0], shards)
    start = pl.multiple_of(jnp.where(is_low, 0, rows - cells_z), cells_z)
    paired, other = (ref[pl.ds(start, cells_z), :] for ref in (paired_ref, other_ref))
    out_ref[0] = jnp.where(even, other, paired)
    out_ref[1 + cells_x] = jnp.where(even, paired, other)

    @pl.when(is_low)
    def _():
        out_ref[1 : 1 + cells_x] = low_ref[...]

    @pl.when(jnp.logical_not(is_low))
    def _():
        out_ref[1 : 1 + cells_x] = high_ref[...]


def y_edge(me, paired, other, low, high, shards, choose):
    cells_x, cells_z, channels = low.shape
    return pl.pallas_call(
        functools.partial(edge_kernel, choose, shards),
        in_specs=[IN_SMEM] + in_vmem(4),
        out_specs=in_vmem(1)[0],
        out_shape=jax.ShapeDtypeStruct((cells_x + 2, cells_z, channels), low.dtype),
        compiler_params=pltpu.CompilerParams(vmem_limit_bytes=10 << 20),
    )(me, paired, other, low, high)


def preload_kernel(first, weight_ref, out_ref, sems):
    count = out_ref.shape[0]
    pieces = sems.shape[0] // count
    modes = out_ref.shape[1] // pieces
    copies = []
    for i in range(count * pieces):
        item, at = i // pieces, pl.ds(i % pieces * modes, modes)
        copies.append(
            pltpu.make_async_copy(
                weight_ref.at[first + item, at], out_ref.at[item, at], sems.at[i]
            )
        )
    for copy in copies:
        copy.start()
    for copy in copies:
        copy.wait()


def preload(weight, pair, count):
    shape = (2 * count, *weight.shape[1:])
    return pl.pallas_call(
        functools.partial(preload_kernel, 2 * pair),
        in_specs=[pl.BlockSpec(memory_space=pltpu.HBM)],
        out_specs=in_vmem(1)[0],
        out_shape=jax.ShapeDtypeStruct(shape, weight.dtype),
        scratch_shapes=[pltpu.SemaphoreType.DMA((2 * 2 * count,))],
        compiler_params=pltpu.CompilerParams(vmem_limit_bytes=36 << 20),
        cost_estimate=pl.CostEstimate(
            flops=0, bytes_accessed=2 * math.prod(shape), transcendentals=0
        ),
    )(weight)


def mixing_kernel(shards, loaded, me_ref, *refs):
    outer, inner = shards
    row_refs, refs = refs[:inner], refs[inner:]
    forward_ref, backward_ref, weight_ref, *refs = refs
    loaded_refs, refs = refs[:loaded], refs[loaded:]
    loaded = sum(ref.shape[0] // 2 for ref in loaded_refs)
    out_refs, (held, sems, wide, left, mixed) = refs[:inner], refs[inner:]

    channels = wide.shape[1]
    _, cells_x, item_rows, _ = row_refs[0].shape
    pairs = item_rows // 2
    full_x = outer * inner * cells_x
    half = channels // 2
    span = 2 * MX
    block = cells_x * item_rows
    _, own_outer, own_inner = place(me_ref[0], shards)

    def copy(pair):
        slot = pair - loaded
        return pltpu.make_async_copy(
            weight_ref.at[pl.ds(2 * pair, 2)], held.at[slot], sems.at[slot]
        )

    for pair in range(loaded, pairs):
        copy(pair).start()

    def rows_of(outer_index, inner_index):
        start = pl.multiple_of((outer_index * inner + inner_index) * block, block)
        return pl.ds(start, block)

    for number, step in enumerate(far_first(inner)):
        source = origin(own_inner, step, inner)
        for slot in range(outer):
            value = row_refs[number][slot].reshape(block, channels)
            at = rows_of(origin(own_outer, slot, outer), source)
            wide[at, :] = value.astype(jnp.float32)
    low = lax.broadcasted_iota(jnp.int32, (span, channels), 1) < half
    for pair in range(pairs):
        columns = [wide[pl.ds(2 * pair + p, full_x, stride=item_rows), :] for p in range(2)]
        columns = jnp.concatenate(columns, axis=0).astype(jnp.bfloat16)
        both = dot(forward_ref[...], columns)
        value, turned = both[:span], both[span:]
        first = jnp.where(low, value, pltpu.roll(turned, half, axis=1))
        second = jnp.where(low, pltpu.roll(value, half, axis=1), turned)
        left[pl.ds(pair * span, span), :channels] = first.astype(left.dtype)
        left[pl.ds(pair * span, span), channels:] = second.astype(left.dtype)

    group = 16
    row = lax.broadcasted_iota(jnp.int32, (group, channels), 0) // 2

    def mix(pair, tile_of):
        for step in range(span // group):
            start = pl.multiple_of(pair * span + step * group, group)
            lhs = left[pl.ds(start, group), :]
            gathered = jnp.zeros((group, channels), jnp.float32)
            for i in range(0, group // 2, 2):
                mode = step * (group // 2) + i
                tiles = [
                    jnp.concatenate([tile_of(h, mode + k) for h in range(2)], axis=0)
                    for k in range(2)
                ]
                product = dot(lhs, jnp.concatenate(tiles, axis=1))
                for k in range(2):
                    gathered = jnp.where(
                        row == i + k, product[:, k * channels : (k + 1) * channels], gathered
                    )
            mixed[pl.ds(start, group), :] = gathered.astype(mixed.dtype)

    pair = 0
    for ref in loaded_refs:
        count = ref.shape[0] // 2

        def ready(i, carry, ref=ref, pair=pair):
            mix(pair + i, lambda h, mode: ref[2 * i + h, mode])
            return carry

        lax.fori_loop(0, count, ready, 0)
        pair += count

    def streamed(pair, carry):
        copy(pair).wait()
        mix(pair, lambda h, mode: held[pair - loaded, h, mode])
        return carry

    lax.fori_loop(loaded, pairs, streamed, 0)

    for pair in range(pairs):
        result = dot(backward_ref[...], mixed[pl.ds(pair * span, span), :])
        for p in range(2):
            wide[pl.ds(2 * pair + p, full_x, stride=item_rows), :] = result[
                p * full_x : (p + 1) * full_x
            ]
    for step in range(inner):
        target = peer(own_inner, step, inner)
        for slot in range(outer):
            value = wide[rows_of(peer(own_outer, slot, outer), target), :]
            value = value.reshape(cells_x, item_rows, channels)
            out_refs[step][slot] = value.astype(out_refs[step].dtype)


def mixing(me, rows, forward_x, backward_x, weight, loaded, shards):
    outer, inner = shards
    _, cells_x, item_rows, channels = rows[0].shape
    pairs = item_rows // 2
    row_count = outer * inner * cells_x * item_rows
    streamed = pairs - sum(part.shape[0] // 2 for part in loaded)
    return pl.pallas_call(
        functools.partial(mixing_kernel, shards, len(loaded)),
        in_specs=[IN_SMEM]
        + in_vmem(inner + 2)
        + [pl.BlockSpec(memory_space=pltpu.HBM)]
        + in_vmem(len(loaded)),
        out_specs=in_vmem(inner),
        out_shape=[jax.ShapeDtypeStruct(rows[0].shape, jnp.bfloat16)] * inner,
        scratch_shapes=[
            pltpu.VMEM((streamed, 2, *weight.shape[1:]), weight.dtype),
            pltpu.SemaphoreType.DMA((streamed,)),
            pltpu.VMEM((row_count, channels), jnp.float32),
            pltpu.VMEM((pairs * 2 * MX, 2 * channels), jnp.bfloat16),
            pltpu.VMEM((pairs * 2 * MX, channels), jnp.bfloat16),
        ],
        compiler_params=pltpu.CompilerParams(vmem_limit_bytes=20 << 20),
        cost_estimate=pl.CostEstimate(
            flops=8 * weight.size, bytes_accessed=2 * weight.size, transcendentals=0
        ),
    )(me, *rows, forward_x, backward_x, weight, *loaded)


def convolution_kernel(x, cells_x, width, shards, shards_y, me_ref, *refs):
    flow_ref, paired_ref, other_ref, front_ref, back_ref, kernel_ref, out_ref, padded = refs
    _, cells_y, cells_z, channels = out_ref.shape
    own_y, _, _ = place(me_ref[0], shards)
    even = is_even(me_ref[0], shards)
    for plane in range(width + 2):
        p = x + plane - 1
        row = front_ref[p + 1]
        padded[plane, 0] = jnp.where(own_y > 0, row, jnp.zeros_like(row))
        row = back_ref[p + 1]
        last = own_y == shards_y - 1
        padded[plane, cells_y + 1] = jnp.where(last, jnp.zeros_like(row), row)
        if 0 <= p < cells_x:
            padded[plane, 1 : cells_y + 1] = flow_ref[p]
        else:
            use_paired = jnp.logical_not(even) if p < 0 else even

            @pl.when(use_paired)
            def _(plane=plane):
                padded[plane, 1 : cells_y + 1] = paired_ref[...]

            @pl.when(jnp.logical_not(use_paired))
            def _(plane=plane):
                padded[plane, 1 : cells_y + 1] = other_ref[...]

    rows = 16 if cells_y % 16 == 0 else 1
    columns = [(k, d) for k in range(width) for d in range(3)]
    columns = [columns[i : i + 2] for i in range(0, len(columns), 2)]
    none = jnp.zeros((channels, channels), kernel_ref.dtype)

    def chunk(index, carry):
        y = index * rows
        products = {}
        for group in columns:
            blocks, kernels = [], []
            for p in range(width + 2):
                if not any(0 <= p - k < 3 for k, _ in group):
                    continue
                for b in range(3):
                    part = padded[p, pl.ds(y + b, rows)]
                    blocks.append(part.reshape(rows * cells_z, channels))
                    parts = [
                        kernel_ref[p - k, b, d] if 0 <= p - k < 3 else none for k, d in group
                    ]
                    kernels.append(jnp.concatenate(parts, axis=1))
            product = dot(jnp.concatenate(blocks, axis=1), jnp.concatenate(kernels, axis=0))
            for i, column in enumerate(group):
                part = product[:, i * channels : (i + 1) * channels]
                products[column] = part.reshape(rows, cells_z, channels)
        z = lax.broadcasted_iota(jnp.int32, (rows, cells_z, channels), 1)
        for k in range(width):
            before = jnp.where(z == 0, 0.0, pltpu.roll(products[k, 0], 1, axis=1))
            after = pltpu.roll(products[k, 2], cells_z - 1, axis=1)
            after = jnp.where(z == cells_z - 1, 0.0, after)
            total = before + products[k, 1] + after
            out_ref[k, pl.ds(y, rows)] = total.astype(out_ref.dtype)
        return carry

    lax.fori_loop(0, cells_y // rows, chunk, 0)


def convolution(me, x, width, flow, halos, kernel, shards, shards_y):
    cells_x, cells_y, cells_z, channels = flow.shape
    shape = (width, cells_y, cells_z, channels)
    return pl.pallas_call(
        functools.partial(convolution_kernel, x, cells_x, width, shards, shards_y),
        in_specs=[IN_SMEM] + in_vmem(2 + len(halos)),
        out_specs=in_vmem(1)[0],
        out_shape=jax.ShapeDtypeStruct(shape, jnp.bfloat16),
        scratch_shapes=[pltpu.VMEM((width + 2, cells_y + 2, cells_z, channels), flow.dtype)],
        compiler_params=pltpu.CompilerParams(vmem_limit_bytes=14 << 20),
        cost_estimate=pl.CostEstimate(
            flops=3 * 27 * width * cells_y * cells_z * channels * channels,
            bytes_accessed=10 * cells_y * cells_z * channels,
            transcendentals=0,
        ),
    )(me, flow, *halos, kernel)


def bundled_slots(count):
    slots = [0] + far_first(count)[:-1]
    cut = (count + 1) // 2
    return [part for part in (slots[:cut], slots[cut:]) if part]


def bundle_kernel(*refs):
    *in_refs, out_ref = refs
    for i, ref in enumerate(in_refs):
        out_ref[i] = ref[...]


def bundle(arrays):
    shape = (len(arrays), *arrays[0].shape)
    return pl.pallas_call(
        bundle_kernel,
        in_specs=in_vmem(len(arrays)),
        out_specs=in_vmem(1)[0],
        out_shape=jax.ShapeDtypeStruct(shape, arrays[0].dtype),
        cost_estimate=pl.CostEstimate(
            flops=math.prod(shape), bytes_accessed=0, transcendentals=0
        ),
        compiler_params=pltpu.CompilerParams(vmem_limit_bytes=10 << 20),
    )(*arrays)


def gather_pieces(me, shards, pieces, held):
    outer, inner = shards
    _, own_outer, own_inner = place(me, shards)
    for number, slot, ref in pieces:
        cells_x, rows = ref.shape[1:3]
        source = (number * outer + origin(own_outer, slot, outer)) * inner
        for part in range(inner):
            at = (source + origin(own_inner, part, inner)) * rows
            for x in range(cells_x):
                held[x, pl.ds(pl.multiple_of(at, rows), rows), :] = ref[part, x]


def inverse(me, shards, shards_y, steps, table_ref, held, part, x, width, positions):
    own_y, _, _ = place(me, shards)
    columns = [held[x + i] for i in range(width)]
    depth = table_ref.shape[2]
    total = None
    for number, step in enumerate(steps):
        source = lax.rem(own_y + (shards_y - step), shards_y)
        rows = pl.ds(pl.multiple_of(part * positions, positions), positions)
        table = table_ref[own_y * shards_y + source, rows, :]
        block = [column[number * depth : (number + 1) * depth] for column in columns]
        product = dot(table, jnp.concatenate(block, axis=1))
        total = product if total is None else total + product
    return total


def own_part_kernel(shards, shards_y, me_ref, table_ref, *refs):
    *piece_refs, bias_ref, out_ref, held = refs
    cells_x, cells_y, cells_z, channels = out_ref.shape
    width = 2 if cells_x % 2 == 0 else 1
    count = -(-cells_x // width)
    piece_refs, convolved_refs = piece_refs[:-count], piece_refs[-count:]
    slots = far_first(shards[0])
    gather_pieces(me_ref[0], shards, [(0, *p) for p in zip(slots, piece_refs)], held)
    bias = bias_ref[...]
    rows = 4 if cells_y % 4 == 0 else 1
    positions = rows * cells_z

    def chunk(part, carry):
        for x in range(0, cells_x, width):
            total = inverse(
                me_ref[0], shards, shards_y, [0], table_ref, held, part, x, width, positions
            )
            for i in range(width):
                spectral = total[:, i * channels : (i + 1) * channels]
                convolved = convolved_refs[x // width][i, pl.ds(part * rows, rows)]
                value = spectral.reshape(rows, cells_z, channels) + convolved + bias
                out_ref[x + i, pl.ds(part * rows, rows)] = value
        return carry

    lax.fori_loop(0, cells_y // rows, chunk, 0)


def last_part_kernel(shards, shards_y, me_ref, table_ref, *refs):
    *bundle_refs, partial_ref, out_ref, held = refs
    cells_x, cells_y, cells_z, channels = out_ref.shape
    bundles = bundled_slots(shards[0])
    steps = list(range(1, shards_y))
    width = 2 if cells_x % 2 == 0 else 1
    part = pl.program_id(0)

    @pl.when(part == 0)
    def _():
        pieces = []
        for i, ref in enumerate(bundle_refs):
            number, bundle = divmod(i, len(bundles))
            pieces += [(number, slot, ref.at[j]) for j, slot in enumerate(bundles[bundle])]
        gather_pieces(me_ref[0], shards, pieces, held)

    for x in range(0, cells_x, width):
        total = inverse(
            me_ref[0], shards, shards_y, steps, table_ref, held, part, x, width,
            cells_y * cells_z,
        )
        for i in range(width):
            spectral = total[:, i * channels : (i + 1) * channels]
            value = partial_ref[x + i, pl.ds(part * cells_y, cells_y)]
            value = value + spectral.reshape(cells_y, cells_z, channels)
            out_ref[x + i] = jax.nn.gelu(value, approximate=True).astype(out_ref.dtype)


def own_part(me, table, pieces, convolved, bias, shards, shards_y):
    width, cells_y, cells_z, channels = convolved[0].shape
    shape = (width * len(convolved), cells_y, cells_z, channels)
    depth = table.shape[2]
    return pl.pallas_call(
        functools.partial(own_part_kernel, shards, shards_y),
        in_specs=[IN_SMEM] + in_vmem(2 + len(pieces) + len(convolved)),
        out_specs=in_vmem(1)[0],
        out_shape=jax.ShapeDtypeStruct(shape, jnp.float32),
        scratch_shapes=[pltpu.VMEM((shape[0], depth, channels), jnp.bfloat16)],
        compiler_params=pltpu.CompilerParams(vmem_limit_bytes=14 << 20),
        cost_estimate=pl.CostEstimate(
            flops=2 * math.prod(shape) * depth,
            bytes_accessed=6 * math.prod(shape),
            transcendentals=0,
        ),
    )(me, table, *pieces, *convolved, bias)


def last_part(me, table, pieces, partial, shards, shards_y):
    cells_x, cells_y, cells_z, channels = partial.shape
    parts = 2 if cells_y % 2 == 0 else 1
    block = (cells_x, cells_y // parts, cells_z, channels)
    depth = table.shape[2] * (shards_y - 1)
    return pl.pallas_call(
        functools.partial(last_part_kernel, shards, shards_y),
        grid_spec=pltpu.PrefetchScalarGridSpec(
            num_scalar_prefetch=1,
            grid=(parts,),
            in_specs=in_vmem(2 + len(pieces)),
            out_specs=pl.BlockSpec(block, lambda i, me: (0, i, 0, 0)),
            scratch_shapes=[pltpu.VMEM((cells_x, depth, channels), jnp.bfloat16)],
        ),
        out_shape=jax.ShapeDtypeStruct(partial.shape, jnp.bfloat16),
        compiler_params=pltpu.CompilerParams(vmem_limit_bytes=14 << 20),
        cost_estimate=pl.CostEstimate(
            flops=2 * partial.size * depth,
            bytes_accessed=6 * partial.size,
            transcendentals=partial.size,
        ),
    )(me, table, *pieces, partial)


def with_halo(array, sides, width):
    for axis, dim in sides:
        size, length = (lax.axis_size(axis), array.shape[dim])
        up = [(i, (i + 1) % size) for i in range(size - 1)]
        down = [(j, i) for i, j in up]
        last = lax.slice_in_dim(array, length - width, length, axis=dim)
        initial = lax.slice_in_dim(array, 0, width, axis=dim)
        before = lax.ppermute(last, axis, up)
        after = lax.ppermute(initial, axis, down)
        array = jnp.concatenate([before, array, after], axis=dim)
    return array


def signed_modes(mode_count):
    position = jnp.arange(mode_count, dtype=jnp.int32)
    return jnp.where(position < mode_count // 2, position, position - mode_count)


def angle_grid(first, second, length):
    phase_turns = first[:, None] * second[None, :] % length
    return phase_turns.astype(jnp.float32) * (2.0 * math.pi / length)


def real_table(first, second, length, factor):
    angles = angle_grid(first, second, length)
    return jnp.stack([jnp.cos(angles) * factor, -jnp.sin(angles) * factor])


def complex_table(first, second, length, factor, direction):
    angles = angle_grid(first, second, length)
    cosine = jnp.cos(angles) * factor
    sine_part = jnp.sin(angles) * factor
    return jnp.stack(
        [jnp.stack([cosine, direction * sine_part]), jnp.stack([-direction * sine_part, cosine])]
    )


def split_pair_spectral(flow_field, spectral_weight):
    highest = lax.Precision.HIGHEST
    cells_x, cells_y, cells_z, channels = flow_field.shape
    count_x = lax.axis_size("gx")
    count_y = lax.axis_size("gy")
    full_x = cells_x * count_x
    full_y = cells_y * count_y
    item_count = spectral_weight.shape[0]
    local_y = lax.axis_index("gy") * cells_y + jnp.arange(cells_y, dtype=jnp.int32)
    grid_x = jnp.arange(full_x, dtype=jnp.int32)
    grid_z = jnp.arange(cells_z, dtype=jnp.int32)
    modes_z = jnp.arange(MZ, dtype=jnp.int32)
    forward_z = real_table(grid_z, modes_z, cells_z, cells_z ** (-0.5)).astype(jnp.bfloat16)
    z_spectrum = jnp.einsum(
        "xyzc,pzk->pxykc", flow_field, forward_z, preferred_element_type=jnp.float32
    )
    columns = lax.all_to_all(
        z_spectrum.astype(jnp.bfloat16), "gy", split_axis=4, concat_axis=2, tiled=True
    ).astype(z_spectrum.dtype)
    whole_y = jnp.arange(full_y, dtype=jnp.int32)
    forward_full = complex_table(whole_y, signed_modes(MY), full_y, full_y ** (-0.5), -1.0)
    y_spectrum = jnp.einsum("pxykc,pqyj->qxjkc", columns, forward_full, precision=highest)
    owned = lax.all_to_all(
        y_spectrum.astype(jnp.bfloat16), "gy", split_axis=2, concat_axis=4, tiled=True
    ).astype(y_spectrum.dtype)
    owned_modes = owned.reshape(2, cells_x, count_x, item_count, channels // 2)
    gathered_rows = lax.all_to_all(
        owned_modes.astype(jnp.bfloat16), "gx", split_axis=2, concat_axis=1, tiled=True
    ).astype(owned_modes.dtype)
    gathered_rows = gathered_rows.reshape(2, full_x, item_count, channels // 2)
    forward_x = complex_table(grid_x, signed_modes(MX), full_x, full_x ** (-0.5), -1.0)
    x_spectrum = jnp.einsum("pxjc,pqxm->qmjc", gathered_rows, forward_x, precision=highest).astype(
        jnp.bfloat16
    )
    products = jnp.einsum(
        "pmjc,jmqco->pqmjo", x_spectrum, spectral_weight, preferred_element_type=jnp.float32
    )
    mixed_modes = jnp.stack([products[0, 0] - products[1, 1], products[0, 1] + products[1, 0]])
    backward_x = complex_table(signed_modes(MX), grid_x, full_x, MX ** (-0.5), 1.0)
    inverse_x = jnp.einsum("pmjc,pqmx->qxjc", mixed_modes, backward_x, precision=highest)
    inverse_x = inverse_x.reshape(2, full_x, 1, item_count, channels)
    returned = lax.all_to_all(
        inverse_x.astype(jnp.bfloat16), "gx", split_axis=1, concat_axis=2, tiled=True
    ).astype(inverse_x.dtype)
    band_rows = MY // count_y
    summed = returned.reshape(2, cells_x, band_rows * MZ, 2, channels).sum(axis=3)
    summed = summed.reshape(2, cells_x, band_rows, MZ, channels)
    coefficients = lax.all_gather(summed.astype(jnp.bfloat16), "gy", axis=2, tiled=True).astype(
        summed.dtype
    )
    backward_y = complex_table(signed_modes(MY), local_y, full_y, MY ** (-0.5), 1.0)
    y_inverse = jnp.einsum("pxjkc,pqjy->qxykc", coefficients, backward_y, precision=highest).astype(
        jnp.bfloat16
    )
    backward_z = real_table(modes_z, grid_z, cells_z, MZ ** (-0.5)).astype(jnp.bfloat16)
    return jnp.einsum("pxykc,pkz->xyzc", y_inverse, backward_z, preferred_element_type=jnp.float32)


def split_pair_convolve(flow_field, conv_weight):
    cells_x, cells_y, cells_z, channels = flow_field.shape
    padded = with_halo(flow_field, (("gx", 0), ("gy", 1)), 1)
    padded = jnp.pad(padded, ((0, 0), (0, 0), (1, 1), (0, 0)))
    stacked = jnp.concatenate(
        [padded[:, :, 0:cells_z], padded[:, :, 1 : cells_z + 1], padded[:, :, 2 : cells_z + 2]],
        axis=3,
    )
    kernel = conv_weight.reshape(3, 3, 3 * channels, channels)
    accumulated = jnp.zeros((cells_x, cells_y, cells_z, channels), jnp.float32)
    for shift_x in range(3):
        for shift_y in range(3):
            accumulated = accumulated + jnp.dot(
                stacked[shift_x : shift_x + cells_x, shift_y : shift_y + cells_y],
                kernel[shift_x, shift_y],
                preferred_element_type=jnp.float32,
            )
    return accumulated


def neighbours(first, last, axis):
    size = lax.axis_size(axis)
    up = [(i, i + 1) for i in range(size - 1)]
    down = [(i + 1, i) for i in range(size - 1)]
    return lax.ppermute(last, axis, up), lax.ppermute(first, axis, down)


def with_neighbour(array, start, axis):
    size = lax.axis_size(axis)
    pairs = [(i, i + 1) for i in range(start, size - 1, 2)]
    return lax.ppermute(array, axis, pairs + [(j, i) for i, j in pairs])


def exchange(array, step, shards, along_outer):
    outer, inner = shards
    pairs = []
    for i in range(outer * inner):
        a, b = divmod(i, inner)
        count, own = (outer, a) if along_outer else (inner, b)
        to = own ^ step if count & (count - 1) == 0 else (own + step) % count
        pairs.append((i, to * inner + b if along_outer else a * inner + to))
    return lax.ppermute(array, "gx", pairs)


def over_y(array, step, shards_y):
    return lax.ppermute(array, "gy", [(i, (i + step) % shards_y) for i in range(shards_y)])


def body(flow, spectral_weight, conv_weight, bias):
    cells_x, cells_y, cells_z, channels = flow.shape
    shards_x, shards_y = lax.axis_size("gx"), lax.axis_size("gy")
    items = spectral_weight.shape[0]
    pairs = items // 2
    if items % 2 or shards_y < 2:
        spectral = split_pair_spectral(flow, spectral_weight)
        convolved = split_pair_convolve(flow, conv_weight)
        return jax.nn.gelu(spectral + convolved + bias, approximate=True).astype(jnp.bfloat16)

    barrier = lax.optimization_barrier
    inner = max(d for d in range(1, shards_x + 1) if shards_x % d == 0 and d * d <= shards_x)
    outer = shards_x // inner
    shards = (outer, inner)
    me = lax.axis_index(("gy", "gx")).astype(jnp.int32).reshape(1)
    sizes = (shards_x, shards_y, pairs, cells_y, cells_z)
    full_x = cells_x * shards_x
    weight = spectral_weight.reshape(items, MX, channels, channels)
    early = pairs // 4

    table = jnp.asarray(forward_yz_table(*sizes))
    columns = flow.reshape(cells_x, cells_y * cells_z, channels)
    order = far_first(outer)
    cut = (outer + 1) // 2
    pieces = [piece for piece in (order[:cut], order[cut:]) if piece]
    arrived = [[] for _ in pieces]
    for step in range(1, shards_y):
        sent = forward_yz(me, table, columns, step, shards, shards_y, pieces)
        sent, columns, weight = barrier((sent, columns, weight))
        for into, piece in zip(arrived, sent):
            into.append(over_y(piece, step, shards_y))
        if step == 1:
            ends = sent[len(pieces) :]
            planes = [with_neighbour(end, start, "gx") for start, end in enumerate(ends)]
    loaded = [preload(weight, 0, early // 2)] if early > 1 else []
    loaded, columns = barrier((loaded, columns))
    kept = forward_yz(me, table, columns, 0, shards, shards_y, pieces, cells_z)
    kept, (low, high) = kept[: len(pieces)], kept[len(pieces) :]

    by_outer = []
    for piece, own, parts in zip(pieces, kept, arrived):
        for step, total in zip(piece, add_pieces(own, parts)):
            by_outer.append(exchange(total, step, shards, True) if step else total)
    if early:
        loaded.append(preload(weight, early // 2, early))
    by_outer, loaded, weight = barrier((by_outer[::-1], loaded, weight))
    by_inner = regroup(me, by_outer[::-1], shards, True)
    by_inner, weight = barrier((by_inner, weight))
    rows = [
        exchange(by_inner[step], step, shards, False) if step else by_inner[0]
        for step in far_first(inner)
    ]
    if early:
        loaded.append(preload(weight, early + early // 2, early))

    rows, loaded, planes = barrier((rows, loaded, planes))
    if shards_y == 2:
        edge = y_edge(me, *planes, low, high, shards, lambda own: own > 0)
        front = back = over_y(edge, 1, shards_y)
    else:
        ends = [
            y_edge(me, *planes, low, high, shards, lambda own, limit=limit: own < limit)
            for limit in (shards_y, 0)
        ]
        front, back = neighbours(*ends, "gy")
    returned = mixing(
        me,
        rows,
        jnp.asarray(forward_x_table(full_x)),
        jnp.asarray(backward_x_table(full_x)),
        weight,
        loaded,
        shards,
    )
    returned, front, back = barrier((list(returned), front, back))
    planes = [plane.reshape(cells_y, cells_z, channels) for plane in planes]
    halos = (*planes, front, back)
    width = 2 if cells_x % 2 == 0 else 1
    convolved = [
        convolution(me, x, width, flow, halos, conv_weight, shards, shards_y)
        for x in range(0, cells_x, width)
    ]

    returned = [
        exchange(returned[step], step, shards, False) if step else returned[0]
        for step in far_first(inner)
    ]
    returned, convolved[0] = barrier((returned, convolved[0]))
    returned = regroup(me, returned, shards, False)
    returned = [
        exchange(returned[step], step, shards, True) if step else returned[0]
        for step in far_first(outer)
    ]
    returned[0], convolved[-1] = barrier((returned[0], convolved[-1]))
    by_slot = dict(zip(far_first(outer), returned))
    bundles = [bundle([by_slot[slot] for slot in slots]) for slots in bundled_slots(outer)]
    others = []
    for step in range(1, shards_y):
        others += [over_y(part, step, shards_y) for part in bundles]
    table = jnp.asarray(backward_yz_table(*sizes))
    bias = bias.reshape(1, channels)
    partial = own_part(me, table, returned, convolved, bias, shards, shards_y)
    return last_part(me, table, others, partial, shards, shards_y)


def solution(mesh):
    placed = (P("gx", "gy", None, None), P(("gy", "gx"), None, None, None, None), P(), P())
    return jax.shard_map(
        body, mesh=mesh, in_specs=placed, out_specs=P("gx", "gy", None, None), check_vma=False
    )
```

```python
import functools
import math

import jax
import jax.numpy as jnp
import numpy as np
from jax import lax
from jax.experimental import pallas as pl
from jax.experimental.pallas import tpu as pltpu
from jax.sharding import PartitionSpec as P

MX = 64
MY = 16
MZ = 16


def frequencies(mode_count):
    position = np.arange(mode_count)
    return np.where(position < mode_count // 2, position, position - mode_count)


def wave(first, second, length, factor):
    turns = (np.asarray(first)[:, None] * np.asarray(second)[None, :]) % length
    angles = turns * (2.0 * math.pi / length)
    return (np.cos(angles) + 1j * np.sin(angles)) * factor


def rounded(values):
    return values.astype(np.float32).astype(jnp.bfloat16).astype(np.float64)


def item_modes(shards_x, shards_y, pairs):
    index = np.arange(shards_y * shards_x * pairs).reshape(shards_y, shards_x, pairs)
    return index // MZ, index % MZ


def forward_yz_table(shards_x, shards_y, pairs, cells_y, cells_z):
    full_y = shards_y * cells_y
    turn_z = wave(np.arange(MZ), np.arange(cells_z), cells_z, cells_z**-0.5)
    turn_z = rounded(turn_z.real) - 1j * rounded(turn_z.imag)
    turn_y = np.conj(wave(frequencies(MY), np.arange(full_y), full_y, full_y**-0.5))
    mode_y, mode_z = item_modes(shards_x, shards_y, pairs)
    table = np.empty((shards_y, shards_y, shards_x, pairs, 2, cells_y, cells_z), np.float32)
    for own in range(shards_y):
        rows = turn_y[:, own * cells_y : (own + 1) * cells_y]
        product = rows[mode_y][..., :, None] * turn_z[mode_z][..., None, :]
        table[own, :, :, :, 0] = product.real
        table[own, :, :, :, 1] = product.imag
    return table.reshape(shards_y, -1, cells_y * cells_z).astype(jnp.bfloat16)


def backward_yz_table(shards_x, shards_y, pairs, cells_y, cells_z):
    full_y = shards_y * cells_y
    turn_z = wave(np.arange(MZ), np.arange(cells_z), cells_z, MZ**-0.5)
    turn_z = rounded(turn_z.real) + 1j * rounded(turn_z.imag)
    turn_y = wave(frequencies(MY), np.arange(full_y), full_y, MY**-0.5)
    mode_y, mode_z = item_modes(shards_x, shards_y, pairs)
    table = np.empty((shards_y, shards_y, cells_y, cells_z, shards_x, pairs, 2), np.float32)
    for own in range(shards_y):
        rows = turn_y[:, own * cells_y : (own + 1) * cells_y]
        product = rows[mode_y][..., :, None] * turn_z[mode_z][..., None, :]
        product = np.moveaxis(product, (3, 4), (1, 2))
        table[own, ..., 0] = product.real
        table[own, ..., 1] = -product.imag
    return table.reshape(shards_y**2, cells_y * cells_z, -1).astype(jnp.bfloat16)


def forward_x_table(full_x):
    turn = np.conj(wave(frequencies(MX), np.arange(full_x), full_x, full_x**-0.5))
    parts = np.empty((2, MX, 2, 2, full_x), np.float32)
    parts[0, :, 0, 0], parts[0, :, 0, 1] = turn.real, -turn.imag
    parts[0, :, 1, 0], parts[0, :, 1, 1] = turn.imag, turn.real
    parts[1, :, 0] = -parts[0, :, 1]
    parts[1, :, 1] = parts[0, :, 0]
    return parts.reshape(2 * MX * 2, 2 * full_x).astype(jnp.bfloat16)


def backward_x_table(full_x):
    turn = wave(frequencies(MX), np.arange(full_x), full_x, MX**-0.5).T
    parts = np.empty((2, full_x, MX, 2), np.float32)
    parts[0, :, :, 0], parts[0, :, :, 1] = turn.real, -turn.imag
    parts[1, :, :, 0], parts[1, :, :, 1] = turn.imag, turn.real
    return parts.reshape(2 * full_x, MX * 2).astype(jnp.bfloat16)


def dot(left, right):
    return jnp.dot(left, right, preferred_element_type=jnp.float32)


def peer(index, step, count):
    if count & (count - 1) == 0:
        return index ^ step
    return lax.rem(index + step, count)


def origin(index, step, count):
    if count & (count - 1) == 0:
        return index ^ step
    return lax.rem(index + (count - step), count)


def far_first(count):
    return list(range(count - 1, -1, -1))


def place(me, shards):
    outer, inner = shards
    across = lax.rem(me, outer * inner)
    return lax.div(me, outer * inner), lax.div(across, inner), lax.rem(across, inner)


def in_vmem(count):
    return [pl.BlockSpec(memory_space=pltpu.VMEM)] * count


IN_SMEM = pl.BlockSpec(memory_space=pltpu.SMEM)


def transform(table, flow_at, cells_x, refs, pieces):
    inner, _, rows, channels = refs[0].shape[1:]
    block = inner * rows
    width = 2 if cells_x % 2 == 0 else 1
    for x in range(0, cells_x, width):
        columns = [flow_at(x + i) for i in range(width)]
        result = dot(table, jnp.concatenate(columns, axis=1))
        for i in range(width):
            part = result[:, i * channels : (i + 1) * channels]
            at = 0
            for ref, piece in zip(refs, pieces):
                for slot in range(len(piece)):
                    value = part[at : at + block].reshape(inner, rows, channels)
                    ref[slot, :, x + i] = value.astype(ref.dtype)
                    at += block


def send_kernel(shards, shards_y, pieces, step, me_ref, table_ref, flow_ref, *refs):
    *refs, table, flow, table_sems, flow_sems = refs
    refs, plane_refs = refs[: len(pieces)], refs[len(pieces) :]
    cells_x = flow.shape[0]
    outer, _ = shards
    block = refs[0].shape[1] * refs[0].shape[3]
    own_y, own, _ = place(me_ref[0], shards)
    owner = lax.rem(own_y + step, shards_y)
    copies = []
    for i, other in enumerate(step for piece in pieces for step in piece):
        start = (owner * outer + peer(own, other, outer)) * block
        source = table_ref.at[own_y, pl.ds(pl.multiple_of(start, block), block)]
        copies.append(
            pltpu.make_async_copy(source, table.at[pl.ds(i * block, block)], table_sems.at[i])
        )
    loads = [
        pltpu.make_async_copy(flow_ref.at[x], flow.at[x], flow_sems.at[x])
        for x in range(cells_x)
    ]
    for copy in copies + loads:
        copy.start()
    for copy in copies:
        copy.wait()

    def flow_at(x):
        loads[x].wait()
        return flow[x]

    transform(table[...], flow_at, cells_x, refs, pieces)
    if plane_refs:
        even = is_even(me_ref[0], shards)
        plane_refs[0][...] = flow[jnp.where(even, cells_x - 1, 0)]
        plane_refs[1][...] = flow[jnp.where(even, 0, cells_x - 1)]


def is_even(me, shards):
    _, own_outer, own_inner = place(me, shards)
    return lax.rem(own_outer * shards[1] + own_inner, 2) == 0


def keep_kernel(shards, shards_y, pieces, me_ref, table_ref, flow_ref, *refs):
    refs, (low, high) = refs[: len(pieces)], refs[len(pieces) :]
    cells_x, positions, _ = flow_ref.shape
    outer, _ = shards
    block = refs[0].shape[1] * refs[0].shape[3]
    own_y, own, _ = place(me_ref[0], shards)
    tables = []
    for other in (step for piece in pieces for step in piece):
        start = (own_y * outer + peer(own, other, outer)) * block
        tables.append(table_ref[own_y, pl.ds(pl.multiple_of(start, block), block), :])
    transform(
        jnp.concatenate(tables, axis=0), lambda x: flow_ref[x], cells_x, refs, pieces
    )
    cells_z = low.shape[1]
    low[...] = flow_ref[:, pl.ds(0, cells_z)]
    high[...] = flow_ref[:, pl.ds(positions - cells_z, cells_z)]


def forward_yz(me, table, flow, step, shards, shards_y, pieces, cells_z=0):
    cells_x, positions, channels = flow.shape
    outer, inner = shards
    rows = table.shape[1] // shards_y
    unit = (inner, cells_x, rows // (outer * inner), channels)
    dtype = jnp.bfloat16 if step else jnp.float32
    shapes = [jax.ShapeDtypeStruct((len(piece), *unit), dtype) for piece in pieces]
    if step == 1:
        shapes += [jax.ShapeDtypeStruct((positions, channels), flow.dtype)] * 2
    if step:
        kernel = functools.partial(send_kernel, shards, shards_y, pieces, step)
        specs = [pl.BlockSpec(memory_space=pltpu.HBM)] * 2
        scratch = [
            pltpu.VMEM((rows, positions), table.dtype),
            pltpu.VMEM(flow.shape, flow.dtype),
            pltpu.SemaphoreType.DMA((outer,)),
            pltpu.SemaphoreType.DMA((cells_x,)),
        ]
    else:
        kernel = functools.partial(keep_kernel, shards, shards_y, pieces)
        specs, scratch = in_vmem(2), []
        edge = jax.ShapeDtypeStruct((cells_x, cells_z, channels), flow.dtype)
        shapes += [edge] * 2
    return pl.pallas_call(
        kernel,
        in_specs=[IN_SMEM] + specs,
        out_specs=in_vmem(len(shapes)),
        out_shape=shapes,
        scratch_shapes=scratch,
        compiler_params=pltpu.CompilerParams(vmem_limit_bytes=(56 if step else 10) << 20),
        cost_estimate=pl.CostEstimate(
            flops=2 * rows * positions * cells_x * channels,
            bytes_accessed=2 * positions * (rows + cells_x * channels),
            transcendentals=0,
        ),
    )(me, table, flow)


def add_kernel(count, *refs):
    out_refs = refs[count:]
    for slot, out_ref in enumerate(out_refs):
        total = refs[0][slot]
        for ref in refs[1:count]:
            total = total + ref[slot].astype(jnp.float32)
        out_ref[...] = total.astype(out_ref.dtype)


def add_pieces(own, arrived):
    slots, *unit = own.shape
    return pl.pallas_call(
        functools.partial(add_kernel, 1 + len(arrived)),
        in_specs=in_vmem(1 + len(arrived)),
        out_specs=in_vmem(slots),
        out_shape=[jax.ShapeDtypeStruct(unit, jnp.bfloat16)] * slots,
        cost_estimate=pl.CostEstimate(flops=own.size, bytes_accessed=0, transcendentals=0),
        compiler_params=pltpu.CompilerParams(vmem_limit_bytes=10 << 20),
    )(own, *arrived)


def regroup_kernel(shards, chosen, me_ref, *refs):
    _, _, own = place(me_ref[0], shards)
    count = refs[0].shape[0]
    in_refs, out_refs = refs[:-count], refs[-count:]
    for step, out_ref in enumerate(out_refs):
        at = peer(own, step, count) if chosen else step
        for number, in_ref in enumerate(in_refs):
            out_ref[far_first(len(in_refs))[number]] = in_ref[at]


def regroup(me, arrays, shards, chosen):
    count, *unit = arrays[0].shape
    return pl.pallas_call(
        functools.partial(regroup_kernel, shards, chosen),
        in_specs=[IN_SMEM] + in_vmem(len(arrays)),
        out_specs=in_vmem(count),
        out_shape=[jax.ShapeDtypeStruct((len(arrays), *unit), arrays[0].dtype)] * count,
        cost_estimate=pl.CostEstimate(
            flops=arrays[0].size, bytes_accessed=0, transcendentals=0
        ),
        compiler_params=pltpu.CompilerParams(vmem_limit_bytes=10 << 20),
    )(me, *arrays)


def edge_kernel(
    choose, shards, me_ref, paired_ref, other_ref, low_ref, high_ref, out_ref
):
    cells_x, cells_z, _ = low_ref.shape
    rows = paired_ref.shape[0]
    own_y, _, _ = place(me_ref[0], shards)
    is_low = choose(own_y)
    even = is_even(me_ref[0], shards)
    start = pl.multiple_of(jnp.where(is_low, 0, rows - cells_z), cells_z)
    paired, other = (ref[pl.ds(start, cells_z), :] for ref in (paired_ref, other_ref))
    out_ref[0] = jnp.where(even, other, paired)
    out_ref[1 + cells_x] = jnp.where(even, paired, other)

    @pl.when(is_low)
    def _():
        out_ref[1 : 1 + cells_x] = low_ref[...]

    @pl.when(jnp.logical_not(is_low))
    def _():
        out_ref[1 : 1 + cells_x] = high_ref[...]


def y_edge(me, paired, other, low, high, shards, choose):
    cells_x, cells_z, channels = low.shape
    return pl.pallas_call(
        functools.partial(edge_kernel, choose, shards),
        in_specs=[IN_SMEM] + in_vmem(4),
        out_specs=in_vmem(1)[0],
        out_shape=jax.ShapeDtypeStruct((cells_x + 2, cells_z, channels), low.dtype),
        compiler_params=pltpu.CompilerParams(vmem_limit_bytes=10 << 20),
    )(me, paired, other, low, high)


def preload_kernel(first, weight_ref, out_ref, sems):
    count = out_ref.shape[0]
    pieces = sems.shape[0] // count
    modes = out_ref.shape[1] // pieces
    copies = []
    for i in range(count * pieces):
        item, at = i // pieces, pl.ds(i % pieces * modes, modes)
        copies.append(
            pltpu.make_async_copy(
                weight_ref.at[first + item, at], out_ref.at[item, at], sems.at[i]
            )
        )
    for copy in copies:
        copy.start()
    for copy in copies:
        copy.wait()


def preload(weight, pair, count):
    shape = (2 * count, *weight.shape[1:])
    return pl.pallas_call(
        functools.partial(preload_kernel, 2 * pair),
        in_specs=[pl.BlockSpec(memory_space=pltpu.HBM)],
        out_specs=in_vmem(1)[0],
        out_shape=jax.ShapeDtypeStruct(shape, weight.dtype),
        scratch_shapes=[pltpu.SemaphoreType.DMA((2 * 2 * count,))],
        compiler_params=pltpu.CompilerParams(vmem_limit_bytes=36 << 20),
        cost_estimate=pl.CostEstimate(
            flops=0, bytes_accessed=2 * math.prod(shape), transcendentals=0
        ),
    )(weight)


def mixing_kernel(shards, loaded, me_ref, *refs):
    outer, inner = shards
    row_refs, refs = refs[:inner], refs[inner:]
    forward_ref, backward_ref, weight_ref, *refs = refs
    loaded_refs, refs = refs[:loaded], refs[loaded:]
    loaded = sum(ref.shape[0] // 2 for ref in loaded_refs)
    out_refs, (held, sems, wide, left, mixed) = refs[:inner], refs[inner:]

    channels = wide.shape[1]
    _, cells_x, item_rows, _ = row_refs[0].shape
    pairs = item_rows // 2
    full_x = outer * inner * cells_x
    half = channels // 2
    span = 2 * MX
    block = cells_x * item_rows
    _, own_outer, own_inner = place(me_ref[0], shards)

    def copy(pair):
        slot = pair - loaded
        return pltpu.make_async_copy(
            weight_ref.at[pl.ds(2 * pair, 2)], held.at[slot], sems.at[slot]
        )

    for pair in range(loaded, pairs):
        copy(pair).start()

    def rows_of(outer_index, inner_index):
        start = pl.multiple_of((outer_index * inner + inner_index) * block, block)
        return pl.ds(start, block)

    for number, step in enumerate(far_first(inner)):
        source = origin(own_inner, step, inner)
        for slot in range(outer):
            value = row_refs[number][slot].reshape(block, channels)
            at = rows_of(origin(own_outer, slot, outer), source)
            wide[at, :] = value.astype(jnp.float32)
    low = lax.broadcasted_iota(jnp.int32, (span, channels), 1) < half
    width = 2 if pairs % 2 == 0 else 1
    for first_pair in range(0, pairs, width):
        columns = []
        for pair in range(first_pair, first_pair + width):
            parts = [wide[pl.ds(2 * pair + p, full_x, stride=item_rows), :] for p in range(2)]
            columns.append(jnp.concatenate(parts, axis=0).astype(jnp.bfloat16))
        both = dot(forward_ref[...], jnp.concatenate(columns, axis=1))
        for i in range(width):
            value = both[:span, i * channels : (i + 1) * channels]
            turned = both[span:, i * channels : (i + 1) * channels]
            first = jnp.where(low, value, pltpu.roll(turned, half, axis=1))
            second = jnp.where(low, pltpu.roll(value, half, axis=1), turned)
            rows = pl.ds((first_pair + i) * span, span)
            left[rows, :channels] = first.astype(left.dtype)
            left[rows, channels:] = second.astype(left.dtype)

    group = 16
    row = lax.broadcasted_iota(jnp.int32, (group, channels), 0) // 2

    def mix(pair, tile_of):
        for step in range(span // group):
            start = pair * span + step * group
            lhs = left[pl.ds(start, group), :]
            gathered = jnp.zeros((group, channels), jnp.float32)
            for i in range(0, group // 2, 2):
                mode = step * (group // 2) + i
                tiles = [
                    jnp.concatenate([tile_of(h, mode + k) for h in range(2)], axis=0)
                    for k in range(2)
                ]
                product = dot(lhs, jnp.concatenate(tiles, axis=1))
                for k in range(2):
                    gathered = jnp.where(
                        row == i + k, product[:, k * channels : (k + 1) * channels], gathered
                    )
            mixed[pl.ds(start, group), :] = gathered.astype(mixed.dtype)

    pair = 0
    for ref in loaded_refs:
        for i in range(ref.shape[0] // 2):
            mix(pair, lambda h, mode, ref=ref, i=i: ref[2 * i + h, mode])
            pair += 1
    for pair in range(loaded, pairs):
        copy(pair).wait()
        mix(pair, lambda h, mode, pair=pair: held[pair - loaded, h, mode])

    for first_pair in range(0, pairs, width):
        columns = [
            mixed[pl.ds(pair * span, span), :] for pair in range(first_pair, first_pair + width)
        ]
        result = dot(backward_ref[...], jnp.concatenate(columns, axis=1))
        for i in range(width):
            for p in range(2):
                rows = pl.ds(2 * (first_pair + i) + p, full_x, stride=item_rows)
                wide[rows, :] = result[
                    p * full_x : (p + 1) * full_x, i * channels : (i + 1) * channels
                ]
    for step in range(inner):
        target = peer(own_inner, step, inner)
        for slot in range(outer):
            value = wide[rows_of(peer(own_outer, slot, outer), target), :]
            value = value.reshape(cells_x, item_rows, channels)
            out_refs[step][slot] = value.astype(out_refs[step].dtype)


def mixing(me, rows, forward_x, backward_x, weight, loaded, shards):
    outer, inner = shards
    _, cells_x, item_rows, channels = rows[0].shape
    pairs = item_rows // 2
    row_count = outer * inner * cells_x * item_rows
    streamed = pairs - sum(part.shape[0] // 2 for part in loaded)
    return pl.pallas_call(
        functools.partial(mixing_kernel, shards, len(loaded)),
        in_specs=[IN_SMEM]
        + in_vmem(inner + 2)
        + [pl.BlockSpec(memory_space=pltpu.HBM)]
        + in_vmem(len(loaded)),
        out_specs=in_vmem(inner),
        out_shape=[jax.ShapeDtypeStruct(rows[0].shape, jnp.bfloat16)] * inner,
        scratch_shapes=[
            pltpu.VMEM((streamed, 2, *weight.shape[1:]), weight.dtype),
            pltpu.SemaphoreType.DMA((streamed,)),
            pltpu.VMEM((row_count, channels), jnp.float32),
            pltpu.VMEM((pairs * 2 * MX, 2 * channels), jnp.bfloat16),
            pltpu.VMEM((pairs * 2 * MX, channels), jnp.bfloat16),
        ],
        compiler_params=pltpu.CompilerParams(vmem_limit_bytes=20 << 20),
        cost_estimate=pl.CostEstimate(
            flops=8 * weight.size, bytes_accessed=2 * weight.size, transcendentals=0
        ),
    )(me, *rows, forward_x, backward_x, weight, *loaded)


def convolution_kernel(x, cells_x, width, shards, shards_y, me_ref, *refs):
    flow_ref, paired_ref, other_ref, front_ref, back_ref, kernel_ref, out_ref, padded = refs
    _, cells_y, cells_z, channels = out_ref.shape
    own_y, _, _ = place(me_ref[0], shards)
    even = is_even(me_ref[0], shards)
    for plane in range(width + 2):
        p = x + plane - 1
        row = front_ref[p + 1]
        padded[plane, 0] = jnp.where(own_y > 0, row, jnp.zeros_like(row))
        row = back_ref[p + 1]
        last = own_y == shards_y - 1
        padded[plane, cells_y + 1] = jnp.where(last, jnp.zeros_like(row), row)
        if 0 <= p < cells_x:
            padded[plane, 1 : cells_y + 1] = flow_ref[p]
        else:
            use_paired = jnp.logical_not(even) if p < 0 else even

            @pl.when(use_paired)
            def _(plane=plane):
                padded[plane, 1 : cells_y + 1] = paired_ref[...]

            @pl.when(jnp.logical_not(use_paired))
            def _(plane=plane):
                padded[plane, 1 : cells_y + 1] = other_ref[...]

    rows = 16 if cells_y % 16 == 0 else 1
    columns = [(k, d) for k in range(width) for d in range(3)]
    columns = [columns[i : i + 2] for i in range(0, len(columns), 2)]
    none = jnp.zeros((channels, channels), kernel_ref.dtype)

    def chunk(index, carry):
        y = index * rows
        products = {}
        for group in columns:
            blocks, kernels = [], []
            for p in range(width + 2):
                if not any(0 <= p - k < 3 for k, _ in group):
                    continue
                for b in range(3):
                    part = padded[p, pl.ds(y + b, rows)]
                    blocks.append(part.reshape(rows * cells_z, channels))
                    parts = [
                        kernel_ref[p - k, b, d] if 0 <= p - k < 3 else none for k, d in group
                    ]
                    kernels.append(jnp.concatenate(parts, axis=1))
            product = dot(jnp.concatenate(blocks, axis=1), jnp.concatenate(kernels, axis=0))
            for i, column in enumerate(group):
                part = product[:, i * channels : (i + 1) * channels]
                products[column] = part.reshape(rows, cells_z, channels)
        z = lax.broadcasted_iota(jnp.int32, (rows, cells_z, channels), 1)
        for k in range(width):
            before = jnp.where(z == 0, 0.0, pltpu.roll(products[k, 0], 1, axis=1))
            after = pltpu.roll(products[k, 2], cells_z - 1, axis=1)
            after = jnp.where(z == cells_z - 1, 0.0, after)
            total = before + products[k, 1] + after
            out_ref[k, pl.ds(y, rows)] = total.astype(out_ref.dtype)
        return carry

    lax.fori_loop(0, cells_y // rows, chunk, 0)


def convolution(me, x, width, flow, halos, kernel, shards, shards_y):
    cells_x, cells_y, cells_z, channels = flow.shape
    shape = (width, cells_y, cells_z, channels)
    return pl.pallas_call(
        functools.partial(convolution_kernel, x, cells_x, width, shards, shards_y),
        in_specs=[IN_SMEM] + in_vmem(2 + len(halos)),
        out_specs=in_vmem(1)[0],
        out_shape=jax.ShapeDtypeStruct(shape, jnp.bfloat16),
        scratch_shapes=[pltpu.VMEM((width + 2, cells_y + 2, cells_z, channels), flow.dtype)],
        compiler_params=pltpu.CompilerParams(vmem_limit_bytes=14 << 20),
        cost_estimate=pl.CostEstimate(
            flops=3 * 27 * width * cells_y * cells_z * channels * channels,
            bytes_accessed=10 * cells_y * cells_z * channels,
            transcendentals=0,
        ),
    )(me, flow, *halos, kernel)


def bundled_slots(count):
    slots = [0] + far_first(count)[:-1]
    cut = (count + 1) // 2
    return [part for part in (slots[:cut], slots[cut:]) if part]


def bundle_kernel(*refs):
    *in_refs, out_ref = refs
    for i, ref in enumerate(in_refs):
        out_ref[i] = ref[...]


def bundle(arrays):
    shape = (len(arrays), *arrays[0].shape)
    return pl.pallas_call(
        bundle_kernel,
        in_specs=in_vmem(len(arrays)),
        out_specs=in_vmem(1)[0],
        out_shape=jax.ShapeDtypeStruct(shape, arrays[0].dtype),
        cost_estimate=pl.CostEstimate(
            flops=math.prod(shape), bytes_accessed=0, transcendentals=0
        ),
        compiler_params=pltpu.CompilerParams(vmem_limit_bytes=10 << 20),
    )(*arrays)


def gather_pieces(me, shards, pieces, held):
    outer, inner = shards
    _, own_outer, own_inner = place(me, shards)
    for number, slot, ref in pieces:
        cells_x, rows = ref.shape[1:3]
        source = (number * outer + origin(own_outer, slot, outer)) * inner
        for part in range(inner):
            at = (source + origin(own_inner, part, inner)) * rows
            for x in range(cells_x):
                held[x, pl.ds(pl.multiple_of(at, rows), rows), :] = ref[part, x]


def inverse(me, shards, shards_y, steps, table_ref, held, part, x, width, positions):
    own_y, _, _ = place(me, shards)
    columns = [held[x + i] for i in range(width)]
    depth = table_ref.shape[2]
    total = None
    for number, step in enumerate(steps):
        source = lax.rem(own_y + (shards_y - step), shards_y)
        rows = pl.ds(pl.multiple_of(part * positions, positions), positions)
        table = table_ref[own_y * shards_y + source, rows, :]
        block = [column[number * depth : (number + 1) * depth] for column in columns]
        product = dot(table, jnp.concatenate(block, axis=1))
        total = product if total is None else total + product
    return total


def own_part_kernel(shards, shards_y, me_ref, table_ref, *refs):
    *piece_refs, bias_ref, out_ref, held = refs
    cells_x, cells_y, cells_z, channels = out_ref.shape
    width = 2 if cells_x % 2 == 0 else 1
    count = -(-cells_x // width)
    piece_refs, convolved_refs = piece_refs[:-count], piece_refs[-count:]
    slots = far_first(shards[0])
    gather_pieces(me_ref[0], shards, [(0, *p) for p in zip(slots, piece_refs)], held)
    bias = bias_ref[...]
    rows = 4 if cells_y % 4 == 0 else 1
    positions = rows * cells_z

    def chunk(part, carry):
        for x in range(0, cells_x, width):
            total = inverse(
                me_ref[0], shards, shards_y, [0], table_ref, held, part, x, width, positions
            )
            for i in range(width):
                spectral = total[:, i * channels : (i + 1) * channels]
                convolved = convolved_refs[x // width][i, pl.ds(part * rows, rows)]
                value = spectral.reshape(rows, cells_z, channels) + convolved + bias
                out_ref[x + i, pl.ds(part * rows, rows)] = value
        return carry

    lax.fori_loop(0, cells_y // rows, chunk, 0)


def last_part_kernel(shards, shards_y, me_ref, table_ref, *refs):
    *bundle_refs, partial_ref, out_ref, held = refs
    cells_x, cells_y, cells_z, channels = out_ref.shape
    bundles = bundled_slots(shards[0])
    steps = list(range(1, shards_y))
    width = 2 if cells_x % 2 == 0 else 1
    part = pl.program_id(0)

    @pl.when(part == 0)
    def _():
        pieces = []
        for i, ref in enumerate(bundle_refs):
            number, bundle = divmod(i, len(bundles))
            pieces += [(number, slot, ref.at[j]) for j, slot in enumerate(bundles[bundle])]
        gather_pieces(me_ref[0], shards, pieces, held)

    for x in range(0, cells_x, width):
        total = inverse(
            me_ref[0], shards, shards_y, steps, table_ref, held, part, x, width,
            cells_y * cells_z,
        )
        for i in range(width):
            spectral = total[:, i * channels : (i + 1) * channels]
            value = partial_ref[x + i, pl.ds(part * cells_y, cells_y)]
            value = value + spectral.reshape(cells_y, cells_z, channels)
            out_ref[x + i] = jax.nn.gelu(value, approximate=True).astype(out_ref.dtype)


def own_part(me, table, pieces, convolved, bias, shards, shards_y):
    width, cells_y, cells_z, channels = convolved[0].shape
    shape = (width * len(convolved), cells_y, cells_z, channels)
    depth = table.shape[2]
    return pl.pallas_call(
        functools.partial(own_part_kernel, shards, shards_y),
        in_specs=[IN_SMEM] + in_vmem(2 + len(pieces) + len(convolved)),
        out_specs=in_vmem(1)[0],
        out_shape=jax.ShapeDtypeStruct(shape, jnp.float32),
        scratch_shapes=[pltpu.VMEM((shape[0], depth, channels), jnp.bfloat16)],
        compiler_params=pltpu.CompilerParams(vmem_limit_bytes=14 << 20),
        cost_estimate=pl.CostEstimate(
            flops=2 * math.prod(shape) * depth,
            bytes_accessed=6 * math.prod(shape),
            transcendentals=0,
        ),
    )(me, table, *pieces, *convolved, bias)


def last_part(me, table, pieces, partial, shards, shards_y):
    cells_x, cells_y, cells_z, channels = partial.shape
    parts = 2 if cells_y % 2 == 0 else 1
    block = (cells_x, cells_y // parts, cells_z, channels)
    depth = table.shape[2] * (shards_y - 1)
    return pl.pallas_call(
        functools.partial(last_part_kernel, shards, shards_y),
        grid_spec=pltpu.PrefetchScalarGridSpec(
            num_scalar_prefetch=1,
            grid=(parts,),
            in_specs=in_vmem(2 + len(pieces)),
            out_specs=pl.BlockSpec(block, lambda i, me: (0, i, 0, 0)),
            scratch_shapes=[pltpu.VMEM((cells_x, depth, channels), jnp.bfloat16)],
        ),
        out_shape=jax.ShapeDtypeStruct(partial.shape, jnp.bfloat16),
        compiler_params=pltpu.CompilerParams(vmem_limit_bytes=14 << 20),
        cost_estimate=pl.CostEstimate(
            flops=2 * partial.size * depth,
            bytes_accessed=6 * partial.size,
            transcendentals=partial.size,
        ),
    )(me, table, *pieces, partial)


def with_halo(array, sides, width):
    for axis, dim in sides:
        size, length = (lax.axis_size(axis), array.shape[dim])
        up = [(i, (i + 1) % size) for i in range(size - 1)]
        down = [(j, i) for i, j in up]
        last = lax.slice_in_dim(array, length - width, length, axis=dim)
        initial = lax.slice_in_dim(array, 0, width, axis=dim)
        before = lax.ppermute(last, axis, up)
        after = lax.ppermute(initial, axis, down)
        array = jnp.concatenate([before, array, after], axis=dim)
    return array


def signed_modes(mode_count):
    position = jnp.arange(mode_count, dtype=jnp.int32)
    return jnp.where(position < mode_count // 2, position, position - mode_count)


def angle_grid(first, second, length):
    phase_turns = first[:, None] * second[None, :] % length
    return phase_turns.astype(jnp.float32) * (2.0 * math.pi / length)


def real_table(first, second, length, factor):
    angles = angle_grid(first, second, length)
    return jnp.stack([jnp.cos(angles) * factor, -jnp.sin(angles) * factor])


def complex_table(first, second, length, factor, direction):
    angles = angle_grid(first, second, length)
    cosine = jnp.cos(angles) * factor
    sine_part = jnp.sin(angles) * factor
    return jnp.stack(
        [jnp.stack([cosine, direction * sine_part]), jnp.stack([-direction * sine_part, cosine])]
    )


def split_pair_spectral(flow_field, spectral_weight):
    highest = lax.Precision.HIGHEST
    cells_x, cells_y, cells_z, channels = flow_field.shape
    count_x = lax.axis_size("gx")
    count_y = lax.axis_size("gy")
    full_x = cells_x * count_x
    full_y = cells_y * count_y
    item_count = spectral_weight.shape[0]
    local_y = lax.axis_index("gy") * cells_y + jnp.arange(cells_y, dtype=jnp.int32)
    grid_x = jnp.arange(full_x, dtype=jnp.int32)
    grid_z = jnp.arange(cells_z, dtype=jnp.int32)
    modes_z = jnp.arange(MZ, dtype=jnp.int32)
    forward_z = real_table(grid_z, modes_z, cells_z, cells_z ** (-0.5)).astype(jnp.bfloat16)
    z_spectrum = jnp.einsum(
        "xyzc,pzk->pxykc", flow_field, forward_z, preferred_element_type=jnp.float32
    )
    columns = lax.all_to_all(
        z_spectrum.astype(jnp.bfloat16), "gy", split_axis=4, concat_axis=2, tiled=True
    ).astype(z_spectrum.dtype)
    whole_y = jnp.arange(full_y, dtype=jnp.int32)
    forward_full = complex_table(whole_y, signed_modes(MY), full_y, full_y ** (-0.5), -1.0)
    y_spectrum = jnp.einsum("pxykc,pqyj->qxjkc", columns, forward_full, precision=highest)
    owned = lax.all_to_all(
        y_spectrum.astype(jnp.bfloat16), "gy", split_axis=2, concat_axis=4, tiled=True
    ).astype(y_spectrum.dtype)
    owned_modes = owned.reshape(2, cells_x, count_x, item_count, channels // 2)
    gathered_rows = lax.all_to_all(
        owned_modes.astype(jnp.bfloat16), "gx", split_axis=2, concat_axis=1, tiled=True
    ).astype(owned_modes.dtype)
    gathered_rows = gathered_rows.reshape(2, full_x, item_count, channels // 2)
    forward_x = complex_table(grid_x, signed_modes(MX), full_x, full_x ** (-0.5), -1.0)
    x_spectrum = jnp.einsum("pxjc,pqxm->qmjc", gathered_rows, forward_x, precision=highest).astype(
        jnp.bfloat16
    )
    products = jnp.einsum(
        "pmjc,jmqco->pqmjo", x_spectrum, spectral_weight, preferred_element_type=jnp.float32
    )
    mixed_modes = jnp.stack([products[0, 0] - products[1, 1], products[0, 1] + products[1, 0]])
    backward_x = complex_table(signed_modes(MX), grid_x, full_x, MX ** (-0.5), 1.0)
    inverse_x = jnp.einsum("pmjc,pqmx->qxjc", mixed_modes, backward_x, precision=highest)
    inverse_x = inverse_x.reshape(2, full_x, 1, item_count, channels)
    returned = lax.all_to_all(
        inverse_x.astype(jnp.bfloat16), "gx", split_axis=1, concat_axis=2, tiled=True
    ).astype(inverse_x.dtype)
    band_rows = MY // count_y
    summed = returned.reshape(2, cells_x, band_rows * MZ, 2, channels).sum(axis=3)
    summed = summed.reshape(2, cells_x, band_rows, MZ, channels)
    coefficients = lax.all_gather(summed.astype(jnp.bfloat16), "gy", axis=2, tiled=True).astype(
        summed.dtype
    )
    backward_y = complex_table(signed_modes(MY), local_y, full_y, MY ** (-0.5), 1.0)
    y_inverse = jnp.einsum("pxjkc,pqjy->qxykc", coefficients, backward_y, precision=highest).astype(
        jnp.bfloat16
    )
    backward_z = real_table(modes_z, grid_z, cells_z, MZ ** (-0.5)).astype(jnp.bfloat16)
    return jnp.einsum("pxykc,pkz->xyzc", y_inverse, backward_z, preferred_element_type=jnp.float32)


def split_pair_convolve(flow_field, conv_weight):
    cells_x, cells_y, cells_z, channels = flow_field.shape
    padded = with_halo(flow_field, (("gx", 0), ("gy", 1)), 1)
    padded = jnp.pad(padded, ((0, 0), (0, 0), (1, 1), (0, 0)))
    stacked = jnp.concatenate(
        [padded[:, :, 0:cells_z], padded[:, :, 1 : cells_z + 1], padded[:, :, 2 : cells_z + 2]],
        axis=3,
    )
    kernel = conv_weight.reshape(3, 3, 3 * channels, channels)
    accumulated = jnp.zeros((cells_x, cells_y, cells_z, channels), jnp.float32)
    for shift_x in range(3):
        for shift_y in range(3):
            accumulated = accumulated + jnp.dot(
                stacked[shift_x : shift_x + cells_x, shift_y : shift_y + cells_y],
                kernel[shift_x, shift_y],
                preferred_element_type=jnp.float32,
            )
    return accumulated


def neighbours(first, last, axis):
    size = lax.axis_size(axis)
    up = [(i, i + 1) for i in range(size - 1)]
    down = [(i + 1, i) for i in range(size - 1)]
    return lax.ppermute(last, axis, up), lax.ppermute(first, axis, down)


def with_neighbour(array, start, axis):
    size = lax.axis_size(axis)
    pairs = [(i, i + 1) for i in range(start, size - 1, 2)]
    return lax.ppermute(array, axis, pairs + [(j, i) for i, j in pairs])


def exchange(array, step, shards, along_outer):
    outer, inner = shards
    pairs = []
    for i in range(outer * inner):
        a, b = divmod(i, inner)
        count, own = (outer, a) if along_outer else (inner, b)
        to = own ^ step if count & (count - 1) == 0 else (own + step) % count
        pairs.append((i, to * inner + b if along_outer else a * inner + to))
    return lax.ppermute(array, "gx", pairs)


def over_y(array, step, shards_y):
    return lax.ppermute(array, "gy", [(i, (i + step) % shards_y) for i in range(shards_y)])


def body(flow, spectral_weight, conv_weight, bias):
    cells_x, cells_y, cells_z, channels = flow.shape
    shards_x, shards_y = lax.axis_size("gx"), lax.axis_size("gy")
    items = spectral_weight.shape[0]
    pairs = items // 2
    if items % 2 or shards_y < 2:
        spectral = split_pair_spectral(flow, spectral_weight)
        convolved = split_pair_convolve(flow, conv_weight)
        return jax.nn.gelu(spectral + convolved + bias, approximate=True).astype(jnp.bfloat16)

    barrier = lax.optimization_barrier
    inner = max(d for d in range(1, shards_x + 1) if shards_x % d == 0 and d * d <= shards_x)
    outer = shards_x // inner
    shards = (outer, inner)
    me = lax.axis_index(("gy", "gx")).astype(jnp.int32).reshape(1)
    sizes = (shards_x, shards_y, pairs, cells_y, cells_z)
    full_x = cells_x * shards_x
    weight = spectral_weight.reshape(items, MX, channels, channels)
    early = pairs // 4

    table = jnp.asarray(forward_yz_table(*sizes))
    columns = flow.reshape(cells_x, cells_y * cells_z, channels)
    order = far_first(outer)
    cut = (outer + 1) // 2
    pieces = [piece for piece in (order[:cut], order[cut:]) if piece]
    arrived = [[] for _ in pieces]
    for step in range(1, shards_y):
        sent = forward_yz(me, table, columns, step, shards, shards_y, pieces)
        sent, columns, weight = barrier((sent, columns, weight))
        for into, piece in zip(arrived, sent):
            into.append(over_y(piece, step, shards_y))
        if step == 1:
            ends = sent[len(pieces) :]
            planes = [with_neighbour(end, start, "gx") for start, end in enumerate(ends)]
    loaded = [preload(weight, 0, early // 2)] if early > 1 else []
    loaded, columns = barrier((loaded, columns))
    kept = forward_yz(me, table, columns, 0, shards, shards_y, pieces, cells_z)
    kept, (low, high) = kept[: len(pieces)], kept[len(pieces) :]

    by_outer = []
    for piece, own, parts in zip(pieces, kept, arrived):
        for step, total in zip(piece, add_pieces(own, parts)):
            by_outer.append(exchange(total, step, shards, True) if step else total)
    if early:
        loaded.append(preload(weight, early // 2, early))
    by_outer, loaded, weight = barrier((by_outer[::-1], loaded, weight))
    by_inner = regroup(me, by_outer[::-1], shards, True)
    by_inner, weight = barrier((by_inner, weight))
    rows = [
        exchange(by_inner[step], step, shards, False) if step else by_inner[0]
        for step in far_first(inner)
    ]
    if early:
        loaded.append(preload(weight, early + early // 2, early))

    rows, loaded, planes = barrier((rows, loaded, planes))
    if shards_y == 2:
        edge = y_edge(me, *planes, low, high, shards, lambda own: own > 0)
        front = back = over_y(edge, 1, shards_y)
    else:
        ends = [
            y_edge(me, *planes, low, high, shards, lambda own, limit=limit: own < limit)
            for limit in (shards_y, 0)
        ]
        front, back = neighbours(*ends, "gy")
    returned = mixing(
        me,
        rows,
        jnp.asarray(forward_x_table(full_x)),
        jnp.asarray(backward_x_table(full_x)),
        weight,
        loaded,
        shards,
    )
    returned, front, back = barrier((list(returned), front, back))
    planes = [plane.reshape(cells_y, cells_z, channels) for plane in planes]
    halos = (*planes, front, back)
    width = 2 if cells_x % 2 == 0 else 1
    convolved = [
        convolution(me, x, width, flow, halos, conv_weight, shards, shards_y)
        for x in range(0, cells_x, width)
    ]

    returned = [
        exchange(returned[step], step, shards, False) if step else returned[0]
        for step in far_first(inner)
    ]
    returned, convolved[0] = barrier((returned, convolved[0]))
    returned = regroup(me, returned, shards, False)
    returned = [
        exchange(returned[step], step, shards, True) if step else returned[0]
        for step in far_first(outer)
    ]
    returned[0], convolved[-1] = barrier((returned[0], convolved[-1]))
    by_slot = dict(zip(far_first(outer), returned))
    bundles = [bundle([by_slot[slot] for slot in slots]) for slots in bundled_slots(outer)]
    others = []
    for step in range(1, shards_y):
        others += [over_y(part, step, shards_y) for part in bundles]
    table = jnp.asarray(backward_yz_table(*sizes))
    bias = bias.reshape(1, channels)
    partial = own_part(me, table, returned, convolved, bias, shards, shards_y)
    return last_part(me, table, others, partial, shards, shards_y)


def solution(mesh):
    placed = (P("gx", "gy", None, None), P(("gy", "gx"), None, None, None, None), P(), P())
    return jax.shard_map(
        body, mesh=mesh, in_specs=placed, out_specs=P("gx", "gy", None, None), check_vma=False
    )
```
